32 devices in a mesh: wall: 4 (over z), span: 8 (over y, x, core).
Axes of the slice: x: 2, y: 2, z: 4, core: 2. Of those that a mesh axis runs over, the one named last changes fastest.
Arguments:
- velocity: float32 [3, 4, 1024, 1024], P(None, None, 'wall', 'span'), may hold values from -6 to 6
- lower_weight: float32 [4, 1024, 1024], P(None, 'wall', 'span'), may hold values from 1000 to 100000
- upper_weight: float32 [4, 1024, 1024], P(None, 'wall', 'span'), may hold values from 1000 to 100000
- forces: float32 [3, 4, 8, 8, 4, 768], P(None, 'wall', 'span'), may hold values from -6 to 6
- cells: int32 [4, 8, 8, 4, 768], P('wall', 'span'), may hold values from 0 to 32767
- counts: int32 [4, 8, 8, 4], P('wall', 'span'), may hold values from 1 to 768, as said below
Outputs:
- velocity_next: float32 [3, 4, 1024, 1024], P(None, None, 'wall', 'span')
- deposit: bfloat16 [3, 4, 1024, 1024], P(None, None, 'wall', 'span')
The draws below stay inside these ranges and needn't reach their ends.
Inputs may be any that keep to these rules, and one draw needn't show every extreme that they name: `counts`: in every wall row one destination receives 768 live slots from every sender in one plane.
All inputs are finite; a program needn't handle non-finite values.
Results may differ from the reference program's by a relative error of at most 0.0024.
Values sent between devices are 32-bit elements; how exact they have to be, the bound alone decides.
No kernel may reach another device: no remote copies, remote signals or barrier semaphores. Data moves between devices by JAX's collectives and lax.ppermute only.
A program may use at most 64 MiB of HBM per device.

```python
import math
import jax
import jax.numpy as jnp
from jax import lax

NY = 1024
CZ = 128
X = 4
CAPX = 768
CY = 256
NZ = 1024
N_WALL = 4
N_SPAN = 8


def draw_counts(key, part):
    key_dense, key_count, key_dest, key_plane = jax.random.split(key, 4)
    shape = (N_WALL, N_SPAN, N_SPAN, X)
    dense = jax.random.randint(key_dense, (N_WALL, N_SPAN, 1, 1), 0, 4) == 0
    ceiling = jnp.where(dense, CAPX + 1, CAPX // 3 + 1)
    drawn = jax.random.randint(key_count, shape, 1, jnp.broadcast_to(ceiling, shape))
    chosen_dest = jax.random.randint(key_dest, (N_WALL, 1, 1, 1), 0, N_SPAN)
    chosen_plane = jax.random.randint(key_plane, (N_WALL, 1, 1, 1), 0, X)
    dest_index = lax.broadcasted_iota(jnp.int32, shape, 1)
    plane_index = lax.broadcasted_iota(jnp.int32, shape, 3)
    filled = (dest_index == chosen_dest) & (plane_index == chosen_plane)
    return jnp.where(filled, CAPX, drawn).astype(jnp.int32)


def set_ends(result, own_key, low, largest):
    longest = result.shape.index(max(result.shape))
    spots = []
    for shift in (0, 1):
        where = [jax.random.randint(jax.random.fold_in(own_key, axis), (), 0, length) for axis, length in enumerate(result.shape)]
        where[longest] = (where[longest] + shift) % result.shape[longest]
        spots.append(tuple(where))
    return result.at[spots[0]].set(low).at[spots[1]].set(largest)


def levels(rng, dims, cuts, low, high):
    def one(dim, shards_of):
        steps = jax.random.uniform(jax.random.fold_in(jax.random.fold_in(rng, 6), dim), (shards_of,), jnp.float32, low / len(cuts), high / len(cuts))
        return jnp.repeat(jnp.exp(steps), dims[dim] // shards_of).reshape((-1,) + (1,) * (len(dims) - dim - 1))

    factor_of = one(*cuts[0])
    for cut in cuts[1:]:
        factor_of = factor_of * one(*cut)
    return factor_of


def gaussian(stream_key, shape, width, most, shards=(), kind=jnp.bfloat16):
    array = width * jax.random.normal(stream_key, shape, jnp.float32)
    if shards:
        array = array * levels(stream_key, shape, shards, -0.22, 0.18)
    return jnp.clip(array, -most, most).astype(kind)


def setup_inputs(seed: int = 0) -> dict:
    keys = jax.random.split(jax.random.key(seed), 7)
    velocity = gaussian(keys[0], (3, X, NY, NZ), 1.0, 6.0, ((2, 4), (3, 8)), jnp.float32)
    lower_weight = jnp.clip(jnp.exp(math.log(100000.0) - 4.6051702 * jax.random.uniform(keys[1], (X, NY, NZ), jnp.float32) ** levels(keys[1], (X, NY, NZ), ((1, 4), (2, 8)), -0.2, 0.2)), 1000.0, 100000.0)
    upper_weight = jnp.clip(jnp.exp(math.log(100000.0) - 4.6051702 * jax.random.uniform(keys[2], (X, NY, NZ), jnp.float32) ** levels(keys[2], (X, NY, NZ), ((1, 4), (2, 8)), -0.2, 0.2)), 1000.0, 100000.0)
    forces = gaussian(keys[3], (3, N_WALL, N_SPAN, N_SPAN, X, CAPX), 1.0, 6.0, ((1, 4), (2, 8)), jnp.float32)
    cells = set_ends(jax.random.randint(keys[4], (N_WALL, N_SPAN, N_SPAN, X, CAPX), 0, CY * CZ), jax.random.fold_in(keys[4], 1), 0, (CY * CZ) - 1).astype(jnp.int32)
    counts = draw_counts(jax.random.fold_in(keys[6], 71), 0)
    return {"velocity": velocity, "lower_weight": lower_weight, "upper_weight": upper_weight, "forces": forces, "cells": cells, "counts": counts}


diffusion_number = 0.2


def deposit_forces(forces, cells, counts):
    moved = jnp.transpose(forces, (0, 1, 3, 2, 4, 5))
    slot = jnp.arange(CAPX, dtype=jnp.int32)
    live = slot[None, None, None, None, :] < counts[..., None]
    plane = jnp.arange(X, dtype=jnp.int32)[None, None, None, :, None]
    wall_row = jnp.arange(N_WALL, dtype=jnp.int32)[:, None, None, None, None]
    span_col = jnp.arange(N_SPAN, dtype=jnp.int32)[None, :, None, None, None]
    height = wall_row * CY + cells // CZ
    across = span_col * CZ + cells % CZ
    target = (plane * NY + height) * NZ + across
    target = jnp.broadcast_to(target, live.shape).reshape(-1).astype(jnp.int32)
    total = X * NY * NZ

    def one_component(component):
        masked = jnp.where(live, component, jnp.zeros_like(component))
        return jax.ops.segment_sum(masked.reshape(-1), target, num_segments=total)

    return jnp.stack([one_component(moved[index]) for index in range(3)]).reshape(3, X, NY, NZ)


def solve_columns(lower_weight, upper_weight, rhs):
    heights = jnp.arange(NY, dtype=jnp.int32)[None, :, None]
    sub = jnp.where(heights == 0, jnp.zeros_like(lower_weight), -lower_weight)
    sup = jnp.where(heights == NY - 1, jnp.zeros_like(upper_weight), -upper_weight)
    diag = 1.0 + lower_weight + upper_weight
    sub_rows = jnp.moveaxis(sub, 1, 0)
    diag_rows = jnp.moveaxis(diag, 1, 0)
    sup_rows = jnp.moveaxis(sup, 1, 0)
    rhs_rows = jnp.moveaxis(rhs, 2, 0)

    def forward(carry, row):
        ratio_prev, value_prev = carry
        sub_row, diag_row, sup_row, rhs_row = row
        pivot = diag_row - sub_row * ratio_prev
        ratio = sup_row / pivot
        value = (rhs_row - sub_row[None] * value_prev) / pivot[None]
        return (ratio, value), (ratio, value)

    start = (jnp.zeros((X, NZ), jnp.float32), jnp.zeros((3, X, NZ), jnp.float32))
    _, (ratios, values) = lax.scan(forward, start, (sub_rows, diag_rows, sup_rows, rhs_rows))

    def backward(after, row):
        ratio, value = row
        current = value - ratio[None] * after
        return current, current

    _, solved = lax.scan(backward, jnp.zeros((3, X, NZ), jnp.float32), (ratios, values), reverse=True)
    return jnp.moveaxis(solved, 0, 2)


def reference(velocity, lower_weight, upper_weight, forces, cells, counts):
    force_field = deposit_forces(forces, cells, counts)
    stream = jnp.roll(velocity, 1, axis=1) + jnp.roll(velocity, -1, axis=1)
    spanwise = jnp.roll(velocity, -1, axis=3) + jnp.roll(velocity, 1, axis=3)
    rhs = velocity + diffusion_number * (stream - 2.0 * velocity) + diffusion_number * (spanwise - 2.0 * velocity) + force_field
    velocity_next = solve_columns(lower_weight, upper_weight, rhs)
    return velocity_next, force_field.astype(jnp.bfloat16)
```

```python
import functools

import jax
import jax.numpy as jnp
from jax import lax
from jax.experimental import pallas as pl
from jax.experimental.pallas import tpu as pltpu
from jax.sharding import PartitionSpec as P

diffusion_number = 0.2
segments = 8
lanes = 128
group = 4
vmem = pltpu.VMEM
smem = pltpu.SMEM


def whole(space):
    return pl.BlockSpec(memory_space=space)


def call(body, out_shape, out_specs, in_specs, scratch, limit, cost, **more):
    return pl.pallas_call(
        body,
        out_shape=out_shape,
        in_specs=in_specs,
        out_specs=out_specs,
        scratch_shapes=scratch,
        compiler_params=pltpu.CompilerParams(vmem_limit_bytes=limit << 20),
        cost_estimate=pl.CostEstimate(flops=cost, bytes_accessed=4 << 20, transcendentals=0),
        **more,
    )


def f32(*shape):
    return jax.ShapeDtypeStruct(shape, jnp.float32)


def lane_iota(shape):
    return lax.broadcasted_iota(jnp.int32, shape, len(shape) - 1)


def pack_kernel(velocity, forces, send, columns, turned):
    components, planes, height, across = velocity.shape
    receivers, capacity = forces.shape[1], forces.shape[3]
    chunks = capacity // lanes
    lines = components * planes
    parts = height // lanes
    slot = components + 1
    lane = lane_iota((height, across))
    columns[...] = jnp.zeros_like(columns)
    for c in range(components):
        for x in range(planes):
            k = c * planes + x
            rolled = pltpu.roll(velocity[c, x], 2 * k + 1, 1)
            columns[...] = jnp.where((lane >> 1) == k, rolled, columns[...])
    for p in range(parts):
        turned[p] = columns[p * lanes : (p + 1) * lanes, :].T
    for d in range(receivers):
        for c in range(components):
            for k in range(chunks):
                value = forces[c, d, :, k * lanes : (k + 1) * lanes]
                send[d, pl.ds(k * slot + c, planes, stride=chunks * slot), :] = value
    me = lax.axis_index("span")
    below = lax.rem(me + receivers - 1, receivers)
    above = lax.rem(me + 1, receivers)
    for p in range(parts):
        target = pl.ds(p * slot + components, lines, stride=parts * slot)
        send[below, target, :] = turned[p, pl.ds(1, lines, stride=2), :]
        send[above, target, :] = turned[p, pl.ds(0, lines, stride=2), :]


def prepare_kernel(
    counts,
    velocity,
    lower,
    upper,
    rhs,
    to_top,
    to_bottom,
    from_bottom,
    from_top,
    inv,
    gain,
    ratio,
    prefix,
    first,
    inner,
    coefs,
    chunk_ids,
    chunk_rests,
    chunk_counts,
    inv_b,
    gain_b,
    alpha,
    rows,
):
    components, planes, height, across = velocity.shape
    steps = height // segments
    last = steps - 1
    senders = counts.shape[0]
    capacity = chunk_ids.shape[1] - group

    def plane_list(x, carry):
        def sender(s, n):
            count = counts[s, x]
            for k in range(capacity // senders):
                chunk_ids[x, n] = s * (capacity // senders) + k
                chunk_rests[x, n] = count - k * lanes
                n = n + jnp.where(count > k * lanes, 1, 0)
            return n

        n = lax.fori_loop(0, senders, sender, 0)
        for extra in range(group):
            chunk_ids[x, n + extra] = 0
            chunk_rests[x, n + extra] = 0
        chunk_counts[x] = lax.div(n + group - 1, group)
        return carry

    lax.fori_loop(0, planes, plane_list, 0)

    def of_step(ref, t):
        return ref[:, pl.ds(t, segments, stride=steps), :]

    one = jnp.ones((planes, segments, across), jnp.float32)

    def factor(t, carry):
        d, d_b = carry
        low, up = of_step(lower, t), of_step(upper, t)
        e = 1.0 + low * d
        inverse = 1.0 / (up + e)
        inv[t] = inverse
        gain[t] = low * inverse
        ratio[t] = up * inverse
        back = last - 1 - t
        low_b, up_b = of_step(lower, back), of_step(upper, back)
        e_b = 1.0 + up_b * d_b
        inverse_b = 1.0 / (low_b + e_b)
        inv_b[back] = inverse_b
        gain_b[back] = up_b * inverse_b
        return e * inverse, e_b * inverse_b

    lax.fori_loop(0, last, factor, (one, one))

    def weigh(t, carry):
        q, p, run, sum_first, sum_last = carry
        omega = inv_b[t] * q
        first[t] = omega
        run = run * gain[t]
        prefix[t] = run
        back = last - 1 - t
        weight = inv[back] * p
        alpha[back] = weight
        return q * gain_b[t], p * gain[back], run, sum_first + omega, sum_last + weight

    zero = jnp.zeros_like(one)
    q, p, _, sum_first, sum_last = lax.fori_loop(0, last, weigh, (one, one, one, zero, zero))

    low_sep, up_sep = of_step(lower, last), of_step(upper, last)
    couple_low = low_sep * p
    couple_high = up_sep * jnp.roll(q, -1, axis=1)
    killing = 1.0 + low_sep * sum_last + up_sep * jnp.roll(sum_first, -1, axis=1)
    own = 1.0 + low_sep * sum_last
    for n, value in enumerate((couple_low, couple_high, killing, own, q, sum_first, up_sep)):
        rows[n] = value.reshape(planes * segments, across)

    def row(n, s):
        return rows[n, pl.ds(s, planes, stride=segments), :]

    inner_count = segments - 1
    top = inner_count
    d = jnp.ones((planes, across), jnp.float32)
    d_b = d
    inv_s, gain_s, ratio_s = [], [], []
    inv_sb, gain_sb = [None] * inner_count, [None] * inner_count
    for s in range(inner_count):
        e = row(2, s) + row(0, s) * d
        inverse = 1.0 / (row(1, s) + e)
        inv_s.append(inverse)
        gain_s.append(row(0, s) * inverse)
        ratio_s.append(row(1, s) * inverse)
        d = e * inverse
        back = inner_count - 1 - s
        e_b = row(2, back) + row(1, back) * d_b
        inverse_b = 1.0 / (row(0, back) + e_b)
        inv_sb[back] = inverse_b
        gain_sb[back] = row(1, back) * inverse_b
        d_b = e_b * inverse_b
    for s in range(inner_count):
        for c in range(components):
            part = slice(c * planes, (c + 1) * planes)
            inner[0, s, part, :] = inv_s[s]
            inner[1, s, part, :] = gain_s[s]
            inner[2, s, part, :] = ratio_s[s]
    one_row = jnp.ones((planes, across), jnp.float32)
    zero_row = jnp.zeros_like(one_row)
    reach_top = [None] * inner_count + [one_row]
    reach_bottom = [None] * inner_count + [zero_row]
    run = row(0, top)
    for s in reversed(range(inner_count)):
        reach_top[s] = run * inv_s[s]
        run = run * gain_s[s]
    run = row(4, 0)
    for s in range(inner_count):
        reach_bottom[s] = run * inv_sb[s]
        run = run * gain_sb[s]
    with_low = [None] * inner_count + [zero_row]
    with_high = [None] * inner_count + [one_row]
    prefixes = []
    run = one_row
    for s in range(inner_count):
        run = run * gain_s[s]
        prefixes.append(run)
    for s in reversed(range(inner_count)):
        with_low[s] = prefixes[s] + ratio_s[s] * with_low[s + 1]
        with_high[s] = ratio_s[s] * with_high[s + 1]
    sum_top = row(3, top)
    sum_bottom = row(5, 0)
    for s in range(inner_count):
        sum_top = sum_top + reach_top[s] * row(2, s)
        sum_bottom = sum_bottom + reach_bottom[s] * row(2, s)
    coef = (
        row(0, top) * with_low[top - 1],
        sum_top,
        row(6, top),
        sum_bottom,
        row(4, 0) * with_high[0],
    )
    for n, value in enumerate(coef):
        coefs[n * planes : (n + 1) * planes, :] = value
    for n, values in enumerate((reach_top, reach_bottom, with_low, with_high)):
        for s in range(segments):
            rows[n, pl.ds(s, planes, stride=segments), :] = values[s]

    def block(n):
        return rows[n].reshape(planes, segments, across)

    segment = lax.broadcasted_iota(jnp.int32, one.shape, 1)
    top_weight, bottom_weight, low_sep_u, high_sep_u = block(0), block(1), block(2), block(3)
    top_next = jnp.where(segment == 0, 0.0, jnp.roll(top_weight * up_sep, 1, axis=1))
    bottom_next = jnp.where(segment == 0, 1.0, jnp.roll(bottom_weight * up_sep, 1, axis=1))
    low_prev = jnp.where(segment == 0, 1.0, jnp.roll(low_sep_u, 1, axis=1))
    high_prev = jnp.where(segment == 0, 0.0, jnp.roll(high_sep_u, 1, axis=1))
    top_own, bottom_own = top_weight * low_sep, bottom_weight * low_sep

    def put(ref, t, value):
        for x in range(planes):
            ref[x, pl.ds(t, segments, stride=steps), :] = value[x]

    put(to_top, last, top_weight)
    put(to_bottom, last, bottom_weight)
    put(from_bottom, last, low_sep_u)
    put(from_top, last, high_sep_u)

    def spread(n, carry):
        low_u, high_u = carry
        t = last - 1 - n
        weight, omega, run, r = alpha[t], first[t], prefix[t], ratio[t]
        put(to_top, t, top_own * weight + top_next * omega)
        put(to_bottom, t, bottom_own * weight + bottom_next * omega)
        low_u = run * low_prev + r * low_u
        high_u = run * high_prev + r * high_u
        put(from_bottom, t, low_u)
        put(from_top, t, high_u)
        return low_u, high_u

    lax.fori_loop(0, last, spread, (low_sep_u, high_sep_u))

    size = 32
    lane = lane_iota((size, across))

    def stencil(n, carry):
        part = pl.ds(n * size, size)
        for c in range(components):
            values = [velocity[c, x, part, :] for x in range(planes)]
            for x in range(planes):
                v = values[x]
                stream = values[(x - 1) % planes] + values[(x + 1) % planes]
                prev = jnp.where(lane == 0, 0.0, pltpu.roll(v, 1, 1))
                following = jnp.where(lane == across - 1, 0.0, pltpu.roll(v, across - 1, 1))
                rhs[c, x, part, :] = (
                    v
                    + diffusion_number * (stream - 2.0 * v)
                    + diffusion_number * (following + prev - 2.0 * v)
                )
        return carry

    lax.fori_loop(0, height // size, stencil, 0)


def deposit_kernel(
    chunk_ids,
    chunk_rests,
    chunk_counts,
    got,
    cells,
    rhs_start,
    to_top,
    to_bottom,
    coefs,
    rhs,
    deposit,
    sums,
    total,
    columns,
    edges,
):
    components, planes, height, across = rhs_start.shape
    senders, chunks = cells.shape[0], cells.shape[2]
    slot = components + 1
    parts = height // lanes
    copies = sums.shape[0]
    shift = across.bit_length() - 1
    lines = components * planes
    kind = jnp.bfloat16 if max(height, across) <= 256 else jnp.float32

    me = lax.axis_index("span")
    below = lax.rem(me + senders - 1, senders)
    above = lax.rem(me + 1, senders)
    for p in range(parts):
        source = pl.ds(p * slot + components, lines, stride=parts * slot)
        columns[p, pl.ds(0, lines, stride=2), :] = got[above, source, :]
        columns[p, pl.ds(1, lines, stride=2), :] = got[below, source, :]
        edges[p * lanes : (p + 1) * lanes, :] = diffusion_number * columns[p].T

    for n in range(copies):
        sums[n, 2 * lines : 2 * lines + coefs.shape[0], :] = coefs[...]

    tile = 16
    base = lax.broadcasted_iota(jnp.int32, (tile, lanes), 0)
    height_ids = [(base + n * tile).astype(jnp.float32).astype(kind) for n in range(height // tile)]
    across_ids = height_ids[: across // tile]
    lane = lane_iota((1, lanes))
    one = jnp.ones((tile, lanes), jnp.bfloat16)
    none = jnp.zeros((tile, lanes), jnp.bfloat16)

    def spread(row, to):
        return jnp.broadcast_to(row, (tile, lanes)).astype(to)

    def plane(x, carry):
        total[...] = jnp.zeros_like(total)

        def step(n, inner_carry):
            lefts, rights = [], []
            for g in range(group):
                ident = chunk_ids[x, n * group + g]
                rest = chunk_rests[x, n * group + g]
                sender = lax.div(ident, chunks)
                chunk = lax.rem(ident, chunks)
                cell = cells[sender, x, pl.ds(chunk, 1), :]
                up = jnp.where(lane < rest, cell >> shift, -1).astype(jnp.float32)
                side = (cell & (across - 1)).astype(jnp.float32)
                up, side = spread(up, kind), spread(side, kind)
                lefts.append(jnp.concatenate([jnp.where(up == i, one, none) for i in height_ids], 0))
                masks = [side == i for i in across_ids]
                highs, lows = [], []
                for c in range(components):
                    force = got[sender, pl.ds((x * chunks + chunk) * slot + c, 1), :]
                    high = force.astype(jnp.bfloat16)
                    low = force - high.astype(jnp.float32)
                    high, low = spread(force, jnp.bfloat16), spread(low, jnp.bfloat16)
                    highs += [jnp.where(m, high, none) for m in masks]
                    lows += [jnp.where(m, low, none) for m in masks]
                rights.append(jnp.concatenate(highs + lows, 0))
            total[...] += lax.dot_general(
                jnp.concatenate(lefts, 1),
                jnp.concatenate(rights, 1),
                (((1,), (1,)), ((), ())),
                preferred_element_type=jnp.float32,
            )
            return inner_carry

        lax.fori_loop(0, chunk_counts[x], step, 0)
        size = 64
        wide = lane_iota((size, across))
        border = (wide == 0) | (wide == across - 1)
        for c in range(components):
            k = c * planes + x

            def combine(n, ends):
                part = pl.ds(pl.multiple_of(n * size, size), size)
                field = (
                    total[part, c * across : (c + 1) * across]
                    + total[part, (components + c) * across : (components + c + 1) * across]
                )
                deposit[c, x, part, :] = field.astype(jnp.bfloat16)
                edge = pltpu.roll(edges[part, :], lanes - 1 - 2 * k, 1)
                value = rhs_start[c, x, part, :] + field + jnp.where(border, edge, 0.0)
                rhs[c, x, part, :] = value
                top, bottom = ends
                folded = (size // 8, 8, across)
                top = top + jnp.sum((to_top[x, part, :] * value).reshape(folded), 0)
                bottom = bottom + jnp.sum((to_bottom[x, part, :] * value).reshape(folded), 0)
                return top, bottom

            start = jnp.zeros((8, across), jnp.float32)
            top, bottom = lax.fori_loop(0, height // size, combine, (start, start))
            top, bottom = jnp.sum(top, 0, keepdims=True), jnp.sum(bottom, 0, keepdims=True)
            for n in range(copies):
                sums[n, pl.ds(k, 1), :] = top
                sums[n, pl.ds(lines + k, 1), :] = bottom
        return carry

    lax.fori_loop(0, planes, plane, 0)


def block_kernel(
    rhs, lower, upper, inv, gain, ratio, prefix, first, inner, solved, values, rows
):
    components, planes, height, across = rhs.shape
    steps = height // segments
    last = steps - 1
    lines = components * planes

    def of_step(t):
        return rhs[:, :, pl.ds(t, segments, stride=steps), :]

    zero = jnp.zeros((components, planes, segments, across), jnp.float32)

    def forward(t, carry):
        value, start = carry
        force = of_step(t)
        value = force * inv[t][None] + gain[t][None] * value
        values[t] = value
        return value, start + first[t][None] * force

    value, start = lax.fori_loop(0, last, forward, (zero, zero))
    low_sep = lower[:, pl.ds(last, segments, stride=steps), :][None]
    up_sep = upper[:, pl.ds(last, segments, stride=steps), :][None]
    reduced = of_step(last) + low_sep * value + up_sep * jnp.roll(start, -1, axis=2)
    rows[...] = reduced.reshape(lines * segments, across)

    def row(s):
        return pl.ds(s, lines, stride=segments)

    run = jnp.zeros((lines, across), jnp.float32)
    found = []
    for s in range(segments - 1):
        run = rows[row(s), :] * inner[0, s] + inner[1, s] * run
        found.append(run)
    run = jnp.zeros((lines, across), jnp.float32)
    rows[row(segments - 1), :] = run
    for s in reversed(range(segments - 1)):
        run = found[s] + inner[2, s] * run
        rows[row(s), :] = run
    separators = rows[...].reshape(zero.shape)
    below = jnp.roll(separators, 1, axis=2)

    def put(t, value):
        for c in range(components):
            for x in range(planes):
                solved[c, x, pl.ds(t, segments, stride=steps), :] = value[c, x]

    put(last, separators)

    def backward(n, value):
        t = last - 1 - n
        value = values[t] + prefix[t][None] * below + ratio[t][None] * value
        put(t, value)
        return value

    lax.fori_loop(0, last, backward, separators)


def finish_kernel(sums, solved, from_bottom, from_top, out, ends):
    components, planes, _, across = out.shape[0], sums.shape[1], 0, out.shape[3]
    planes = ends.shape[1] // components
    lines = components * planes
    walls = sums.shape[0]
    x = pl.program_id(0)

    @pl.when(x == 0)
    def _():
        def coef(k, n):
            start = 2 * lines + n * planes
            return sums[k, start : start + planes, :]

        def wide(value):
            return jnp.concatenate([value] * components, 0)

        d = jnp.ones((planes, across), jnp.float32)
        value = jnp.zeros((lines, across), jnp.float32)
        values, ratios = [], []
        for k in range(walls):
            low, own, up = coef(k, 0), coef(k, 1), coef(k, 2)
            reduced = sums[k, :lines, :]
            if k + 1 < walls:
                high = up * coef(k + 1, 4)
                killing = own + up * coef(k + 1, 3)
                reduced = reduced + wide(up) * sums[k + 1, lines : 2 * lines, :]
            else:
                high = jnp.zeros_like(up)
                killing = own + up
            e = killing + low * d
            inverse = 1.0 / (high + e)
            d = e * inverse
            value = (reduced + wide(low) * value) * wide(inverse)
            values.append(value)
            ratios.append(wide(high * inverse))
        ends[0] = jnp.zeros((lines, across), jnp.float32)
        ends[walls] = values[-1]
        for k in reversed(range(walls - 1)):
            values[k] = values[k] + ratios[k] * values[k + 1]
            ends[k + 1] = values[k]

    me = lax.axis_index("wall")
    for c in range(components):
        row = pl.ds(c * planes + x, 1)
        bottom, top = ends[me, row, :], ends[me + 1, row, :]
        out[c, 0] = solved[c, 0] + from_bottom[0] * bottom + from_top[0] * top


def local(velocity, lower_weight, upper_weight, forces, cells, counts):
    components, planes, height, across = velocity.shape
    receivers, capacity = forces.shape[3], forces.shape[5]
    senders = cells.shape[2]
    walls = lax.axis_size("wall")
    lines = components * planes
    steps = height // segments
    chunks = capacity // lanes
    forces = forces.reshape(components, receivers, planes, capacity)
    cells = cells.reshape(senders, planes, chunks, lanes)
    counts = counts.reshape(senders, planes)

    send = call(
        pack_kernel,
        f32(receivers, planes * chunks * (components + 1), lanes),
        whole(vmem),
        [whole(vmem)] * 2,
        [
            vmem((height, across), jnp.float32),
            vmem((height // lanes, lanes, lanes), jnp.float32),
        ],
        16,
        1 << 22,
    )(velocity, forces)
    got = lax.all_to_all(send, "span", 0, 0, tiled=True)

    step_shape = (steps, planes, segments, across)
    plane_shape = (planes, height, across)
    list_shape = (planes, senders * chunks + group)
    prepared = call(
        prepare_kernel,
        (
            f32(*velocity.shape),
            *[f32(*plane_shape)] * 4,
            *[f32(*step_shape)] * 5,
            f32(3, segments, lines, across),
            f32(5 * planes, across),
            jax.ShapeDtypeStruct(list_shape, jnp.int32),
            jax.ShapeDtypeStruct(list_shape, jnp.int32),
            jax.ShapeDtypeStruct((planes,), jnp.int32),
        ),
        (*[whole(vmem)] * 12, *[whole(smem)] * 3),
        [whole(smem)] + [whole(vmem)] * 3,
        [
            *[vmem(step_shape, jnp.float32)] * 3,
            vmem((7, planes * segments, across), jnp.float32),
        ],
        24,
        1 << 24,
    )(counts, velocity, lower_weight, upper_weight)
    (rhs_start, to_top, to_bottom, from_bottom, from_top) = prepared[:5]
    (inv, gain, ratio, prefix, first, inner, coefs) = prepared[5:12]

    sum_rows = -(-(2 * lines + 5 * planes) // 8) * 8
    rhs, deposit, sums = call(
        deposit_kernel,
        (
            f32(*velocity.shape),
            jax.ShapeDtypeStruct(velocity.shape, jnp.bfloat16),
            f32(walls, sum_rows, across),
        ),
        (whole(vmem),) * 3,
        [whole(smem)] * 3 + [whole(vmem)] * 6,
        [
            vmem((height, 2 * components * across), jnp.float32),
            vmem((height // lanes, lanes, lanes), jnp.float32),
            vmem((height, lanes), jnp.float32),
        ],
        24,
        1 << 32,
    )(*prepared[12:], got, cells, rhs_start, to_top, to_bottom, coefs)
    all_sums = lax.all_to_all(sums, "wall", 0, 0, tiled=True)

    solved = call(
        block_kernel,
        f32(*velocity.shape),
        whole(vmem),
        [whole(vmem)] * 9,
        [
            vmem((steps, components, planes, segments, across), jnp.float32),
            vmem((lines * segments, across), jnp.float32),
        ],
        24,
        1 << 22,
    )(rhs, lower_weight, upper_weight, inv, gain, ratio, prefix, first, inner)

    block = (components, 1, height, across)
    velocity_next = pl.pallas_call(
        finish_kernel,
        out_shape=f32(*velocity.shape),
        grid=(planes,),
        in_specs=[
            whole(vmem),
            pl.BlockSpec(block, lambda x: (0, x, 0, 0)),
            pl.BlockSpec(block[1:], lambda x: (x, 0, 0)),
            pl.BlockSpec(block[1:], lambda x: (x, 0, 0)),
        ],
        out_specs=pl.BlockSpec(block, lambda x: (0, x, 0, 0)),
        scratch_shapes=[vmem((walls + 1, lines, across), jnp.float32)],
        compiler_params=pltpu.CompilerParams(vmem_limit_bytes=12 << 20),
        cost_estimate=pl.CostEstimate(flops=1 << 22, bytes_accessed=4 << 20, transcendentals=0),
    )(all_sums, solved, from_bottom, from_top)
    return (velocity_next, deposit)


def solution(mesh):
    placed = (
        P(None, None, "wall", "span"),
        P(None, "wall", "span"),
        P(None, "wall", "span"),
        P(None, "wall", "span", None, None, None),
        P("wall", "span", None, None, None),
        P("wall", "span", None, None),
    )
    return jax.shard_map(
        local,
        mesh=mesh,
        in_specs=placed,
        out_specs=(P(None, None, "wall", "span"), P(None, None, "wall", "span")),
        check_vma=False,
    )
```

```python
import jax
import jax.numpy as jnp
from jax import lax
from jax.experimental import pallas as pl
from jax.experimental.pallas import tpu as pltpu
from jax.sharding import PartitionSpec as P

diffusion_number = 0.2
segments = 8
lanes = 128
group = 4
in_vmem = pl.BlockSpec(memory_space=pltpu.VMEM)
in_smem = pl.BlockSpec(memory_space=pltpu.SMEM)
in_hbm = pl.BlockSpec(memory_space=pltpu.HBM)


def call(body, out_shape, out_specs, in_specs, scratch, mebibytes, flops):
    return pl.pallas_call(
        body,
        out_shape=out_shape,
        in_specs=in_specs,
        out_specs=out_specs,
        scratch_shapes=scratch,
        compiler_params=pltpu.CompilerParams(vmem_limit_bytes=mebibytes << 20),
        cost_estimate=pl.CostEstimate(flops=flops, bytes_accessed=4 << 20, transcendentals=0),
    )


def f32(*shape):
    return jax.ShapeDtypeStruct(shape, jnp.float32)


def scratch(*shape):
    return pltpu.VMEM(shape, jnp.float32)


def lane_iota(shape):
    return lax.broadcasted_iota(jnp.int32, shape, len(shape) - 1)


def reciprocal(value):
    rough = pl.reciprocal(value, approx=True)
    return rough * (2.0 - value * rough)


def pack_kernel(velocity_hbm, forces_hbm, *refs):
    components, planes, height, across = velocity_hbm.shape
    receivers, capacity = forces_hbm.shape[1], forces_hbm.shape[3]
    send = refs[:receivers]
    velocity, forces, columns, turned, sems = refs[receivers:]
    chunks = capacity // lanes
    lines = components * planes
    parts = height // lanes
    slot = components + 1
    copies = [
        pltpu.make_async_copy(forces_hbm.at[c], forces.at[c], sems.at[c]) for c in range(components)
    ]
    for k in range(lines):
        here = (k // planes, k % planes)
        copies.append(
            pltpu.make_async_copy(velocity_hbm.at[here], velocity.at[here], sems.at[components + k])
        )
    for copy in copies:
        copy.start()
    columns[...] = jnp.zeros_like(columns)
    me = lax.axis_index("span")
    for c in range(components):
        copies[c].wait()
        for d in range(receivers):
            owner = lax.rem(me + d, receivers)
            for k in range(chunks):
                value = forces[c, owner, :, k * lanes : (k + 1) * lanes]
                send[d][pl.ds(k * slot + c, planes, stride=chunks * slot), :] = value
    lane = lane_iota((height, across))
    for k in range(lines):
        copies[components + k].wait()
        rolled = pltpu.roll(velocity[k // planes, k % planes], 2 * k + 1, 1)
        columns[...] = jnp.where((lane >> 1) == k, rolled, columns[...])
    for p in range(parts):
        turned[p] = columns[p * lanes : (p + 1) * lanes, :].T
        target = pl.ds(p * slot + components, lines, stride=parts * slot)
        send[receivers - 1][target, :] = turned[p, pl.ds(1, lines, stride=2), :]
        send[1][target, :] = turned[p, pl.ds(0, lines, stride=2), :]


def prepare_kernel(
    counts,
    cells,
    velocity,
    lower,
    upper,
    rhs,
    inv,
    gain,
    first,
    ratio,
    prefix,
    inner,
    ends,
    coefs,
    cell_rows,
    work,
    inv_b,
    gain_b,
    rows,
):
    components, planes, height, across = velocity.shape
    steps = height // segments
    last = steps - 1
    senders, capacity = cells.shape[0], cells.shape[2]
    chunks = capacity // lanes

    def one_sender(s, carry):
        for k in range(chunks):
            start = s * planes * chunks + k
            value = cells[s, :, k * lanes : (k + 1) * lanes]
            cell_rows[pl.ds(start, planes, stride=chunks), :] = value
        return carry

    lax.fori_loop(0, senders, one_sender, 0)

    def one_plane(x, n):
        def sender(s, n):
            count = counts[x, s]
            start = (s * planes + x) * chunks
            for k in range(chunks):
                work[0, n + k] = start + k
                work[1, n + k] = count - k * lanes
                work[2, n + k] = x
            return n + lax.div(count + lanes - 1, lanes)

        n = lax.fori_loop(0, senders, sender, n)
        for extra in range(group):
            work[0, n + extra] = 0
            work[1, n + extra] = 0
            work[2, n + extra] = x
        return lax.div(n + group - 1, group) * group

    total = lax.fori_loop(0, planes, one_plane, 0)
    for extra in range(2 * group):
        work[0, total + extra] = 0
        work[1, total + extra] = 0
        work[2, total + extra] = 0
    work[3, 0] = lax.div(total + 2 * group - 1, 2 * group)

    def of_step(ref, t):
        return ref[:, pl.ds(t, segments, stride=steps), :]

    one = jnp.ones((planes, segments, across), jnp.float32)
    zero = jnp.zeros_like(one)
    size = 8
    lane = lane_iota((size, across))

    def stencil(n):
        part = pl.ds(pl.multiple_of(n * size, size), size)
        for c in range(components):
            values = [velocity[c, x, part, :] for x in range(planes)]
            for x in range(planes):
                v = values[x]
                stream = values[(x - 1) % planes] + values[(x + 1) % planes]
                before = jnp.where(lane == 0, 0.0, pltpu.roll(v, 1, 1))
                after = jnp.where(lane == across - 1, 0.0, pltpu.roll(v, across - 1, 1))
                rhs[c, x, part, :] = (
                    v
                    + diffusion_number * (stream - 2.0 * v)
                    + diffusion_number * (after + before - 2.0 * v)
                )

    def factor(t, carry):
        d, d_b, run, run_b, sum_last, sum_first = carry
        low, up = of_step(lower, t), of_step(upper, t)
        e = 1.0 + low * d
        inverse = reciprocal(up + e)
        g = low * inverse
        run = run * g
        inv[t] = inverse
        gain[t] = g
        ratio[t] = up * inverse
        prefix[t] = run
        back = last - 1 - t
        low_b, up_b = of_step(lower, back), of_step(upper, back)
        e_b = 1.0 + up_b * d_b
        inverse_b = reciprocal(low_b + e_b)
        g_b = up_b * inverse_b
        inv_b[back] = inverse_b
        gain_b[back] = g_b
        stencil(t)
        return (
            e * inverse,
            e_b * inverse_b,
            run,
            run_b * g_b,
            inverse + g * sum_last,
            inverse_b + g_b * sum_first,
        )

    carry = lax.fori_loop(0, last, factor, (one, one, one, one, zero, zero))
    _, _, low_gain, high_gain, sum_last, sum_first = carry
    for n in range(last, height // size):
        stencil(n)

    def weigh(t, q):
        first[t] = inv_b[t] * q
        return q * gain_b[t]

    lax.fori_loop(0, last, weigh, one)

    low_sep, up_sep = of_step(lower, last), of_step(upper, last)
    couple_low = low_sep * low_gain
    couple_high = up_sep * jnp.roll(high_gain, -1, axis=1)
    own = 1.0 + low_sep * sum_last
    killing = own + up_sep * jnp.roll(sum_first, -1, axis=1)
    for n, value in enumerate(
        (couple_low, couple_high, killing, own, high_gain, sum_first, up_sep)
    ):
        rows[n] = value.reshape(planes * segments, across)
    ends[2] = low_sep
    ends[3] = up_sep

    def row(n, s):
        return rows[n, pl.ds(s, planes, stride=segments), :]

    top = segments - 1
    d = jnp.ones((planes, across), jnp.float32)
    d_b = d
    inv_s, gain_s, ratio_s = [], [], []
    inv_sb, gain_sb = [None] * top, [None] * top
    for s in range(top):
        e = row(2, s) + row(0, s) * d
        inverse = reciprocal(row(1, s) + e)
        inv_s.append(inverse)
        gain_s.append(row(0, s) * inverse)
        ratio_s.append(row(1, s) * inverse)
        d = e * inverse
        back = top - 1 - s
        e_b = row(2, back) + row(1, back) * d_b
        inverse_b = reciprocal(row(0, back) + e_b)
        inv_sb[back] = inverse_b
        gain_sb[back] = row(1, back) * inverse_b
        d_b = e_b * inverse_b
    for s in range(top):
        for c in range(components):
            part = slice(c * planes, (c + 1) * planes)
            inner[0, s, part, :] = inv_s[s]
            inner[1, s, part, :] = gain_s[s]
            inner[2, s, part, :] = ratio_s[s]
    one_row = jnp.ones((planes, across), jnp.float32)
    zero_row = jnp.zeros_like(one_row)
    reach_top = [None] * top + [one_row]
    reach_bottom = [None] * top + [zero_row]
    low_total = one_row
    run = row(0, top)
    for s in reversed(range(top)):
        reach_top[s] = run * inv_s[s]
        run = run * gain_s[s]
        low_total = low_total * gain_s[s]
    run = row(4, 0)
    high_total = one_row
    for s in range(top):
        reach_bottom[s] = run * inv_sb[s]
        run = run * gain_sb[s]
        high_total = high_total * ratio_s[s]
    sum_top = row(3, top)
    sum_bottom = row(5, 0)
    for s in range(top):
        sum_top = sum_top + reach_top[s] * row(2, s)
        sum_bottom = sum_bottom + reach_bottom[s] * row(2, s)
    coef = (
        row(0, top) * low_total,
        sum_top,
        row(6, top),
        sum_bottom,
        row(4, 0) * high_total,
    )
    for n, value in enumerate(coef):
        coefs[n * planes : (n + 1) * planes, :] = value
    for n, values in enumerate((reach_top, reach_bottom)):
        for s in range(segments):
            rows[n, pl.ds(s, planes, stride=segments), :] = values[s]
        ends[n] = rows[n].reshape(planes, segments, across)


def deposit_kernel(work, cell_rows, rhs_start, inv, gain, first, ends, coefs, *refs):
    components, planes, height, across = rhs_start.shape
    steps = height // segments
    last = steps - 1
    senders = len(refs) - 14
    got = refs[:senders]
    (deposit_hbm, swept, reduced, sums) = refs[senders : senders + 4]
    (field, rhs, slots, total, lefts, rights, columns, edges, sems, spare) = refs[senders + 4 :]
    slot = components + 1
    chunks = got[0].shape[0] // (planes * slot)
    parts = height // lanes
    shift = across.bit_length() - 1
    lines = components * planes
    kind = jnp.bfloat16 if max(height, across) <= 256 else jnp.float32

    me = lax.axis_index("span")
    block = planes * chunks * slot
    for n in range(senders):
        owner = lax.rem(me + senders - n, senders)
        slots[pl.ds(pl.multiple_of(owner * block, 8), block), :] = got[n][...]
    total[...] = jnp.zeros_like(total)
    sums[2 * lines : 2 * lines + coefs.shape[0], :] = coefs[...]

    tile = 16
    base = lax.broadcasted_iota(jnp.int32, (tile, lanes), 0)
    height_ids = [(base + n * tile).astype(jnp.float32).astype(kind) for n in range(height // tile)]
    across_ids = height_ids[: across // tile]
    lane = lane_iota((1, lanes))
    one = jnp.ones((tile, lanes), jnp.bfloat16)
    none = jnp.zeros((tile, lanes), jnp.bfloat16)

    def spread(row, to):
        return jnp.broadcast_to(row, (tile, lanes)).astype(to)

    def build(n, half):
        for g in range(group):
            ident = work[0, n * group + g]
            rest = work[1, n * group + g]
            there = slice(g * lanes, (g + 1) * lanes)
            cell = cell_rows[pl.ds(ident, 1), :]
            up = jnp.where(lane < rest, cell >> shift, -1).astype(jnp.float32)
            side = (cell & (across - 1)).astype(jnp.float32)
            up, side = spread(up, kind), spread(side, kind)
            for i, ids in enumerate(height_ids):
                lefts[half][i * tile : (i + 1) * tile, there] = jnp.where(up == ids, one, none)
            masks = [side == ids for ids in across_ids]
            for c in range(components):
                force = slots[pl.ds(ident * slot + c, 1), :]
                rest_of = force - force.astype(jnp.bfloat16).astype(jnp.float32)
                for m, value in enumerate((force, rest_of)):
                    value = spread(value, jnp.bfloat16)
                    start = (m * components + c) * across
                    for i, mask in enumerate(masks):
                        place = slice(start + i * tile, start + (i + 1) * tile)
                        rights[half][place, there] = jnp.where(mask, value, none)

    def add(n, half):
        total[work[2, n * group]] += lax.dot_general(
            rights[half][...],
            lefts[half][...],
            (((1,), (1,)), ((), ())),
            preferred_element_type=jnp.float32,
        )

    def two_steps(n, carry):
        build(2 * n + 1, 1)
        add(2 * n, 0)
        build(2 * n + 2, 0)
        add(2 * n + 1, 1)
        return carry

    build(0, 0)
    lax.fori_loop(0, work[3, 0], two_steps, 0)

    for p in range(parts):
        source = pl.ds(p * slot + components, lines, stride=parts * slot)
        columns[p, pl.ds(0, lines, stride=2), :] = got[senders - 1][source, :]
        columns[p, pl.ds(1, lines, stride=2), :] = got[1][source, :]
        edges[p * lanes : (p + 1) * lanes, :] = diffusion_number * columns[p].T
    wide = lane_iota((lanes, across))
    border = (wide == 0) | (wide == across - 1)

    def place(x):
        return [
            pltpu.make_async_copy(field.at[c, x], deposit_hbm.at[c, x], sems.at[c, x])
            for c in range(components)
        ]

    def combine(x, carry):
        for c in range(components):
            for p in range(parts):
                part = slice(p * lanes, (p + 1) * lanes)
                high = total[x, c * across : (c + 1) * across, part]
                low = total[x, (components + c) * across : (components + c + 1) * across, part]
                value = (high + low).T
                field[c, x, part, :] = value.astype(jnp.bfloat16)
                edge = pltpu.roll(edges[part, :], lanes - 1 - 2 * (c * planes + x), 1)
                rhs[c, x, part, :] = rhs_start[c, x, part, :] + value + jnp.where(border, edge, 0.0)
        for copy in place(x):
            copy.start()
        return carry

    lax.fori_loop(0, planes, combine, 0)

    zero = jnp.zeros((components, planes, segments, across), jnp.float32)

    def of_step(t):
        return rhs[:, :, pl.ds(t, segments, stride=steps), :]

    def forward(t, carry):
        value, start = carry
        force = of_step(t)
        value = force * inv[t][None] + gain[t][None] * value
        swept[t] = value
        return value, start + first[t][None] * force

    value, start = lax.fori_loop(0, last, forward, (zero, zero))
    segment = lax.broadcasted_iota(jnp.int32, zero.shape, 2)
    above = jnp.where(segment == segments - 1, 0.0, jnp.roll(start, -1, axis=2))
    value = of_step(last) + ends[2][None] * value + ends[3][None] * above
    reduced[...] = value.reshape(lines * segments, across)
    at_top = ends[0][None] * value
    at_bottom = ends[1][None] * value + jnp.where(segment == 0, start, 0.0)
    for c in range(components):
        for x in range(planes):
            k = c * planes + x
            sums[k : k + 1, :] = jnp.sum(at_top[c, x], 0, keepdims=True)
            sums[lines + k : lines + k + 1, :] = jnp.sum(at_bottom[c, x], 0, keepdims=True)

    for x in range(planes):
        for copy in place(x):
            copy.wait()


def finish_kernel(inner, reduced, swept, ratio, prefix, *refs):
    walls = len(refs) - 7
    received = refs[:walls]
    out_hbm, sums, tops, after, before, out, sems = refs[walls:]
    components, planes, height, across = out.shape
    steps = height // segments
    last = steps - 1
    lines = components * planes
    me = lax.axis_index("wall")
    for n in range(walls):
        sums[lax.rem(me + walls - n, walls)] = received[n][...]

    def coef(k, n):
        start = 2 * lines + n * planes
        return sums[k, start : start + planes, :]

    def wide(value):
        return jnp.concatenate([value] * components, 0)

    d = jnp.ones((planes, across), jnp.float32)
    value = jnp.zeros((lines, across), jnp.float32)
    values, ratios = [], []
    for k in range(walls):
        low, own, up = coef(k, 0), coef(k, 1), coef(k, 2)
        right = sums[k, :lines, :]
        if k + 1 < walls:
            high = up * coef(k + 1, 4)
            killing = own + up * coef(k + 1, 3)
            right = right + wide(up) * sums[k + 1, lines : 2 * lines, :]
        else:
            high = jnp.zeros_like(up)
            killing = own + up
        e = killing + low * d
        inverse = reciprocal(high + e)
        d = e * inverse
        value = (right + wide(low) * value) * wide(inverse)
        values.append(value)
        ratios.append(wide(high * inverse))
    tops[0] = jnp.zeros((lines, across), jnp.float32)
    tops[walls] = values[-1]
    for k in reversed(range(walls - 1)):
        values[k] = values[k] + ratios[k] * values[k + 1]
        tops[k + 1] = values[k]

    def row(s):
        return pl.ds(s, lines, stride=segments)

    run = tops[me]
    before[row(0), :] = run
    found = []
    for s in range(segments - 1):
        run = reduced[row(s), :] * inner[0, s] + inner[1, s] * run
        found.append(run)
    run = tops[me + 1]
    after[row(segments - 1), :] = run
    for s in reversed(range(segments - 1)):
        run = found[s] + inner[2, s] * run
        after[row(s), :] = run
        before[row(s + 1), :] = run
    shape = (components, planes, segments, across)
    above = after[...].reshape(shape)
    below = before[...].reshape(shape)

    def put(part, t, value):
        for c in range(components):
            for n, x in enumerate(part):
                out[c, x, pl.ds(t, segments, stride=steps), :] = value[c, n]

    copies = []
    half = planes // 2 if planes % 2 == 0 else planes
    for start in range(0, planes, half):
        part = range(start, start + half)
        bottom = below[:, start : start + half]

        def backward(n, value):
            t = last - 1 - n
            here = (slice(None), slice(start, start + half))
            gains = prefix[t, start : start + half][None]
            ratios_t = ratio[t, start : start + half][None]
            value = swept[(t, *here)] + gains * bottom + ratios_t * value
            put(part, t, value)
            return value

        put(part, last, above[:, start : start + half])
        lax.fori_loop(0, last, backward, above[:, start : start + half], unroll=2)
        for c in range(components):
            for x in part:
                here = (c, x)
                copy = pltpu.make_async_copy(out.at[here], out_hbm.at[here], sems.at[here])
                copy.start()
                copies.append(copy)
    for copy in copies:
        copy.wait()


def everyone(block, axis, by_distance):
    length = lax.axis_size(axis)
    found = [by_distance[0]]
    for distance in range(1, length):
        route = [(i, (i + distance) % length) for i in range(length)]
        found.append(lax.ppermute(by_distance[distance], axis, route))
    return found


def local(velocity, lower_weight, upper_weight, forces, cells, counts):
    components, planes, height, across = velocity.shape
    receivers, capacity = forces.shape[3], forces.shape[5]
    senders = cells.shape[2]
    walls = lax.axis_size("wall")
    lines = components * planes
    steps = height // segments
    chunks = capacity // lanes
    slot = components + 1
    forces = forces.reshape(components, receivers, planes, capacity)
    cells = cells.reshape(senders, planes, capacity)
    counts = counts.reshape(senders, planes).T

    send = call(
        pack_kernel,
        [f32(planes * chunks * slot, lanes)] * receivers,
        [in_vmem] * receivers,
        [in_hbm] * 2,
        [
            scratch(*velocity.shape),
            scratch(*forces.shape),
            scratch(height, across),
            scratch(height // lanes, lanes, lanes),
            pltpu.SemaphoreType.DMA((components + lines,)),
        ],
        8,
        1 << 22,
    )(velocity, forces)
    got = everyone(send, "span", send)

    step_shape = (steps, planes, segments, across)
    work_length = planes * (senders * chunks + group) + 3 * group
    prepared = call(
        prepare_kernel,
        (
            f32(*velocity.shape),
            *[f32(*step_shape)] * 5,
            f32(3, segments, lines, across),
            f32(4, planes, segments, across),
            f32(5 * planes, across),
            jax.ShapeDtypeStruct((senders * planes * chunks, lanes), jnp.int32),
            jax.ShapeDtypeStruct((4, work_length), jnp.int32),
        ),
        (*[in_vmem] * 10, in_smem),
        [in_smem] + [in_vmem] * 4,
        [
            scratch(*step_shape),
            scratch(*step_shape),
            scratch(7, planes * segments, across),
        ],
        8,
        1 << 24,
    )(counts, cells, velocity, lower_weight, upper_weight)
    (rhs_start, inv, gain, first, ratio, prefix, inner, ends, coefs, cell_rows, work) = prepared

    sum_rows = -(-(2 * lines + 5 * planes) // 8) * 8
    wide = 2 * components * across
    deposit, swept, reduced, sums = call(
        deposit_kernel,
        (
            jax.ShapeDtypeStruct(velocity.shape, jnp.bfloat16),
            f32(steps, components, planes, segments, across),
            f32(lines * segments, across),
            f32(sum_rows, across),
        ),
        (in_hbm, *[in_vmem] * 3),
        [in_smem] + [in_vmem] * (7 + receivers),
        [
            pltpu.VMEM(velocity.shape, jnp.bfloat16),
            scratch(*velocity.shape),
            scratch(senders * planes * chunks * slot, lanes),
            scratch(planes, wide, height),
            [pltpu.VMEM((height, group * lanes), jnp.bfloat16)] * 2,
            [pltpu.VMEM((wide, group * lanes), jnp.bfloat16)] * 2,
            scratch(height // lanes, lanes, lanes),
            scratch(height, lanes),
            pltpu.SemaphoreType.DMA((components, planes)),
            scratch(8, lanes),
        ],
        20,
        1 << 32,
    )(work, cell_rows, rhs_start, inv, gain, first, ends, coefs, *got)
    all_sums = everyone(sums, "wall", [sums] * walls)

    velocity_next = call(
        finish_kernel,
        f32(*velocity.shape),
        in_hbm,
        [in_vmem] * (5 + walls),
        [
            scratch(walls, sum_rows, across),
            scratch(walls + 1, lines, across),
            scratch(lines * segments, across),
            scratch(lines * segments, across),
            scratch(*velocity.shape),
            pltpu.SemaphoreType.DMA((components, planes)),
        ],
        8,
        1 << 22,
    )(inner, reduced, swept, ratio, prefix, *all_sums)
    return (velocity_next, deposit)


def solution(mesh):
    placed = (
        P(None, None, "wall", "span"),
        P(None, "wall", "span"),
        P(None, "wall", "span"),
        P(None, "wall", "span", None, None, None),
        P("wall", "span", None, None, None),
        P("wall", "span", None, None),
    )
    return jax.shard_map(
        local,
        mesh=mesh,
        in_specs=placed,
        out_specs=(P(None, None, "wall", "span"), P(None, None, "wall", "span")),
        check_vma=False,
    )
```

```python
import jax
import jax.numpy as jnp
from jax import lax
from jax.experimental import pallas as pl
from jax.experimental.pallas import tpu as pltpu
from jax.sharding import PartitionSpec as P

diffusion_number = 0.2
segments = 8
lanes = 128
group = 8
in_vmem = pl.BlockSpec(memory_space=pltpu.VMEM)
in_smem = pl.BlockSpec(memory_space=pltpu.SMEM)
in_hbm = pl.BlockSpec(memory_space=pltpu.HBM)


def call(body, out_shape, out_specs, in_specs, scratch, mebibytes, flops):
    return pl.pallas_call(
        body,
        out_shape=out_shape,
        in_specs=in_specs,
        out_specs=out_specs,
        scratch_shapes=scratch,
        compiler_params=pltpu.CompilerParams(vmem_limit_bytes=mebibytes << 20),
        cost_estimate=pl.CostEstimate(flops=flops, bytes_accessed=4 << 20, transcendentals=0),
    )


def f32(*shape):
    return jax.ShapeDtypeStruct(shape, jnp.float32)


def scratch(*shape):
    return pltpu.VMEM(shape, jnp.float32)


def lane_iota(shape):
    return lax.broadcasted_iota(jnp.int32, shape, len(shape) - 1)


def reciprocal(value):
    rough = pl.reciprocal(value, approx=True)
    return rough * (2.0 - value * rough)


def start_all(copies):
    for copy in copies:
        copy.start()


def wait_all(copies):
    for copy in copies:
        copy.wait()


def copies_of(sources, targets, sems, first=0):
    return [
        pltpu.make_async_copy(source, target, sems.at[first + n])
        for n, (source, target) in enumerate(zip(sources, targets))
    ]


def pack_kernel(velocity_hbm, forces_hbm, send_hbm, velocity, forces, send, columns, turned, sems):
    components, planes, height, across = velocity_hbm.shape
    receivers, capacity = forces_hbm.shape[1], forces_hbm.shape[3]
    chunks = capacity // lanes
    lines = components * planes
    parts = height // lanes
    slot = components + 1
    copies = copies_of(
        [forces_hbm.at[c] for c in range(components)],
        [forces.at[c] for c in range(components)],
        sems,
    )
    places = [(c, x) for c in range(components) for x in range(planes)]
    copies += copies_of(
        [velocity_hbm.at[here] for here in places],
        [velocity.at[here] for here in places],
        sems,
        components,
    )
    start_all(copies)
    me = lax.axis_index("span")
    wait_all(copies[:components])
    outgoing = []
    for d in range(receivers):
        owner = lax.rem(me + d, receivers)
        for c in range(components):
            for k in range(chunks):
                value = forces[c, owner, :, k * lanes : (k + 1) * lanes]
                send[owner, pl.ds(k * slot + c, planes, stride=chunks * slot), :] = value
        index = components + lines + d
        copy = pltpu.make_async_copy(send.at[owner], send_hbm.at[owner], sems.at[index])
        outgoing.append(copy)
        if d not in (1, receivers - 1):
            copy.start()
    lane = lane_iota((height, across))
    picked = jnp.zeros((height, across), jnp.float32)
    for k in range(lines):
        copies[components + k].wait()
        rolled = pltpu.roll(velocity[k // planes, k % planes], 2 * k + 1, 1)
        picked = jnp.where((lane >> 1) == k, rolled, picked)
    columns[...] = picked
    below = lax.rem(me + receivers - 1, receivers)
    above = lax.rem(me + 1, receivers)
    for p in range(parts):
        turned[p] = columns[p * lanes : (p + 1) * lanes, :].T
        target = pl.ds(p * slot + components, lines, stride=parts * slot)
        send[below, target, :] = turned[p, pl.ds(1, lines, stride=2), :]
        send[above, target, :] = turned[p, pl.ds(0, lines, stride=2), :]
    outgoing[1].start()
    outgoing[receivers - 1].start()
    wait_all(outgoing)


def prepare_kernel(counts, cells, velocity, lower, upper, *refs):
    outputs, inner_refs, (work, inv_b, gain_b, rows, sems) = refs[:11], refs[11:21], refs[21:]
    rhs, inv, gain, first, ratio, prefix, inner, ends, coefs, cell_rows = inner_refs
    outgoing = copies_of((*inner_refs, work), outputs, sems)
    components, planes, height, across = velocity.shape
    steps = inv.shape[0] + 1
    last = steps - 1
    rest = height - segments * steps
    knots = segments + rest
    senders, capacity = cells.shape[0], cells.shape[2]
    chunks = capacity // lanes

    def one_sender(s, carry):
        for k in range(chunks):
            start = s * planes * chunks + k
            value = cells[s, :, k * lanes : (k + 1) * lanes]
            cell_rows[pl.ds(start, planes, stride=chunks), :] = value
        return carry

    lax.fori_loop(0, senders, one_sender, 0)

    def one_plane(x, n):
        def sender(s, n):
            count = counts[x, s]
            start = (s * planes + x) * chunks
            for k in range(chunks):
                work[0, n + k] = start + k
                work[1, n + k] = count - k * lanes
                work[2, n + k] = x
            return n + lax.div(count + lanes - 1, lanes)

        n = lax.fori_loop(0, senders, sender, n)
        for extra in range(group):
            work[0, n + extra] = 0
            work[1, n + extra] = 0
            work[2, n + extra] = x
        return lax.div(n + group - 1, group) * group

    total = lax.fori_loop(0, planes, one_plane, 0)
    for extra in range(2 * group):
        work[0, total + extra] = 0
        work[1, total + extra] = 0
        work[2, total + extra] = 0
    work[3, 0] = lax.div(total + 2 * group - 1, 2 * group)
    start_all(outgoing[9:])

    def of_step(ref, t):
        return ref[:, pl.ds(t, segments, stride=steps), :]

    one = jnp.ones((planes, segments, across), jnp.float32)
    zero = jnp.zeros_like(one)
    size = 8
    lane = lane_iota((size, across))

    def stencil(n):
        part = pl.ds(pl.multiple_of(n * size, size), size)
        for c in range(components):
            values = [velocity[c, x, part, :] for x in range(planes)]
            for x in range(planes):
                v = values[x]
                stream = values[(x - 1) % planes] + values[(x + 1) % planes]
                before = jnp.where(lane == 0, 0.0, pltpu.roll(v, 1, 1))
                after = jnp.where(lane == across - 1, 0.0, pltpu.roll(v, across - 1, 1))
                rhs[c, x, part, :] = (
                    v
                    + diffusion_number * (stream - 2.0 * v)
                    + diffusion_number * (after + before - 2.0 * v)
                )

    def factor(t, carry):
        d, d_b, run, run_b, sum_last, sum_first = carry
        low, up = of_step(lower, t), of_step(upper, t)
        e = 1.0 + low * d
        inverse = reciprocal(up + e)
        g = low * inverse
        run = run * g
        inv[t] = inverse
        gain[t] = g
        ratio[t] = up * inverse
        prefix[t] = run
        back = last - 1 - t
        low_b, up_b = of_step(lower, back), of_step(upper, back)
        e_b = 1.0 + up_b * d_b
        inverse_b = reciprocal(low_b + e_b)
        g_b = up_b * inverse_b
        inv_b[back] = inverse_b
        gain_b[back] = g_b
        stencil(t)
        return (
            e * inverse,
            e_b * inverse_b,
            run,
            run_b * g_b,
            inverse + g * sum_last,
            inverse_b + g_b * sum_first,
        )

    carry = lax.fori_loop(0, last, factor, (one, one, one, one, zero, zero))
    _, _, low_gain, high_gain, sum_last, sum_first = carry
    for n in range(last, height // size):
        stencil(n)
    start_all([outgoing[n] for n in (0, 1, 2, 4, 5)])

    def weigh(t, q):
        first[t] = inv_b[t] * q
        return q * gain_b[t]

    lax.fori_loop(0, last, weigh, one, unroll=4)
    outgoing[3].start()

    low_sep, up_sep = of_step(lower, last), of_step(upper, last)
    segment = lax.broadcasted_iota(jnp.int32, one.shape, 1)
    is_end = segment == segments - 1
    above = jnp.where(is_end, 0.0, jnp.roll(sum_first, -1, axis=1))
    couple_high = up_sep * jnp.where(is_end, 1.0, jnp.roll(high_gain, -1, axis=1))
    killing = 1.0 + low_sep * sum_last + up_sep * above
    ends[2, :, :segments, :] = low_sep
    ends[3, :, :segments, :] = up_sep
    tail = slice(height - rest, height)
    low_rest, up_rest = lower[:, tail, :], upper[:, tail, :]
    for n, (value, other) in enumerate(
        (
            (low_sep * low_gain, low_rest),
            (couple_high, up_rest),
            (killing, jnp.ones_like(low_rest)),
        )
    ):
        for x in range(planes):
            rows[n, x * knots : x * knots + segments, :] = value[x]
            rows[n, x * knots + segments : (x + 1) * knots, :] = other[x]
    for x in range(planes):
        rows[3, x * knots : x * knots + segments, :] = high_gain[x]
        rows[4, x * knots : x * knots + segments, :] = sum_first[x]

    def row(n, s):
        return rows[n, pl.ds(s, planes, stride=knots), :]

    top = knots - 1
    one_row = jnp.ones((planes, across), jnp.float32)
    d, d_b = one_row, one_row
    inv_s, gain_s, ratio_s = [], [], []
    inv_sb, gain_sb = [None] * top, [None] * top
    for s in range(top):
        e = row(2, s) + row(0, s) * d
        inverse = reciprocal(row(1, s) + e)
        inv_s.append(inverse)
        gain_s.append(row(0, s) * inverse)
        ratio_s.append(row(1, s) * inverse)
        d = e * inverse
        back = top - 1 - s
        e_b = row(2, back) + row(1, back) * d_b
        inverse_b = reciprocal(row(0, back) + e_b)
        inv_sb[back] = inverse_b
        gain_sb[back] = row(1, back) * inverse_b
        d_b = e_b * inverse_b
        for c in range(components):
            part = slice(c * planes, (c + 1) * planes)
            inner[0, s, part, :] = inv_s[s]
            inner[1, s, part, :] = gain_s[s]
            inner[2, s, part, :] = ratio_s[s]
    outgoing[6].start()
    run = row(0, top)
    low_total = one_row
    sum_top = one_row
    rows[5, pl.ds(top, planes, stride=knots), :] = one_row
    for s in reversed(range(top)):
        weight = run * inv_s[s]
        rows[5, pl.ds(s, planes, stride=knots), :] = weight
        sum_top = sum_top + weight * row(2, s)
        run = run * gain_s[s]
        low_total = low_total * gain_s[s]
    run = row(3, 0)
    high_total = one_row
    sum_bottom = row(4, 0)
    rows[6, pl.ds(top, planes, stride=knots), :] = jnp.zeros_like(one_row)
    for s in range(top):
        weight = run * inv_sb[s]
        rows[6, pl.ds(s, planes, stride=knots), :] = weight
        sum_bottom = sum_bottom + weight * row(2, s)
        run = run * gain_sb[s]
        high_total = high_total * ratio_s[s]
    coef = (
        row(0, top) * low_total,
        sum_top,
        row(1, top),
        sum_bottom,
        row(3, 0) * high_total,
    )
    for n, value in enumerate(coef):
        coefs[n * planes : (n + 1) * planes, :] = value
    for n in range(2):
        for x in range(planes):
            ends[n, x] = rows[5 + n, x * knots : (x + 1) * knots, :]
    start_all(outgoing[7:9])
    wait_all(outgoing)


def deposit_kernel(got, *refs):
    sources, (deposit_hbm, swept, reduced, sums) = refs[:8], refs[8:12]
    (work, cell_rows, rhs, inv, gain, first, ends, coefs) = refs[12:20]
    (field, total, lefts, rights, columns, edges, in_sems, sems) = refs[20:]
    incoming = copies_of(sources, refs[12:20], in_sems)
    start_all(incoming)
    components, planes, height, across = rhs.shape
    steps = inv.shape[0] + 1
    last = steps - 1
    knots = ends.shape[2]
    rest = knots - segments
    slot = components + 1
    senders = lax.axis_size("span")
    block = got.shape[0] // senders
    parts = height // lanes
    shift = across.bit_length() - 1
    lines = components * planes
    kind = jnp.bfloat16 if max(height, across) <= 256 else jnp.float32

    me = lax.axis_index("span")
    below = lax.rem(me + senders - 1, senders)
    above = lax.rem(me + 1, senders)
    total[...] = jnp.zeros_like(total)
    for p in range(parts):
        for n, owner in enumerate((above, below)):
            start = owner * block + p * slot + components
            columns[p, pl.ds(n, lines, stride=2), :] = got[pl.ds(start, lines, stride=parts * slot), :]
        edges[p * lanes : (p + 1) * lanes, :] = diffusion_number * columns[p].T

    tile = 16
    base = lax.broadcasted_iota(jnp.int32, (tile, lanes), 0)
    height_ids = [(base + n * tile).astype(jnp.float32).astype(kind) for n in range(height // tile)]
    across_ids = height_ids[: across // tile]
    lane = lane_iota((1, lanes))
    one = jnp.ones((tile, lanes), jnp.bfloat16)
    none = jnp.zeros((tile, lanes), jnp.bfloat16)

    def spread(row, to):
        return jnp.broadcast_to(row, (tile, lanes)).astype(to)

    def build(n, half):
        for g in range(group):
            ident = work[0, n * group + g]
            live = work[1, n * group + g]
            there = slice(g * lanes, (g + 1) * lanes)
            cell = cell_rows[pl.ds(ident, 1), :]
            up = jnp.where(lane < live, cell >> shift, -1).astype(jnp.float32)
            side = (cell & (across - 1)).astype(jnp.float32)
            up, side = spread(up, kind), spread(side, kind)
            for i, ids in enumerate(height_ids):
                lefts[half][i * tile : (i + 1) * tile, there] = jnp.where(up == ids, one, none)
            masks = [side == ids for ids in across_ids]
            for c in range(components):
                force = got[pl.ds(ident * slot + c, 1), :]
                rest_of = force - force.astype(jnp.bfloat16).astype(jnp.float32)
                for m, value in enumerate((force, rest_of)):
                    value = spread(value, jnp.bfloat16)
                    start = (m * components + c) * across
                    for i, mask in enumerate(masks):
                        place = slice(start + i * tile, start + (i + 1) * tile)
                        rights[half][place, there] = jnp.where(mask, value, none)

    def add(n, half):
        total[work[2, n * group]] += lax.dot_general(
            rights[half][...],
            lefts[half][...],
            (((1,), (1,)), ((), ())),
            preferred_element_type=jnp.float32,
        )

    def two_steps(n, carry):
        build(2 * n + 1, 1)
        add(2 * n, 0)
        build(2 * n + 2, 0)
        add(2 * n + 1, 1)
        return carry

    wait_all(incoming[:2])
    build(0, 0)
    lax.fori_loop(0, work[3, 0], two_steps, 0)
    wait_all(incoming[2:])

    wide = lane_iota((lanes, across))
    border = (wide == 0) | (wide == across - 1)

    def place(x):
        return [
            pltpu.make_async_copy(field.at[c, x], deposit_hbm.at[c, x], sems.at[c, x])
            for c in range(components)
        ]

    def combine(x, carry):
        for c in range(components):
            for p in range(parts):
                part = slice(p * lanes, (p + 1) * lanes)
                high = total[x, c * across : (c + 1) * across, part]
                low = total[x, (components + c) * across : (components + c + 1) * across, part]
                value = (high + low).T
                field[c, x, part, :] = value.astype(jnp.bfloat16)
                edge = pltpu.roll(edges[part, :], lanes - 1 - 2 * (c * planes + x), 1)
                rhs[c, x, part, :] = rhs[c, x, part, :] + value + jnp.where(border, edge, 0.0)
        start_all(place(x))
        return carry

    lax.fori_loop(0, planes, combine, 0)
    sums[2 * lines : 2 * lines + coefs.shape[0], :] = coefs[...]

    zero = jnp.zeros((components, planes, segments, across), jnp.float32)

    def of_step(t):
        return rhs[:, :, pl.ds(t, segments, stride=steps), :]

    def forward(t, carry):
        value, start = carry
        force = of_step(t)
        value = force * inv[t][None] + gain[t][None] * value
        swept[t] = value
        return value, start + first[t][None] * force

    value, start = lax.fori_loop(0, last, forward, (zero, zero), unroll=3)
    segment = lax.broadcasted_iota(jnp.int32, zero.shape, 2)
    after = jnp.where(segment == segments - 1, 0.0, jnp.roll(start, -1, axis=2))
    low_sep, up_sep = ends[2, :, :segments, :], ends[3, :, :segments, :]
    value = of_step(last) + low_sep[None] * value + up_sep[None] * after
    others = rhs[:, :, height - rest :, :]
    at_top = ends[0, :, :segments, :][None] * value + ends[0, :, segments:, :][None] * others
    at_bottom = ends[1, :, :segments, :][None] * value + ends[1, :, segments:, :][None] * others
    at_bottom = at_bottom + jnp.where(segment == 0, start, 0.0)
    for c in range(components):
        for x in range(planes):
            k = c * planes + x
            reduced[k * knots : k * knots + segments, :] = value[c, x]
            reduced[k * knots + segments : (k + 1) * knots, :] = others[c, x]
            sums[k : k + 1, :] = jnp.sum(at_top[c, x], 0, keepdims=True)
            sums[lines + k : lines + k + 1, :] = jnp.sum(at_bottom[c, x], 0, keepdims=True)

    for x in range(planes):
        wait_all(place(x))


def finish_kernel(inner, reduced, swept, ratio, prefix, *refs):
    walls = len(refs) - 7
    received = refs[:walls]
    out_hbm, sums, tops, after, before, out, sems = refs[walls:]
    components, planes, height, across = out.shape
    steps = swept.shape[0] + 1
    last = steps - 1
    lines = components * planes
    knots = inner.shape[1] + 1
    rest = knots - segments
    me = lax.axis_index("wall")
    for n in range(walls):
        sums[lax.rem(me + walls - n, walls)] = received[n][...]

    def coef(k, n):
        start = 2 * lines + n * planes
        return sums[k, start : start + planes, :]

    def wide(value):
        return jnp.concatenate([value] * components, 0)

    d = jnp.ones((planes, across), jnp.float32)
    value = jnp.zeros((lines, across), jnp.float32)
    values, ratios = [], []
    for k in range(walls):
        low, own, up = coef(k, 0), coef(k, 1), coef(k, 2)
        right = sums[k, :lines, :]
        if k + 1 < walls:
            high = up * coef(k + 1, 4)
            killing = own + up * coef(k + 1, 3)
            right = right + wide(up) * sums[k + 1, lines : 2 * lines, :]
        else:
            high = jnp.zeros_like(up)
            killing = own + up
        e = killing + low * d
        inverse = reciprocal(high + e)
        d = e * inverse
        value = (right + wide(low) * value) * wide(inverse)
        values.append(value)
        ratios.append(wide(high * inverse))
    tops[0] = jnp.zeros((lines, across), jnp.float32)
    tops[walls] = values[-1]
    for k in reversed(range(walls - 1)):
        values[k] = values[k] + ratios[k] * values[k + 1]
        tops[k + 1] = values[k]

    def row(s):
        return pl.ds(s, lines, stride=knots)

    run = tops[me]
    before[row(0), :] = run
    found = []
    for s in range(knots - 1):
        run = reduced[row(s), :] * inner[0, s] + inner[1, s] * run
        found.append(run)
    run = tops[me + 1]
    after[row(knots - 1), :] = run
    for s in reversed(range(knots - 1)):
        run = found[s] + inner[2, s] * run
        after[row(s), :] = run
        if s + 1 < segments:
            before[row(s + 1), :] = run

    def put(c, x, t, value):
        out[c, x, pl.ds(t, segments, stride=steps), :] = value

    copies = []
    half = planes // 2 if planes % 2 == 0 else planes
    for start in range(0, planes, half):
        part = [(c, x) for c in range(components) for x in range(start, start + half)]
        bottoms, starts = [], []
        for c, x in part:
            base = (c * planes + x) * knots
            bottoms.append(before[base : base + segments, :])
            starts.append(after[base : base + segments, :])
            out[c, x, height - rest :, :] = after[base + segments : base + knots, :]
            put(c, x, last, starts[-1])

        def backward(n, values):
            t = last - 1 - n
            found = []
            for (c, x), value, bottom in zip(part, values, bottoms):
                value = (swept[t, c, x] + prefix[t, x] * bottom) + ratio[t, x] * value
                put(c, x, t, value)
                found.append(value)
            return tuple(found)

        lax.fori_loop(0, last, backward, tuple(starts), unroll=3)
        for here in part:
            copy = pltpu.make_async_copy(out.at[here], out_hbm.at[here], sems.at[here])
            copy.start()
            copies.append(copy)
    wait_all(copies)


def everyone(block, axis, by_distance):
    length = lax.axis_size(axis)
    found = [by_distance[0]]
    for distance in range(1, length):
        route = [(i, (i + distance) % length) for i in range(length)]
        found.append(lax.ppermute(by_distance[distance], axis, route))
    return found


def local(velocity, lower_weight, upper_weight, forces, cells, counts):
    components, planes, height, across = velocity.shape
    receivers, capacity = forces.shape[3], forces.shape[5]
    senders = cells.shape[2]
    walls = lax.axis_size("wall")
    lines = components * planes
    chunks = capacity // lanes
    slot = components + 1
    forces = forces.reshape(components, receivers, planes, capacity)
    cells = cells.reshape(senders, planes, capacity)
    counts = counts.reshape(senders, planes).T

    def hbm(*arrays):
        return [pltpu.with_memory_space_constraint(array, pltpu.HBM) for array in arrays]

    send = call(
        pack_kernel,
        f32(receivers, planes * chunks * slot, lanes),
        in_hbm,
        [in_hbm] * 2,
        [
            scratch(*velocity.shape),
            scratch(*forces.shape),
            scratch(receivers, planes * chunks * slot, lanes),
            scratch(height, across),
            scratch(height // lanes, lanes, lanes),
            pltpu.SemaphoreType.DMA((components + lines + receivers,)),
        ],
        8,
        1 << 22,
    )(*hbm(velocity, forces))
    got = lax.all_to_all(send, "span", 0, 0, tiled=True)

    steps = height // segments - 1
    knots = height - segments * steps + segments
    step_shape = (steps - 1, planes, segments, across)
    work_length = planes * (senders * chunks + group) + 3 * group
    staged = [
        velocity.shape,
        *[step_shape] * 5,
        (3, knots - 1, lines, across),
        (4, planes, knots, across),
        (5 * planes, across),
    ]
    cell_shape = (senders * planes * chunks, lanes)
    work_shape = (4, work_length)
    prepared = call(
        prepare_kernel,
        (
            *[f32(*shape) for shape in staged],
            jax.ShapeDtypeStruct(cell_shape, jnp.int32),
            jax.ShapeDtypeStruct(work_shape, jnp.int32),
        ),
        [in_hbm] * 11,
        [in_smem] + [in_vmem] * 4,
        [
            *[scratch(*shape) for shape in staged],
            pltpu.VMEM(cell_shape, jnp.int32),
            pltpu.SMEM(work_shape, jnp.int32),
            scratch(*step_shape),
            scratch(*step_shape),
            scratch(7, planes * knots, across),
            pltpu.SemaphoreType.DMA((11,)),
        ],
        16,
        1 << 24,
    )(counts, cells, velocity, lower_weight, upper_weight)
    (rhs_start, inv, gain, first, ratio, prefix, inner, ends, coefs, cell_rows, work) = prepared

    sum_rows = -(-(2 * lines + 5 * planes) // 8) * 8
    wide = 2 * components * across
    deposit, swept, reduced, sums = call(
        deposit_kernel,
        (
            jax.ShapeDtypeStruct(velocity.shape, jnp.bfloat16),
            f32(steps - 1, components, planes, segments, across),
            f32(lines * knots, across),
            f32(sum_rows, across),
        ),
        (in_hbm, *[in_vmem] * 3),
        [in_vmem] + [in_hbm] * 8,
        [
            pltpu.SMEM(work_shape, jnp.int32),
            pltpu.VMEM(cell_shape, jnp.int32),
            scratch(*velocity.shape),
            *[scratch(*step_shape)] * 3,
            scratch(*staged[7]),
            scratch(*staged[8]),
            pltpu.VMEM(velocity.shape, jnp.bfloat16),
            scratch(planes, wide, height),
            [pltpu.VMEM((height, group * lanes), jnp.bfloat16)] * 2,
            [pltpu.VMEM((wide, group * lanes), jnp.bfloat16)] * 2,
            scratch(height // lanes, lanes, lanes),
            scratch(height, lanes),
            pltpu.SemaphoreType.DMA((8,)),
            pltpu.SemaphoreType.DMA((components, planes)),
        ],
        24,
        1 << 32,
    )(
        got.reshape(-1, lanes),
        *hbm(work, cell_rows, rhs_start, inv, gain, first, ends, coefs),
    )
    all_sums = everyone(sums, "wall", [sums] * walls)

    velocity_next = call(
        finish_kernel,
        f32(*velocity.shape),
        in_hbm,
        [in_vmem] * (5 + walls),
        [
            scratch(walls, sum_rows, across),
            scratch(walls + 1, lines, across),
            scratch(lines * knots, across),
            scratch(lines * knots, across),
            scratch(*velocity.shape),
            pltpu.SemaphoreType.DMA((components, planes)),
        ],
        8,
        1 << 22,
    )(inner, reduced, swept, ratio, prefix, *all_sums)
    return (velocity_next, deposit)


def solution(mesh):
    placed = (
        P(None, None, "wall", "span"),
        P(None, "wall", "span"),
        P(None, "wall", "span"),
        P(None, "wall", "span", None, None, None),
        P("wall", "span", None, None, None),
        P("wall", "span", None, None),
    )
    return jax.shard_map(
        local,
        mesh=mesh,
        in_specs=placed,
        out_specs=(P(None, None, "wall", "span"), P(None, None, "wall", "span")),
        check_vma=False,
    )
```

```python
import jax
import jax.numpy as jnp
from jax import lax
from jax.experimental import pallas as pl
from jax.experimental.pallas import tpu as pltpu
from jax.sharding import PartitionSpec as P

diffusion_number = 0.2
segments = 8
lanes = 128
group = 8
count_bits, plane_bit = 10, 24
in_vmem = pl.BlockSpec(memory_space=pltpu.VMEM)
in_smem = pl.BlockSpec(memory_space=pltpu.SMEM)
in_hbm = pl.BlockSpec(memory_space=pltpu.HBM)


def call(body, out_shape, out_specs, in_specs, scratch, mebibytes, flops):
    return pl.pallas_call(
        body,
        out_shape=out_shape,
        in_specs=in_specs,
        out_specs=out_specs,
        scratch_shapes=scratch,
        compiler_params=pltpu.CompilerParams(vmem_limit_bytes=mebibytes << 20),
        cost_estimate=pl.CostEstimate(flops=flops, bytes_accessed=4 << 20, transcendentals=0),
    )


def f32(*shape):
    return jax.ShapeDtypeStruct(shape, jnp.float32)


def scratch(*shape):
    return pltpu.VMEM(shape, jnp.float32)


def lane_iota(shape):
    return lax.broadcasted_iota(jnp.int32, shape, len(shape) - 1)


def reciprocal(value):
    rough = pl.reciprocal(value, approx=True)
    return rough * (2.0 - value * rough)


def start_all(copies):
    for copy in copies:
        copy.start()


def wait_all(copies):
    for copy in copies:
        copy.wait()


def copies_of(sources, targets, sems, first=0):
    return [
        pltpu.make_async_copy(source, target, sems.at[first + n])
        for n, (source, target) in enumerate(zip(sources, targets))
    ]


def pack_kernel(velocity_hbm, forces_hbm, send_hbm, velocity, forces, send, columns, turned, sems):
    components, planes, height, across = velocity_hbm.shape
    receivers, capacity = forces_hbm.shape[1], forces_hbm.shape[3]
    chunks = capacity // lanes
    lines = components * planes
    parts = height // lanes
    slot = components + 1
    copies = copies_of(
        [forces_hbm.at[c] for c in range(components)],
        [forces.at[c] for c in range(components)],
        sems,
    )
    places = [(c, x) for c in range(components) for x in range(planes)]
    copies += copies_of(
        [velocity_hbm.at[here] for here in places],
        [velocity.at[here] for here in places],
        sems,
        components,
    )
    start_all(copies)
    me = lax.axis_index("span")
    wait_all(copies[:components])
    outgoing = []
    for d in range(receivers):
        owner = lax.rem(me + d, receivers)
        for c in range(components):
            for k in range(chunks):
                value = forces[c, owner, :, k * lanes : (k + 1) * lanes]
                send[owner, pl.ds(k * slot + c, planes, stride=chunks * slot), :] = value
        index = components + lines + d
        copy = pltpu.make_async_copy(send.at[owner], send_hbm.at[owner], sems.at[index])
        outgoing.append(copy)
        if d not in (1, receivers - 1):
            copy.start()
    lane = lane_iota((height, across))
    picked = jnp.zeros((height, across), jnp.float32)
    for k in range(lines):
        copies[components + k].wait()
        rolled = pltpu.roll(velocity[k // planes, k % planes], 2 * k + 1, 1)
        picked = jnp.where((lane >> 1) == k, rolled, picked)
    columns[...] = picked
    below = lax.rem(me + receivers - 1, receivers)
    above = lax.rem(me + 1, receivers)
    for p in range(parts):
        turned[p] = columns[p * lanes : (p + 1) * lanes, :].T
        target = pl.ds(p * slot + components, lines, stride=parts * slot)
        send[below, target, :] = turned[p, pl.ds(1, lines, stride=2), :]
        send[above, target, :] = turned[p, pl.ds(0, lines, stride=2), :]
    outgoing[1].start()
    outgoing[receivers - 1].start()
    wait_all(outgoing)


def prepare_kernel(counts, cells, velocity, lower, upper, *refs):
    (rhs, inv, first, inner, ends, coefs, cell_rows, work_out) = refs[:8]
    (work, inv_b, gain_b, rows, sem) = refs[8:]
    components, planes, height, across = velocity.shape
    steps = inv.shape[0] + 1
    last = steps - 1
    rest = height - segments * steps
    knots = segments + rest
    senders, capacity = cells.shape[0], cells.shape[2]
    chunks = capacity // lanes
    pairs = planes * senders
    pairs_each = -(-pairs // last)

    def one_sender(s, carry):
        for k in range(chunks):
            start = s * planes * chunks + k
            value = cells[s, :, k * lanes : (k + 1) * lanes]
            cell_rows[pl.ds(start, planes, stride=chunks), :] = value
        return carry

    lax.fori_loop(0, senders, one_sender, 0, unroll=4)

    def list_pair(i, n):
        used = jnp.minimum(i, pairs - 1)
        x = lax.div(used, senders)
        s = used - x * senders
        count = jnp.where(i < pairs, counts[x, s], 0)
        base = (x << plane_bit) + (((s * planes + x) * chunks) << count_bits)
        for k in range(chunks):
            live = jnp.maximum(count - k * lanes, 0)
            work[group + n + k] = base + (k << count_bits) + live
        n = n + lax.div(count + lanes - 1, lanes)
        for extra in range(group):
            work[group + n + extra] = 0
        return jnp.where(s == senders - 1, lax.div(n + group - 1, group) * group, n)

    def of_step(ref, t):
        return ref[:, pl.ds(t, segments, stride=steps), :]

    one = jnp.ones((planes, segments, across), jnp.float32)
    zero = jnp.zeros_like(one)
    size = 8
    lane = lane_iota((size, across))

    def stencil(n):
        part = pl.ds(pl.multiple_of(n * size, size), size)
        for c in range(components):
            values = [velocity[c, x, part, :] for x in range(planes)]
            for x in range(planes):
                v = values[x]
                around = values[(x - 1) % planes] + values[(x + 1) % planes]
                around = around + jnp.where(lane == 0, 0.0, pltpu.roll(v, 1, 1))
                around = around + jnp.where(lane == across - 1, 0.0, pltpu.roll(v, across - 1, 1))
                rhs[c, x, part, :] = (1.0 - 4.0 * diffusion_number) * v + diffusion_number * around

    def factor(t, carry):
        d, d_b, low_gain, high_gain, sum_last, sum_first, n = carry
        low, up = of_step(lower, t), of_step(upper, t)
        e = 1.0 + low * d
        inverse = reciprocal(up + e)
        g = low * inverse
        inv[t] = inverse
        back = last - 1 - t
        low_b, up_b = of_step(lower, back), of_step(upper, back)
        e_b = 1.0 + up_b * d_b
        inverse_b = reciprocal(low_b + e_b)
        g_b = up_b * inverse_b
        inv_b[back] = inverse_b
        gain_b[back] = g_b
        stencil(t)
        for extra in range(pairs_each):
            n = list_pair(t * pairs_each + extra, n)
        return (
            e * inverse,
            e_b * inverse_b,
            low_gain * g,
            high_gain * g_b,
            inverse + g * sum_last,
            inverse_b + g_b * sum_first,
            n,
        )

    carry = lax.fori_loop(0, last, factor, (one, one, one, one, zero, zero, 0))
    _, _, low_gain, high_gain, sum_last, sum_first, total = carry
    for extra in range(2 * group):
        work[group + total + extra] = 0
    work[0] = lax.div(total + 2 * group - 1, 2 * group)
    list_copy = pltpu.make_async_copy(work, work_out, sem)
    list_copy.start()
    for n in range(last, height // size):
        stencil(n)

    def weigh(t, q):
        first[t] = inv_b[t] * q
        return q * gain_b[t]

    lax.fori_loop(0, last, weigh, one, unroll=6)

    low_sep, up_sep = of_step(lower, last), of_step(upper, last)
    segment = lax.broadcasted_iota(jnp.int32, one.shape, 1)
    is_end = segment == segments - 1
    above = jnp.where(is_end, 0.0, jnp.roll(sum_first, -1, axis=1))
    couple_high = up_sep * jnp.where(is_end, 1.0, jnp.roll(high_gain, -1, axis=1))
    killing = 1.0 + low_sep * sum_last + up_sep * above
    ends[2, :, :segments, :] = low_sep
    ends[3, :, :segments, :] = up_sep
    tail = slice(height - rest, height)
    low_rest, up_rest = lower[:, tail, :], upper[:, tail, :]
    for n, (value, other) in enumerate(
        (
            (low_sep * low_gain, low_rest),
            (couple_high, up_rest),
            (killing, jnp.ones_like(low_rest)),
        )
    ):
        for x in range(planes):
            rows[n, x * knots : x * knots + segments, :] = value[x]
            rows[n, x * knots + segments : (x + 1) * knots, :] = other[x]
    for x in range(planes):
        rows[3, x * knots : x * knots + segments, :] = high_gain[x]
        rows[4, x * knots : x * knots + segments, :] = sum_first[x]

    def row(n, s):
        return rows[n, pl.ds(s, planes, stride=knots), :]

    top = knots - 1
    one_row = jnp.ones((planes, across), jnp.float32)
    d, d_b = one_row, one_row
    inv_s, gain_s, ratio_s = [], [], []
    inv_sb, gain_sb = [None] * top, [None] * top
    for s in range(top):
        e = row(2, s) + row(0, s) * d
        inverse = reciprocal(row(1, s) + e)
        inv_s.append(inverse)
        gain_s.append(row(0, s) * inverse)
        ratio_s.append(row(1, s) * inverse)
        d = e * inverse
        back = top - 1 - s
        e_b = row(2, back) + row(1, back) * d_b
        inverse_b = reciprocal(row(0, back) + e_b)
        inv_sb[back] = inverse_b
        gain_sb[back] = row(1, back) * inverse_b
        d_b = e_b * inverse_b
        inner[0, s] = inv_s[s]
        inner[1, s] = gain_s[s]
        inner[2, s] = ratio_s[s]
    run = row(0, top)
    low_total = one_row
    sum_top = one_row
    rows[5, pl.ds(top, planes, stride=knots), :] = one_row
    for s in reversed(range(top)):
        weight = run * inv_s[s]
        rows[5, pl.ds(s, planes, stride=knots), :] = weight
        sum_top = sum_top + weight * row(2, s)
        run = run * gain_s[s]
        low_total = low_total * gain_s[s]
    run = row(3, 0)
    high_total = one_row
    sum_bottom = row(4, 0)
    rows[6, pl.ds(top, planes, stride=knots), :] = jnp.zeros_like(one_row)
    for s in range(top):
        weight = run * inv_sb[s]
        rows[6, pl.ds(s, planes, stride=knots), :] = weight
        sum_bottom = sum_bottom + weight * row(2, s)
        run = run * gain_sb[s]
        high_total = high_total * ratio_s[s]
    coef = (
        row(0, top) * low_total,
        sum_top,
        row(1, top),
        sum_bottom,
        row(3, 0) * high_total,
    )
    for n, value in enumerate(coef):
        coefs[n * planes : (n + 1) * planes, :] = value
    for n in range(2):
        for x in range(planes):
            ends[n, x] = rows[5 + n, x * knots : (x + 1) * knots, :]
    list_copy.wait()


def deposit_kernel(
    got, cell_rows, rhs_start, inv, first, ends, coefs, work_in, lower_hbm, *refs
):
    (deposit_hbm, swept, prefix, reduced, sums) = refs[:5]
    (work, lower, rhs, field, total, lefts, rights, columns, edges, in_sems, sems) = refs[5:]
    incoming = copies_of([work_in, lower_hbm], [work, lower], in_sems)
    start_all(incoming)
    components, planes, height, across = rhs.shape
    steps = inv.shape[0] + 1
    last = steps - 1
    knots = ends.shape[2]
    rest = knots - segments
    slot = components + 1
    senders = lax.axis_size("span")
    block = got.shape[0] // senders
    parts = height // lanes
    shift = across.bit_length() - 1
    lines = components * planes
    kind = jnp.bfloat16 if max(height, across) <= 256 else jnp.float32

    me = lax.axis_index("span")
    below = lax.rem(me + senders - 1, senders)
    above = lax.rem(me + 1, senders)
    total[...] = jnp.zeros_like(total)
    for p in range(parts):
        for n, owner in enumerate((above, below)):
            start = owner * block + p * slot + components
            columns[p, pl.ds(n, lines, stride=2), :] = got[pl.ds(start, lines, stride=parts * slot), :]
        edges[p * lanes : (p + 1) * lanes, :] = diffusion_number * columns[p].T

    tile = 16
    base = lax.broadcasted_iota(jnp.int32, (tile, lanes), 0)
    height_ids = [(base + n * tile).astype(jnp.float32).astype(kind) for n in range(height // tile)]
    across_ids = height_ids[: across // tile]
    lane = lane_iota((1, lanes))
    one = jnp.ones((tile, lanes), jnp.bfloat16)
    none = jnp.zeros((tile, lanes), jnp.bfloat16)

    def spread(row, to):
        return jnp.broadcast_to(row, (tile, lanes)).astype(to)

    def build(n, half):
        for g in range(group):
            word = work[(n + 1) * group + g]
            ident = (word >> count_bits) & ((1 << (plane_bit - count_bits)) - 1)
            live = word & ((1 << count_bits) - 1)
            there = slice(g * lanes, (g + 1) * lanes)
            cell = cell_rows[pl.ds(ident, 1), :]
            up = jnp.where(lane < live, cell >> shift, -1).astype(jnp.float32)
            side = (cell & (across - 1)).astype(jnp.float32)
            up, side = spread(up, kind), spread(side, kind)
            for i, ids in enumerate(height_ids):
                lefts[half][i * tile : (i + 1) * tile, there] = jnp.where(up == ids, one, none)
            masks = [side == ids for ids in across_ids]
            for c in range(components):
                force = got[pl.ds(ident * slot + c, 1), :]
                rest_of = force - force.astype(jnp.bfloat16).astype(jnp.float32)
                for m, value in enumerate((force, rest_of)):
                    value = spread(value, jnp.bfloat16)
                    start = (m * components + c) * across
                    for i, mask in enumerate(masks):
                        place = slice(start + i * tile, start + (i + 1) * tile)
                        rights[half][place, there] = jnp.where(mask, value, none)

    def add(n, half):
        total[work[(n + 1) * group] >> plane_bit] += lax.dot_general(
            rights[half][...],
            lefts[half][...],
            (((1,), (1,)), ((), ())),
            preferred_element_type=jnp.float32,
        )

    def two_steps(n, carry):
        build(2 * n + 1, 1)
        add(2 * n, 0)
        build(2 * n + 2, 0)
        add(2 * n + 1, 1)
        return carry

    incoming[0].wait()
    build(0, 0)
    lax.fori_loop(0, work[0], two_steps, 0)
    incoming[1].wait()

    wide = lane_iota((lanes, across))
    border = (wide == 0) | (wide == across - 1)

    def place(x):
        return [
            pltpu.make_async_copy(field.at[c, x], deposit_hbm.at[c, x], sems.at[c, x])
            for c in range(components)
        ]

    def combine(x, carry):
        for c in range(components):
            for p in range(parts):
                part = slice(p * lanes, (p + 1) * lanes)
                high = total[x, c * across : (c + 1) * across, part]
                low = total[x, (components + c) * across : (components + c + 1) * across, part]
                value = (high + low).T
                field[c, x, part, :] = value.astype(jnp.bfloat16)
                edge = pltpu.roll(edges[part, :], lanes - 1 - 2 * (c * planes + x), 1)
                rhs[c, x, part, :] = rhs_start[c, x, part, :] + value + jnp.where(border, edge, 0.0)
        start_all(place(x))
        return carry

    lax.fori_loop(0, planes, combine, 0)
    sums[2 * lines : 2 * lines + coefs.shape[0], :] = coefs[...]

    zero = jnp.zeros((components, planes, segments, across), jnp.float32)

    def of_step(t):
        return rhs[:, :, pl.ds(t, segments, stride=steps), :]

    def forward(t, carry):
        value, start, run, before = carry
        force = of_step(t)
        low, inverse = lower[:, pl.ds(t, segments, stride=steps), :], inv[t]
        value = force + (low * before)[None] * value
        swept[t] = inverse[None] * value
        run = run * (low * inverse)
        prefix[t] = run
        return value, start + first[t][None] * force, run, inverse

    one = jnp.ones((planes, segments, across), jnp.float32)
    value, start, _, inverse = lax.fori_loop(0, last, forward, (zero, zero, one, one), unroll=3)
    value = inverse[None] * value
    segment = lax.broadcasted_iota(jnp.int32, zero.shape, 2)
    after = jnp.where(segment == segments - 1, 0.0, jnp.roll(start, -1, axis=2))
    low_sep, up_sep = ends[2, :, :segments, :], ends[3, :, :segments, :]
    value = of_step(last) + low_sep[None] * value + up_sep[None] * after
    others = rhs[:, :, height - rest :, :]
    at_top = ends[0, :, :segments, :][None] * value + ends[0, :, segments:, :][None] * others
    at_bottom = ends[1, :, :segments, :][None] * value + ends[1, :, segments:, :][None] * others
    at_bottom = at_bottom + jnp.where(segment == 0, start, 0.0)
    for c in range(components):
        for x in range(planes):
            k = c * planes + x
            reduced[k * knots : k * knots + segments, :] = value[c, x]
            reduced[k * knots + segments : (k + 1) * knots, :] = others[c, x]
            sums[k : k + 1, :] = jnp.sum(at_top[c, x], 0, keepdims=True)
            sums[lines + k : lines + k + 1, :] = jnp.sum(at_bottom[c, x], 0, keepdims=True)

    for x in range(planes):
        wait_all(place(x))


def finish_kernel(inner, reduced, swept, inv, prefix, upper, *refs):
    walls = len(refs) - 7
    received = refs[:walls]
    out_hbm, sums, tops, after, before, out, sems = refs[walls:]
    components, planes, height, across = out.shape
    steps = swept.shape[0] + 1
    last = steps - 1
    lines = components * planes
    knots = inner.shape[1] + 1
    rest = knots - segments
    me = lax.axis_index("wall")
    for n in range(walls):
        sums[lax.rem(me + walls - n, walls)] = received[n][...]

    def coef(k, n):
        start = 2 * lines + n * planes
        return sums[k, start : start + planes, :]

    def wide(value):
        return jnp.concatenate([value] * components, 0)

    d = jnp.ones((planes, across), jnp.float32)
    value = jnp.zeros((lines, across), jnp.float32)
    values, ratios = [], []
    for k in range(walls):
        low, own, up = coef(k, 0), coef(k, 1), coef(k, 2)
        right = sums[k, :lines, :]
        if k + 1 < walls:
            high = up * coef(k + 1, 4)
            killing = own + up * coef(k + 1, 3)
            right = right + wide(up) * sums[k + 1, lines : 2 * lines, :]
        else:
            high = jnp.zeros_like(up)
            killing = own + up
        e = killing + low * d
        inverse = reciprocal(high + e)
        d = e * inverse
        value = (right + wide(low) * value) * wide(inverse)
        values.append(value)
        ratios.append(wide(high * inverse))
    tops[0] = jnp.zeros((lines, across), jnp.float32)
    tops[walls] = values[-1]
    for k in reversed(range(walls - 1)):
        values[k] = values[k] + ratios[k] * values[k + 1]
        tops[k + 1] = values[k]

    def row(s):
        return pl.ds(s, lines, stride=knots)

    run = tops[me]
    before[row(0), :] = run
    found = []
    for s in range(knots - 1):
        run = reduced[row(s), :] * wide(inner[0, s]) + wide(inner[1, s]) * run
        found.append(run)
    run = tops[me + 1]
    after[row(knots - 1), :] = run
    for s in reversed(range(knots - 1)):
        run = found[s] + wide(inner[2, s]) * run
        after[row(s), :] = run
        if s + 1 < segments:
            before[row(s + 1), :] = run

    def put(c, x, t, value):
        out[c, x, pl.ds(t, segments, stride=steps), :] = value

    copies = []
    half = planes // 2 if planes % 2 == 0 else planes
    for start in range(0, planes, half):
        part = [(c, x) for c in range(components) for x in range(start, start + half)]
        bottoms, starts = [], []
        for c, x in part:
            base = (c * planes + x) * knots
            bottoms.append(before[base : base + segments, :])
            starts.append(after[base : base + segments, :])
            out[c, x, height - rest :, :] = after[base + segments : base + knots, :]
            put(c, x, last, starts[-1])

        def backward(n, values):
            t = last - 1 - n
            found = []
            ratios = {}
            for x in range(start, start + half):
                ratios[x] = upper[x, pl.ds(t, segments, stride=steps), :] * inv[t, x]
            for (c, x), value, bottom in zip(part, values, bottoms):
                value = (swept[t, c, x] + prefix[t, x] * bottom) + ratios[x] * value
                put(c, x, t, value)
                found.append(value)
            return tuple(found)

        lax.fori_loop(0, last, backward, tuple(starts), unroll=3)
        for here in part:
            copy = pltpu.make_async_copy(out.at[here], out_hbm.at[here], sems.at[here])
            copy.start()
            copies.append(copy)
    wait_all(copies)


def everyone(block, axis, by_distance):
    length = lax.axis_size(axis)
    found = [by_distance[0]]
    for distance in range(1, length):
        route = [(i, (i + distance) % length) for i in range(length)]
        found.append(lax.ppermute(by_distance[distance], axis, route))
    return found


def local(velocity, lower_weight, upper_weight, forces, cells, counts):
    components, planes, height, across = velocity.shape
    receivers, capacity = forces.shape[3], forces.shape[5]
    senders = cells.shape[2]
    walls = lax.axis_size("wall")
    lines = components * planes
    chunks = capacity // lanes
    slot = components + 1
    forces = forces.reshape(components, receivers, planes, capacity)
    cells = cells.reshape(senders, planes, capacity)
    counts = counts.reshape(senders, planes).T

    def hbm(*arrays):
        return [pltpu.with_memory_space_constraint(array, pltpu.HBM) for array in arrays]

    send, velocity_near = call(
        pack_kernel,
        (f32(receivers, planes * chunks * slot, lanes), f32(*velocity.shape)),
        (in_hbm, in_vmem),
        [in_hbm] * 2,
        [
            scratch(*forces.shape),
            scratch(receivers, planes * chunks * slot, lanes),
            scratch(height, across),
            scratch(height // lanes, lanes, lanes),
            pltpu.SemaphoreType.DMA((components + lines + receivers,)),
        ],
        8,
        1 << 22,
    )(*hbm(velocity, forces))
    got = lax.all_to_all(send, "span", 0, 0, tiled=True)

    steps = height // segments - 1
    knots = height - segments * steps + segments
    step_shape = (steps - 1, planes, segments, across)
    work_shape = (planes * (senders * chunks + group) + 4 * group,)
    prepared = call(
        prepare_kernel,
        (
            f32(*velocity.shape),
            f32(*step_shape),
            f32(*step_shape),
            f32(3, knots - 1, planes, across),
            f32(4, planes, knots, across),
            f32(5 * planes, across),
            jax.ShapeDtypeStruct((senders * planes * chunks, lanes), jnp.int32),
            jax.ShapeDtypeStruct(work_shape, jnp.int32),
        ),
        [in_vmem] * 8,
        [in_smem] + [in_vmem] * 4,
        [
            pltpu.SMEM(work_shape, jnp.int32),
            scratch(*step_shape),
            scratch(*step_shape),
            scratch(7, planes * knots, across),
            pltpu.SemaphoreType.DMA,
        ],
        8,
        1 << 24,
    )(counts, cells, velocity_near, lower_weight, upper_weight)
    (rhs_start, inv, first, inner, ends, coefs, cell_rows, work) = prepared

    sum_rows = -(-(2 * lines + 5 * planes) // 8) * 8
    wide = 2 * components * across
    deposit, swept, prefix, reduced, sums = call(
        deposit_kernel,
        (
            jax.ShapeDtypeStruct(velocity.shape, jnp.bfloat16),
            f32(steps - 1, components, planes, segments, across),
            f32(*step_shape),
            f32(lines * knots, across),
            f32(sum_rows, across),
        ),
        (in_hbm, *[in_vmem] * 4),
        [in_vmem] * 8 + [in_hbm],
        [
            pltpu.SMEM(work_shape, jnp.int32),
            scratch(*lower_weight.shape),
            scratch(*velocity.shape),
            pltpu.VMEM(velocity.shape, jnp.bfloat16),
            scratch(planes, wide, height),
            [pltpu.VMEM((height, group * lanes), jnp.bfloat16)] * 2,
            [pltpu.VMEM((wide, group * lanes), jnp.bfloat16)] * 2,
            scratch(height // lanes, lanes, lanes),
            scratch(height, lanes),
            pltpu.SemaphoreType.DMA((2,)),
            pltpu.SemaphoreType.DMA((components, planes)),
        ],
        24,
        1 << 32,
    )(
        got.reshape(-1, lanes),
        cell_rows,
        rhs_start,
        inv,
        first,
        ends,
        coefs,
        work,
        *hbm(lower_weight),
    )
    all_sums = everyone(sums, "wall", [sums] * walls)

    velocity_next = call(
        finish_kernel,
        f32(*velocity.shape),
        in_hbm,
        [in_vmem] * (6 + walls),
        [
            scratch(walls, sum_rows, across),
            scratch(walls + 1, lines, across),
            scratch(lines * knots, across),
            scratch(lines * knots, across),
            scratch(*velocity.shape),
            pltpu.SemaphoreType.DMA((components, planes)),
        ],
        8,
        1 << 22,
    )(inner, reduced, swept, inv, prefix, upper_weight, *all_sums)
    return (velocity_next, deposit)


def solution(mesh):
    placed = (
        P(None, None, "wall", "span"),
        P(None, "wall", "span"),
        P(None, "wall", "span"),
        P(None, "wall", "span", None, None, None),
        P("wall", "span", None, None, None),
        P("wall", "span", None, None),
    )
    return jax.shard_map(
        local,
        mesh=mesh,
        in_specs=placed,
        out_specs=(P(None, None, "wall", "span"), P(None, None, "wall", "span")),
        check_vma=False,
    )
```

```python
import jax
import jax.numpy as jnp
from jax import lax
from jax.experimental import pallas as pl
from jax.experimental.pallas import tpu as pltpu
from jax.sharding import PartitionSpec as P

diffusion_number = 0.2
segments = 8
lanes = 128
group = 8
count_bits, plane_bit = 10, 24
in_vmem = pl.BlockSpec(memory_space=pltpu.VMEM)
in_smem = pl.BlockSpec(memory_space=pltpu.SMEM)
in_hbm = pl.BlockSpec(memory_space=pltpu.HBM)


def call(body, out_shape, out_specs, in_specs, scratch, mebibytes, flops):
    return pl.pallas_call(
        body,
        out_shape=out_shape,
        in_specs=in_specs,
        out_specs=out_specs,
        scratch_shapes=scratch,
        compiler_params=pltpu.CompilerParams(vmem_limit_bytes=mebibytes << 20),
        cost_estimate=pl.CostEstimate(flops=flops, bytes_accessed=4 << 20, transcendentals=0),
    )


def f32(*shape):
    return jax.ShapeDtypeStruct(shape, jnp.float32)


def scratch(*shape):
    return pltpu.VMEM(shape, jnp.float32)


def lane_iota(shape):
    return lax.broadcasted_iota(jnp.int32, shape, len(shape) - 1)


def reciprocal(value):
    rough = pl.reciprocal(value, approx=True)
    return rough * (2.0 - value * rough)


def start_all(copies):
    for copy in copies:
        copy.start()


def wait_all(copies):
    for copy in copies:
        copy.wait()


def copies_of(sources, targets, sems, first=0):
    return [
        pltpu.make_async_copy(source, target, sems.at[first + n])
        for n, (source, target) in enumerate(zip(sources, targets))
    ]


def pack_kernel(velocity_hbm, forces_hbm, send_hbm, velocity, forces, send, columns, turned, sems):
    components, planes, height, across = velocity_hbm.shape
    receivers, capacity = forces_hbm.shape[1], forces_hbm.shape[3]
    chunks = capacity // lanes
    lines = components * planes
    parts = height // lanes
    slot = components + 1
    copies = copies_of(
        [forces_hbm.at[c] for c in range(components)],
        [forces.at[c] for c in range(components)],
        sems,
    )
    places = [(c, x) for c in range(components) for x in range(planes)]
    copies += copies_of(
        [velocity_hbm.at[here] for here in places],
        [velocity.at[here] for here in places],
        sems,
        components,
    )
    start_all(copies)
    me = lax.axis_index("span")
    wait_all(copies[:components])
    outgoing = []
    for d in range(receivers):
        owner = lax.rem(me + d, receivers)
        for c in range(components):
            for k in range(chunks):
                value = forces[c, owner, :, k * lanes : (k + 1) * lanes]
                send[owner, pl.ds(k * slot + c, planes, stride=chunks * slot), :] = value
        index = components + lines + d
        copy = pltpu.make_async_copy(send.at[owner], send_hbm.at[owner], sems.at[index])
        outgoing.append(copy)
        if d not in (1, receivers - 1):
            copy.start()
    lane = lane_iota((height, across))
    picked = jnp.zeros((height, across), jnp.float32)
    for k in range(lines):
        copies[components + k].wait()
        rolled = pltpu.roll(velocity[k // planes, k % planes], 2 * k + 1, 1)
        picked = jnp.where((lane >> 1) == k, rolled, picked)
    columns[...] = picked
    below = lax.rem(me + receivers - 1, receivers)
    above = lax.rem(me + 1, receivers)
    for p in range(parts):
        turned[p] = columns[p * lanes : (p + 1) * lanes, :].T
        target = pl.ds(p * slot + components, lines, stride=parts * slot)
        send[below, target, :] = turned[p, pl.ds(1, lines, stride=2), :]
        send[above, target, :] = turned[p, pl.ds(0, lines, stride=2), :]
    outgoing[1].start()
    outgoing[receivers - 1].start()
    wait_all(outgoing)


def prepare_kernel(counts, cells_hbm, velocity, lower, upper, *refs):
    (rhs, inv, first, inner, ends, coefs, cell_rows, work) = refs[8:16]
    (cells, inv_b, gain_b, rows, sems) = refs[16:]
    outgoing = copies_of(refs[8:16], refs[:8], sems)
    cells_copy = pltpu.make_async_copy(cells_hbm, cells, sems.at[8])
    cells_copy.start()
    components, planes, height, across = velocity.shape
    steps = inv.shape[0] + 1
    last = steps - 1
    rest = height - segments * steps
    knots = segments + rest
    senders, capacity = cells.shape[0], cells.shape[2]
    chunks = capacity // lanes
    pairs = planes * senders
    pairs_each = -(-pairs // last)

    def list_pair(i, n):
        used = jnp.minimum(i, pairs - 1)
        x = lax.div(used, senders)
        s = used - x * senders
        count = jnp.where(i < pairs, counts[x, s], 0)
        base = (x << plane_bit) + (((s * planes + x) * chunks) << count_bits)
        for k in range(chunks):
            live = jnp.maximum(count - k * lanes, 0)
            work[group + n + k] = base + (k << count_bits) + live
        n = n + lax.div(count + lanes - 1, lanes)
        for extra in range(group):
            work[group + n + extra] = 0
        return jnp.where(s == senders - 1, lax.div(n + group - 1, group) * group, n)

    def of_step(ref, t):
        return ref[:, pl.ds(t, segments, stride=steps), :]

    one = jnp.ones((planes, segments, across), jnp.float32)
    zero = jnp.zeros_like(one)
    size = 8
    lane = lane_iota((size, across))

    def stencil(n):
        part = pl.ds(pl.multiple_of(n * size, size), size)
        for c in range(components):
            values = [velocity[c, x, part, :] for x in range(planes)]
            for x in range(planes):
                v = values[x]
                around = values[(x - 1) % planes] + values[(x + 1) % planes]
                around = around + jnp.where(lane == 0, 0.0, pltpu.roll(v, 1, 1))
                around = around + jnp.where(lane == across - 1, 0.0, pltpu.roll(v, across - 1, 1))
                rhs[c, x, part, :] = (1.0 - 4.0 * diffusion_number) * v + diffusion_number * around

    def factor(t, carry):
        d, d_b, low_gain, high_gain, sum_last, sum_first, n = carry
        low, up = of_step(lower, t), of_step(upper, t)
        e = 1.0 + low * d
        inverse = reciprocal(up + e)
        g = low * inverse
        inv[t] = inverse
        back = last - 1 - t
        low_b, up_b = of_step(lower, back), of_step(upper, back)
        e_b = 1.0 + up_b * d_b
        inverse_b = reciprocal(low_b + e_b)
        g_b = up_b * inverse_b
        inv_b[back] = inverse_b
        gain_b[back] = g_b
        stencil(t)
        for extra in range(pairs_each):
            n = list_pair(t * pairs_each + extra, n)
        return (
            e * inverse,
            e_b * inverse_b,
            low_gain * g,
            high_gain * g_b,
            inverse + g * sum_last,
            inverse_b + g_b * sum_first,
            n,
        )

    carry = lax.fori_loop(0, last, factor, (one, one, one, one, zero, zero, 0))
    _, _, low_gain, high_gain, sum_last, sum_first, total = carry
    for extra in range(2 * group):
        work[group + total + extra] = (planes - 1) << plane_bit
    work[0] = lax.div(total + 2 * group - 1, 2 * group)
    for n in range(last, height // size):
        stencil(n)
    start_all([outgoing[7], outgoing[0], outgoing[1]])
    cells_copy.wait()

    def one_sender(s, carry):
        for k in range(chunks):
            start = s * planes * chunks + k
            value = cells[s, :, k * lanes : (k + 1) * lanes]
            cell_rows[pl.ds(start, planes, stride=chunks), :] = value
        return carry

    lax.fori_loop(0, senders, one_sender, 0, unroll=4)
    outgoing[6].start()

    def weigh(t, q):
        first[t] = inv_b[t] * q
        return q * gain_b[t]

    lax.fori_loop(0, last, weigh, one, unroll=6)
    outgoing[2].start()

    low_sep, up_sep = of_step(lower, last), of_step(upper, last)
    segment = lax.broadcasted_iota(jnp.int32, one.shape, 1)
    is_end = segment == segments - 1
    above = jnp.where(is_end, 0.0, jnp.roll(sum_first, -1, axis=1))
    couple_high = up_sep * jnp.where(is_end, 1.0, jnp.roll(high_gain, -1, axis=1))
    killing = 1.0 + low_sep * sum_last + up_sep * above
    ends[2, :, :segments, :] = low_sep
    ends[3, :, :segments, :] = up_sep
    tail = slice(height - rest, height)
    low_rest, up_rest = lower[:, tail, :], upper[:, tail, :]
    for n, (value, other) in enumerate(
        (
            (low_sep * low_gain, low_rest),
            (couple_high, up_rest),
            (killing, jnp.ones_like(low_rest)),
        )
    ):
        for x in range(planes):
            rows[n, x * knots : x * knots + segments, :] = value[x]
            rows[n, x * knots + segments : (x + 1) * knots, :] = other[x]
    for x in range(planes):
        rows[3, x * knots : x * knots + segments, :] = high_gain[x]
        rows[4, x * knots : x * knots + segments, :] = sum_first[x]

    def row(n, s):
        return rows[n, pl.ds(s, planes, stride=knots), :]

    top = knots - 1
    one_row = jnp.ones((planes, across), jnp.float32)
    d, d_b = one_row, one_row
    inv_s, gain_s, ratio_s = [], [], []
    inv_sb, gain_sb = [None] * top, [None] * top
    for s in range(top):
        e = row(2, s) + row(0, s) * d
        inverse = reciprocal(row(1, s) + e)
        inv_s.append(inverse)
        gain_s.append(row(0, s) * inverse)
        ratio_s.append(row(1, s) * inverse)
        d = e * inverse
        back = top - 1 - s
        e_b = row(2, back) + row(1, back) * d_b
        inverse_b = reciprocal(row(0, back) + e_b)
        inv_sb[back] = inverse_b
        gain_sb[back] = row(1, back) * inverse_b
        d_b = e_b * inverse_b
        inner[0, s] = inv_s[s]
        inner[1, s] = gain_s[s]
        inner[2, s] = ratio_s[s]
    outgoing[3].start()
    run = row(0, top)
    low_total = one_row
    sum_top = one_row
    rows[5, pl.ds(top, planes, stride=knots), :] = one_row
    for s in reversed(range(top)):
        weight = run * inv_s[s]
        rows[5, pl.ds(s, planes, stride=knots), :] = weight
        sum_top = sum_top + weight * row(2, s)
        run = run * gain_s[s]
        low_total = low_total * gain_s[s]
    run = row(3, 0)
    high_total = one_row
    sum_bottom = row(4, 0)
    rows[6, pl.ds(top, planes, stride=knots), :] = jnp.zeros_like(one_row)
    for s in range(top):
        weight = run * inv_sb[s]
        rows[6, pl.ds(s, planes, stride=knots), :] = weight
        sum_bottom = sum_bottom + weight * row(2, s)
        run = run * gain_sb[s]
        high_total = high_total * ratio_s[s]
    coef = (
        row(0, top) * low_total,
        sum_top,
        row(1, top),
        sum_bottom,
        row(3, 0) * high_total,
    )
    for n, value in enumerate(coef):
        coefs[n * planes : (n + 1) * planes, :] = value
    for n in range(2):
        for x in range(planes):
            ends[n, x] = rows[5 + n, x * knots : (x + 1) * knots, :]
    start_all(outgoing[4:6])
    wait_all(outgoing)


def deposit_kernel(got, *refs):
    (deposit_hbm, swept, prefix, reduced, sums) = refs[8:13]
    (work, cell_rows, rhs, inv, first, ends, coefs, lower) = refs[13:21]
    (field, total, part_sum, lefts, rights, columns, edges, in_sems, sems) = refs[21:]
    incoming = copies_of(refs[:8], refs[13:21], in_sems)
    start_all(incoming)
    components, planes, height, across = rhs.shape
    steps = inv.shape[0] + 1
    last = steps - 1
    knots = ends.shape[2]
    rest = knots - segments
    slot = components + 1
    senders = lax.axis_size("span")
    block = got.shape[0] // senders
    parts = height // lanes
    shift = across.bit_length() - 1
    lines = components * planes
    kind = jnp.bfloat16 if max(height, across) <= 256 else jnp.float32

    me = lax.axis_index("span")
    below = lax.rem(me + senders - 1, senders)
    above = lax.rem(me + 1, senders)
    part_sum[...] = jnp.zeros_like(part_sum)
    for p in range(parts):
        for n, owner in enumerate((above, below)):
            start = owner * block + p * slot + components
            columns[p, pl.ds(n, lines, stride=2), :] = got[pl.ds(start, lines, stride=parts * slot), :]
        edges[p * lanes : (p + 1) * lanes, :] = diffusion_number * columns[p].T

    tile = 16
    base = lax.broadcasted_iota(jnp.int32, (tile, lanes), 0)
    height_ids = [(base + n * tile).astype(jnp.float32).astype(kind) for n in range(height // tile)]
    across_ids = height_ids[: across // tile]
    lane = lane_iota((1, lanes))
    one = jnp.ones((tile, lanes), jnp.bfloat16)
    none = jnp.zeros((tile, lanes), jnp.bfloat16)

    def spread(row, to):
        return jnp.broadcast_to(row, (tile, lanes)).astype(to)

    def build(n, half):
        for g in range(group):
            word = work[(n + 1) * group + g]
            ident = (word >> count_bits) & ((1 << (plane_bit - count_bits)) - 1)
            live = word & ((1 << count_bits) - 1)
            there = slice(g * lanes, (g + 1) * lanes)
            cell = cell_rows[pl.ds(ident, 1), :]
            up = jnp.where(lane < live, cell >> shift, -1).astype(jnp.float32)
            side = (cell & (across - 1)).astype(jnp.float32)
            up, side = spread(up, kind), spread(side, kind)
            for i, ids in enumerate(height_ids):
                lefts[half][i * tile : (i + 1) * tile, there] = jnp.where(up == ids, one, none)
            masks = [side == ids for ids in across_ids]
            for c in range(components):
                force = got[pl.ds(ident * slot + c, 1), :]
                rest_of = force - force.astype(jnp.bfloat16).astype(jnp.float32)
                for m, value in enumerate((force, rest_of)):
                    value = spread(value, jnp.bfloat16)
                    start = (m * components + c) * across
                    for i, mask in enumerate(masks):
                        place = slice(start + i * tile, start + (i + 1) * tile)
                        rights[half][place, there] = jnp.where(mask, value, none)

    def plane_of(n):
        return work[(n + 1) * group] >> plane_bit

    def step(n, half):
        now = plane_of(n)
        before = plane_of(jnp.maximum(n - 1, 0))

        @pl.when(now != before)
        def _():
            total[before] = part_sum[...]
            part_sum[...] = jnp.zeros_like(part_sum)

        build(n + 1, 1 - half)
        part_sum[...] += lax.dot_general(
            rights[half][...],
            lefts[half][...],
            (((1,), (1,)), ((), ())),
            preferred_element_type=jnp.float32,
        )

    def two_steps(n, carry):
        step(2 * n, 0)
        step(2 * n + 1, 1)
        return carry

    wait_all(incoming[:2])
    build(0, 0)
    lax.fori_loop(0, work[0], two_steps, 0)
    total[planes - 1] = part_sum[...]
    wait_all(incoming[2:])

    wide = lane_iota((lanes, across))
    border = (wide == 0) | (wide == across - 1)

    def place(x):
        return [
            pltpu.make_async_copy(field.at[c, x], deposit_hbm.at[c, x], sems.at[c, x])
            for c in range(components)
        ]

    def combine(x, carry):
        for c in range(components):
            for p in range(parts):
                part = slice(p * lanes, (p + 1) * lanes)
                high = total[x, c * across : (c + 1) * across, part]
                low = total[x, (components + c) * across : (components + c + 1) * across, part]
                value = (high + low).T
                field[c, x, part, :] = value.astype(jnp.bfloat16)
                edge = pltpu.roll(edges[part, :], lanes - 1 - 2 * (c * planes + x), 1)
                rhs[c, x, part, :] = rhs[c, x, part, :] + value + jnp.where(border, edge, 0.0)
        start_all(place(x))
        return carry

    lax.fori_loop(0, planes, combine, 0)
    sums[2 * lines : 2 * lines + coefs.shape[0], :] = coefs[...]

    zero = jnp.zeros((components, planes, segments, across), jnp.float32)

    def of_step(t):
        return rhs[:, :, pl.ds(t, segments, stride=steps), :]

    def forward(t, carry):
        value, start, run, before = carry
        force = of_step(t)
        low, inverse = lower[:, pl.ds(t, segments, stride=steps), :], inv[t]
        value = force + (low * before)[None] * value
        swept[t] = inverse[None] * value
        run = run * (low * inverse)
        prefix[t] = run
        return value, start + first[t][None] * force, run, inverse

    one = jnp.ones((planes, segments, across), jnp.float32)
    value, start, _, inverse = lax.fori_loop(0, last, forward, (zero, zero, one, one), unroll=3)
    value = inverse[None] * value
    segment = lax.broadcasted_iota(jnp.int32, zero.shape, 2)
    after = jnp.where(segment == segments - 1, 0.0, jnp.roll(start, -1, axis=2))
    low_sep, up_sep = ends[2, :, :segments, :], ends[3, :, :segments, :]
    value = of_step(last) + low_sep[None] * value + up_sep[None] * after
    others = rhs[:, :, height - rest :, :]
    at_top = ends[0, :, :segments, :][None] * value + ends[0, :, segments:, :][None] * others
    at_bottom = ends[1, :, :segments, :][None] * value + ends[1, :, segments:, :][None] * others
    at_bottom = at_bottom + jnp.where(segment == 0, start, 0.0)
    for c in range(components):
        for x in range(planes):
            k = c * planes + x
            reduced[k * knots : k * knots + segments, :] = value[c, x]
            reduced[k * knots + segments : (k + 1) * knots, :] = others[c, x]
            sums[k : k + 1, :] = jnp.sum(at_top[c, x], 0, keepdims=True)
            sums[lines + k : lines + k + 1, :] = jnp.sum(at_bottom[c, x], 0, keepdims=True)

    for x in range(planes):
        wait_all(place(x))


def finish_kernel(inner, reduced, swept, inv, prefix, upper, *refs):
    walls = len(refs) - 7
    received = refs[:walls]
    out_hbm, sums, tops, after, before, out, sems = refs[walls:]
    components, planes, height, across = out.shape
    steps = swept.shape[0] + 1
    last = steps - 1
    lines = components * planes
    knots = inner.shape[1] + 1
    rest = knots - segments
    me = lax.axis_index("wall")
    for n in range(walls):
        sums[lax.rem(me + walls - n, walls)] = received[n][...]

    def coef(k, n):
        start = 2 * lines + n * planes
        return sums[k, start : start + planes, :]

    def wide(value):
        return jnp.concatenate([value] * components, 0)

    d = jnp.ones((planes, across), jnp.float32)
    value = jnp.zeros((lines, across), jnp.float32)
    values, ratios = [], []
    for k in range(walls):
        low, own, up = coef(k, 0), coef(k, 1), coef(k, 2)
        right = sums[k, :lines, :]
        if k + 1 < walls:
            high = up * coef(k + 1, 4)
            killing = own + up * coef(k + 1, 3)
            right = right + wide(up) * sums[k + 1, lines : 2 * lines, :]
        else:
            high = jnp.zeros_like(up)
            killing = own + up
        e = killing + low * d
        inverse = reciprocal(high + e)
        d = e * inverse
        value = (right + wide(low) * value) * wide(inverse)
        values.append(value)
        ratios.append(wide(high * inverse))
    tops[0] = jnp.zeros((lines, across), jnp.float32)
    tops[walls] = values[-1]
    for k in reversed(range(walls - 1)):
        values[k] = values[k] + ratios[k] * values[k + 1]
        tops[k + 1] = values[k]

    def row(s):
        return pl.ds(s, lines, stride=knots)

    run = tops[me]
    before[row(0), :] = run
    found = []
    for s in range(knots - 1):
        run = reduced[row(s), :] * wide(inner[0, s]) + wide(inner[1, s]) * run
        found.append(run)
    run = tops[me + 1]
    after[row(knots - 1), :] = run
    for s in reversed(range(knots - 1)):
        run = found[s] + wide(inner[2, s]) * run
        after[row(s), :] = run
        if s + 1 < segments:
            before[row(s + 1), :] = run

    def put(c, x, t, value):
        out[c, x, pl.ds(t, segments, stride=steps), :] = value

    copies = []
    half = planes // 2 if planes % 2 == 0 else planes
    for start in range(0, planes, half):
        part = [(c, x) for c in range(components) for x in range(start, start + half)]
        bottoms, starts = [], []
        for c, x in part:
            base = (c * planes + x) * knots
            bottoms.append(before[base : base + segments, :])
            starts.append(after[base : base + segments, :])
            out[c, x, height - rest :, :] = after[base + segments : base + knots, :]
            put(c, x, last, starts[-1])

        def backward(n, values):
            t = last - 1 - n
            found = []
            ratios = {}
            for x in range(start, start + half):
                ratios[x] = upper[x, pl.ds(t, segments, stride=steps), :] * inv[t, x]
            for (c, x), value, bottom in zip(part, values, bottoms):
                value = (swept[t, c, x] + prefix[t, x] * bottom) + ratios[x] * value
                put(c, x, t, value)
                found.append(value)
            return tuple(found)

        lax.fori_loop(0, last, backward, tuple(starts), unroll=3)
        for here in part:
            copy = pltpu.make_async_copy(out.at[here], out_hbm.at[here], sems.at[here])
            copy.start()
            copies.append(copy)
    wait_all(copies)


def everyone(block, axis, by_distance):
    length = lax.axis_size(axis)
    found = [by_distance[0]]
    for distance in range(1, length):
        route = [(i, (i + distance) % length) for i in range(length)]
        found.append(lax.ppermute(by_distance[distance], axis, route))
    return found


def local(velocity, lower_weight, upper_weight, forces, cells, counts):
    components, planes, height, across = velocity.shape
    receivers, capacity = forces.shape[3], forces.shape[5]
    senders = cells.shape[2]
    walls = lax.axis_size("wall")
    lines = components * planes
    chunks = capacity // lanes
    slot = components + 1
    forces = forces.reshape(components, receivers, planes, capacity)
    cells = cells.reshape(senders, planes, capacity)
    counts = counts.reshape(senders, planes).T

    def hbm(*arrays):
        return [pltpu.with_memory_space_constraint(array, pltpu.HBM) for array in arrays]

    send, velocity_near = call(
        pack_kernel,
        (f32(receivers, planes * chunks * slot, lanes), f32(*velocity.shape)),
        (in_hbm, in_vmem),
        [in_hbm] * 2,
        [
            scratch(*forces.shape),
            scratch(receivers, planes * chunks * slot, lanes),
            scratch(height, across),
            scratch(height // lanes, lanes, lanes),
            pltpu.SemaphoreType.DMA((components + lines + receivers,)),
        ],
        8,
        1 << 22,
    )(*hbm(velocity, forces))
    got = lax.all_to_all(send, "span", 0, 0, tiled=True)

    steps = height // segments - 1
    knots = height - segments * steps + segments
    step_shape = (steps - 1, planes, segments, across)
    work_shape = (planes * (senders * chunks + group) + 4 * group,)
    staged = [
        (velocity.shape, jnp.float32),
        (step_shape, jnp.float32),
        (step_shape, jnp.float32),
        ((3, knots - 1, planes, across), jnp.float32),
        ((4, planes, knots, across), jnp.float32),
        ((5 * planes, across), jnp.float32),
        ((senders * planes * chunks, lanes), jnp.int32),
    ]
    prepared = call(
        prepare_kernel,
        [pltpu.HBM(*entry) for entry in staged] + [pltpu.HBM(work_shape, jnp.int32)],
        [in_hbm] * 8,
        [in_smem, in_hbm] + [in_vmem] * 3,
        [
            *[pltpu.VMEM(*entry) for entry in staged],
            pltpu.SMEM(work_shape, jnp.int32),
            pltpu.VMEM(cells.shape, jnp.int32),
            scratch(*step_shape),
            scratch(*step_shape),
            scratch(7, planes * knots, across),
            pltpu.SemaphoreType.DMA((9,)),
        ],
        12,
        1 << 24,
    )(counts, *hbm(cells), velocity_near, lower_weight, upper_weight)
    (rhs_start, inv, first, inner, ends, coefs, cell_rows, work) = prepared

    sum_rows = -(-(2 * lines + 5 * planes) // 8) * 8
    wide = 2 * components * across
    deposit, swept, prefix, reduced, sums = call(
        deposit_kernel,
        (
            jax.ShapeDtypeStruct(velocity.shape, jnp.bfloat16),
            f32(steps - 1, components, planes, segments, across),
            f32(*step_shape),
            f32(lines * knots, across),
            f32(sum_rows, across),
        ),
        (in_hbm, *[in_vmem] * 4),
        [in_vmem] + [in_hbm] * 8,
        [
            pltpu.SMEM(work_shape, jnp.int32),
            pltpu.VMEM(*staged[6]),
            *[pltpu.VMEM(*staged[n]) for n in (0, 1, 2, 4, 5)],
            scratch(*lower_weight.shape),
            pltpu.VMEM(velocity.shape, jnp.bfloat16),
            scratch(planes, wide, height),
            scratch(wide, height),
            [pltpu.VMEM((height, group * lanes), jnp.bfloat16)] * 2,
            [pltpu.VMEM((wide, group * lanes), jnp.bfloat16)] * 2,
            scratch(height // lanes, lanes, lanes),
            scratch(height, lanes),
            pltpu.SemaphoreType.DMA((8,)),
            pltpu.SemaphoreType.DMA((components, planes)),
        ],
        24,
        1 << 32,
    )(
        got.reshape(-1, lanes),
        *hbm(work, cell_rows, rhs_start, inv, first, ends, coefs, lower_weight),
    )
    all_sums = everyone(sums, "wall", [sums] * walls)

    velocity_next = call(
        finish_kernel,
        f32(*velocity.shape),
        in_hbm,
        [in_vmem] * (6 + walls),
        [
            scratch(walls, sum_rows, across),
            scratch(walls + 1, lines, across),
            scratch(lines * knots, across),
            scratch(lines * knots, across),
            scratch(*velocity.shape),
            pltpu.SemaphoreType.DMA((components, planes)),
        ],
        8,
        1 << 22,
    )(inner, reduced, swept, inv, prefix, upper_weight, *all_sums)
    return (velocity_next, deposit)


def solution(mesh):
    placed = (
        P(None, None, "wall", "span"),
        P(None, "wall", "span"),
        P(None, "wall", "span"),
        P(None, "wall", "span", None, None, None),
        P("wall", "span", None, None, None),
        P("wall", "span", None, None),
    )
    return jax.shard_map(
        local,
        mesh=mesh,
        in_specs=placed,
        out_specs=(P(None, None, "wall", "span"), P(None, None, "wall", "span")),
        check_vma=False,
    )
```

```python
import jax
import jax.numpy as jnp
from jax import lax
from jax.experimental import pallas as pl
from jax.experimental.pallas import tpu as pltpu
from jax.sharding import PartitionSpec as P

diffusion_number = 0.2
segments = 8
lanes = 128
group = 4
count_bits, plane_bit = 10, 24
in_vmem = pl.BlockSpec(memory_space=pltpu.VMEM)
in_smem = pl.BlockSpec(memory_space=pltpu.SMEM)
in_hbm = pl.BlockSpec(memory_space=pltpu.HBM)


def call(body, out_shape, out_specs, in_specs, scratch, mebibytes, flops):
    return pl.pallas_call(
        body,
        out_shape=out_shape,
        in_specs=in_specs,
        out_specs=out_specs,
        scratch_shapes=scratch,
        compiler_params=pltpu.CompilerParams(vmem_limit_bytes=mebibytes << 20),
        cost_estimate=pl.CostEstimate(flops=flops, bytes_accessed=4 << 20, transcendentals=0),
    )


def f32(*shape):
    return jax.ShapeDtypeStruct(shape, jnp.float32)


def scratch(*shape):
    return pltpu.VMEM(shape, jnp.float32)


def lane_iota(shape):
    return lax.broadcasted_iota(jnp.int32, shape, len(shape) - 1)


def reciprocal(value):
    rough = pl.reciprocal(value, approx=True)
    return rough * (2.0 - value * rough)


def start_all(copies):
    for copy in copies:
        copy.start()


def wait_all(copies):
    for copy in copies:
        copy.wait()


def copies_of(sources, targets, sems, first=0):
    return [
        pltpu.make_async_copy(source, target, sems.at[first + n])
        for n, (source, target) in enumerate(zip(sources, targets))
    ]


def pack_kernel(velocity_hbm, forces_hbm, send_hbm, velocity, forces, send, columns, turned, sems):
    components, planes, height, across = velocity_hbm.shape
    receivers, capacity = forces_hbm.shape[1], forces_hbm.shape[3]
    chunks = capacity // lanes
    lines = components * planes
    parts = height // lanes
    slot = components + 1
    copies = copies_of(
        [forces_hbm.at[c] for c in range(components)],
        [forces.at[c] for c in range(components)],
        sems,
    )
    places = [(c, x) for c in range(components) for x in range(planes)]
    copies += copies_of(
        [velocity_hbm.at[here] for here in places],
        [velocity.at[here] for here in places],
        sems,
        components,
    )
    start_all(copies)
    me = lax.axis_index("span")
    wait_all(copies[:components])
    outgoing = []
    for d in range(receivers):
        owner = lax.rem(me + d, receivers)
        for c in range(components):
            for k in range(chunks):
                value = forces[c, owner, :, k * lanes : (k + 1) * lanes]
                send[owner, pl.ds(k * slot + c, planes, stride=chunks * slot), :] = value
        index = components + lines + d
        copy = pltpu.make_async_copy(send.at[owner], send_hbm.at[owner], sems.at[index])
        outgoing.append(copy)
        if d not in (1, receivers - 1):
            copy.start()
    lane = lane_iota((height, across))
    picked = jnp.zeros((height, across), jnp.float32)
    for k in range(lines):
        copies[components + k].wait()
        rolled = pltpu.roll(velocity[k // planes, k % planes], 2 * k + 1, 1)
        picked = jnp.where((lane >> 1) == k, rolled, picked)
    columns[...] = picked
    below = lax.rem(me + receivers - 1, receivers)
    above = lax.rem(me + 1, receivers)
    for p in range(parts):
        turned[p] = columns[p * lanes : (p + 1) * lanes, :].T
        target = pl.ds(p * slot + components, lines, stride=parts * slot)
        send[below, target, :] = turned[p, pl.ds(1, lines, stride=2), :]
        send[above, target, :] = turned[p, pl.ds(0, lines, stride=2), :]
    outgoing[1].start()
    outgoing[receivers - 1].start()
    wait_all(outgoing)


def prepare_kernel(counts, cells_hbm, velocity, lower, upper, *refs):
    (rhs, inv, first, inner, ends, coefs, cell_rows, work) = refs[8:16]
    (cells, inv_b, gain_b, rows, sems) = refs[16:]
    outgoing = copies_of(refs[8:16], refs[:8], sems)
    cells_copy = pltpu.make_async_copy(cells_hbm, cells, sems.at[8])
    cells_copy.start()
    components, planes, height, across = velocity.shape
    steps = inv.shape[0] + 1
    last = steps - 1
    rest = height - segments * steps
    knots = segments + rest
    senders, capacity = cells.shape[0], cells.shape[2]
    chunks = capacity // lanes
    pairs = planes * senders
    pairs_each = -(-pairs // last)

    def list_pair(i, n):
        used = jnp.minimum(i, pairs - 1)
        x = lax.div(used, senders)
        s = used - x * senders
        count = jnp.where(i < pairs, counts[x, s], 0)
        base = (x << plane_bit) + (((s * planes + x) * chunks) << count_bits)
        for k in range(chunks):
            live = jnp.maximum(count - k * lanes, 0)
            work[group + n + k] = base + (k << count_bits) + live
        n = n + lax.div(count + lanes - 1, lanes)
        for extra in range(group):
            work[group + n + extra] = 0
        return jnp.where(s == senders - 1, lax.div(n + group - 1, group) * group, n)

    def of_step(ref, t):
        return ref[:, pl.ds(t, segments, stride=steps), :]

    one = jnp.ones((planes, segments, across), jnp.float32)
    zero = jnp.zeros_like(one)
    size = 8
    lane = lane_iota((size, across))

    def stencil(n):
        part = pl.ds(pl.multiple_of(n * size, size), size)
        for c in range(components):
            values = [velocity[c, x, part, :] for x in range(planes)]
            for x in range(planes):
                v = values[x]
                around = values[(x - 1) % planes] + values[(x + 1) % planes]
                around = around + jnp.where(lane == 0, 0.0, pltpu.roll(v, 1, 1))
                around = around + jnp.where(lane == across - 1, 0.0, pltpu.roll(v, across - 1, 1))
                rhs[c, x, part, :] = (1.0 - 4.0 * diffusion_number) * v + diffusion_number * around

    def factor(t, carry):
        d, d_b, low_gain, high_gain, sum_last, sum_first, n = carry
        low, up = of_step(lower, t), of_step(upper, t)
        e = 1.0 + low * d
        inverse = reciprocal(up + e)
        g = low * inverse
        inv[t] = inverse
        back = last - 1 - t
        low_b, up_b = of_step(lower, back), of_step(upper, back)
        e_b = 1.0 + up_b * d_b
        inverse_b = reciprocal(low_b + e_b)
        g_b = up_b * inverse_b
        inv_b[back] = inverse_b
        gain_b[back] = g_b
        stencil(t)
        for extra in range(pairs_each):
            n = list_pair(t * pairs_each + extra, n)
        return (
            e * inverse,
            e_b * inverse_b,
            low_gain * g,
            high_gain * g_b,
            inverse + g * sum_last,
            inverse_b + g_b * sum_first,
            n,
        )

    carry = lax.fori_loop(0, last, factor, (one, one, one, one, zero, zero, 0))
    _, _, low_gain, high_gain, sum_last, sum_first, total = carry
    for extra in range(2 * group):
        work[group + total + extra] = (planes - 1) << plane_bit
    work[0] = lax.div(total + 2 * group - 1, 2 * group)
    for n in range(last, height // size):
        stencil(n)
    start_all([outgoing[7], outgoing[0], outgoing[1]])
    cells_copy.wait()

    def one_sender(s, carry):
        for k in range(chunks):
            start = s * planes * chunks + k
            value = cells[s, :, k * lanes : (k + 1) * lanes]
            cell_rows[pl.ds(start, planes, stride=chunks), :] = value
        return carry

    lax.fori_loop(0, senders, one_sender, 0, unroll=4)
    outgoing[6].start()

    def weigh(t, q):
        first[t] = inv_b[t] * q
        return q * gain_b[t]

    lax.fori_loop(0, last, weigh, one, unroll=6)
    outgoing[2].start()

    low_sep, up_sep = of_step(lower, last), of_step(upper, last)
    segment = lax.broadcasted_iota(jnp.int32, one.shape, 1)
    is_end = segment == segments - 1
    above = jnp.where(is_end, 0.0, jnp.roll(sum_first, -1, axis=1))
    couple_high = up_sep * jnp.where(is_end, 1.0, jnp.roll(high_gain, -1, axis=1))
    killing = 1.0 + low_sep * sum_last + up_sep * above
    ends[2, :, :segments, :] = low_sep
    ends[3, :, :segments, :] = up_sep
    tail = slice(height - rest, height)
    low_rest, up_rest = lower[:, tail, :], upper[:, tail, :]
    for n, (value, other) in enumerate(
        (
            (low_sep * low_gain, low_rest),
            (couple_high, up_rest),
            (killing, jnp.ones_like(low_rest)),
        )
    ):
        for x in range(planes):
            rows[n, x * knots : x * knots + segments, :] = value[x]
            rows[n, x * knots + segments : (x + 1) * knots, :] = other[x]
    for x in range(planes):
        rows[3, x * knots : x * knots + segments, :] = high_gain[x]
        rows[4, x * knots : x * knots + segments, :] = sum_first[x]

    def row(n, s):
        return rows[n, pl.ds(s, planes, stride=knots), :]

    top = knots - 1
    one_row = jnp.ones((planes, across), jnp.float32)
    d, d_b = one_row, one_row
    inv_s, gain_s, ratio_s = [], [], []
    inv_sb, gain_sb = [None] * top, [None] * top
    for s in range(top):
        e = row(2, s) + row(0, s) * d
        inverse = reciprocal(row(1, s) + e)
        inv_s.append(inverse)
        gain_s.append(row(0, s) * inverse)
        ratio_s.append(row(1, s) * inverse)
        d = e * inverse
        back = top - 1 - s
        e_b = row(2, back) + row(1, back) * d_b
        inverse_b = reciprocal(row(0, back) + e_b)
        inv_sb[back] = inverse_b
        gain_sb[back] = row(1, back) * inverse_b
        d_b = e_b * inverse_b
        inner[0, s] = inv_s[s]
        inner[1, s] = gain_s[s]
        inner[2, s] = ratio_s[s]
    outgoing[3].start()
    run = row(0, top)
    low_total = one_row
    sum_top = one_row
    rows[5, pl.ds(top, planes, stride=knots), :] = one_row
    for s in reversed(range(top)):
        weight = run * inv_s[s]
        rows[5, pl.ds(s, planes, stride=knots), :] = weight
        sum_top = sum_top + weight * row(2, s)
        run = run * gain_s[s]
        low_total = low_total * gain_s[s]
    run = row(3, 0)
    high_total = one_row
    sum_bottom = row(4, 0)
    rows[6, pl.ds(top, planes, stride=knots), :] = jnp.zeros_like(one_row)
    for s in range(top):
        weight = run * inv_sb[s]
        rows[6, pl.ds(s, planes, stride=knots), :] = weight
        sum_bottom = sum_bottom + weight * row(2, s)
        run = run * gain_sb[s]
        high_total = high_total * ratio_s[s]
    coef = (
        row(0, top) * low_total,
        sum_top,
        row(1, top),
        sum_bottom,
        row(3, 0) * high_total,
    )
    for n, value in enumerate(coef):
        coefs[n * planes : (n + 1) * planes, :] = value
    for n in range(2):
        for x in range(planes):
            ends[n, x] = rows[5 + n, x * knots : (x + 1) * knots, :]
    start_all(outgoing[4:6])
    wait_all(outgoing)


def deposit_kernel(got, *refs):
    (deposit_hbm, swept, prefix, reduced, sums) = refs[8:13]
    (work, cell_rows, rhs, inv, first, ends, coefs, lower) = refs[13:21]
    (field, total, lefts, rights, columns, edges, in_sems, sems) = refs[21:]
    incoming = copies_of(refs[:8], refs[13:21], in_sems)
    start_all(incoming)
    components, planes, height, across = rhs.shape
    steps = inv.shape[0] + 1
    last = steps - 1
    knots = ends.shape[2]
    rest = knots - segments
    slot = components + 1
    senders = lax.axis_size("span")
    block = got.shape[0] // senders
    parts = height // lanes
    shift = across.bit_length() - 1
    lines = components * planes
    kind = jnp.bfloat16 if max(height, across) <= 256 else jnp.float32

    me = lax.axis_index("span")
    below = lax.rem(me + senders - 1, senders)
    above = lax.rem(me + 1, senders)
    total[...] = jnp.zeros_like(total)
    for p in range(parts):
        for n, owner in enumerate((above, below)):
            start = owner * block + p * slot + components
            columns[p, pl.ds(n, lines, stride=2), :] = got[pl.ds(start, lines, stride=parts * slot), :]
        edges[p * lanes : (p + 1) * lanes, :] = diffusion_number * columns[p].T

    tile = 16
    base = lax.broadcasted_iota(jnp.int32, (tile, lanes), 0)
    height_ids = [(base + n * tile).astype(jnp.float32).astype(kind) for n in range(height // tile)]
    across_ids = height_ids[: across // tile]
    lane = lane_iota((1, lanes))
    one = jnp.ones((tile, lanes), jnp.bfloat16)
    none = jnp.zeros((tile, lanes), jnp.bfloat16)

    def spread(row, to):
        return jnp.broadcast_to(row, (tile, lanes)).astype(to)

    def build(n, half):
        for g in range(group):
            word = work[(n + 1) * group + g]
            ident = (word >> count_bits) & ((1 << (plane_bit - count_bits)) - 1)
            live = word & ((1 << count_bits) - 1)
            there = slice(g * lanes, (g + 1) * lanes)
            cell = cell_rows[pl.ds(ident, 1), :]
            up = jnp.where(lane < live, cell >> shift, -1).astype(jnp.float32)
            side = (cell & (across - 1)).astype(jnp.float32)
            up, side = spread(up, kind), spread(side, kind)
            for i, ids in enumerate(height_ids):
                lefts[half][i * tile : (i + 1) * tile, there] = jnp.where(up == ids, one, none)
            masks = [side == ids for ids in across_ids]
            for c in range(components):
                force = got[pl.ds(ident * slot + c, 1), :]
                rest_of = force - force.astype(jnp.bfloat16).astype(jnp.float32)
                for m, value in enumerate((force, rest_of)):
                    value = spread(value, jnp.bfloat16)
                    start = (m * components + c) * across
                    for i, mask in enumerate(masks):
                        place = slice(start + i * tile, start + (i + 1) * tile)
                        rights[half][place, there] = jnp.where(mask, value, none)

    def add(n, half):
        total[work[(n + 1) * group] >> plane_bit] += lax.dot_general(
            rights[half][...],
            lefts[half][...],
            (((1,), (1,)), ((), ())),
            preferred_element_type=jnp.float32,
        )

    def two_steps(n, carry):
        build(2 * n + 1, 1)
        add(2 * n, 0)
        build(2 * n + 2, 0)
        add(2 * n + 1, 1)
        return carry

    wait_all(incoming[:2])
    build(0, 0)
    lax.fori_loop(0, work[0], two_steps, 0)
    wait_all(incoming[2:])

    wide = lane_iota((lanes, across))
    border = (wide == 0) | (wide == across - 1)

    def place(x):
        return [
            pltpu.make_async_copy(field.at[c, x], deposit_hbm.at[c, x], sems.at[c, x])
            for c in range(components)
        ]

    def combine(x, carry):
        for c in range(components):
            for p in range(parts):
                part = slice(p * lanes, (p + 1) * lanes)
                high = total[x, c * across : (c + 1) * across, part]
                low = total[x, (components + c) * across : (components + c + 1) * across, part]
                value = (high + low).T
                field[c, x, part, :] = value.astype(jnp.bfloat16)
                edge = pltpu.roll(edges[part, :], lanes - 1 - 2 * (c * planes + x), 1)
                rhs[c, x, part, :] = rhs[c, x, part, :] + value + jnp.where(border, edge, 0.0)
        start_all(place(x))
        return carry

    lax.fori_loop(0, planes, combine, 0)
    sums[2 * lines : 2 * lines + coefs.shape[0], :] = coefs[...]

    zero = jnp.zeros((components, planes, segments, across), jnp.float32)

    def of_step(t):
        return rhs[:, :, pl.ds(t, segments, stride=steps), :]

    def forward(t, carry):
        value, start, run, before = carry
        force = of_step(t)
        low, inverse = lower[:, pl.ds(t, segments, stride=steps), :], inv[t]
        value = force + (low * before)[None] * value
        swept[t] = inverse[None] * value
        run = run * (low * inverse)
        prefix[t] = run
        return value, start + first[t][None] * force, run, inverse

    one = jnp.ones((planes, segments, across), jnp.float32)
    value, start, _, inverse = lax.fori_loop(0, last, forward, (zero, zero, one, one), unroll=3)
    value = inverse[None] * value
    segment = lax.broadcasted_iota(jnp.int32, zero.shape, 2)
    after = jnp.where(segment == segments - 1, 0.0, jnp.roll(start, -1, axis=2))
    low_sep, up_sep = ends[2, :, :segments, :], ends[3, :, :segments, :]
    value = of_step(last) + low_sep[None] * value + up_sep[None] * after
    others = rhs[:, :, height - rest :, :]
    at_top = ends[0, :, :segments, :][None] * value + ends[0, :, segments:, :][None] * others
    at_bottom = ends[1, :, :segments, :][None] * value + ends[1, :, segments:, :][None] * others
    at_bottom = at_bottom + jnp.where(segment == 0, start, 0.0)
    for c in range(components):
        for x in range(planes):
            k = c * planes + x
            reduced[k * knots : k * knots + segments, :] = value[c, x]
            reduced[k * knots + segments : (k + 1) * knots, :] = others[c, x]
            sums[k : k + 1, :] = jnp.sum(at_top[c, x], 0, keepdims=True)
            sums[lines + k : lines + k + 1, :] = jnp.sum(at_bottom[c, x], 0, keepdims=True)

    for x in range(planes):
        wait_all(place(x))


def finish_kernel(inner, reduced, swept, inv, prefix, upper, *refs):
    walls = len(refs) - 7
    received = refs[:walls]
    out_hbm, sums, tops, after, before, out, sems = refs[walls:]
    components, planes, height, across = out.shape
    steps = swept.shape[0] + 1
    last = steps - 1
    lines = components * planes
    knots = inner.shape[1] + 1
    rest = knots - segments
    me = lax.axis_index("wall")
    for n in range(walls):
        sums[lax.rem(me + walls - n, walls)] = received[n][...]

    def coef(k, n):
        start = 2 * lines + n * planes
        return sums[k, start : start + planes, :]

    def wide(value):
        return jnp.concatenate([value] * components, 0)

    d = jnp.ones((planes, across), jnp.float32)
    value = jnp.zeros((lines, across), jnp.float32)
    values, ratios = [], []
    for k in range(walls):
        low, own, up = coef(k, 0), coef(k, 1), coef(k, 2)
        right = sums[k, :lines, :]
        if k + 1 < walls:
            high = up * coef(k + 1, 4)
            killing = own + up * coef(k + 1, 3)
            right = right + wide(up) * sums[k + 1, lines : 2 * lines, :]
        else:
            high = jnp.zeros_like(up)
            killing = own + up
        e = killing + low * d
        inverse = reciprocal(high + e)
        d = e * inverse
        value = (right + wide(low) * value) * wide(inverse)
        values.append(value)
        ratios.append(wide(high * inverse))
    tops[0] = jnp.zeros((lines, across), jnp.float32)
    tops[walls] = values[-1]
    for k in reversed(range(walls - 1)):
        values[k] = values[k] + ratios[k] * values[k + 1]
        tops[k + 1] = values[k]

    def row(s):
        return pl.ds(s, lines, stride=knots)

    run = tops[me]
    before[row(0), :] = run
    found = []
    for s in range(knots - 1):
        run = reduced[row(s), :] * wide(inner[0, s]) + wide(inner[1, s]) * run
        found.append(run)
    run = tops[me + 1]
    after[row(knots - 1), :] = run
    for s in reversed(range(knots - 1)):
        run = found[s] + wide(inner[2, s]) * run
        after[row(s), :] = run
        if s + 1 < segments:
            before[row(s + 1), :] = run

    def put(c, x, t, value):
        out[c, x, pl.ds(t, segments, stride=steps), :] = value

    copies = []
    half = planes // 2 if planes % 2 == 0 else planes
    for start in range(0, planes, half):
        part = [(c, x) for c in range(components) for x in range(start, start + half)]
        bottoms, starts = [], []
        for c, x in part:
            base = (c * planes + x) * knots
            bottoms.append(before[base : base + segments, :])
            starts.append(after[base : base + segments, :])
            out[c, x, height - rest :, :] = after[base + segments : base + knots, :]
            put(c, x, last, starts[-1])

        def backward(n, values):
            t = last - 1 - n
            found = []
            ratios = {}
            for x in range(start, start + half):
                ratios[x] = upper[x, pl.ds(t, segments, stride=steps), :] * inv[t, x]
            for (c, x), value, bottom in zip(part, values, bottoms):
                value = (swept[t, c, x] + prefix[t, x] * bottom) + ratios[x] * value
                put(c, x, t, value)
                found.append(value)
            return tuple(found)

        lax.fori_loop(0, last, backward, tuple(starts), unroll=3)
        for here in part:
            copy = pltpu.make_async_copy(out.at[here], out_hbm.at[here], sems.at[here])
            copy.start()
            copies.append(copy)
    wait_all(copies)


def everyone(block, axis, by_distance):
    length = lax.axis_size(axis)
    found = [by_distance[0]]
    for distance in range(1, length):
        route = [(i, (i + distance) % length) for i in range(length)]
        found.append(lax.ppermute(by_distance[distance], axis, route))
    return found


def local(velocity, lower_weight, upper_weight, forces, cells, counts):
    components, planes, height, across = velocity.shape
    receivers, capacity = forces.shape[3], forces.shape[5]
    senders = cells.shape[2]
    walls = lax.axis_size("wall")
    lines = components * planes
    chunks = capacity // lanes
    slot = components + 1
    forces = forces.reshape(components, receivers, planes, capacity)
    cells = cells.reshape(senders, planes, capacity)
    counts = counts.reshape(senders, planes).T

    def hbm(*arrays):
        return [pltpu.with_memory_space_constraint(array, pltpu.HBM) for array in arrays]

    send, velocity_near = call(
        pack_kernel,
        (f32(receivers, planes * chunks * slot, lanes), f32(*velocity.shape)),
        (in_hbm, in_vmem),
        [in_hbm] * 2,
        [
            scratch(*forces.shape),
            scratch(receivers, planes * chunks * slot, lanes),
            scratch(height, across),
            scratch(height // lanes, lanes, lanes),
            pltpu.SemaphoreType.DMA((components + lines + receivers,)),
        ],
        8,
        1 << 22,
    )(*hbm(velocity, forces))
    got = lax.all_to_all(send, "span", 0, 0, tiled=True)

    steps = height // segments - 1
    knots = height - segments * steps + segments
    step_shape = (steps - 1, planes, segments, across)
    work_shape = (planes * (senders * chunks + group) + 4 * group,)
    staged = [
        (velocity.shape, jnp.float32),
        (step_shape, jnp.float32),
        (step_shape, jnp.float32),
        ((3, knots - 1, planes, across), jnp.float32),
        ((4, planes, knots, across), jnp.float32),
        ((5 * planes, across), jnp.float32),
        ((senders * planes * chunks, lanes), jnp.int32),
    ]
    prepared = call(
        prepare_kernel,
        [pltpu.HBM(*entry) for entry in staged] + [pltpu.HBM(work_shape, jnp.int32)],
        [in_hbm] * 8,
        [in_smem, in_hbm] + [in_vmem] * 3,
        [
            *[pltpu.VMEM(*entry) for entry in staged],
            pltpu.SMEM(work_shape, jnp.int32),
            pltpu.VMEM(cells.shape, jnp.int32),
            scratch(*step_shape),
            scratch(*step_shape),
            scratch(7, planes * knots, across),
            pltpu.SemaphoreType.DMA((9,)),
        ],
        12,
        1 << 24,
    )(counts, *hbm(cells), velocity_near, lower_weight, upper_weight)
    (rhs_start, inv, first, inner, ends, coefs, cell_rows, work) = prepared

    sum_rows = -(-(2 * lines + 5 * planes) // 8) * 8
    wide = 2 * components * across
    deposit, swept, prefix, reduced, sums = call(
        deposit_kernel,
        (
            jax.ShapeDtypeStruct(velocity.shape, jnp.bfloat16),
            f32(steps - 1, components, planes, segments, across),
            f32(*step_shape),
            f32(lines * knots, across),
            f32(sum_rows, across),
        ),
        (in_hbm, *[in_vmem] * 4),
        [in_vmem] + [in_hbm] * 8,
        [
            pltpu.SMEM(work_shape, jnp.int32),
            pltpu.VMEM(*staged[6]),
            *[pltpu.VMEM(*staged[n]) for n in (0, 1, 2, 4, 5)],
            scratch(*lower_weight.shape),
            pltpu.VMEM(velocity.shape, jnp.bfloat16),
            scratch(planes, wide, height),
            [pltpu.VMEM((height, group * lanes), jnp.bfloat16)] * 2,
            [pltpu.VMEM((wide, group * lanes), jnp.bfloat16)] * 2,
            scratch(height // lanes, lanes, lanes),
            scratch(height, lanes),
            pltpu.SemaphoreType.DMA((8,)),
            pltpu.SemaphoreType.DMA((components, planes)),
        ],
        24,
        1 << 32,
    )(
        got.reshape(-1, lanes),
        *hbm(work, cell_rows, rhs_start, inv, first, ends, coefs, lower_weight),
    )
    all_sums = everyone(sums, "wall", [sums] * walls)

    velocity_next = call(
        finish_kernel,
        f32(*velocity.shape),
        in_hbm,
        [in_vmem] * (6 + walls),
        [
            scratch(walls, sum_rows, across),
            scratch(walls + 1, lines, across),
            scratch(lines * knots, across),
            scratch(lines * knots, across),
            scratch(*velocity.shape),
            pltpu.SemaphoreType.DMA((components, planes)),
        ],
        8,
        1 << 22,
    )(inner, reduced, swept, inv, prefix, upper_weight, *all_sums)
    return (velocity_next, deposit)


def solution(mesh):
    placed = (
        P(None, None, "wall", "span"),
        P(None, "wall", "span"),
        P(None, "wall", "span"),
        P(None, "wall", "span", None, None, None),
        P("wall", "span", None, None, None),
        P("wall", "span", None, None),
    )
    return jax.shard_map(
        local,
        mesh=mesh,
        in_specs=placed,
        out_specs=(P(None, None, "wall", "span"), P(None, None, "wall", "span")),
        check_vma=False,
    )
```

```python
import jax
import jax.numpy as jnp
from jax import lax
from jax.experimental import pallas as pl
from jax.experimental.pallas import tpu as pltpu
from jax.sharding import PartitionSpec as P

diffusion_number = 0.2
segments = 8
lanes = 128
group = 4
count_bits, plane_bit = 10, 24
in_vmem = pl.BlockSpec(memory_space=pltpu.VMEM)
in_smem = pl.BlockSpec(memory_space=pltpu.SMEM)
in_hbm = pl.BlockSpec(memory_space=pltpu.HBM)


def call(body, out_shape, out_specs, in_specs, scratch, mebibytes, flops):
    return pl.pallas_call(
        body,
        out_shape=out_shape,
        in_specs=in_specs,
        out_specs=out_specs,
        scratch_shapes=scratch,
        compiler_params=pltpu.CompilerParams(vmem_limit_bytes=mebibytes << 20),
        cost_estimate=pl.CostEstimate(flops=flops, bytes_accessed=4 << 20, transcendentals=0),
    )


def f32(*shape):
    return jax.ShapeDtypeStruct(shape, jnp.float32)


def scratch(*shape):
    return pltpu.VMEM(shape, jnp.float32)


def lane_iota(shape):
    return lax.broadcasted_iota(jnp.int32, shape, len(shape) - 1)


def reciprocal(value):
    rough = pl.reciprocal(value, approx=True)
    return rough * (2.0 - value * rough)


def start_all(copies):
    for copy in copies:
        copy.start()


def wait_all(copies):
    for copy in copies:
        copy.wait()


def copies_of(sources, targets, sems, first=0):
    return [
        pltpu.make_async_copy(source, target, sems.at[first + n])
        for n, (source, target) in enumerate(zip(sources, targets))
    ]


def pack_kernel(velocity_hbm, forces_hbm, send_hbm, velocity, forces, send, columns, turned, sems):
    components, planes, height, across = velocity_hbm.shape
    receivers, capacity = forces_hbm.shape[1], forces_hbm.shape[3]
    chunks = capacity // lanes
    lines = components * planes
    parts = height // lanes
    slot = components + 1
    copies = copies_of(
        [forces_hbm.at[c] for c in range(components)],
        [forces.at[c] for c in range(components)],
        sems,
    )
    places = [(c, x) for c in range(components) for x in range(planes)]
    copies += copies_of(
        [velocity_hbm.at[here] for here in places],
        [velocity.at[here] for here in places],
        sems,
        components,
    )
    start_all(copies)
    me = lax.axis_index("span")
    wait_all(copies[:components])
    outgoing = []
    for d in range(receivers):
        owner = lax.rem(me + d, receivers)
        for c in range(components):
            for k in range(chunks):
                value = forces[c, owner, :, k * lanes : (k + 1) * lanes]
                send[owner, pl.ds(k * slot + c, planes, stride=chunks * slot), :] = value
        index = components + lines + d
        copy = pltpu.make_async_copy(send.at[owner], send_hbm.at[owner], sems.at[index])
        outgoing.append(copy)
        if d not in (1, receivers - 1):
            copy.start()
    lane = lane_iota((height, across))
    picked = jnp.zeros((height, across), jnp.float32)
    for k in range(lines):
        copies[components + k].wait()
        rolled = pltpu.roll(velocity[k // planes, k % planes], 2 * k + 1, 1)
        picked = jnp.where((lane >> 1) == k, rolled, picked)
    columns[...] = picked
    below = lax.rem(me + receivers - 1, receivers)
    above = lax.rem(me + 1, receivers)
    for p in range(parts):
        turned[p] = columns[p * lanes : (p + 1) * lanes, :].T
        target = pl.ds(p * slot + components, lines, stride=parts * slot)
        send[below, target, :] = turned[p, pl.ds(1, lines, stride=2), :]
        send[above, target, :] = turned[p, pl.ds(0, lines, stride=2), :]
    outgoing[1].start()
    outgoing[receivers - 1].start()
    wait_all(outgoing)


def prepare_kernel(counts, cells_hbm, velocity, lower, upper, *refs):
    (rhs, inv, first, inner, ends, coefs, cell_rows, work) = refs[8:16]
    (cells, inv_b, gain_b, rows, sems) = refs[16:]
    outgoing = copies_of(refs[8:16], refs[:8], sems)
    cells_copy = pltpu.make_async_copy(cells_hbm, cells, sems.at[8])
    cells_copy.start()
    components, planes, height, across = velocity.shape
    steps = inv.shape[0] + 1
    last = steps - 1
    rest = height - segments * steps
    knots = segments + rest
    senders, capacity = cells.shape[0], cells.shape[2]
    chunks = capacity // lanes
    pairs = planes * senders
    pairs_each = -(-pairs // last)

    def list_pair(i, n):
        used = jnp.minimum(i, pairs - 1)
        x = lax.div(used, senders)
        s = used - x * senders
        count = jnp.where(i < pairs, counts[x, s], 0)
        base = (x << plane_bit) + (((s * planes + x) * chunks) << count_bits)
        for k in range(chunks):
            live = jnp.maximum(count - k * lanes, 0)
            work[group + n + k] = base + (k << count_bits) + live
        n = n + lax.div(count + lanes - 1, lanes)
        for extra in range(group):
            work[group + n + extra] = 0
        return jnp.where(s == senders - 1, lax.div(n + group - 1, group) * group, n)

    def of_step(ref, t):
        return ref[:, pl.ds(t, segments, stride=steps), :]

    one = jnp.ones((planes, segments, across), jnp.float32)
    zero = jnp.zeros_like(one)
    size = 8
    lane = lane_iota((size, across))

    def stencil(n):
        part = pl.ds(pl.multiple_of(n * size, size), size)
        for c in range(components):
            values = [velocity[c, x, part, :] for x in range(planes)]
            for x in range(planes):
                v = values[x]
                around = values[(x - 1) % planes] + values[(x + 1) % planes]
                around = around + jnp.where(lane == 0, 0.0, pltpu.roll(v, 1, 1))
                around = around + jnp.where(lane == across - 1, 0.0, pltpu.roll(v, across - 1, 1))
                rhs[c, x, part, :] = (1.0 - 4.0 * diffusion_number) * v + diffusion_number * around

    def factor(t, carry):
        d, d_b, low_gain, high_gain, sum_last, sum_first, n = carry
        low, up = of_step(lower, t), of_step(upper, t)
        e = 1.0 + low * d
        inverse = reciprocal(up + e)
        g = low * inverse
        inv[t] = inverse
        back = last - 1 - t
        low_b, up_b = of_step(lower, back), of_step(upper, back)
        e_b = 1.0 + up_b * d_b
        inverse_b = reciprocal(low_b + e_b)
        g_b = up_b * inverse_b
        inv_b[back] = inverse_b
        gain_b[back] = g_b
        stencil(t)
        for extra in range(pairs_each):
            n = list_pair(t * pairs_each + extra, n)
        return (
            e * inverse,
            e_b * inverse_b,
            low_gain * g,
            high_gain * g_b,
            inverse + g * sum_last,
            inverse_b + g_b * sum_first,
            n,
        )

    carry = lax.fori_loop(0, last, factor, (one, one, one, one, zero, zero, 0))
    _, _, low_gain, high_gain, sum_last, sum_first, total = carry
    for extra in range(2 * group):
        work[group + total + extra] = (planes - 1) << plane_bit
    work[0] = lax.div(total + 2 * group - 1, 2 * group)
    for n in range(last, height // size):
        stencil(n)
    start_all([outgoing[7], outgoing[0], outgoing[1]])
    cells_copy.wait()

    def one_sender(s, carry):
        for k in range(chunks):
            start = s * planes * chunks + k
            value = cells[s, :, k * lanes : (k + 1) * lanes]
            cell_rows[pl.ds(start, planes, stride=chunks), :] = value
        return carry

    lax.fori_loop(0, senders, one_sender, 0, unroll=4)
    outgoing[6].start()

    def weigh(t, q):
        first[t] = inv_b[t] * q
        return q * gain_b[t]

    lax.fori_loop(0, last, weigh, one, unroll=6)
    outgoing[2].start()

    low_sep, up_sep = of_step(lower, last), of_step(upper, last)
    segment = lax.broadcasted_iota(jnp.int32, one.shape, 1)
    is_end = segment == segments - 1
    above = jnp.where(is_end, 0.0, jnp.roll(sum_first, -1, axis=1))
    couple_high = up_sep * jnp.where(is_end, 1.0, jnp.roll(high_gain, -1, axis=1))
    killing = 1.0 + low_sep * sum_last + up_sep * above
    ends[2, :, :segments, :] = low_sep
    ends[3, :, :segments, :] = up_sep
    tail = slice(height - rest, height)
    low_rest, up_rest = lower[:, tail, :], upper[:, tail, :]
    for n, (value, other) in enumerate(
        (
            (low_sep * low_gain, low_rest),
            (couple_high, up_rest),
            (killing, jnp.ones_like(low_rest)),
        )
    ):
        for x in range(planes):
            rows[n, x * knots : x * knots + segments, :] = value[x]
            rows[n, x * knots + segments : (x + 1) * knots, :] = other[x]
    for x in range(planes):
        rows[3, x * knots : x * knots + segments, :] = high_gain[x]
        rows[4, x * knots : x * knots + segments, :] = sum_first[x]

    def row(n, s):
        return rows[n, pl.ds(s, planes, stride=knots), :]

    top = knots - 1
    one_row = jnp.ones((planes, across), jnp.float32)
    d, d_b = one_row, one_row
    inv_s, gain_s, ratio_s = [], [], []
    inv_sb, gain_sb = [None] * top, [None] * top
    for s in range(top):
        e = row(2, s) + row(0, s) * d
        inverse = reciprocal(row(1, s) + e)
        inv_s.append(inverse)
        gain_s.append(row(0, s) * inverse)
        ratio_s.append(row(1, s) * inverse)
        d = e * inverse
        back = top - 1 - s
        e_b = row(2, back) + row(1, back) * d_b
        inverse_b = reciprocal(row(0, back) + e_b)
        inv_sb[back] = inverse_b
        gain_sb[back] = row(1, back) * inverse_b
        d_b = e_b * inverse_b
        inner[0, s] = inv_s[s]
        inner[1, s] = gain_s[s]
        inner[2, s] = ratio_s[s]
    outgoing[3].start()
    run = row(0, top)
    low_total = one_row
    sum_top = one_row
    rows[5, pl.ds(top, planes, stride=knots), :] = one_row
    for s in reversed(range(top)):
        weight = run * inv_s[s]
        rows[5, pl.ds(s, planes, stride=knots), :] = weight
        sum_top = sum_top + weight * row(2, s)
        run = run * gain_s[s]
        low_total = low_total * gain_s[s]
    run = row(3, 0)
    high_total = one_row
    sum_bottom = row(4, 0)
    rows[6, pl.ds(top, planes, stride=knots), :] = jnp.zeros_like(one_row)
    for s in range(top):
        weight = run * inv_sb[s]
        rows[6, pl.ds(s, planes, stride=knots), :] = weight
        sum_bottom = sum_bottom + weight * row(2, s)
        run = run * gain_sb[s]
        high_total = high_total * ratio_s[s]
    coef = (
        row(0, top) * low_total,
        sum_top,
        row(1, top),
        sum_bottom,
        row(3, 0) * high_total,
    )
    for n, value in enumerate(coef):
        coefs[n * planes : (n + 1) * planes, :] = value
    for n in range(2):
        for x in range(planes):
            ends[n, x] = rows[5 + n, x * knots : (x + 1) * knots, :]
    start_all(outgoing[4:6])
    wait_all(outgoing)


def deposit_kernel(got, *refs):
    (deposit_hbm, swept, prefix, reduced, sums) = refs[8:13]
    (work, cell_rows, rhs, inv, first, ends, coefs, lower) = refs[13:21]
    (field, total, ups, lefts, rights, columns, edges, in_sems, sems) = refs[21:]
    incoming = copies_of(refs[:8], refs[13:21], in_sems)
    start_all(incoming)
    components, planes, height, across = rhs.shape
    steps = inv.shape[0] + 1
    last = steps - 1
    knots = ends.shape[2]
    rest = knots - segments
    slot = components + 1
    senders = lax.axis_size("span")
    block = got.shape[0] // senders
    parts = height // lanes
    shift = across.bit_length() - 1
    lines = components * planes
    kind = jnp.bfloat16 if across <= 256 else jnp.float32

    me = lax.axis_index("span")
    below = lax.rem(me + senders - 1, senders)
    above = lax.rem(me + 1, senders)
    total[...] = jnp.zeros_like(total)
    for half in range(2):
        ups[half][...] = jnp.zeros((8, lanes), jnp.float32)
    for p in range(parts):
        for n, owner in enumerate((above, below)):
            start = owner * block + p * slot + components
            columns[p, pl.ds(n, lines, stride=2), :] = got[pl.ds(start, lines, stride=parts * slot), :]
        edges[p * lanes : (p + 1) * lanes, :] = diffusion_number * columns[p].T

    tile = 16
    base = lax.broadcasted_iota(jnp.int32, (tile, lanes), 0)
    across_ids = [(base + n * tile).astype(jnp.float32).astype(kind) for n in range(across // tile)]
    every_height = lane_iota((lanes, height)).astype(jnp.float32)
    lane = lane_iota((1, lanes))
    none = jnp.zeros((tile, lanes), jnp.bfloat16)

    def spread(row, to):
        return jnp.broadcast_to(row, (tile, lanes)).astype(to)

    def build(n, half):
        for g in range(group):
            word = work[(n + 1) * group + g]
            ident = (word >> count_bits) & ((1 << (plane_bit - count_bits)) - 1)
            live = word & ((1 << count_bits) - 1)
            there = slice(g * lanes, (g + 1) * lanes)
            cell = cell_rows[pl.ds(ident, 1), :]
            up = jnp.where(lane < live, cell >> shift, -1).astype(jnp.float32)
            side = (cell & (across - 1)).astype(jnp.float32)
            ups[half][g : g + 1, :] = up
            side = spread(side, kind)
            masks = [side == ids for ids in across_ids]
            for c in range(components):
                force = got[pl.ds(ident * slot + c, 1), :]
                rest_of = force - force.astype(jnp.bfloat16).astype(jnp.float32)
                for m, value in enumerate((force, rest_of)):
                    value = spread(value, jnp.bfloat16)
                    start = (m * components + c) * across
                    for i, mask in enumerate(masks):
                        place = slice(start + i * tile, start + (i + 1) * tile)
                        rights[half][place, there] = jnp.where(mask, value, none)
        turned = ups[half][...].T
        for g in range(group):
            hot = jnp.where(turned[:, g : g + 1] == every_height, 1.0, 0.0)
            lefts[half][g * lanes : (g + 1) * lanes, :] = hot.astype(jnp.bfloat16)

    def add(n, half):
        total[work[(n + 1) * group] >> plane_bit] += lax.dot_general(
            rights[half][...],
            lefts[half][...],
            (((1,), (0,)), ((), ())),
            preferred_element_type=jnp.float32,
        )

    def two_steps(n, carry):
        build(2 * n + 1, 1)
        add(2 * n, 0)
        build(2 * n + 2, 0)
        add(2 * n + 1, 1)
        return carry

    wait_all(incoming[:2])
    build(0, 0)
    lax.fori_loop(0, work[0], two_steps, 0)
    wait_all(incoming[2:])

    wide = lane_iota((lanes, across))
    border = (wide == 0) | (wide == across - 1)

    def place(x):
        return [
            pltpu.make_async_copy(field.at[c, x], deposit_hbm.at[c, x], sems.at[c, x])
            for c in range(components)
        ]

    def combine(x, carry):
        for c in range(components):
            for p in range(parts):
                part = slice(p * lanes, (p + 1) * lanes)
                high = total[x, c * across : (c + 1) * across, part]
                low = total[x, (components + c) * across : (components + c + 1) * across, part]
                value = (high + low).T
                field[c, x, part, :] = value.astype(jnp.bfloat16)
                edge = pltpu.roll(edges[part, :], lanes - 1 - 2 * (c * planes + x), 1)
                rhs[c, x, part, :] = rhs[c, x, part, :] + value + jnp.where(border, edge, 0.0)
        start_all(place(x))
        return carry

    lax.fori_loop(0, planes, combine, 0)
    sums[2 * lines : 2 * lines + coefs.shape[0], :] = coefs[...]

    zero = jnp.zeros((components, planes, segments, across), jnp.float32)

    def of_step(t):
        return rhs[:, :, pl.ds(t, segments, stride=steps), :]

    def forward(t, carry):
        value, start, run, before = carry
        force = of_step(t)
        low, inverse = lower[:, pl.ds(t, segments, stride=steps), :], inv[t]
        value = force + (low * before)[None] * value
        swept[t] = inverse[None] * value
        run = run * (low * inverse)
        prefix[t] = run
        return value, start + first[t][None] * force, run, inverse

    one = jnp.ones((planes, segments, across), jnp.float32)
    value, start, _, inverse = lax.fori_loop(0, last, forward, (zero, zero, one, one), unroll=3)
    value = inverse[None] * value
    segment = lax.broadcasted_iota(jnp.int32, zero.shape, 2)
    after = jnp.where(segment == segments - 1, 0.0, jnp.roll(start, -1, axis=2))
    low_sep, up_sep = ends[2, :, :segments, :], ends[3, :, :segments, :]
    value = of_step(last) + low_sep[None] * value + up_sep[None] * after
    others = rhs[:, :, height - rest :, :]
    at_top = ends[0, :, :segments, :][None] * value + ends[0, :, segments:, :][None] * others
    at_bottom = ends[1, :, :segments, :][None] * value + ends[1, :, segments:, :][None] * others
    at_bottom = at_bottom + jnp.where(segment == 0, start, 0.0)
    for c in range(components):
        for x in range(planes):
            k = c * planes + x
            reduced[k * knots : k * knots + segments, :] = value[c, x]
            reduced[k * knots + segments : (k + 1) * knots, :] = others[c, x]
            sums[k : k + 1, :] = jnp.sum(at_top[c, x], 0, keepdims=True)
            sums[lines + k : lines + k + 1, :] = jnp.sum(at_bottom[c, x], 0, keepdims=True)

    for x in range(planes):
        wait_all(place(x))


def finish_kernel(inner, reduced, swept, inv, prefix, upper, *refs):
    walls = len(refs) - 7
    received = refs[:walls]
    out_hbm, sums, tops, after, before, out, sems = refs[walls:]
    components, planes, height, across = out.shape
    steps = swept.shape[0] + 1
    last = steps - 1
    lines = components * planes
    knots = inner.shape[1] + 1
    rest = knots - segments
    me = lax.axis_index("wall")
    for n in range(walls):
        sums[lax.rem(me + walls - n, walls)] = received[n][...]

    def coef(k, n):
        start = 2 * lines + n * planes
        return sums[k, start : start + planes, :]

    def wide(value):
        return jnp.concatenate([value] * components, 0)

    d = jnp.ones((planes, across), jnp.float32)
    value = jnp.zeros((lines, across), jnp.float32)
    values, ratios = [], []
    for k in range(walls):
        low, own, up = coef(k, 0), coef(k, 1), coef(k, 2)
        right = sums[k, :lines, :]
        if k + 1 < walls:
            high = up * coef(k + 1, 4)
            killing = own + up * coef(k + 1, 3)
            right = right + wide(up) * sums[k + 1, lines : 2 * lines, :]
        else:
            high = jnp.zeros_like(up)
            killing = own + up
        e = killing + low * d
        inverse = reciprocal(high + e)
        d = e * inverse
        value = (right + wide(low) * value) * wide(inverse)
        values.append(value)
        ratios.append(wide(high * inverse))
    tops[0] = jnp.zeros((lines, across), jnp.float32)
    tops[walls] = values[-1]
    for k in reversed(range(walls - 1)):
        values[k] = values[k] + ratios[k] * values[k + 1]
        tops[k + 1] = values[k]

    def row(s):
        return pl.ds(s, lines, stride=knots)

    run = tops[me]
    before[row(0), :] = run
    found = []
    for s in range(knots - 1):
        run = reduced[row(s), :] * wide(inner[0, s]) + wide(inner[1, s]) * run
        found.append(run)
    run = tops[me + 1]
    after[row(knots - 1), :] = run
    for s in reversed(range(knots - 1)):
        run = found[s] + wide(inner[2, s]) * run
        after[row(s), :] = run
        if s + 1 < segments:
            before[row(s + 1), :] = run

    def put(c, x, t, value):
        out[c, x, pl.ds(t, segments, stride=steps), :] = value

    copies = []
    half = planes // 2 if planes % 2 == 0 else planes
    for start in range(0, planes, half):
        part = [(c, x) for c in range(components) for x in range(start, start + half)]
        bottoms, starts = [], []
        for c, x in part:
            base = (c * planes + x) * knots
            bottoms.append(before[base : base + segments, :])
            starts.append(after[base : base + segments, :])
            out[c, x, height - rest :, :] = after[base + segments : base + knots, :]
            put(c, x, last, starts[-1])

        def backward(n, values):
            t = last - 1 - n
            found = []
            ratios = {}
            for x in range(start, start + half):
                ratios[x] = upper[x, pl.ds(t, segments, stride=steps), :] * inv[t, x]
            for (c, x), value, bottom in zip(part, values, bottoms):
                value = (swept[t, c, x] + prefix[t, x] * bottom) + ratios[x] * value
                put(c, x, t, value)
                found.append(value)
            return tuple(found)

        lax.fori_loop(0, last, backward, tuple(starts), unroll=3)
        for here in part:
            copy = pltpu.make_async_copy(out.at[here], out_hbm.at[here], sems.at[here])
            copy.start()
            copies.append(copy)
    wait_all(copies)


def everyone(block, axis, by_distance):
    length = lax.axis_size(axis)
    found = [by_distance[0]]
    for distance in range(1, length):
        route = [(i, (i + distance) % length) for i in range(length)]
        found.append(lax.ppermute(by_distance[distance], axis, route))
    return found


def local(velocity, lower_weight, upper_weight, forces, cells, counts):
    components, planes, height, across = velocity.shape
    receivers, capacity = forces.shape[3], forces.shape[5]
    senders = cells.shape[2]
    walls = lax.axis_size("wall")
    lines = components * planes
    chunks = capacity // lanes
    slot = components + 1
    forces = forces.reshape(components, receivers, planes, capacity)
    cells = cells.reshape(senders, planes, capacity)
    counts = counts.reshape(senders, planes).T

    def hbm(*arrays):
        return [pltpu.with_memory_space_constraint(array, pltpu.HBM) for array in arrays]

    send, velocity_near = call(
        pack_kernel,
        (f32(receivers, planes * chunks * slot, lanes), f32(*velocity.shape)),
        (in_hbm, in_vmem),
        [in_hbm] * 2,
        [
            scratch(*forces.shape),
            scratch(receivers, planes * chunks * slot, lanes),
            scratch(height, across),
            scratch(height // lanes, lanes, lanes),
            pltpu.SemaphoreType.DMA((components + lines + receivers,)),
        ],
        8,
        1 << 22,
    )(*hbm(velocity, forces))
    got = lax.all_to_all(send, "span", 0, 0, tiled=True)

    steps = height // segments - 1
    knots = height - segments * steps + segments
    step_shape = (steps - 1, planes, segments, across)
    work_shape = (planes * (senders * chunks + group) + 4 * group,)
    staged = [
        (velocity.shape, jnp.float32),
        (step_shape, jnp.float32),
        (step_shape, jnp.float32),
        ((3, knots - 1, planes, across), jnp.float32),
        ((4, planes, knots, across), jnp.float32),
        ((5 * planes, across), jnp.float32),
        ((senders * planes * chunks, lanes), jnp.int32),
    ]
    prepared = call(
        prepare_kernel,
        [pltpu.HBM(*entry) for entry in staged] + [pltpu.HBM(work_shape, jnp.int32)],
        [in_hbm] * 8,
        [in_smem, in_hbm] + [in_vmem] * 3,
        [
            *[pltpu.VMEM(*entry) for entry in staged],
            pltpu.SMEM(work_shape, jnp.int32),
            pltpu.VMEM(cells.shape, jnp.int32),
            scratch(*step_shape),
            scratch(*step_shape),
            scratch(7, planes * knots, across),
            pltpu.SemaphoreType.DMA((9,)),
        ],
        12,
        1 << 24,
    )(counts, *hbm(cells), velocity_near, lower_weight, upper_weight)
    (rhs_start, inv, first, inner, ends, coefs, cell_rows, work) = prepared

    sum_rows = -(-(2 * lines + 5 * planes) // 8) * 8
    wide = 2 * components * across
    deposit, swept, prefix, reduced, sums = call(
        deposit_kernel,
        (
            jax.ShapeDtypeStruct(velocity.shape, jnp.bfloat16),
            f32(steps - 1, components, planes, segments, across),
            f32(*step_shape),
            f32(lines * knots, across),
            f32(sum_rows, across),
        ),
        (in_hbm, *[in_vmem] * 4),
        [in_vmem] + [in_hbm] * 8,
        [
            pltpu.SMEM(work_shape, jnp.int32),
            pltpu.VMEM(*staged[6]),
            *[pltpu.VMEM(*staged[n]) for n in (0, 1, 2, 4, 5)],
            scratch(*lower_weight.shape),
            pltpu.VMEM(velocity.shape, jnp.bfloat16),
            scratch(planes, wide, height),
            [scratch(8, lanes)] * 2,
            [pltpu.VMEM((group * lanes, height), jnp.bfloat16)] * 2,
            [pltpu.VMEM((wide, group * lanes), jnp.bfloat16)] * 2,
            scratch(height // lanes, lanes, lanes),
            scratch(height, lanes),
            pltpu.SemaphoreType.DMA((8,)),
            pltpu.SemaphoreType.DMA((components, planes)),
        ],
        24,
        1 << 32,
    )(
        got.reshape(-1, lanes),
        *hbm(work, cell_rows, rhs_start, inv, first, ends, coefs, lower_weight),
    )
    all_sums = everyone(sums, "wall", [sums] * walls)

    velocity_next = call(
        finish_kernel,
        f32(*velocity.shape),
        in_hbm,
        [in_vmem] * (6 + walls),
        [
            scratch(walls, sum_rows, across),
            scratch(walls + 1, lines, across),
            scratch(lines * knots, across),
            scratch(lines * knots, across),
            scratch(*velocity.shape),
            pltpu.SemaphoreType.DMA((components, planes)),
        ],
        8,
        1 << 22,
    )(inner, reduced, swept, inv, prefix, upper_weight, *all_sums)
    return (velocity_next, deposit)


def solution(mesh):
    placed = (
        P(None, None, "wall", "span"),
        P(None, "wall", "span"),
        P(None, "wall", "span"),
        P(None, "wall", "span", None, None, None),
        P("wall", "span", None, None, None),
        P("wall", "span", None, None),
    )
    return jax.shard_map(
        local,
        mesh=mesh,
        in_specs=placed,
        out_specs=(P(None, None, "wall", "span"), P(None, None, "wall", "span")),
        check_vma=False,
    )
```

```python
import jax
import jax.numpy as jnp
from jax import lax
from jax.experimental import pallas as pl
from jax.experimental.pallas import tpu as pltpu
from jax.sharding import PartitionSpec as P

diffusion_number = 0.2
segments = 8
lanes = 128
group = 8
in_vmem = pl.BlockSpec(memory_space=pltpu.VMEM)
in_smem = pl.BlockSpec(memory_space=pltpu.SMEM)
in_hbm = pl.BlockSpec(memory_space=pltpu.HBM)


def call(body, out_shape, out_specs, in_specs, scratch, mebibytes, flops):
    return pl.pallas_call(
        body,
        out_shape=out_shape,
        in_specs=in_specs,
        out_specs=out_specs,
        scratch_shapes=scratch,
        compiler_params=pltpu.CompilerParams(vmem_limit_bytes=mebibytes << 20),
        cost_estimate=pl.CostEstimate(flops=flops, bytes_accessed=4 << 20, transcendentals=0),
    )


def f32(*shape):
    return jax.ShapeDtypeStruct(shape, jnp.float32)


def scratch(*shape):
    return pltpu.VMEM(shape, jnp.float32)


def lane_iota(shape):
    return lax.broadcasted_iota(jnp.int32, shape, len(shape) - 1)


def reciprocal(value):
    rough = pl.reciprocal(value, approx=True)
    return rough * (2.0 - value * rough)


def start_all(copies):
    for copy in copies:
        copy.start()


def wait_all(copies):
    for copy in copies:
        copy.wait()


def copies_of(sources, targets, sems, first=0):
    return [
        pltpu.make_async_copy(source, target, sems.at[first + n])
        for n, (source, target) in enumerate(zip(sources, targets))
    ]


def pack_kernel(velocity_hbm, forces_hbm, send_hbm, velocity, forces, send, columns, turned, sems):
    components, planes, height, across = velocity_hbm.shape
    receivers, capacity = forces_hbm.shape[1], forces_hbm.shape[3]
    chunks = capacity // lanes
    lines = components * planes
    parts = height // lanes
    slot = components + 1
    copies = copies_of(
        [forces_hbm.at[c] for c in range(components)],
        [forces.at[c] for c in range(components)],
        sems,
    )
    places = [(c, x) for c in range(components) for x in range(planes)]
    copies += copies_of(
        [velocity_hbm.at[here] for here in places],
        [velocity.at[here] for here in places],
        sems,
        components,
    )
    start_all(copies)
    me = lax.axis_index("span")
    wait_all(copies[:components])
    outgoing = []
    for d in range(receivers):
        owner = lax.rem(me + d, receivers)
        for c in range(components):
            for k in range(chunks):
                value = forces[c, owner, :, k * lanes : (k + 1) * lanes]
                send[owner, pl.ds(k * slot + c, planes, stride=chunks * slot), :] = value
        index = components + lines + d
        copy = pltpu.make_async_copy(send.at[owner], send_hbm.at[owner], sems.at[index])
        outgoing.append(copy)
        if d not in (1, receivers - 1):
            copy.start()
    lane = lane_iota((height, across))
    picked = jnp.zeros((height, across), jnp.float32)
    for k in range(lines):
        copies[components + k].wait()
        rolled = pltpu.roll(velocity[k // planes, k % planes], 2 * k + 1, 1)
        picked = jnp.where((lane >> 1) == k, rolled, picked)
    columns[...] = picked
    below = lax.rem(me + receivers - 1, receivers)
    above = lax.rem(me + 1, receivers)
    for p in range(parts):
        turned[p] = columns[p * lanes : (p + 1) * lanes, :].T
        target = pl.ds(p * slot + components, lines, stride=parts * slot)
        send[below, target, :] = turned[p, pl.ds(1, lines, stride=2), :]
        send[above, target, :] = turned[p, pl.ds(0, lines, stride=2), :]
    outgoing[1].start()
    outgoing[receivers - 1].start()
    wait_all(outgoing)


def prepare_kernel(cells_hbm, lower_hbm, upper_hbm, velocity, *refs):
    (cell_rows, rhs, inv, first, inner, ends, coefs) = refs[0], *refs[7:13]
    (lower, upper, cells, inv_b, gain_b, rows, sems) = refs[13:]
    outgoing = copies_of(refs[7:13], refs[1:7], sems)
    incoming = copies_of([lower_hbm, upper_hbm, cells_hbm], [lower, upper, cells], sems, 6)
    start_all(incoming)
    components, planes, height, across = velocity.shape
    steps = inv.shape[0] + 1
    last = steps - 1
    rest = height - segments * steps
    knots = segments + rest
    senders, capacity = cells.shape[0], cells.shape[2]
    chunks = capacity // lanes
    slot = components + 1
    wait_all(incoming[:2])

    def of_step(ref, t):
        return ref[:, pl.ds(t, segments, stride=steps), :]

    one = jnp.ones((planes, segments, across), jnp.float32)
    zero = jnp.zeros_like(one)
    size = 8
    lane = lane_iota((size, across))

    def stencil(n):
        part = pl.ds(pl.multiple_of(n * size, size), size)
        for c in range(components):
            values = [velocity[c, x, part, :] for x in range(planes)]
            for x in range(planes):
                v = values[x]
                around = values[(x - 1) % planes] + values[(x + 1) % planes]
                around = around + jnp.where(lane == 0, 0.0, pltpu.roll(v, 1, 1))
                around = around + jnp.where(lane == across - 1, 0.0, pltpu.roll(v, across - 1, 1))
                rhs[c, x, part, :] = (1.0 - 4.0 * diffusion_number) * v + diffusion_number * around

    def factor(t, carry):
        d, d_b, low_gain, high_gain, sum_last, sum_first = carry
        low, up = of_step(lower, t), of_step(upper, t)
        e = 1.0 + low * d
        inverse = reciprocal(up + e)
        g = low * inverse
        inv[t] = inverse
        back = last - 1 - t
        low_b, up_b = of_step(lower, back), of_step(upper, back)
        e_b = 1.0 + up_b * d_b
        inverse_b = reciprocal(low_b + e_b)
        g_b = up_b * inverse_b
        inv_b[back] = inverse_b
        gain_b[back] = g_b
        stencil(t)
        return (
            e * inverse,
            e_b * inverse_b,
            low_gain * g,
            high_gain * g_b,
            inverse + g * sum_last,
            inverse_b + g_b * sum_first,
        )

    carry = lax.fori_loop(0, last, factor, (one, one, one, one, zero, zero))
    _, _, low_gain, high_gain, sum_last, sum_first = carry
    for n in range(last, height // size):
        stencil(n)
    start_all(outgoing[:2])
    incoming[2].wait()

    def one_sender(s, carry):
        for k in range(chunks):
            start = (s * planes * chunks + k) * slot + components
            value = cells[s, :, k * lanes : (k + 1) * lanes].astype(jnp.float32)
            cell_rows[pl.ds(start, planes, stride=chunks * slot), :] = value
        return carry

    lax.fori_loop(0, senders, one_sender, 0, unroll=4)

    def weigh(t, q):
        first[t] = inv_b[t] * q
        return q * gain_b[t]

    lax.fori_loop(0, last, weigh, one, unroll=6)
    outgoing[2].start()

    low_sep, up_sep = of_step(lower, last), of_step(upper, last)
    segment = lax.broadcasted_iota(jnp.int32, one.shape, 1)
    is_end = segment == segments - 1
    above = jnp.where(is_end, 0.0, jnp.roll(sum_first, -1, axis=1))
    couple_high = up_sep * jnp.where(is_end, 1.0, jnp.roll(high_gain, -1, axis=1))
    killing = 1.0 + low_sep * sum_last + up_sep * above
    ends[2, :, :segments, :] = low_sep
    ends[3, :, :segments, :] = up_sep
    tail = slice(height - rest, height)
    low_rest, up_rest = lower[:, tail, :], upper[:, tail, :]
    for n, (value, other) in enumerate(
        (
            (low_sep * low_gain, low_rest),
            (couple_high, up_rest),
            (killing, jnp.ones_like(low_rest)),
        )
    ):
        for x in range(planes):
            rows[n, x * knots : x * knots + segments, :] = value[x]
            rows[n, x * knots + segments : (x + 1) * knots, :] = other[x]
    for x in range(planes):
        rows[3, x * knots : x * knots + segments, :] = high_gain[x]
        rows[4, x * knots : x * knots + segments, :] = sum_first[x]

    def row(n, s):
        return rows[n, pl.ds(s, planes, stride=knots), :]

    top = knots - 1
    one_row = jnp.ones((planes, across), jnp.float32)
    d, d_b = one_row, one_row
    inv_s, gain_s, ratio_s = [], [], []
    inv_sb, gain_sb = [None] * top, [None] * top
    for s in range(top):
        e = row(2, s) + row(0, s) * d
        inverse = reciprocal(row(1, s) + e)
        inv_s.append(inverse)
        gain_s.append(row(0, s) * inverse)
        ratio_s.append(row(1, s) * inverse)
        d = e * inverse
        back = top - 1 - s
        e_b = row(2, back) + row(1, back) * d_b
        inverse_b = reciprocal(row(0, back) + e_b)
        inv_sb[back] = inverse_b
        gain_sb[back] = row(1, back) * inverse_b
        d_b = e_b * inverse_b
        inner[0, s] = inv_s[s]
        inner[1, s] = gain_s[s]
        inner[2, s] = ratio_s[s]
    outgoing[3].start()
    run = row(0, top)
    low_total = one_row
    sum_top = one_row
    rows[5, pl.ds(top, planes, stride=knots), :] = one_row
    for s in reversed(range(top)):
        weight = run * inv_s[s]
        rows[5, pl.ds(s, planes, stride=knots), :] = weight
        sum_top = sum_top + weight * row(2, s)
        run = run * gain_s[s]
        low_total = low_total * gain_s[s]
    run = row(3, 0)
    high_total = one_row
    sum_bottom = row(4, 0)
    rows[6, pl.ds(top, planes, stride=knots), :] = jnp.zeros_like(one_row)
    for s in range(top):
        weight = run * inv_sb[s]
        rows[6, pl.ds(s, planes, stride=knots), :] = weight
        sum_bottom = sum_bottom + weight * row(2, s)
        run = run * gain_sb[s]
        high_total = high_total * ratio_s[s]
    coef = (
        row(0, top) * low_total,
        sum_top,
        row(1, top),
        sum_bottom,
        row(3, 0) * high_total,
    )
    for n, value in enumerate(coef):
        coefs[n * planes : (n + 1) * planes, :] = value
    for n in range(2):
        for x in range(planes):
            ends[n, x] = rows[5 + n, x * knots : (x + 1) * knots, :]
    start_all(outgoing[4:6])
    wait_all(outgoing)


def deposit_kernel(counts, got, cell_rows, *refs):
    (deposit_hbm, swept, prefix, reduced, sums) = refs[6:11]
    (rhs, inv, first, ends, coefs, lower) = refs[11:17]
    (stream, field, total, lefts, rights, columns, edges, in_sems, sems) = refs[17:]
    incoming = copies_of(refs[:6], refs[11:17], in_sems)
    start_all(incoming)
    components, planes, height, across = rhs.shape
    steps = inv.shape[0] + 1
    last = steps - 1
    knots = ends.shape[2]
    rest = knots - segments
    slot = components + 1
    senders = counts.shape[1]
    block = got.shape[0] // senders
    chunks = block // (planes * slot)
    parts = height // lanes
    shift = across.bit_length() - 1
    lines = components * planes
    kind = jnp.bfloat16 if max(height, across) <= 256 else jnp.float32

    me = lax.axis_index("span")
    below = lax.rem(me + senders - 1, senders)
    above = lax.rem(me + 1, senders)
    total[...] = jnp.zeros_like(total)
    for p in range(parts):
        for n, owner in enumerate((above, below)):
            start = owner * block + p * slot + components
            columns[p, pl.ds(n, lines, stride=2), :] = got[pl.ds(start, lines, stride=parts * slot), :]
        edges[p * lanes : (p + 1) * lanes, :] = diffusion_number * columns[p].T

    tile = 16
    base = lax.broadcasted_iota(jnp.int32, (tile, lanes), 0)
    height_ids = [(base + n * tile).astype(jnp.float32).astype(kind) for n in range(height // tile)]
    across_ids = height_ids[: across // tile]
    lane = lane_iota((1, lanes))
    one = jnp.ones((tile, lanes), jnp.bfloat16)
    none = jnp.zeros((tile, lanes), jnp.bfloat16)

    def spread(row, to):
        return jnp.broadcast_to(row, (tile, lanes)).astype(to)

    pair = 2 * slot
    pair_row = lax.broadcasted_iota(jnp.int32, (pair, lanes), 0)
    pair_lane = lane_iota((pair, lanes))
    is_cell = (pair_row & (slot - 1)) == components
    is_upper = pair_row >= slot

    def one_sender(s, ends_of):
        found = []
        for x in range(planes):
            start = ends_of[x]
            turn = start & (lanes - 1)
            tile_at = lax.div(start, lanes)
            here = pair_lane >= turn
            base = s * block + x * chunks * slot
            goal = tile_at * slot
            before = stream[x, pl.ds(goal, slot), :]
            before = jnp.concatenate([before, before], 0)
            for k in range(0, chunks, 2):
                rows = pl.ds(pl.multiple_of(base + k * slot, pair), pair)
                value = jnp.where(is_cell, cell_rows[rows, :], got[rows, :])
                value = pltpu.roll(value, turn, 1)
                swapped = pltpu.roll(jnp.where(is_upper, before, value), slot, 0)
                stream[x, pl.ds(goal + k * slot, pair), :] = jnp.where(here, value, swapped)
                before = value
            stream[x, pl.ds(goal + chunks * slot, slot), :] = before[slot:, :]
            found.append(start + counts[x, s])
        return tuple(found)

    lengths = lax.fori_loop(0, senders, one_sender, (0,) * planes)
    bounds = []
    count = 0
    for x in range(planes):
        count = count + lax.div(lengths[x] + group * lanes - 1, group * lanes)
        bounds.append(count)

    def locate(n):
        x, start, length = 0, 0, lengths[0]
        for later in range(1, planes):
            reached = n >= bounds[later - 1]
            x = jnp.where(reached, later, x)
            start = jnp.where(reached, bounds[later - 1], start)
            length = jnp.where(reached, lengths[later], length)
        return x, n - start, length

    def build(n, half):
        x, local_step, length = locate(n)
        for g in range(group):
            there = slice(g * lanes, (g + 1) * lanes)
            index = local_step * group + g
            live = length - index * lanes
            tile_rows = stream.at[x]
            cell = tile_rows[pl.ds(index * slot + components, 1), :].astype(jnp.int32)
            up = jnp.where(lane < live, cell >> shift, -1).astype(jnp.float32)
            side = jnp.where(lane < live, cell & (across - 1), -1).astype(jnp.float32)
            up, side = spread(up, kind), spread(side, kind)
            for i, ids in enumerate(height_ids):
                lefts[half][i * tile : (i + 1) * tile, there] = jnp.where(up == ids, one, none)
            masks = [side == ids for ids in across_ids]
            for c in range(components):
                force = tile_rows[pl.ds(index * slot + c, 1), :]
                rest_of = force - force.astype(jnp.bfloat16).astype(jnp.float32)
                for m, value in enumerate((force, rest_of)):
                    value = spread(value, jnp.bfloat16)
                    start = (m * components + c) * across
                    for i, mask in enumerate(masks):
                        place = slice(start + i * tile, start + (i + 1) * tile)
                        rights[half][place, there] = jnp.where(mask, value, none)

    def add(n, half):
        total[locate(n)[0]] += lax.dot_general(
            rights[half][...],
            lefts[half][...],
            (((1,), (1,)), ((), ())),
            preferred_element_type=jnp.float32,
        )

    def two_steps(n, carry):
        build(2 * n + 1, 1)
        add(2 * n, 0)
        build(2 * n + 2, 0)
        add(2 * n + 1, 1)
        return carry

    build(0, 0)
    lax.fori_loop(0, lax.div(count + 1, 2), two_steps, 0)
    wait_all(incoming)

    wide = lane_iota((lanes, across))
    border = (wide == 0) | (wide == across - 1)

    def place(x):
        return [
            pltpu.make_async_copy(field.at[c, x], deposit_hbm.at[c, x], sems.at[c, x])
            for c in range(components)
        ]

    def combine(x, carry):
        for c in range(components):
            for p in range(parts):
                part = slice(p * lanes, (p + 1) * lanes)
                high = total[x, c * across : (c + 1) * across, part]
                low = total[x, (components + c) * across : (components + c + 1) * across, part]
                value = (high + low).T
                field[c, x, part, :] = value.astype(jnp.bfloat16)
                edge = pltpu.roll(edges[part, :], lanes - 1 - 2 * (c * planes + x), 1)
                rhs[c, x, part, :] = rhs[c, x, part, :] + value + jnp.where(border, edge, 0.0)
        start_all(place(x))
        return carry

    lax.fori_loop(0, planes, combine, 0)
    sums[2 * lines : 2 * lines + coefs.shape[0], :] = coefs[...]

    zero = jnp.zeros((components, planes, segments, across), jnp.float32)

    def of_step(t):
        return rhs[:, :, pl.ds(t, segments, stride=steps), :]

    def forward(t, carry):
        value, start, run, before = carry
        force = of_step(t)
        low, inverse = lower[:, pl.ds(t, segments, stride=steps), :], inv[t]
        value = force + (low * before)[None] * value
        swept[t] = inverse[None] * value
        run = run * (low * inverse)
        prefix[t] = run
        return value, start + first[t][None] * force, run, inverse

    one = jnp.ones((planes, segments, across), jnp.float32)
    value, start, _, inverse = lax.fori_loop(0, last, forward, (zero, zero, one, one), unroll=3)
    value = inverse[None] * value
    segment = lax.broadcasted_iota(jnp.int32, zero.shape, 2)
    after = jnp.where(segment == segments - 1, 0.0, jnp.roll(start, -1, axis=2))
    low_sep, up_sep = ends[2, :, :segments, :], ends[3, :, :segments, :]
    value = of_step(last) + low_sep[None] * value + up_sep[None] * after
    others = rhs[:, :, height - rest :, :]
    at_top = ends[0, :, :segments, :][None] * value + ends[0, :, segments:, :][None] * others
    at_bottom = ends[1, :, :segments, :][None] * value + ends[1, :, segments:, :][None] * others
    at_bottom = at_bottom + jnp.where(segment == 0, start, 0.0)
    for c in range(components):
        for x in range(planes):
            k = c * planes + x
            reduced[k * knots : k * knots + segments, :] = value[c, x]
            reduced[k * knots + segments : (k + 1) * knots, :] = others[c, x]
            sums[k : k + 1, :] = jnp.sum(at_top[c, x], 0, keepdims=True)
            sums[lines + k : lines + k + 1, :] = jnp.sum(at_bottom[c, x], 0, keepdims=True)

    for x in range(planes):
        wait_all(place(x))


def finish_kernel(inner, reduced, swept, inv, prefix, upper, *refs):
    walls = len(refs) - 7
    received = refs[:walls]
    out_hbm, sums, tops, after, before, out, sems = refs[walls:]
    components, planes, height, across = out.shape
    steps = swept.shape[0] + 1
    last = steps - 1
    lines = components * planes
    knots = inner.shape[1] + 1
    rest = knots - segments
    me = lax.axis_index("wall")
    for n in range(walls):
        sums[lax.rem(me + walls - n, walls)] = received[n][...]

    def coef(k, n):
        start = 2 * lines + n * planes
        return sums[k, start : start + planes, :]

    def wide(value):
        return jnp.concatenate([value] * components, 0)

    d = jnp.ones((planes, across), jnp.float32)
    value = jnp.zeros((lines, across), jnp.float32)
    values, ratios = [], []
    for k in range(walls):
        low, own, up = coef(k, 0), coef(k, 1), coef(k, 2)
        right = sums[k, :lines, :]
        if k + 1 < walls:
            high = up * coef(k + 1, 4)
            killing = own + up * coef(k + 1, 3)
            right = right + wide(up) * sums[k + 1, lines : 2 * lines, :]
        else:
            high = jnp.zeros_like(up)
            killing = own + up
        e = killing + low * d
        inverse = reciprocal(high + e)
        d = e * inverse
        value = (right + wide(low) * value) * wide(inverse)
        values.append(value)
        ratios.append(wide(high * inverse))
    tops[0] = jnp.zeros((lines, across), jnp.float32)
    tops[walls] = values[-1]
    for k in reversed(range(walls - 1)):
        values[k] = values[k] + ratios[k] * values[k + 1]
        tops[k + 1] = values[k]

    def row(s):
        return pl.ds(s, lines, stride=knots)

    run = tops[me]
    before[row(0), :] = run
    found = []
    for s in range(knots - 1):
        run = reduced[row(s), :] * wide(inner[0, s]) + wide(inner[1, s]) * run
        found.append(run)
    run = tops[me + 1]
    after[row(knots - 1), :] = run
    for s in reversed(range(knots - 1)):
        run = found[s] + wide(inner[2, s]) * run
        after[row(s), :] = run
        if s + 1 < segments:
            before[row(s + 1), :] = run

    def put(c, x, t, value):
        out[c, x, pl.ds(t, segments, stride=steps), :] = value

    copies = []
    half = planes // 2 if planes % 2 == 0 else planes
    for start in range(0, planes, half):
        part = [(c, x) for c in range(components) for x in range(start, start + half)]
        bottoms, starts = [], []
        for c, x in part:
            base = (c * planes + x) * knots
            bottoms.append(before[base : base + segments, :])
            starts.append(after[base : base + segments, :])
            out[c, x, height - rest :, :] = after[base + segments : base + knots, :]
            put(c, x, last, starts[-1])

        def backward(n, values):
            t = last - 1 - n
            found = []
            ratios = {}
            for x in range(start, start + half):
                ratios[x] = upper[x, pl.ds(t, segments, stride=steps), :] * inv[t, x]
            for (c, x), value, bottom in zip(part, values, bottoms):
                value = (swept[t, c, x] + prefix[t, x] * bottom) + ratios[x] * value
                put(c, x, t, value)
                found.append(value)
            return tuple(found)

        lax.fori_loop(0, last, backward, tuple(starts), unroll=3)
        for here in part:
            copy = pltpu.make_async_copy(out.at[here], out_hbm.at[here], sems.at[here])
            copy.start()
            copies.append(copy)
    wait_all(copies)


def everyone(block, axis, by_distance):
    length = lax.axis_size(axis)
    found = [by_distance[0]]
    for distance in range(1, length):
        route = [(i, (i + distance) % length) for i in range(length)]
        found.append(lax.ppermute(by_distance[distance], axis, route))
    return found


def local(velocity, lower_weight, upper_weight, forces, cells, counts):
    components, planes, height, across = velocity.shape
    receivers, capacity = forces.shape[3], forces.shape[5]
    senders = cells.shape[2]
    walls = lax.axis_size("wall")
    lines = components * planes
    chunks = capacity // lanes
    slot = components + 1
    forces = forces.reshape(components, receivers, planes, capacity)
    cells = cells.reshape(senders, planes, capacity)
    counts = counts.reshape(senders, planes).T

    def hbm(*arrays):
        return [pltpu.with_memory_space_constraint(array, pltpu.HBM) for array in arrays]

    send, velocity_near = call(
        pack_kernel,
        (f32(receivers, planes * chunks * slot, lanes), f32(*velocity.shape)),
        (in_hbm, in_vmem),
        [in_hbm] * 2,
        [
            scratch(*forces.shape),
            scratch(receivers, planes * chunks * slot, lanes),
            scratch(height, across),
            scratch(height // lanes, lanes, lanes),
            pltpu.SemaphoreType.DMA((components + lines + receivers,)),
        ],
        8,
        1 << 22,
    )(*hbm(velocity, forces))
    got = lax.all_to_all(send, "span", 0, 0, tiled=True)

    steps = height // segments - 1
    knots = height - segments * steps + segments
    step_shape = (steps - 1, planes, segments, across)
    staged = [
        velocity.shape,
        step_shape,
        step_shape,
        (3, knots - 1, planes, across),
        (4, planes, knots, across),
        (5 * planes, across),
    ]
    cell_shape = (senders * planes * chunks * slot, lanes)
    prepared = call(
        prepare_kernel,
        [f32(*cell_shape)] + [pltpu.HBM(shape, jnp.float32) for shape in staged],
        [in_vmem] + [in_hbm] * 6,
        [in_hbm] * 3 + [in_vmem],
        [
            *[scratch(*shape) for shape in staged],
            *[scratch(*lower_weight.shape)] * 2,
            pltpu.VMEM(cells.shape, jnp.int32),
            scratch(*step_shape),
            scratch(*step_shape),
            scratch(7, planes * knots, across),
            pltpu.SemaphoreType.DMA((9,)),
        ],
        12,
        1 << 24,
    )(*hbm(cells, lower_weight, upper_weight), velocity_near)
    (cell_rows, rhs_start, inv, first, inner, ends, coefs) = prepared

    sum_rows = -(-(2 * lines + 5 * planes) // 8) * 8
    wide = 2 * components * across
    deposit, swept, prefix, reduced, sums = call(
        deposit_kernel,
        (
            jax.ShapeDtypeStruct(velocity.shape, jnp.bfloat16),
            f32(steps - 1, components, planes, segments, across),
            f32(*step_shape),
            f32(lines * knots, across),
            f32(sum_rows, across),
        ),
        (in_hbm, *[in_vmem] * 4),
        [in_smem] + [in_vmem] * 2 + [in_hbm] * 6,
        [
            *[scratch(*staged[n]) for n in (0, 1, 2, 4, 5)],
            scratch(*lower_weight.shape),
            scratch(planes, (senders * chunks + 3 * group) * slot, lanes),
            pltpu.VMEM(velocity.shape, jnp.bfloat16),
            scratch(planes, wide, height),
            [pltpu.VMEM((height, group * lanes), jnp.bfloat16)] * 2,
            [pltpu.VMEM((wide, group * lanes), jnp.bfloat16)] * 2,
            scratch(height // lanes, lanes, lanes),
            scratch(height, lanes),
            pltpu.SemaphoreType.DMA((6,)),
            pltpu.SemaphoreType.DMA((components, planes)),
        ],
        24,
        1 << 32,
    )(
        counts,
        got.reshape(-1, lanes),
        cell_rows,
        *hbm(rhs_start, inv, first, ends, coefs, lower_weight),
    )
    all_sums = everyone(sums, "wall", [sums] * walls)

    velocity_next = call(
        finish_kernel,
        f32(*velocity.shape),
        in_hbm,
        [in_vmem] * (6 + walls),
        [
            scratch(walls, sum_rows, across),
            scratch(walls + 1, lines, across),
            scratch(lines * knots, across),
            scratch(lines * knots, across),
            scratch(*velocity.shape),
            pltpu.SemaphoreType.DMA((components, planes)),
        ],
        8,
        1 << 22,
    )(inner, reduced, swept, inv, prefix, upper_weight, *all_sums)
    return (velocity_next, deposit)


def solution(mesh):
    placed = (
        P(None, None, "wall", "span"),
        P(None, "wall", "span"),
        P(None, "wall", "span"),
        P(None, "wall", "span", None, None, None),
        P("wall", "span", None, None, None),
        P("wall", "span", None, None),
    )
    return jax.shard_map(
        local,
        mesh=mesh,
        in_specs=placed,
        out_specs=(P(None, None, "wall", "span"), P(None, None, "wall", "span")),
        check_vma=False,
    )
```

```python
import jax
import jax.numpy as jnp
from jax import lax
from jax.experimental import pallas as pl
from jax.experimental.pallas import tpu as pltpu
from jax.sharding import PartitionSpec as P

diffusion_number = 0.2
segments = 8
lanes = 128
group = 8
in_vmem = pl.BlockSpec(memory_space=pltpu.VMEM)
in_smem = pl.BlockSpec(memory_space=pltpu.SMEM)
in_hbm = pl.BlockSpec(memory_space=pltpu.HBM)


def call(body, out_shape, out_specs, in_specs, scratch, mebibytes, flops):
    return pl.pallas_call(
        body,
        out_shape=out_shape,
        in_specs=in_specs,
        out_specs=out_specs,
        scratch_shapes=scratch,
        compiler_params=pltpu.CompilerParams(vmem_limit_bytes=mebibytes << 20),
        cost_estimate=pl.CostEstimate(flops=flops, bytes_accessed=4 << 20, transcendentals=0),
    )


def f32(*shape):
    return jax.ShapeDtypeStruct(shape, jnp.float32)


def scratch(*shape):
    return pltpu.VMEM(shape, jnp.float32)


def lane_iota(shape):
    return lax.broadcasted_iota(jnp.int32, shape, len(shape) - 1)


def reciprocal(value):
    rough = pl.reciprocal(value, approx=True)
    return rough * (2.0 - value * rough)


def start_all(copies):
    for copy in copies:
        copy.start()


def wait_all(copies):
    for copy in copies:
        copy.wait()


def copies_of(sources, targets, sems, first=0):
    return [
        pltpu.make_async_copy(source, target, sems.at[first + n])
        for n, (source, target) in enumerate(zip(sources, targets))
    ]


def pack_kernel(velocity_hbm, forces_hbm, send_hbm, velocity, forces, send, columns, turned, sems):
    components, planes, height, across = velocity_hbm.shape
    receivers, capacity = forces_hbm.shape[1], forces_hbm.shape[3]
    chunks = capacity // lanes
    lines = components * planes
    parts = height // lanes
    slot = components + 1
    copies = copies_of(
        [forces_hbm.at[c] for c in range(components)],
        [forces.at[c] for c in range(components)],
        sems,
    )
    places = [(c, x) for c in range(components) for x in range(planes)]
    copies += copies_of(
        [velocity_hbm.at[here] for here in places],
        [velocity.at[here] for here in places],
        sems,
        components,
    )
    start_all(copies)
    me = lax.axis_index("span")
    wait_all(copies[:components])
    outgoing = []
    for d in range(receivers):
        owner = lax.rem(me + d, receivers)
        for c in range(components):
            for k in range(chunks):
                value = forces[c, owner, :, k * lanes : (k + 1) * lanes]
                send[owner, pl.ds(k * slot + c, planes, stride=chunks * slot), :] = value
        index = components + lines + d
        copy = pltpu.make_async_copy(send.at[owner], send_hbm.at[owner], sems.at[index])
        outgoing.append(copy)
        if d not in (1, receivers - 1):
            copy.start()
    lane = lane_iota((height, across))
    picked = jnp.zeros((height, across), jnp.float32)
    for k in range(lines):
        copies[components + k].wait()
        rolled = pltpu.roll(velocity[k // planes, k % planes], 2 * k + 1, 1)
        picked = jnp.where((lane >> 1) == k, rolled, picked)
    columns[...] = picked
    below = lax.rem(me + receivers - 1, receivers)
    above = lax.rem(me + 1, receivers)
    for p in range(parts):
        turned[p] = columns[p * lanes : (p + 1) * lanes, :].T
        target = pl.ds(p * slot + components, lines, stride=parts * slot)
        send[below, target, :] = turned[p, pl.ds(1, lines, stride=2), :]
        send[above, target, :] = turned[p, pl.ds(0, lines, stride=2), :]
    outgoing[1].start()
    outgoing[receivers - 1].start()
    wait_all(outgoing)


def prepare_kernel(cells_hbm, lower_hbm, upper_hbm, velocity, *refs):
    (cell_rows, rhs, inv, first, inner, ends, coefs) = refs[0], *refs[7:13]
    (lower, upper, cells, inv_b, gain_b, rows, sems) = refs[13:]
    outgoing = copies_of(refs[7:13], refs[1:7], sems)
    incoming = copies_of([lower_hbm, upper_hbm, cells_hbm], [lower, upper, cells], sems, 6)
    start_all(incoming)
    components, planes, height, across = velocity.shape
    steps = inv.shape[0] + 1
    last = steps - 1
    rest = height - segments * steps
    knots = segments + rest
    senders, capacity = cells.shape[0], cells.shape[2]
    chunks = capacity // lanes
    slot = components + 1
    wait_all(incoming[:2])

    def of_step(ref, t):
        return ref[:, pl.ds(t, segments, stride=steps), :]

    one = jnp.ones((planes, segments, across), jnp.float32)
    zero = jnp.zeros_like(one)
    size = 8
    lane = lane_iota((size, across))

    def stencil(n):
        part = pl.ds(pl.multiple_of(n * size, size), size)
        for c in range(components):
            values = [velocity[c, x, part, :] for x in range(planes)]
            for x in range(planes):
                v = values[x]
                around = values[(x - 1) % planes] + values[(x + 1) % planes]
                around = around + jnp.where(lane == 0, 0.0, pltpu.roll(v, 1, 1))
                around = around + jnp.where(lane == across - 1, 0.0, pltpu.roll(v, across - 1, 1))
                rhs[c, x, part, :] = (1.0 - 4.0 * diffusion_number) * v + diffusion_number * around

    def factor(t, carry):
        d, d_b, low_gain, high_gain, sum_last, sum_first = carry
        low, up = of_step(lower, t), of_step(upper, t)
        e = 1.0 + low * d
        inverse = reciprocal(up + e)
        g = low * inverse
        inv[t] = inverse
        back = last - 1 - t
        low_b, up_b = of_step(lower, back), of_step(upper, back)
        e_b = 1.0 + up_b * d_b
        inverse_b = reciprocal(low_b + e_b)
        g_b = up_b * inverse_b
        inv_b[back] = inverse_b
        gain_b[back] = g_b
        stencil(t)
        return (
            e * inverse,
            e_b * inverse_b,
            low_gain * g,
            high_gain * g_b,
            inverse + g * sum_last,
            inverse_b + g_b * sum_first,
        )

    carry = lax.fori_loop(0, last, factor, (one, one, one, one, zero, zero))
    _, _, low_gain, high_gain, sum_last, sum_first = carry
    for n in range(last, height // size):
        stencil(n)
    start_all(outgoing[:2])
    incoming[2].wait()

    def one_sender(s, carry):
        for k in range(chunks):
            start = (s * planes * chunks + k) * slot + components
            value = cells[s, :, k * lanes : (k + 1) * lanes].astype(jnp.float32)
            cell_rows[pl.ds(start, planes, stride=chunks * slot), :] = value
        return carry

    lax.fori_loop(0, senders, one_sender, 0, unroll=4)

    def weigh(t, q):
        first[t] = inv_b[t] * q
        return q * gain_b[t]

    lax.fori_loop(0, last, weigh, one, unroll=6)
    outgoing[2].start()

    low_sep, up_sep = of_step(lower, last), of_step(upper, last)
    segment = lax.broadcasted_iota(jnp.int32, one.shape, 1)
    is_end = segment == segments - 1
    above = jnp.where(is_end, 0.0, jnp.roll(sum_first, -1, axis=1))
    couple_high = up_sep * jnp.where(is_end, 1.0, jnp.roll(high_gain, -1, axis=1))
    killing = 1.0 + low_sep * sum_last + up_sep * above
    ends[2, :, :segments, :] = low_sep
    ends[3, :, :segments, :] = up_sep
    tail = slice(height - rest, height)
    low_rest, up_rest = lower[:, tail, :], upper[:, tail, :]
    for n, (value, other) in enumerate(
        (
            (low_sep * low_gain, low_rest),
            (couple_high, up_rest),
            (killing, jnp.ones_like(low_rest)),
        )
    ):
        for x in range(planes):
            rows[n, x * knots : x * knots + segments, :] = value[x]
            rows[n, x * knots + segments : (x + 1) * knots, :] = other[x]
    for x in range(planes):
        rows[3, x * knots : x * knots + segments, :] = high_gain[x]
        rows[4, x * knots : x * knots + segments, :] = sum_first[x]

    def row(n, s):
        return rows[n, pl.ds(s, planes, stride=knots), :]

    top = knots - 1
    one_row = jnp.ones((planes, across), jnp.float32)
    d, d_b = one_row, one_row
    inv_s, gain_s, ratio_s = [], [], []
    inv_sb, gain_sb = [None] * top, [None] * top
    for s in range(top):
        e = row(2, s) + row(0, s) * d
        inverse = reciprocal(row(1, s) + e)
        inv_s.append(inverse)
        gain_s.append(row(0, s) * inverse)
        ratio_s.append(row(1, s) * inverse)
        d = e * inverse
        back = top - 1 - s
        e_b = row(2, back) + row(1, back) * d_b
        inverse_b = reciprocal(row(0, back) + e_b)
        inv_sb[back] = inverse_b
        gain_sb[back] = row(1, back) * inverse_b
        d_b = e_b * inverse_b
        inner[0, s] = inv_s[s]
        inner[1, s] = gain_s[s]
        inner[2, s] = ratio_s[s]
    outgoing[3].start()
    run = row(0, top)
    low_total = one_row
    sum_top = one_row
    rows[5, pl.ds(top, planes, stride=knots), :] = one_row
    for s in reversed(range(top)):
        weight = run * inv_s[s]
        rows[5, pl.ds(s, planes, stride=knots), :] = weight
        sum_top = sum_top + weight * row(2, s)
        run = run * gain_s[s]
        low_total = low_total * gain_s[s]
    run = row(3, 0)
    high_total = one_row
    sum_bottom = row(4, 0)
    rows[6, pl.ds(top, planes, stride=knots), :] = jnp.zeros_like(one_row)
    for s in range(top):
        weight = run * inv_sb[s]
        rows[6, pl.ds(s, planes, stride=knots), :] = weight
        sum_bottom = sum_bottom + weight * row(2, s)
        run = run * gain_sb[s]
        high_total = high_total * ratio_s[s]
    coef = (
        row(0, top) * low_total,
        sum_top,
        row(1, top),
        sum_bottom,
        row(3, 0) * high_total,
    )
    for n, value in enumerate(coef):
        coefs[n * planes : (n + 1) * planes, :] = value
    for n in range(2):
        for x in range(planes):
            ends[n, x] = rows[5 + n, x * knots : (x + 1) * knots, :]
    start_all(outgoing[4:6])
    wait_all(outgoing)


def deposit_kernel(counts, got, cell_rows, *refs):
    (deposit_hbm, swept, prefix, reduced, sums) = refs[6:11]
    (rhs, inv, first, ends, coefs, lower) = refs[11:17]
    (stream, field, total, lefts, rights, columns, edges, in_sems, sems) = refs[17:]
    incoming = copies_of(refs[:6], refs[11:17], in_sems)
    start_all(incoming)
    components, planes, height, across = rhs.shape
    steps = inv.shape[0] + 1
    last = steps - 1
    knots = ends.shape[2]
    rest = knots - segments
    slot = components + 1
    senders = counts.shape[1]
    block = got.shape[0] // senders
    chunks = block // (planes * slot)
    parts = height // lanes
    shift = across.bit_length() - 1
    lines = components * planes
    kind = jnp.bfloat16 if max(height, across) <= 256 else jnp.float32

    me = lax.axis_index("span")
    below = lax.rem(me + senders - 1, senders)
    above = lax.rem(me + 1, senders)
    total[...] = jnp.zeros_like(total)
    for p in range(parts):
        for n, owner in enumerate((above, below)):
            start = owner * block + p * slot + components
            columns[p, pl.ds(n, lines, stride=2), :] = got[pl.ds(start, lines, stride=parts * slot), :]
        edges[p * lanes : (p + 1) * lanes, :] = diffusion_number * columns[p].T

    tile = 16
    base = lax.broadcasted_iota(jnp.int32, (tile, lanes), 0)
    height_ids = [(base + n * tile).astype(jnp.float32).astype(kind) for n in range(height // tile)]
    across_ids = height_ids[: across // tile]
    lane = lane_iota((1, lanes))
    one = jnp.ones((tile, lanes), jnp.bfloat16)
    none = jnp.zeros((tile, lanes), jnp.bfloat16)

    def spread(row, to):
        return jnp.broadcast_to(row, (tile, lanes)).astype(to)

    pair = 2 * slot
    pair_row = lax.broadcasted_iota(jnp.int32, (pair, lanes), 0)
    pair_lane = lane_iota((pair, lanes))
    is_cell = (pair_row & (slot - 1)) == components
    is_upper = pair_row >= slot

    def one_sender(s, ends_of):
        found, values = [], []
        for x in range(planes):
            start = ends_of[x]
            turn = start & (lanes - 1)
            goal = lax.div(start, lanes) * slot
            base = s * block + x * chunks * slot
            before = stream[x, pl.ds(goal, slot), :]
            turned = [jnp.concatenate([before, before], 0)]
            for k in range(0, chunks, 2):
                rows = pl.ds(pl.multiple_of(base + k * slot, pair), pair)
                value = jnp.where(is_cell, cell_rows[rows, :], got[rows, :])
                turned.append(pltpu.roll(value, turn, 1))
            values.append((goal, pair_lane >= turn, turned))
            found.append(start + counts[x, s])
        for x, (goal, here, turned) in enumerate(values):
            for k in range(len(turned) - 1):
                before, value = turned[k], turned[k + 1]
                swapped = pltpu.roll(jnp.where(is_upper, before, value), slot, 0)
                place = pl.ds(goal + k * pair, pair)
                stream[x, place, :] = jnp.where(here, value, swapped)
            stream[x, pl.ds(goal + chunks * slot, slot), :] = turned[-1][slot:, :]
        return tuple(found)

    lengths = lax.fori_loop(0, senders, one_sender, (0,) * planes)
    bounds = []
    count = 0
    for x in range(planes):
        count = count + lax.div(lengths[x] + group * lanes - 1, group * lanes)
        bounds.append(count)

    def locate(n):
        x, start, length = 0, 0, lengths[0]
        for later in range(1, planes):
            reached = n >= bounds[later - 1]
            x = jnp.where(reached, later, x)
            start = jnp.where(reached, bounds[later - 1], start)
            length = jnp.where(reached, lengths[later], length)
        return x, n - start, length

    position = lax.broadcasted_iota(jnp.int32, (group, lanes), 0) * lanes
    position = position + lane_iota((group, lanes))

    def fetch(n):
        x, local_step, length = locate(n)
        tiles = stream.at[x]
        first_row = local_step * (group * slot)

        def rows(c):
            return tiles[pl.ds(first_row + c, group, stride=slot), :]

        live = position < length - local_step * (group * lanes)
        cell = rows(components).astype(jnp.int32)
        up = jnp.where(live, cell >> shift, -1).astype(jnp.float32)
        side = jnp.where(live, cell & (across - 1), -1).astype(jnp.float32)
        forces = [rows(c) for c in range(components)]
        highs = [force.astype(jnp.bfloat16).astype(jnp.float32) for force in forces]
        lows = [force - high for force, high in zip(forces, highs)]
        return (up, side, *highs, *lows)

    def build(fetched, half):
        for g in range(group):
            there = slice(g * lanes, (g + 1) * lanes)
            up, side, *values = [value[g : g + 1, :] for value in fetched]
            up, side = spread(up, kind), spread(side, kind)
            for i, ids in enumerate(height_ids):
                lefts[half][i * tile : (i + 1) * tile, there] = jnp.where(up == ids, one, none)
            masks = [side == ids for ids in across_ids]
            for n, value in enumerate(values):
                value = spread(value, jnp.bfloat16)
                for i, mask in enumerate(masks):
                    place = slice(n * across + i * tile, n * across + (i + 1) * tile)
                    rights[half][place, there] = jnp.where(mask, value, none)

    def add(n, half):
        total[locate(n)[0]] += lax.dot_general(
            rights[half][...],
            lefts[half][...],
            (((1,), (1,)), ((), ())),
            preferred_element_type=jnp.float32,
        )

    def two_steps(n, fetched):
        later = fetch(2 * n + 2)
        build(fetched, 1)
        add(2 * n, 0)
        fetched = fetch(2 * n + 3)
        build(later, 0)
        add(2 * n + 1, 1)
        return fetched

    build(fetch(0), 0)
    lax.fori_loop(0, lax.div(count + 1, 2), two_steps, fetch(1))
    wait_all(incoming)

    wide = lane_iota((lanes, across))
    border = (wide == 0) | (wide == across - 1)

    def place(x):
        return [
            pltpu.make_async_copy(field.at[c, x], deposit_hbm.at[c, x], sems.at[c, x])
            for c in range(components)
        ]

    def combine(x, carry):
        for c in range(components):
            for p in range(parts):
                part = slice(p * lanes, (p + 1) * lanes)
                high = total[x, c * across : (c + 1) * across, part]
                low = total[x, (components + c) * across : (components + c + 1) * across, part]
                value = (high + low).T
                field[c, x, part, :] = value.astype(jnp.bfloat16)
                edge = pltpu.roll(edges[part, :], lanes - 1 - 2 * (c * planes + x), 1)
                rhs[c, x, part, :] = rhs[c, x, part, :] + value + jnp.where(border, edge, 0.0)
        start_all(place(x))
        return carry

    lax.fori_loop(0, planes, combine, 0)
    sums[2 * lines : 2 * lines + coefs.shape[0], :] = coefs[...]

    zero = jnp.zeros((components, planes, segments, across), jnp.float32)

    def of_step(t):
        return rhs[:, :, pl.ds(t, segments, stride=steps), :]

    def forward(t, carry):
        value, start, run, before = carry
        force = of_step(t)
        low, inverse = lower[:, pl.ds(t, segments, stride=steps), :], inv[t]
        value = force + (low * before)[None] * value
        swept[t] = inverse[None] * value
        run = run * (low * inverse)
        prefix[t] = run
        return value, start + first[t][None] * force, run, inverse

    one = jnp.ones((planes, segments, across), jnp.float32)
    value, start, _, inverse = lax.fori_loop(0, last, forward, (zero, zero, one, one), unroll=3)
    value = inverse[None] * value
    segment = lax.broadcasted_iota(jnp.int32, zero.shape, 2)
    after = jnp.where(segment == segments - 1, 0.0, jnp.roll(start, -1, axis=2))
    low_sep, up_sep = ends[2, :, :segments, :], ends[3, :, :segments, :]
    value = of_step(last) + low_sep[None] * value + up_sep[None] * after
    others = rhs[:, :, height - rest :, :]
    at_top = ends[0, :, :segments, :][None] * value + ends[0, :, segments:, :][None] * others
    at_bottom = ends[1, :, :segments, :][None] * value + ends[1, :, segments:, :][None] * others
    at_bottom = at_bottom + jnp.where(segment == 0, start, 0.0)
    for c in range(components):
        for x in range(planes):
            k = c * planes + x
            reduced[k * knots : k * knots + segments, :] = value[c, x]
            reduced[k * knots + segments : (k + 1) * knots, :] = others[c, x]
            sums[k : k + 1, :] = jnp.sum(at_top[c, x], 0, keepdims=True)
            sums[lines + k : lines + k + 1, :] = jnp.sum(at_bottom[c, x], 0, keepdims=True)

    for x in range(planes):
        wait_all(place(x))


def finish_kernel(sums, inner, reduced, swept, inv, prefix, upper, *refs):
    walls = sums.shape[0]
    out_hbm, tops, after, before, out, sems = refs
    components, planes, height, across = out.shape
    steps = swept.shape[0] + 1
    last = steps - 1
    lines = components * planes
    knots = inner.shape[1] + 1
    rest = knots - segments
    me = lax.axis_index("wall")

    def coef(k, n):
        start = 2 * lines + n * planes
        return sums[k, start : start + planes, :]

    def wide(value):
        return jnp.concatenate([value] * components, 0)

    d = jnp.ones((planes, across), jnp.float32)
    value = jnp.zeros((lines, across), jnp.float32)
    values, ratios = [], []
    for k in range(walls):
        low, own, up = coef(k, 0), coef(k, 1), coef(k, 2)
        right = sums[k, :lines, :]
        if k + 1 < walls:
            high = up * coef(k + 1, 4)
            killing = own + up * coef(k + 1, 3)
            right = right + wide(up) * sums[k + 1, lines : 2 * lines, :]
        else:
            high = jnp.zeros_like(up)
            killing = own + up
        e = killing + low * d
        inverse = reciprocal(high + e)
        d = e * inverse
        value = (right + wide(low) * value) * wide(inverse)
        values.append(value)
        ratios.append(wide(high * inverse))
    tops[0] = jnp.zeros((lines, across), jnp.float32)
    tops[walls] = values[-1]
    for k in reversed(range(walls - 1)):
        values[k] = values[k] + ratios[k] * values[k + 1]
        tops[k + 1] = values[k]

    def row(s):
        return pl.ds(s, lines, stride=knots)

    run = tops[me]
    before[row(0), :] = run
    found = []
    for s in range(knots - 1):
        run = reduced[row(s), :] * wide(inner[0, s]) + wide(inner[1, s]) * run
        found.append(run)
    run = tops[me + 1]
    after[row(knots - 1), :] = run
    for s in reversed(range(knots - 1)):
        run = found[s] + wide(inner[2, s]) * run
        after[row(s), :] = run
        if s + 1 < segments:
            before[row(s + 1), :] = run

    def put(c, x, t, value):
        out[c, x, pl.ds(t, segments, stride=steps), :] = value

    copies = []
    half = planes // 2 if planes % 2 == 0 else planes
    for start in range(0, planes, half):
        part = [(c, x) for c in range(components) for x in range(start, start + half)]
        bottoms, starts = [], []
        for c, x in part:
            base = (c * planes + x) * knots
            bottoms.append(before[base : base + segments, :])
            starts.append(after[base : base + segments, :])
            out[c, x, height - rest :, :] = after[base + segments : base + knots, :]
            put(c, x, last, starts[-1])

        def backward(n, values):
            t = last - 1 - n
            found = []
            ratios = {}
            for x in range(start, start + half):
                ratios[x] = upper[x, pl.ds(t, segments, stride=steps), :] * inv[t, x]
            for (c, x), value, bottom in zip(part, values, bottoms):
                value = (swept[t, c, x] + prefix[t, x] * bottom) + ratios[x] * value
                put(c, x, t, value)
                found.append(value)
            return tuple(found)

        lax.fori_loop(0, last, backward, tuple(starts), unroll=3)
        for here in part:
            copy = pltpu.make_async_copy(out.at[here], out_hbm.at[here], sems.at[here])
            copy.start()
            copies.append(copy)
    wait_all(copies)


def local(velocity, lower_weight, upper_weight, forces, cells, counts):
    components, planes, height, across = velocity.shape
    receivers, capacity = forces.shape[3], forces.shape[5]
    senders = cells.shape[2]
    walls = lax.axis_size("wall")
    lines = components * planes
    chunks = capacity // lanes
    slot = components + 1
    forces = forces.reshape(components, receivers, planes, capacity)
    cells = cells.reshape(senders, planes, capacity)
    counts = counts.reshape(senders, planes).T

    def hbm(*arrays):
        return [pltpu.with_memory_space_constraint(array, pltpu.HBM) for array in arrays]

    send, velocity_near = call(
        pack_kernel,
        (f32(receivers, planes * chunks * slot, lanes), f32(*velocity.shape)),
        (in_hbm, in_vmem),
        [in_hbm] * 2,
        [
            scratch(*forces.shape),
            scratch(receivers, planes * chunks * slot, lanes),
            scratch(height, across),
            scratch(height // lanes, lanes, lanes),
            pltpu.SemaphoreType.DMA((components + lines + receivers,)),
        ],
        8,
        1 << 22,
    )(*hbm(velocity, forces))
    got = lax.all_to_all(send, "span", 0, 0, tiled=True)

    steps = height // segments - 1
    knots = height - segments * steps + segments
    step_shape = (steps - 1, planes, segments, across)
    staged = [
        velocity.shape,
        step_shape,
        step_shape,
        (3, knots - 1, planes, across),
        (4, planes, knots, across),
        (5 * planes, across),
    ]
    cell_shape = (senders * planes * chunks * slot, lanes)
    prepared = call(
        prepare_kernel,
        [f32(*cell_shape)] + [pltpu.HBM(shape, jnp.float32) for shape in staged],
        [in_vmem] + [in_hbm] * 6,
        [in_hbm] * 3 + [in_vmem],
        [
            *[scratch(*shape) for shape in staged],
            *[scratch(*lower_weight.shape)] * 2,
            pltpu.VMEM(cells.shape, jnp.int32),
            scratch(*step_shape),
            scratch(*step_shape),
            scratch(7, planes * knots, across),
            pltpu.SemaphoreType.DMA((9,)),
        ],
        12,
        1 << 24,
    )(*hbm(cells, lower_weight, upper_weight), velocity_near)
    (cell_rows, rhs_start, inv, first, inner, ends, coefs) = prepared

    sum_rows = -(-(2 * lines + 5 * planes) // 8) * 8
    wide = 2 * components * across
    deposit, swept, prefix, reduced, sums = call(
        deposit_kernel,
        (
            jax.ShapeDtypeStruct(velocity.shape, jnp.bfloat16),
            f32(steps - 1, components, planes, segments, across),
            f32(*step_shape),
            f32(lines * knots, across),
            f32(sum_rows, across),
        ),
        (in_hbm, *[in_vmem] * 4),
        [in_smem] + [in_vmem] * 2 + [in_hbm] * 6,
        [
            *[scratch(*staged[n]) for n in (0, 1, 2, 4, 5)],
            scratch(*lower_weight.shape),
            scratch(planes, (senders * chunks + 4 * group) * slot, lanes),
            pltpu.VMEM(velocity.shape, jnp.bfloat16),
            scratch(planes, wide, height),
            [pltpu.VMEM((height, group * lanes), jnp.bfloat16)] * 2,
            [pltpu.VMEM((wide, group * lanes), jnp.bfloat16)] * 2,
            scratch(height // lanes, lanes, lanes),
            scratch(height, lanes),
            pltpu.SemaphoreType.DMA((6,)),
            pltpu.SemaphoreType.DMA((components, planes)),
        ],
        24,
        1 << 32,
    )(
        counts,
        got.reshape(-1, lanes),
        cell_rows,
        *hbm(rhs_start, inv, first, ends, coefs, lower_weight),
    )
    all_sums = lax.all_gather(sums, "wall")

    velocity_next = call(
        finish_kernel,
        f32(*velocity.shape),
        in_hbm,
        [in_vmem] * 7,
        [
            scratch(walls + 1, lines, across),
            scratch(lines * knots, across),
            scratch(lines * knots, across),
            scratch(*velocity.shape),
            pltpu.SemaphoreType.DMA((components, planes)),
        ],
        8,
        1 << 22,
    )(all_sums, inner, reduced, swept, inv, prefix, upper_weight)
    return (velocity_next, deposit)


def solution(mesh):
    placed = (
        P(None, None, "wall", "span"),
        P(None, "wall", "span"),
        P(None, "wall", "span"),
        P(None, "wall", "span", None, None, None),
        P("wall", "span", None, None, None),
        P("wall", "span", None, None),
    )
    return jax.shard_map(
        local,
        mesh=mesh,
        in_specs=placed,
        out_specs=(P(None, None, "wall", "span"), P(None, None, "wall", "span")),
        check_vma=False,
    )
```

```python
import jax
import jax.numpy as jnp
from jax import lax
from jax.experimental import pallas as pl
from jax.experimental.pallas import tpu as pltpu
from jax.sharding import PartitionSpec as P

diffusion_number = 0.2
segments = 8
lanes = 128
group = 8
in_vmem = pl.BlockSpec(memory_space=pltpu.VMEM)
in_smem = pl.BlockSpec(memory_space=pltpu.SMEM)
in_hbm = pl.BlockSpec(memory_space=pltpu.HBM)


def call(body, out_shape, out_specs, in_specs, scratch, mebibytes, flops):
    return pl.pallas_call(
        body,
        out_shape=out_shape,
        in_specs=in_specs,
        out_specs=out_specs,
        scratch_shapes=scratch,
        compiler_params=pltpu.CompilerParams(vmem_limit_bytes=mebibytes << 20),
        cost_estimate=pl.CostEstimate(flops=flops, bytes_accessed=4 << 20, transcendentals=0),
    )


def f32(*shape):
    return jax.ShapeDtypeStruct(shape, jnp.float32)


def scratch(*shape):
    return pltpu.VMEM(shape, jnp.float32)


def lane_iota(shape):
    return lax.broadcasted_iota(jnp.int32, shape, len(shape) - 1)


def reciprocal(value):
    rough = pl.reciprocal(value, approx=True)
    return rough * (2.0 - value * rough)


def start_all(copies):
    for copy in copies:
        copy.start()


def wait_all(copies):
    for copy in copies:
        copy.wait()


def copies_of(sources, targets, sems, first=0):
    return [
        pltpu.make_async_copy(source, target, sems.at[first + n])
        for n, (source, target) in enumerate(zip(sources, targets))
    ]


def pack_kernel(velocity_hbm, forces_hbm, send_hbm, velocity, forces, send, columns, turned, sems):
    components, planes, height, across = velocity_hbm.shape
    receivers, capacity = forces_hbm.shape[1], forces_hbm.shape[3]
    chunks = capacity // lanes
    lines = components * planes
    parts = height // lanes
    slot = components + 1
    copies = copies_of(
        [forces_hbm.at[c] for c in range(components)],
        [forces.at[c] for c in range(components)],
        sems,
    )
    places = [(c, x) for c in range(components) for x in range(planes)]
    copies += copies_of(
        [velocity_hbm.at[here] for here in places],
        [velocity.at[here] for here in places],
        sems,
        components,
    )
    start_all(copies)
    me = lax.axis_index("span")
    wait_all(copies[:components])
    outgoing = []
    for d in range(receivers):
        owner = lax.rem(me + d, receivers)
        for c in range(components):
            for k in range(chunks):
                value = forces[c, owner, :, k * lanes : (k + 1) * lanes]
                send[owner, pl.ds(k * slot + c, planes, stride=chunks * slot), :] = value
        index = components + lines + d
        copy = pltpu.make_async_copy(send.at[owner], send_hbm.at[owner], sems.at[index])
        outgoing.append(copy)
        if d not in (1, receivers - 1):
            copy.start()
    lane = lane_iota((height, across))
    picked = jnp.zeros((height, across), jnp.float32)
    for k in range(lines):
        copies[components + k].wait()
        rolled = pltpu.roll(velocity[k // planes, k % planes], 2 * k + 1, 1)
        picked = jnp.where((lane >> 1) == k, rolled, picked)
    columns[...] = picked
    below = lax.rem(me + receivers - 1, receivers)
    above = lax.rem(me + 1, receivers)
    for p in range(parts):
        turned[p] = columns[p * lanes : (p + 1) * lanes, :].T
        target = pl.ds(p * slot + components, lines, stride=parts * slot)
        send[below, target, :] = turned[p, pl.ds(1, lines, stride=2), :]
        send[above, target, :] = turned[p, pl.ds(0, lines, stride=2), :]
    outgoing[1].start()
    outgoing[receivers - 1].start()
    wait_all(outgoing)


def prepare_kernel(cells_hbm, lower_hbm, upper_hbm, velocity, *refs):
    (cell_rows, rhs, inv, first, inner, ends, coefs) = refs[0], *refs[7:13]
    (lower, upper, cells, inv_b, gain_b, rows, sems) = refs[13:]
    outgoing = copies_of(refs[7:13], refs[1:7], sems)
    incoming = copies_of([lower_hbm, upper_hbm, cells_hbm], [lower, upper, cells], sems, 6)
    start_all(incoming)
    components, planes, height, across = velocity.shape
    steps = inv.shape[0] + 1
    last = steps - 1
    rest = height - segments * steps
    knots = segments + rest
    senders, capacity = cells.shape[0], cells.shape[2]
    chunks = capacity // lanes
    slot = components + 1
    wait_all(incoming[:2])

    def of_step(ref, t):
        return ref[:, pl.ds(t, segments, stride=steps), :]

    one = jnp.ones((planes, segments, across), jnp.float32)
    zero = jnp.zeros_like(one)
    size = 8
    lane = lane_iota((size, across))

    def stencil(n):
        part = pl.ds(pl.multiple_of(n * size, size), size)
        for c in range(components):
            values = [velocity[c, x, part, :] for x in range(planes)]
            for x in range(planes):
                v = values[x]
                around = values[(x - 1) % planes] + values[(x + 1) % planes]
                around = around + jnp.where(lane == 0, 0.0, pltpu.roll(v, 1, 1))
                around = around + jnp.where(lane == across - 1, 0.0, pltpu.roll(v, across - 1, 1))
                rhs[c, x, part, :] = (1.0 - 4.0 * diffusion_number) * v + diffusion_number * around

    def factor(t, carry):
        d, d_b, low_gain, high_gain, sum_last, sum_first = carry
        low, up = of_step(lower, t), of_step(upper, t)
        e = 1.0 + low * d
        inverse = reciprocal(up + e)
        g = low * inverse
        inv[t] = inverse
        back = last - 1 - t
        low_b, up_b = of_step(lower, back), of_step(upper, back)
        e_b = 1.0 + up_b * d_b
        inverse_b = reciprocal(low_b + e_b)
        g_b = up_b * inverse_b
        inv_b[back] = inverse_b
        gain_b[back] = g_b
        stencil(t)
        return (
            e * inverse,
            e_b * inverse_b,
            low_gain * g,
            high_gain * g_b,
            inverse + g * sum_last,
            inverse_b + g_b * sum_first,
        )

    carry = lax.fori_loop(0, last, factor, (one, one, one, one, zero, zero))
    _, _, low_gain, high_gain, sum_last, sum_first = carry
    for n in range(last, height // size):
        stencil(n)
    start_all(outgoing[:2])
    incoming[2].wait()

    def one_sender(s, carry):
        for k in range(chunks):
            start = (s * planes * chunks + k) * slot + components
            value = cells[s, :, k * lanes : (k + 1) * lanes].astype(jnp.float32)
            cell_rows[pl.ds(start, planes, stride=chunks * slot), :] = value
        return carry

    lax.fori_loop(0, senders, one_sender, 0, unroll=4)

    def weigh(t, q):
        first[t] = inv_b[t] * q
        return q * gain_b[t]

    lax.fori_loop(0, last, weigh, one, unroll=6)
    outgoing[2].start()

    low_sep, up_sep = of_step(lower, last), of_step(upper, last)
    segment = lax.broadcasted_iota(jnp.int32, one.shape, 1)
    is_end = segment == segments - 1
    above = jnp.where(is_end, 0.0, jnp.roll(sum_first, -1, axis=1))
    couple_high = up_sep * jnp.where(is_end, 1.0, jnp.roll(high_gain, -1, axis=1))
    killing = 1.0 + low_sep * sum_last + up_sep * above
    ends[2, :, :segments, :] = low_sep
    ends[3, :, :segments, :] = up_sep
    tail = slice(height - rest, height)
    low_rest, up_rest = lower[:, tail, :], upper[:, tail, :]
    for n, (value, other) in enumerate(
        (
            (low_sep * low_gain, low_rest),
            (couple_high, up_rest),
            (killing, jnp.ones_like(low_rest)),
        )
    ):
        for x in range(planes):
            rows[n, x * knots : x * knots + segments, :] = value[x]
            rows[n, x * knots + segments : (x + 1) * knots, :] = other[x]
    for x in range(planes):
        rows[3, x * knots : x * knots + segments, :] = high_gain[x]
        rows[4, x * knots : x * knots + segments, :] = sum_first[x]

    def row(n, s):
        return rows[n, pl.ds(s, planes, stride=knots), :]

    top = knots - 1
    one_row = jnp.ones((planes, across), jnp.float32)
    d, d_b = one_row, one_row
    inv_s, gain_s, ratio_s = [], [], []
    inv_sb, gain_sb = [None] * top, [None] * top
    for s in range(top):
        e = row(2, s) + row(0, s) * d
        inverse = reciprocal(row(1, s) + e)
        inv_s.append(inverse)
        gain_s.append(row(0, s) * inverse)
        ratio_s.append(row(1, s) * inverse)
        d = e * inverse
        back = top - 1 - s
        e_b = row(2, back) + row(1, back) * d_b
        inverse_b = reciprocal(row(0, back) + e_b)
        inv_sb[back] = inverse_b
        gain_sb[back] = row(1, back) * inverse_b
        d_b = e_b * inverse_b
        inner[0, s] = inv_s[s]
        inner[1, s] = gain_s[s]
        inner[2, s] = ratio_s[s]
    outgoing[3].start()
    run = row(0, top)
    low_total = one_row
    sum_top = one_row
    rows[5, pl.ds(top, planes, stride=knots), :] = one_row
    for s in reversed(range(top)):
        weight = run * inv_s[s]
        rows[5, pl.ds(s, planes, stride=knots), :] = weight
        sum_top = sum_top + weight * row(2, s)
        run = run * gain_s[s]
        low_total = low_total * gain_s[s]
    run = row(3, 0)
    high_total = one_row
    sum_bottom = row(4, 0)
    rows[6, pl.ds(top, planes, stride=knots), :] = jnp.zeros_like(one_row)
    for s in range(top):
        weight = run * inv_sb[s]
        rows[6, pl.ds(s, planes, stride=knots), :] = weight
        sum_bottom = sum_bottom + weight * row(2, s)
        run = run * gain_sb[s]
        high_total = high_total * ratio_s[s]
    coef = (
        row(0, top) * low_total,
        sum_top,
        row(1, top),
        sum_bottom,
        row(3, 0) * high_total,
    )
    for n, value in enumerate(coef):
        coefs[n * planes : (n + 1) * planes, :] = value
    for n in range(2):
        for x in range(planes):
            ends[n, x] = rows[5 + n, x * knots : (x + 1) * knots, :]
    start_all(outgoing[4:6])
    wait_all(outgoing)


def deposit_kernel(got, cell_rows, *refs):
    (deposit_hbm, swept, prefix, reduced, sums) = refs[7:12]
    (counts, rhs, inv, first, ends, coefs, lower) = refs[12:19]
    (stream, ready, field, total, lefts, rights, columns, edges, in_sems, sems) = refs[19:]
    incoming = copies_of(refs[:7], refs[12:19], in_sems)
    start_all(incoming)
    components, planes, height, across = rhs.shape
    steps = inv.shape[0] + 1
    last = steps - 1
    knots = ends.shape[2]
    rest = knots - segments
    slot = components + 1
    senders = counts.shape[1]
    block = got.shape[0] // senders
    chunks = block // (planes * slot)
    parts = height // lanes
    shift = across.bit_length() - 1
    lines = components * planes
    kind = jnp.bfloat16 if max(height, across) <= 256 else jnp.float32

    me = lax.axis_index("span")
    below = lax.rem(me + senders - 1, senders)
    above = lax.rem(me + 1, senders)
    total[...] = jnp.zeros_like(total)
    for p in range(parts):
        for n, owner in enumerate((above, below)):
            start = owner * block + p * slot + components
            columns[p, pl.ds(n, lines, stride=2), :] = got[pl.ds(start, lines, stride=parts * slot), :]
        edges[p * lanes : (p + 1) * lanes, :] = diffusion_number * columns[p].T

    tile = 16
    base = lax.broadcasted_iota(jnp.int32, (tile, lanes), 0)
    height_ids = [(base + n * tile).astype(jnp.float32).astype(kind) for n in range(height // tile)]
    across_ids = height_ids[: across // tile]
    lane = lane_iota((1, lanes))
    one = jnp.ones((tile, lanes), jnp.bfloat16)
    none = jnp.zeros((tile, lanes), jnp.bfloat16)

    def spread(row, to):
        return jnp.broadcast_to(row, (tile, lanes)).astype(to)

    pair = 2 * slot
    pair_row = lax.broadcasted_iota(jnp.int32, (pair, lanes), 0)
    pair_lane = lane_iota((pair, lanes))
    is_cell = (pair_row & (slot - 1)) == components
    is_upper = pair_row >= slot

    def one_sender(s, ends_of):
        found, values = [], []
        for x in range(planes):
            start = ends_of[x]
            turn = start & (lanes - 1)
            goal = lax.div(start, lanes) * slot
            base = s * block + x * chunks * slot
            before = stream[x, pl.ds(goal, slot), :]
            turned = [jnp.concatenate([before, before], 0)]
            for k in range(0, chunks, 2):
                rows = pl.ds(pl.multiple_of(base + k * slot, pair), pair)
                value = jnp.where(is_cell, cell_rows[rows, :], got[rows, :])
                turned.append(pltpu.roll(value, turn, 1))
            values.append((goal, pair_lane >= turn, turned))
            found.append(start + counts[x, s])
        for x, (goal, here, turned) in enumerate(values):
            for k in range(len(turned) - 1):
                before, value = turned[k], turned[k + 1]
                swapped = pltpu.roll(jnp.where(is_upper, before, value), slot, 0)
                place = pl.ds(goal + k * pair, pair)
                stream[x, place, :] = jnp.where(here, value, swapped)
            stream[x, pl.ds(goal + chunks * slot, slot), :] = turned[-1][slot:, :]
        return tuple(found)

    incoming[0].wait()
    lengths = lax.fori_loop(0, senders, one_sender, (0,) * planes)
    bounds = []
    count = 0
    for x in range(planes):
        count = count + lax.div(lengths[x] + group * lanes - 1, group * lanes)
        bounds.append(count)

    def locate(n):
        x, start, length = 0, 0, lengths[0]
        for later in range(1, planes):
            reached = n >= bounds[later - 1]
            x = jnp.where(reached, later, x)
            start = jnp.where(reached, bounds[later - 1], start)
            length = jnp.where(reached, lengths[later], length)
        return x, n - start, length

    position = lax.broadcasted_iota(jnp.int32, (group, lanes), 0) * lanes
    position = position + lane_iota((group, lanes))

    def fetch(n, half):
        x, local_step, length = locate(n)
        tiles = stream.at[x]
        first_row = local_step * (group * slot)

        def rows(c):
            return tiles[pl.ds(first_row + c, group, stride=slot), :]

        live = position < length - local_step * (group * lanes)
        cell = rows(components).astype(jnp.int32)
        up = jnp.where(live, cell >> shift, -1).astype(jnp.float32)
        side = jnp.where(live, cell & (across - 1), -1).astype(jnp.float32)
        forces = [rows(c) for c in range(components)]
        highs = [force.astype(jnp.bfloat16).astype(jnp.float32) for force in forces]
        lows = [force - high for force, high in zip(forces, highs)]
        for k, value in enumerate((up, side, *highs, *lows)):
            ready[half][k] = value

    def build(half):
        for g in range(group):
            there = slice(g * lanes, (g + 1) * lanes)
            up, side, *values = [ready[half][k, g : g + 1, :] for k in range(2 + 2 * components)]
            up, side = spread(up, kind), spread(side, kind)
            for i, ids in enumerate(height_ids):
                lefts[half][i * tile : (i + 1) * tile, there] = jnp.where(up == ids, one, none)
            masks = [side == ids for ids in across_ids]
            for n, value in enumerate(values):
                value = spread(value, jnp.bfloat16)
                for i, mask in enumerate(masks):
                    place = slice(n * across + i * tile, n * across + (i + 1) * tile)
                    rights[half][place, there] = jnp.where(mask, value, none)

    def add(n, half):
        total[locate(n)[0]] += lax.dot_general(
            rights[half][...],
            lefts[half][...],
            (((1,), (1,)), ((), ())),
            preferred_element_type=jnp.float32,
        )

    def two_steps(n, carry):
        fetch(2 * n + 2, 0)
        build(1)
        add(2 * n, 0)
        fetch(2 * n + 3, 1)
        build(0)
        add(2 * n + 1, 1)
        return carry

    fetch(0, 0)
    fetch(1, 1)
    build(0)
    lax.fori_loop(0, lax.div(count + 1, 2), two_steps, 0)
    wait_all(incoming[1:])

    wide = lane_iota((lanes, across))
    border = (wide == 0) | (wide == across - 1)

    def place(x):
        return [
            pltpu.make_async_copy(field.at[c, x], deposit_hbm.at[c, x], sems.at[c, x])
            for c in range(components)
        ]

    def combine(x, carry):
        for c in range(components):
            for p in range(parts):
                part = slice(p * lanes, (p + 1) * lanes)
                high = total[x, c * across : (c + 1) * across, part]
                low = total[x, (components + c) * across : (components + c + 1) * across, part]
                value = (high + low).T
                field[c, x, part, :] = value.astype(jnp.bfloat16)
                edge = pltpu.roll(edges[part, :], lanes - 1 - 2 * (c * planes + x), 1)
                rhs[c, x, part, :] = rhs[c, x, part, :] + value + jnp.where(border, edge, 0.0)
        start_all(place(x))
        return carry

    lax.fori_loop(0, planes, combine, 0)
    sums[2 * lines : 2 * lines + coefs.shape[0], :] = coefs[...]

    zero = jnp.zeros((components, planes, segments, across), jnp.float32)

    def of_step(t):
        return rhs[:, :, pl.ds(t, segments, stride=steps), :]

    def forward(t, carry):
        value, start, run, before = carry
        force = of_step(t)
        low, inverse = lower[:, pl.ds(t, segments, stride=steps), :], inv[t]
        value = force + (low * before)[None] * value
        swept[t] = inverse[None] * value
        run = run * (low * inverse)
        prefix[t] = run
        return value, start + first[t][None] * force, run, inverse

    one = jnp.ones((planes, segments, across), jnp.float32)
    value, start, _, inverse = lax.fori_loop(0, last, forward, (zero, zero, one, one), unroll=3)
    value = inverse[None] * value
    segment = lax.broadcasted_iota(jnp.int32, zero.shape, 2)
    after = jnp.where(segment == segments - 1, 0.0, jnp.roll(start, -1, axis=2))
    low_sep, up_sep = ends[2, :, :segments, :], ends[3, :, :segments, :]
    value = of_step(last) + low_sep[None] * value + up_sep[None] * after
    others = rhs[:, :, height - rest :, :]
    at_top = ends[0, :, :segments, :][None] * value + ends[0, :, segments:, :][None] * others
    at_bottom = ends[1, :, :segments, :][None] * value + ends[1, :, segments:, :][None] * others
    at_bottom = at_bottom + jnp.where(segment == 0, start, 0.0)
    for c in range(components):
        for x in range(planes):
            k = c * planes + x
            reduced[k * knots : k * knots + segments, :] = value[c, x]
            reduced[k * knots + segments : (k + 1) * knots, :] = others[c, x]
            sums[k : k + 1, :] = jnp.sum(at_top[c, x], 0, keepdims=True)
            sums[lines + k : lines + k + 1, :] = jnp.sum(at_bottom[c, x], 0, keepdims=True)

    for x in range(planes):
        wait_all(place(x))


def finish_kernel(inner, reduced, swept, inv, prefix, upper, *refs):
    walls = len(refs) - 7
    received = refs[:walls]
    out_hbm, sums, tops, after, before, out, sems = refs[walls:]
    components, planes, height, across = out.shape
    steps = swept.shape[0] + 1
    last = steps - 1
    lines = components * planes
    knots = inner.shape[1] + 1
    rest = knots - segments
    me = lax.axis_index("wall")
    for n in range(walls):
        sums[lax.rem(me + walls - n, walls)] = received[n][...]

    def coef(k, n):
        start = 2 * lines + n * planes
        return sums[k, start : start + planes, :]

    def wide(value):
        return jnp.concatenate([value] * components, 0)

    d = jnp.ones((planes, across), jnp.float32)
    value = jnp.zeros((lines, across), jnp.float32)
    values, ratios = [], []
    for k in range(walls):
        low, own, up = coef(k, 0), coef(k, 1), coef(k, 2)
        right = sums[k, :lines, :]
        if k + 1 < walls:
            high = up * coef(k + 1, 4)
            killing = own + up * coef(k + 1, 3)
            right = right + wide(up) * sums[k + 1, lines : 2 * lines, :]
        else:
            high = jnp.zeros_like(up)
            killing = own + up
        e = killing + low * d
        inverse = reciprocal(high + e)
        d = e * inverse
        value = (right + wide(low) * value) * wide(inverse)
        values.append(value)
        ratios.append(wide(high * inverse))
    tops[0] = jnp.zeros((lines, across), jnp.float32)
    tops[walls] = values[-1]
    for k in reversed(range(walls - 1)):
        values[k] = values[k] + ratios[k] * values[k + 1]
        tops[k + 1] = values[k]

    def row(s):
        return pl.ds(s, lines, stride=knots)

    run = tops[me]
    before[row(0), :] = run
    found = []
    for s in range(knots - 1):
        run = reduced[row(s), :] * wide(inner[0, s]) + wide(inner[1, s]) * run
        found.append(run)
    run = tops[me + 1]
    after[row(knots - 1), :] = run
    for s in reversed(range(knots - 1)):
        run = found[s] + wide(inner[2, s]) * run
        after[row(s), :] = run
        if s + 1 < segments:
            before[row(s + 1), :] = run

    def put(c, x, t, value):
        out[c, x, pl.ds(t, segments, stride=steps), :] = value

    copies = []
    half = planes // 2 if planes % 2 == 0 else planes
    for start in range(0, planes, half):
        part = [(c, x) for c in range(components) for x in range(start, start + half)]
        bottoms, starts = [], []
        for c, x in part:
            base = (c * planes + x) * knots
            bottoms.append(before[base : base + segments, :])
            starts.append(after[base : base + segments, :])
            out[c, x, height - rest :, :] = after[base + segments : base + knots, :]
            put(c, x, last, starts[-1])

        def backward(n, values):
            t = last - 1 - n
            found = []
            ratios = {}
            for x in range(start, start + half):
                ratios[x] = upper[x, pl.ds(t, segments, stride=steps), :] * inv[t, x]
            for (c, x), value, bottom in zip(part, values, bottoms):
                value = (swept[t, c, x] + prefix[t, x] * bottom) + ratios[x] * value
                put(c, x, t, value)
                found.append(value)
            return tuple(found)

        lax.fori_loop(0, last, backward, tuple(starts), unroll=3)
        for here in part:
            copy = pltpu.make_async_copy(out.at[here], out_hbm.at[here], sems.at[here])
            copy.start()
            copies.append(copy)
    wait_all(copies)


def everyone(block, axis):
    length = lax.axis_size(axis)
    found = [block]
    for distance in range(1, length):
        route = [(i, (i + distance) % length) for i in range(length)]
        found.append(lax.ppermute(block, axis, route))
    return found


def local(velocity, lower_weight, upper_weight, forces, cells, counts):
    components, planes, height, across = velocity.shape
    receivers, capacity = forces.shape[3], forces.shape[5]
    senders = cells.shape[2]
    walls = lax.axis_size("wall")
    lines = components * planes
    chunks = capacity // lanes
    slot = components + 1
    forces = forces.reshape(components, receivers, planes, capacity)
    cells = cells.reshape(senders, planes, capacity)
    counts = counts.reshape(senders, planes).T

    def hbm(*arrays):
        return [pltpu.with_memory_space_constraint(array, pltpu.HBM) for array in arrays]

    send, velocity_near = call(
        pack_kernel,
        (f32(receivers, planes * chunks * slot, lanes), f32(*velocity.shape)),
        (in_hbm, in_vmem),
        [in_hbm] * 2,
        [
            scratch(*forces.shape),
            scratch(receivers, planes * chunks * slot, lanes),
            scratch(height, across),
            scratch(height // lanes, lanes, lanes),
            pltpu.SemaphoreType.DMA((components + lines + receivers,)),
        ],
        8,
        1 << 22,
    )(*hbm(velocity, forces))
    got = lax.all_to_all(send, "span", 0, 0, tiled=True)

    steps = height // segments - 1
    knots = height - segments * steps + segments
    step_shape = (steps - 1, planes, segments, across)
    staged = [
        velocity.shape,
        step_shape,
        step_shape,
        (3, knots - 1, planes, across),
        (4, planes, knots, across),
        (5 * planes, across),
    ]
    cell_shape = (senders * planes * chunks * slot, lanes)
    prepared = call(
        prepare_kernel,
        [f32(*cell_shape)] + [pltpu.HBM(shape, jnp.float32) for shape in staged],
        [in_vmem] + [in_hbm] * 6,
        [in_hbm] * 3 + [in_vmem],
        [
            *[scratch(*shape) for shape in staged],
            *[scratch(*lower_weight.shape)] * 2,
            pltpu.VMEM(cells.shape, jnp.int32),
            scratch(*step_shape),
            scratch(*step_shape),
            scratch(7, planes * knots, across),
            pltpu.SemaphoreType.DMA((9,)),
        ],
        12,
        1 << 24,
    )(*hbm(cells, lower_weight, upper_weight), velocity_near)
    (cell_rows, rhs_start, inv, first, inner, ends, coefs) = prepared

    sum_rows = -(-(2 * lines + 5 * planes) // 8) * 8
    wide = 2 * components * across
    deposit, swept, prefix, reduced, sums = call(
        deposit_kernel,
        (
            jax.ShapeDtypeStruct(velocity.shape, jnp.bfloat16),
            f32(steps - 1, components, planes, segments, across),
            f32(*step_shape),
            f32(lines * knots, across),
            f32(sum_rows, across),
        ),
        (in_hbm, *[in_vmem] * 4),
        [in_vmem] * 2 + [in_hbm] * 7,
        [
            pltpu.SMEM(counts.shape, jnp.int32),
            *[scratch(*staged[n]) for n in (0, 1, 2, 4, 5)],
            scratch(*lower_weight.shape),
            scratch(planes, (senders * chunks + 4 * group) * slot, lanes),
            [scratch(2 + 2 * components, group, lanes)] * 2,
            pltpu.VMEM(velocity.shape, jnp.bfloat16),
            scratch(planes, wide, height),
            [pltpu.VMEM((height, group * lanes), jnp.bfloat16)] * 2,
            [pltpu.VMEM((wide, group * lanes), jnp.bfloat16)] * 2,
            scratch(height // lanes, lanes, lanes),
            scratch(height, lanes),
            pltpu.SemaphoreType.DMA((7,)),
            pltpu.SemaphoreType.DMA((components, planes)),
        ],
        24,
        1 << 32,
    )(
        got.reshape(-1, lanes),
        cell_rows,
        *hbm(counts, rhs_start, inv, first, ends, coefs, lower_weight),
    )
    all_sums = everyone(sums, "wall")

    velocity_next = call(
        finish_kernel,
        f32(*velocity.shape),
        in_hbm,
        [in_vmem] * (6 + walls),
        [
            scratch(walls, sum_rows, across),
            scratch(walls + 1, lines, across),
            scratch(lines * knots, across),
            scratch(lines * knots, across),
            scratch(*velocity.shape),
            pltpu.SemaphoreType.DMA((components, planes)),
        ],
        8,
        1 << 22,
    )(inner, reduced, swept, inv, prefix, upper_weight, *all_sums)
    return (velocity_next, deposit)


def solution(mesh):
    placed = (
        P(None, None, "wall", "span"),
        P(None, "wall", "span"),
        P(None, "wall", "span"),
        P(None, "wall", "span", None, None, None),
        P("wall", "span", None, None, None),
        P("wall", "span", None, None),
    )
    return jax.shard_map(
        local,
        mesh=mesh,
        in_specs=placed,
        out_specs=(P(None, None, "wall", "span"), P(None, None, "wall", "span")),
        check_vma=False,
    )
```

```python
import jax
import jax.numpy as jnp
from jax import lax
from jax.experimental import pallas as pl
from jax.experimental.pallas import tpu as pltpu
from jax.sharding import PartitionSpec as P

diffusion_number = 0.2
segments = 8
lanes = 128
group = 8
count_bits, plane_bit = 10, 24
in_vmem = pl.BlockSpec(memory_space=pltpu.VMEM)
in_smem = pl.BlockSpec(memory_space=pltpu.SMEM)
in_hbm = pl.BlockSpec(memory_space=pltpu.HBM)


def call(body, out_shape, out_specs, in_specs, scratch, mebibytes, flops):
    return pl.pallas_call(
        body,
        out_shape=out_shape,
        in_specs=in_specs,
        out_specs=out_specs,
        scratch_shapes=scratch,
        compiler_params=pltpu.CompilerParams(vmem_limit_bytes=mebibytes << 20),
        cost_estimate=pl.CostEstimate(flops=flops, bytes_accessed=4 << 20, transcendentals=0),
    )


def f32(*shape):
    return jax.ShapeDtypeStruct(shape, jnp.float32)


def scratch(*shape):
    return pltpu.VMEM(shape, jnp.float32)


def lane_iota(shape):
    return lax.broadcasted_iota(jnp.int32, shape, len(shape) - 1)


def reciprocal(value):
    rough = pl.reciprocal(value, approx=True)
    return rough * (2.0 - value * rough)


def start_all(copies):
    for copy in copies:
        copy.start()


def wait_all(copies):
    for copy in copies:
        copy.wait()


def copies_of(sources, targets, sems, first=0):
    return [
        pltpu.make_async_copy(source, target, sems.at[first + n])
        for n, (source, target) in enumerate(zip(sources, targets))
    ]


def edge_kernel(velocity, after, first_out, last_out, columns, turned):
    del after
    components, planes, height, across = velocity.shape
    lines = components * planes
    lane = lane_iota((height, across))
    picked = jnp.zeros((height, across), jnp.float32)
    for k in range(lines):
        rolled = pltpu.roll(velocity[k // planes, k % planes], 2 * k + 1, 1)
        picked = jnp.where((lane >> 1) == k, rolled, picked)
    columns[...] = picked
    for p in range(height // lanes):
        turned[p] = columns[p * lanes : (p + 1) * lanes, :].T
        part = slice(p * lines, (p + 1) * lines)
        first_out[part, :] = turned[p, pl.ds(1, lines, stride=2), :]
        last_out[part, :] = turned[p, pl.ds(0, lines, stride=2), :]


def prepare_kernel(counts, cells_hbm, velocity, lower, upper, cell_rows, *refs):
    (rhs, inv, first, inner, ends, coefs, work) = refs[7:14]
    (cells, inv_b, gain_b, rows, sems) = refs[14:]
    outgoing = copies_of(refs[7:14], refs[:7], sems)
    cells_copy = pltpu.make_async_copy(cells_hbm, cells, sems.at[7])
    cells_copy.start()
    components, planes, height, across = velocity.shape
    steps = inv.shape[0] + 1
    last = steps - 1
    rest = height - segments * steps
    knots = segments + rest
    senders, capacity = cells.shape[0], cells.shape[2]
    chunks = capacity // lanes
    pairs = planes * senders
    pairs_each = -(-pairs // last)

    def list_pair(i, n):
        used = jnp.minimum(i, pairs - 1)
        x = lax.div(used, senders)
        s = used - x * senders
        count = jnp.where(i < pairs, counts[x, s], 0)
        base = (x << plane_bit) + (((s * planes + x) * chunks) << count_bits)
        for k in range(chunks):
            live = jnp.maximum(count - k * lanes, 0)
            work[group + n + k] = base + (k << count_bits) + live
        n = n + lax.div(count + lanes - 1, lanes)
        for extra in range(group):
            work[group + n + extra] = 0
        return jnp.where(s == senders - 1, lax.div(n + group - 1, group) * group, n)

    def of_step(ref, t):
        return ref[:, pl.ds(t, segments, stride=steps), :]

    one = jnp.ones((planes, segments, across), jnp.float32)
    zero = jnp.zeros_like(one)
    size = 8
    lane = lane_iota((size, across))

    def stencil(n):
        part = pl.ds(pl.multiple_of(n * size, size), size)
        for c in range(components):
            values = [velocity[c, x, part, :] for x in range(planes)]
            for x in range(planes):
                v = values[x]
                around = values[(x - 1) % planes] + values[(x + 1) % planes]
                around = around + jnp.where(lane == 0, 0.0, pltpu.roll(v, 1, 1))
                around = around + jnp.where(lane == across - 1, 0.0, pltpu.roll(v, across - 1, 1))
                rhs[c, x, part, :] = (1.0 - 4.0 * diffusion_number) * v + diffusion_number * around

    def factor(t, carry):
        d, d_b, low_gain, high_gain, sum_last, sum_first, n = carry
        low, up = of_step(lower, t), of_step(upper, t)
        e = 1.0 + low * d
        inverse = reciprocal(up + e)
        g = low * inverse
        inv[t] = inverse
        back = last - 1 - t
        low_b, up_b = of_step(lower, back), of_step(upper, back)
        e_b = 1.0 + up_b * d_b
        inverse_b = reciprocal(low_b + e_b)
        g_b = up_b * inverse_b
        inv_b[back] = inverse_b
        gain_b[back] = g_b
        stencil(t)
        for extra in range(pairs_each):
            n = list_pair(t * pairs_each + extra, n)
        return (
            e * inverse,
            e_b * inverse_b,
            low_gain * g,
            high_gain * g_b,
            inverse + g * sum_last,
            inverse_b + g_b * sum_first,
            n,
        )

    carry = lax.fori_loop(0, last, factor, (one, one, one, one, zero, zero, 0))
    _, _, low_gain, high_gain, sum_last, sum_first, total = carry
    for extra in range(2 * group):
        work[group + total + extra] = (planes - 1) << plane_bit
    work[0] = lax.div(total + 2 * group - 1, 2 * group)
    for n in range(last, height // size):
        stencil(n)
    start_all([outgoing[6], outgoing[0], outgoing[1]])
    cells_copy.wait()

    def one_sender(s, carry):
        for k in range(chunks):
            start = s * planes * chunks + k
            value = cells[s, :, k * lanes : (k + 1) * lanes]
            cell_rows[pl.ds(start, planes, stride=chunks), :] = value
        return carry

    lax.fori_loop(0, senders, one_sender, 0, unroll=4)

    def weigh(t, q):
        first[t] = inv_b[t] * q
        return q * gain_b[t]

    lax.fori_loop(0, last, weigh, one, unroll=6)
    outgoing[2].start()

    low_sep, up_sep = of_step(lower, last), of_step(upper, last)
    segment = lax.broadcasted_iota(jnp.int32, one.shape, 1)
    is_end = segment == segments - 1
    above = jnp.where(is_end, 0.0, jnp.roll(sum_first, -1, axis=1))
    couple_high = up_sep * jnp.where(is_end, 1.0, jnp.roll(high_gain, -1, axis=1))
    killing = 1.0 + low_sep * sum_last + up_sep * above
    ends[2, :, :segments, :] = low_sep
    ends[3, :, :segments, :] = up_sep
    tail = slice(height - rest, height)
    low_rest, up_rest = lower[:, tail, :], upper[:, tail, :]
    for n, (value, other) in enumerate(
        (
            (low_sep * low_gain, low_rest),
            (couple_high, up_rest),
            (killing, jnp.ones_like(low_rest)),
        )
    ):
        for x in range(planes):
            rows[n, x * knots : x * knots + segments, :] = value[x]
            rows[n, x * knots + segments : (x + 1) * knots, :] = other[x]
    for x in range(planes):
        rows[3, x * knots : x * knots + segments, :] = high_gain[x]
        rows[4, x * knots : x * knots + segments, :] = sum_first[x]

    def row(n, s):
        return rows[n, pl.ds(s, planes, stride=knots), :]

    top = knots - 1
    one_row = jnp.ones((planes, across), jnp.float32)
    d, d_b = one_row, one_row
    inv_s, gain_s, ratio_s = [], [], []
    inv_sb, gain_sb = [None] * top, [None] * top
    for s in range(top):
        e = row(2, s) + row(0, s) * d
        inverse = reciprocal(row(1, s) + e)
        inv_s.append(inverse)
        gain_s.append(row(0, s) * inverse)
        ratio_s.append(row(1, s) * inverse)
        d = e * inverse
        back = top - 1 - s
        e_b = row(2, back) + row(1, back) * d_b
        inverse_b = reciprocal(row(0, back) + e_b)
        inv_sb[back] = inverse_b
        gain_sb[back] = row(1, back) * inverse_b
        d_b = e_b * inverse_b
        inner[0, s] = inv_s[s]
        inner[1, s] = gain_s[s]
        inner[2, s] = ratio_s[s]
    outgoing[3].start()
    run = row(0, top)
    low_total = one_row
    sum_top = one_row
    rows[5, pl.ds(top, planes, stride=knots), :] = one_row
    for s in reversed(range(top)):
        weight = run * inv_s[s]
        rows[5, pl.ds(s, planes, stride=knots), :] = weight
        sum_top = sum_top + weight * row(2, s)
        run = run * gain_s[s]
        low_total = low_total * gain_s[s]
    run = row(3, 0)
    high_total = one_row
    sum_bottom = row(4, 0)
    rows[6, pl.ds(top, planes, stride=knots), :] = jnp.zeros_like(one_row)
    for s in range(top):
        weight = run * inv_sb[s]
        rows[6, pl.ds(s, planes, stride=knots), :] = weight
        sum_bottom = sum_bottom + weight * row(2, s)
        run = run * gain_sb[s]
        high_total = high_total * ratio_s[s]
    coef = (
        row(0, top) * low_total,
        sum_top,
        row(1, top),
        sum_bottom,
        row(3, 0) * high_total,
    )
    for n, value in enumerate(coef):
        coefs[n * planes : (n + 1) * planes, :] = value
    for n in range(2):
        for x in range(planes):
            ends[n, x] = rows[5 + n, x * knots : (x + 1) * knots, :]
    start_all(outgoing[4:6])
    wait_all(outgoing)


def deposit_kernel(got, from_above, from_below, cell_rows, *refs):
    (deposit_hbm, swept, prefix, reduced, sums) = refs[7:12]
    (work, rhs, inv, first, ends, coefs, lower) = refs[12:19]
    (slots, field, total, lefts, rights, columns, edges, in_sems, sems) = refs[19:]
    incoming = copies_of(refs[:7], refs[12:19], in_sems)
    start_all(incoming)
    components, planes, height, across = rhs.shape
    steps = inv.shape[0] + 1
    last = steps - 1
    knots = ends.shape[2]
    rest = knots - segments
    senders, _, _, capacity = got.shape
    chunks = capacity // lanes
    parts = height // lanes
    shift = across.bit_length() - 1
    lines = components * planes
    kind = jnp.bfloat16 if max(height, across) <= 256 else jnp.float32

    def one_sender(s, carry):
        for c in range(components):
            for k in range(chunks):
                start = (s * planes * chunks + k) * components + c
                value = got[s, c, :, k * lanes : (k + 1) * lanes]
                slots[pl.ds(start, planes, stride=chunks * components), :] = value
        return carry

    lax.fori_loop(0, senders, one_sender, 0)
    total[...] = jnp.zeros_like(total)
    for p in range(parts):
        part = slice(p * lines, (p + 1) * lines)
        columns[p, pl.ds(0, lines, stride=2), :] = from_above[part, :]
        columns[p, pl.ds(1, lines, stride=2), :] = from_below[part, :]
        edges[p * lanes : (p + 1) * lanes, :] = diffusion_number * columns[p].T

    tile = 16
    base = lax.broadcasted_iota(jnp.int32, (tile, lanes), 0)
    height_ids = [(base + n * tile).astype(jnp.float32).astype(kind) for n in range(height // tile)]
    across_ids = height_ids[: across // tile]
    lane = lane_iota((1, lanes))
    one = jnp.ones((tile, lanes), jnp.bfloat16)
    none = jnp.zeros((tile, lanes), jnp.bfloat16)

    def spread(row, to):
        return jnp.broadcast_to(row, (tile, lanes)).astype(to)

    def build(n, half):
        for g in range(group):
            word = work[(n + 1) * group + g]
            ident = (word >> count_bits) & ((1 << (plane_bit - count_bits)) - 1)
            live = word & ((1 << count_bits) - 1)
            there = slice(g * lanes, (g + 1) * lanes)
            cell = cell_rows[pl.ds(ident, 1), :]
            up = jnp.where(lane < live, cell >> shift, -1).astype(jnp.float32)
            side = (cell & (across - 1)).astype(jnp.float32)
            up, side = spread(up, kind), spread(side, kind)
            for i, ids in enumerate(height_ids):
                lefts[half][i * tile : (i + 1) * tile, there] = jnp.where(up == ids, one, none)
            masks = [side == ids for ids in across_ids]
            for c in range(components):
                force = slots[pl.ds(ident * components + c, 1), :]
                rest_of = force - force.astype(jnp.bfloat16).astype(jnp.float32)
                for m, value in enumerate((force, rest_of)):
                    value = spread(value, jnp.bfloat16)
                    start = (m * components + c) * across
                    for i, mask in enumerate(masks):
                        place = slice(start + i * tile, start + (i + 1) * tile)
                        rights[half][place, there] = jnp.where(mask, value, none)

    def add(n, half):
        total[work[(n + 1) * group] >> plane_bit] += lax.dot_general(
            rights[half][...],
            lefts[half][...],
            (((1,), (1,)), ((), ())),
            preferred_element_type=jnp.float32,
        )

    def two_steps(n, carry):
        build(2 * n + 1, 1)
        add(2 * n, 0)
        build(2 * n + 2, 0)
        add(2 * n + 1, 1)
        return carry

    incoming[0].wait()
    build(0, 0)
    lax.fori_loop(0, work[0], two_steps, 0)
    wait_all(incoming[1:])

    wide = lane_iota((lanes, across))
    border = (wide == 0) | (wide == across - 1)

    def place(x):
        return [
            pltpu.make_async_copy(field.at[c, x], deposit_hbm.at[c, x], sems.at[c, x])
            for c in range(components)
        ]

    def combine(x, carry):
        for c in range(components):
            for p in range(parts):
                part = slice(p * lanes, (p + 1) * lanes)
                high = total[x, c * across : (c + 1) * across, part]
                low = total[x, (components + c) * across : (components + c + 1) * across, part]
                value = (high + low).T
                field[c, x, part, :] = value.astype(jnp.bfloat16)
                edge = pltpu.roll(edges[part, :], lanes - 1 - 2 * (c * planes + x), 1)
                rhs[c, x, part, :] = rhs[c, x, part, :] + value + jnp.where(border, edge, 0.0)
        start_all(place(x))
        return carry

    lax.fori_loop(0, planes, combine, 0)
    sums[2 * lines : 2 * lines + coefs.shape[0], :] = coefs[...]

    zero = jnp.zeros((components, planes, segments, across), jnp.float32)

    def of_step(t):
        return rhs[:, :, pl.ds(t, segments, stride=steps), :]

    def forward(t, carry):
        value, start, run, before = carry
        force = of_step(t)
        low, inverse = lower[:, pl.ds(t, segments, stride=steps), :], inv[t]
        value = force + (low * before)[None] * value
        swept[t] = inverse[None] * value
        run = run * (low * inverse)
        prefix[t] = run
        return value, start + first[t][None] * force, run, inverse

    one = jnp.ones((planes, segments, across), jnp.float32)
    value, start, _, inverse = lax.fori_loop(0, last, forward, (zero, zero, one, one), unroll=3)
    value = inverse[None] * value
    segment = lax.broadcasted_iota(jnp.int32, zero.shape, 2)
    after = jnp.where(segment == segments - 1, 0.0, jnp.roll(start, -1, axis=2))
    low_sep, up_sep = ends[2, :, :segments, :], ends[3, :, :segments, :]
    value = of_step(last) + low_sep[None] * value + up_sep[None] * after
    others = rhs[:, :, height - rest :, :]
    at_top = ends[0, :, :segments, :][None] * value + ends[0, :, segments:, :][None] * others
    at_bottom = ends[1, :, :segments, :][None] * value + ends[1, :, segments:, :][None] * others
    at_bottom = at_bottom + jnp.where(segment == 0, start, 0.0)
    for c in range(components):
        for x in range(planes):
            k = c * planes + x
            reduced[k * knots : k * knots + segments, :] = value[c, x]
            reduced[k * knots + segments : (k + 1) * knots, :] = others[c, x]
            sums[k : k + 1, :] = jnp.sum(at_top[c, x], 0, keepdims=True)
            sums[lines + k : lines + k + 1, :] = jnp.sum(at_bottom[c, x], 0, keepdims=True)

    for x in range(planes):
        wait_all(place(x))


def finish_kernel(inner, reduced, swept, inv, prefix, upper, *refs):
    walls = len(refs) - 7
    received = refs[:walls]
    out_hbm, sums, tops, after, before, out, sems = refs[walls:]
    components, planes, height, across = out.shape
    steps = swept.shape[0] + 1
    last = steps - 1
    lines = components * planes
    knots = inner.shape[1] + 1
    rest = knots - segments
    me = lax.axis_index("wall")
    for n in range(walls):
        sums[lax.rem(me + walls - n, walls)] = received[n][...]

    def coef(k, n):
        start = 2 * lines + n * planes
        return sums[k, start : start + planes, :]

    def wide(value):
        return jnp.concatenate([value] * components, 0)

    d = jnp.ones((planes, across), jnp.float32)
    value = jnp.zeros((lines, across), jnp.float32)
    values, ratios = [], []
    for k in range(walls):
        low, own, up = coef(k, 0), coef(k, 1), coef(k, 2)
        right = sums[k, :lines, :]
        if k + 1 < walls:
            high = up * coef(k + 1, 4)
            killing = own + up * coef(k + 1, 3)
            right = right + wide(up) * sums[k + 1, lines : 2 * lines, :]
        else:
            high = jnp.zeros_like(up)
            killing = own + up
        e = killing + low * d
        inverse = reciprocal(high + e)
        d = e * inverse
        value = (right + wide(low) * value) * wide(inverse)
        values.append(value)
        ratios.append(wide(high * inverse))
    tops[0] = jnp.zeros((lines, across), jnp.float32)
    tops[walls] = values[-1]
    for k in reversed(range(walls - 1)):
        values[k] = values[k] + ratios[k] * values[k + 1]
        tops[k + 1] = values[k]

    def row(s):
        return pl.ds(s, lines, stride=knots)

    run = tops[me]
    before[row(0), :] = run
    found = []
    for s in range(knots - 1):
        run = reduced[row(s), :] * wide(inner[0, s]) + wide(inner[1, s]) * run
        found.append(run)
    run = tops[me + 1]
    after[row(knots - 1), :] = run
    for s in reversed(range(knots - 1)):
        run = found[s] + wide(inner[2, s]) * run
        after[row(s), :] = run
        if s + 1 < segments:
            before[row(s + 1), :] = run

    def put(c, x, t, value):
        out[c, x, pl.ds(t, segments, stride=steps), :] = value

    copies = []
    half = planes // 2 if planes % 2 == 0 else planes
    for start in range(0, planes, half):
        part = [(c, x) for c in range(components) for x in range(start, start + half)]
        bottoms, starts = [], []
        for c, x in part:
            base = (c * planes + x) * knots
            bottoms.append(before[base : base + segments, :])
            starts.append(after[base : base + segments, :])
            out[c, x, height - rest :, :] = after[base + segments : base + knots, :]
            put(c, x, last, starts[-1])

        def backward(n, values):
            t = last - 1 - n
            found = []
            ratios = {}
            for x in range(start, start + half):
                ratios[x] = upper[x, pl.ds(t, segments, stride=steps), :] * inv[t, x]
            for (c, x), value, bottom in zip(part, values, bottoms):
                value = (swept[t, c, x] + prefix[t, x] * bottom) + ratios[x] * value
                put(c, x, t, value)
                found.append(value)
            return tuple(found)

        lax.fori_loop(0, last, backward, tuple(starts), unroll=3)
        for here in part:
            copy = pltpu.make_async_copy(out.at[here], out_hbm.at[here], sems.at[here])
            copy.start()
            copies.append(copy)
    wait_all(copies)


def shifted(block, axis, distance):
    length = lax.axis_size(axis)
    route = [(i, (i + distance) % length) for i in range(length)]
    return lax.ppermute(block, axis, route)


def everyone(block, axis):
    return [block] + [shifted(block, axis, n) for n in range(1, lax.axis_size(axis))]


def local(velocity, lower_weight, upper_weight, forces, cells, counts):
    components, planes, height, across = velocity.shape
    receivers, capacity = forces.shape[3], forces.shape[5]
    senders = cells.shape[2]
    walls = lax.axis_size("wall")
    lines = components * planes
    chunks = capacity // lanes
    forces = forces.reshape(components, receivers, planes, capacity)
    cells = cells.reshape(senders, planes, capacity)
    counts = counts.reshape(senders, planes).T

    def hbm(*arrays):
        return [pltpu.with_memory_space_constraint(array, pltpu.HBM) for array in arrays]

    send = jnp.transpose(forces, (1, 0, 2, 3))
    got = lax.all_to_all(send, "span", 0, 0, tiled=True)
    edge_shape = (lines * height // lanes, lanes)
    first_column, last_column = call(
        edge_kernel,
        (f32(*edge_shape), f32(*edge_shape)),
        (in_vmem, in_vmem),
        [in_vmem, in_hbm],
        [scratch(height, across), scratch(height // lanes, lanes, lanes)],
        8,
        1 << 20,
    )(velocity, *hbm(send))
    from_above = shifted(first_column, "span", -1)
    from_below = shifted(last_column, "span", 1)

    steps = height // segments - 1
    knots = height - segments * steps + segments
    step_shape = (steps - 1, planes, segments, across)
    work_shape = (planes * (senders * chunks + group) + 4 * group,)
    staged = [
        velocity.shape,
        step_shape,
        step_shape,
        (3, knots - 1, planes, across),
        (4, planes, knots, across),
        (5 * planes, across),
    ]
    prepared = call(
        prepare_kernel,
        (
            jax.ShapeDtypeStruct((senders * planes * chunks, lanes), jnp.int32),
            *[pltpu.HBM(shape, jnp.float32) for shape in staged],
            pltpu.HBM(work_shape, jnp.int32),
        ),
        [in_vmem] + [in_hbm] * 7,
        [in_smem, in_hbm] + [in_vmem] * 3,
        [
            *[scratch(*shape) for shape in staged],
            pltpu.SMEM(work_shape, jnp.int32),
            pltpu.VMEM(cells.shape, jnp.int32),
            scratch(*step_shape),
            scratch(*step_shape),
            scratch(7, planes * knots, across),
            pltpu.SemaphoreType.DMA((8,)),
        ],
        12,
        1 << 24,
    )(counts, *hbm(cells), velocity, lower_weight, upper_weight)
    (cell_rows, rhs_start, inv, first, inner, ends, coefs, work) = prepared

    sum_rows = -(-(2 * lines + 5 * planes) // 8) * 8
    wide = 2 * components * across
    deposit, swept, prefix, reduced, sums = call(
        deposit_kernel,
        (
            jax.ShapeDtypeStruct(velocity.shape, jnp.bfloat16),
            f32(steps - 1, components, planes, segments, across),
            f32(*step_shape),
            f32(lines * knots, across),
            f32(sum_rows, across),
        ),
        (in_hbm, *[in_vmem] * 4),
        [in_vmem] * 4 + [in_hbm] * 7,
        [
            pltpu.SMEM(work_shape, jnp.int32),
            *[scratch(*staged[n]) for n in (0, 1, 2, 4, 5)],
            scratch(*lower_weight.shape),
            scratch(senders * planes * chunks * components, lanes),
            pltpu.VMEM(velocity.shape, jnp.bfloat16),
            scratch(planes, wide, height),
            [pltpu.VMEM((height, group * lanes), jnp.bfloat16)] * 2,
            [pltpu.VMEM((wide, group * lanes), jnp.bfloat16)] * 2,
            scratch(height // lanes, lanes, lanes),
            scratch(height, lanes),
            pltpu.SemaphoreType.DMA((7,)),
            pltpu.SemaphoreType.DMA((components, planes)),
        ],
        24,
        1 << 32,
    )(
        got,
        from_above,
        from_below,
        cell_rows,
        *hbm(work, rhs_start, inv, first, ends, coefs, lower_weight),
    )
    all_sums = everyone(sums, "wall")

    velocity_next = call(
        finish_kernel,
        f32(*velocity.shape),
        in_hbm,
        [in_vmem] * (6 + walls),
        [
            scratch(walls, sum_rows, across),
            scratch(walls + 1, lines, across),
            scratch(lines * knots, across),
            scratch(lines * knots, across),
            scratch(*velocity.shape),
            pltpu.SemaphoreType.DMA((components, planes)),
        ],
        8,
        1 << 22,
    )(inner, reduced, swept, inv, prefix, upper_weight, *all_sums)
    return (velocity_next, deposit)


def solution(mesh):
    placed = (
        P(None, None, "wall", "span"),
        P(None, "wall", "span"),
        P(None, "wall", "span"),
        P(None, "wall", "span", None, None, None),
        P("wall", "span", None, None, None),
        P("wall", "span", None, None),
    )
    return jax.shard_map(
        local,
        mesh=mesh,
        in_specs=placed,
        out_specs=(P(None, None, "wall", "span"), P(None, None, "wall", "span")),
        check_vma=False,
    )
```

```python
import jax
import jax.numpy as jnp
from jax import lax
from jax.experimental import pallas as pl
from jax.experimental.pallas import tpu as pltpu
from jax.sharding import PartitionSpec as P

diffusion_number = 0.2
segments = 8
lanes = 128
group = 8
count_bits, plane_bit = 10, 24
in_vmem = pl.BlockSpec(memory_space=pltpu.VMEM)
in_smem = pl.BlockSpec(memory_space=pltpu.SMEM)
in_hbm = pl.BlockSpec(memory_space=pltpu.HBM)


def call(body, out_shape, out_specs, in_specs, scratch, mebibytes, flops):
    return pl.pallas_call(
        body,
        out_shape=out_shape,
        in_specs=in_specs,
        out_specs=out_specs,
        scratch_shapes=scratch,
        compiler_params=pltpu.CompilerParams(vmem_limit_bytes=mebibytes << 20),
        cost_estimate=pl.CostEstimate(flops=flops, bytes_accessed=4 << 20, transcendentals=0),
    )


def f32(*shape):
    return jax.ShapeDtypeStruct(shape, jnp.float32)


def scratch(*shape):
    return pltpu.VMEM(shape, jnp.float32)


def lane_iota(shape):
    return lax.broadcasted_iota(jnp.int32, shape, len(shape) - 1)


def reciprocal(value):
    rough = pl.reciprocal(value, approx=True)
    return rough * (2.0 - value * rough)


def start_all(copies):
    for copy in copies:
        copy.start()


def wait_all(copies):
    for copy in copies:
        copy.wait()


def copies_of(sources, targets, sems, first=0):
    return [
        pltpu.make_async_copy(source, target, sems.at[first + n])
        for n, (source, target) in enumerate(zip(sources, targets))
    ]


def load_kernel(forces, velocity, lower, upper, cells, counts, send, *refs):
    near, sems = refs[:5], refs[5]
    components = forces.shape[0]
    sources = [forces.at[c] for c in range(components)]
    targets = [send.at[:, c] for c in range(components)]
    sources += [velocity.at[c] for c in range(components)] + [lower, upper, cells, counts]
    targets += [near[0].at[c] for c in range(components)] + list(near[1:])
    copies = copies_of(sources, targets, sems)
    start_all(copies)
    wait_all(copies)


def edge_kernel(velocity, first_out, last_out, columns, turned):
    components, planes, height, across = velocity.shape
    lines = components * planes
    lane = lane_iota((height, across))
    picked = jnp.zeros((height, across), jnp.float32)
    for k in range(lines):
        rolled = pltpu.roll(velocity[k // planes, k % planes], 2 * k + 1, 1)
        picked = jnp.where((lane >> 1) == k, rolled, picked)
    columns[...] = picked
    for p in range(height // lanes):
        turned[p] = columns[p * lanes : (p + 1) * lanes, :].T
        part = slice(p * lines, (p + 1) * lines)
        first_out[part, :] = turned[p, pl.ds(1, lines, stride=2), :]
        last_out[part, :] = turned[p, pl.ds(0, lines, stride=2), :]


def prepare_kernel(counts_in, cells, velocity, lower, upper, cell_rows, *refs):
    (rhs, inv, first, inner, ends, coefs, work) = refs[7:14]
    (counts, inv_b, gain_b, rows, sems) = refs[14:]
    outgoing = copies_of(refs[7:14], refs[:7], sems)
    counts_copy = pltpu.make_async_copy(counts_in, counts, sems.at[7])
    counts_copy.start()
    components, planes, height, across = velocity.shape
    steps = inv.shape[0] + 1
    last = steps - 1
    rest = height - segments * steps
    knots = segments + rest
    senders, capacity = cells.shape[0], cells.shape[2]
    chunks = capacity // lanes
    pairs = planes * senders
    pairs_each = -(-pairs // last)

    def one_sender(s, carry):
        for k in range(chunks):
            start = s * planes * chunks + k
            value = cells[s, :, k * lanes : (k + 1) * lanes]
            cell_rows[pl.ds(start, planes, stride=chunks), :] = value
        return carry

    lax.fori_loop(0, senders, one_sender, 0, unroll=4)

    counts_copy.wait()

    def list_pair(i, n):
        used = jnp.minimum(i, pairs - 1)
        x = lax.div(used, senders)
        s = used - x * senders
        count = jnp.where(i < pairs, counts[x, s], 0)
        base = (x << plane_bit) + (((s * planes + x) * chunks) << count_bits)
        for k in range(chunks):
            live = jnp.maximum(count - k * lanes, 0)
            work[group + n + k] = base + (k << count_bits) + live
        n = n + lax.div(count + lanes - 1, lanes)
        for extra in range(group):
            work[group + n + extra] = 0
        n = jnp.where(s == senders - 1, lax.div(n + group - 1, group) * group, n)
        work[1 + x] = lax.div(n, group)
        return n

    def of_step(ref, t):
        return ref[:, pl.ds(t, segments, stride=steps), :]

    one = jnp.ones((planes, segments, across), jnp.float32)
    zero = jnp.zeros_like(one)
    size = 8
    lane = lane_iota((size, across))

    def stencil_rows(n):
        return pl.ds(pl.multiple_of(n * size, size), size)

    def read_rows(n):
        part = stencil_rows(n)
        return [[velocity[c, x, part, :] for x in range(planes)] for c in range(components)]

    def stencil(values):
        found = []
        for x in range(planes):
            v = values[x]
            around = values[(x - 1) % planes] + values[(x + 1) % planes]
            around = around + jnp.where(lane == 0, 0.0, pltpu.roll(v, 1, 1))
            around = around + jnp.where(lane == across - 1, 0.0, pltpu.roll(v, across - 1, 1))
            found.append((1.0 - 4.0 * diffusion_number) * v + diffusion_number * around)
        return found

    def write_rows(n, values):
        part = stencil_rows(n)
        for c in range(components):
            for x in range(planes):
                rhs[c, x, part, :] = values[c][x]

    def factor(t, carry):
        d, d_b, low_gain, high_gain, sum_last, sum_first, n = carry
        back = last - 1 - t
        low, up = of_step(lower, t), of_step(upper, t)
        low_b, up_b = of_step(lower, back), of_step(upper, back)
        velocities = read_rows(t)
        e = 1.0 + low * d
        inverse = reciprocal(up + e)
        g = low * inverse
        e_b = 1.0 + up_b * d_b
        inverse_b = reciprocal(low_b + e_b)
        g_b = up_b * inverse_b
        found = [stencil(values) for values in velocities]
        for extra in range(pairs_each):
            n = list_pair(t * pairs_each + extra, n)
        inv[t] = inverse
        inv_b[back] = inverse_b
        gain_b[back] = g_b
        write_rows(t, found)
        return (
            e * inverse,
            e_b * inverse_b,
            low_gain * g,
            high_gain * g_b,
            inverse + g * sum_last,
            inverse_b + g_b * sum_first,
            n,
        )

    carry = lax.fori_loop(0, last, factor, (one, one, one, one, zero, zero, 0))
    _, _, low_gain, high_gain, sum_last, sum_first, total = carry
    for extra in range(2 * group):
        work[group + total + extra] = (planes - 1) << plane_bit
    for n in range(last, height // size):
        write_rows(n, [stencil(values) for values in read_rows(n)])
    start_all([outgoing[6], outgoing[0], outgoing[1]])
    def weigh(t, q):
        first[t] = inv_b[t] * q
        return q * gain_b[t]

    lax.fori_loop(0, last, weigh, one, unroll=6)
    outgoing[2].start()

    low_sep, up_sep = of_step(lower, last), of_step(upper, last)
    segment = lax.broadcasted_iota(jnp.int32, one.shape, 1)
    is_end = segment == segments - 1
    above = jnp.where(is_end, 0.0, jnp.roll(sum_first, -1, axis=1))
    couple_high = up_sep * jnp.where(is_end, 1.0, jnp.roll(high_gain, -1, axis=1))
    killing = 1.0 + low_sep * sum_last + up_sep * above
    ends[2, :, :segments, :] = low_sep
    ends[3, :, :segments, :] = up_sep
    tail = slice(height - rest, height)
    low_rest, up_rest = lower[:, tail, :], upper[:, tail, :]
    for n, (value, other) in enumerate(
        (
            (low_sep * low_gain, low_rest),
            (couple_high, up_rest),
            (killing, jnp.ones_like(low_rest)),
        )
    ):
        for x in range(planes):
            rows[n, x * knots : x * knots + segments, :] = value[x]
            rows[n, x * knots + segments : (x + 1) * knots, :] = other[x]
    for x in range(planes):
        rows[3, x * knots : x * knots + segments, :] = high_gain[x]
        rows[4, x * knots : x * knots + segments, :] = sum_first[x]

    def row(n, s):
        return rows[n, pl.ds(s, planes, stride=knots), :]

    top = knots - 1
    one_row = jnp.ones((planes, across), jnp.float32)
    d, d_b = one_row, one_row
    inv_s, gain_s, ratio_s = [], [], []
    inv_sb, gain_sb = [None] * top, [None] * top
    for s in range(top):
        e = row(2, s) + row(0, s) * d
        inverse = reciprocal(row(1, s) + e)
        inv_s.append(inverse)
        gain_s.append(row(0, s) * inverse)
        ratio_s.append(row(1, s) * inverse)
        d = e * inverse
        back = top - 1 - s
        e_b = row(2, back) + row(1, back) * d_b
        inverse_b = reciprocal(row(0, back) + e_b)
        inv_sb[back] = inverse_b
        gain_sb[back] = row(1, back) * inverse_b
        d_b = e_b * inverse_b
        inner[0, s] = inv_s[s]
        inner[1, s] = gain_s[s]
        inner[2, s] = ratio_s[s]
    outgoing[3].start()
    run = row(0, top)
    low_total = one_row
    sum_top = one_row
    rows[5, pl.ds(top, planes, stride=knots), :] = one_row
    for s in reversed(range(top)):
        weight = run * inv_s[s]
        rows[5, pl.ds(s, planes, stride=knots), :] = weight
        sum_top = sum_top + weight * row(2, s)
        run = run * gain_s[s]
        low_total = low_total * gain_s[s]
    run = row(3, 0)
    high_total = one_row
    sum_bottom = row(4, 0)
    rows[6, pl.ds(top, planes, stride=knots), :] = jnp.zeros_like(one_row)
    for s in range(top):
        weight = run * inv_sb[s]
        rows[6, pl.ds(s, planes, stride=knots), :] = weight
        sum_bottom = sum_bottom + weight * row(2, s)
        run = run * gain_sb[s]
        high_total = high_total * ratio_s[s]
    coef = (
        row(0, top) * low_total,
        sum_top,
        row(1, top),
        sum_bottom,
        row(3, 0) * high_total,
    )
    for n, value in enumerate(coef):
        coefs[n * planes : (n + 1) * planes, :] = value
    for n in range(2):
        for x in range(planes):
            ends[n, x] = rows[5 + n, x * knots : (x + 1) * knots, :]
    start_all(outgoing[4:6])
    wait_all(outgoing)


def deposit_kernel(got, from_above, from_below, cell_rows, *refs):
    (deposit_hbm, swept, prefix, reduced, sums) = refs[7:12]
    (work, rhs, inv, first, ends, coefs, lower) = refs[12:19]
    (slots, raw, ready, field, total, left, right, columns, edges, in_sems, sems) = refs[19:]
    incoming = copies_of(refs[:7], refs[12:19], in_sems)
    start_all(incoming)
    components, planes, height, across = rhs.shape
    steps = inv.shape[0] + 1
    last = steps - 1
    knots = ends.shape[2]
    rest = knots - segments
    senders, _, _, capacity = got.shape
    chunks = capacity // lanes
    parts = height // lanes
    shift = across.bit_length() - 1
    lines = components * planes
    kind = jnp.bfloat16 if max(height, across) <= 256 else jnp.float32

    def one_sender(s, carry):
        for c in range(components):
            for k in range(chunks):
                start = (s * planes * chunks + k) * components + c
                value = got[s, c, :, k * lanes : (k + 1) * lanes]
                slots[pl.ds(start, planes, stride=chunks * components), :] = value
        return carry

    lax.fori_loop(0, senders, one_sender, 0)
    total[...] = jnp.zeros_like(total)
    for p in range(parts):
        part = slice(p * lines, (p + 1) * lines)
        columns[p, pl.ds(0, lines, stride=2), :] = from_above[part, :]
        columns[p, pl.ds(1, lines, stride=2), :] = from_below[part, :]
        edges[p * lanes : (p + 1) * lanes, :] = diffusion_number * columns[p].T

    tile = 16
    base = lax.broadcasted_iota(jnp.int32, (tile, lanes), 0)
    height_ids = [(base + n * tile).astype(jnp.float32).astype(kind) for n in range(height // tile)]
    across_ids = height_ids[: across // tile]
    lane = lane_iota((1, lanes))
    one = jnp.ones((tile, lanes), jnp.bfloat16)
    none = jnp.zeros((tile, lanes), jnp.bfloat16)

    def spread(row, to):
        return jnp.broadcast_to(row, (tile, lanes)).astype(to)

    def fetch(n):
        for g in range(group):
            word = work[(n + 1) * group + g]
            ident = (word >> count_bits) & ((1 << (plane_bit - count_bits)) - 1)
            live = word & ((1 << count_bits) - 1)
            cell = jnp.where(lane < live, cell_rows[pl.ds(ident, 1), :], -1)
            raw[components, g : g + 1, :] = cell.astype(jnp.float32)
            for c in range(components):
                raw[c, g : g + 1, :] = slots[pl.ds(ident * components + c, 1), :]

    def convert():
        cell = raw[components].astype(jnp.int32)
        ready[0] = (cell >> shift).astype(jnp.float32)
        ready[1] = jnp.where(cell < 0, -1, cell & (across - 1)).astype(jnp.float32)
        for c in range(components):
            force = raw[c]
            high = force.astype(jnp.bfloat16).astype(jnp.float32)
            ready[2 + c] = high
            ready[2 + components + c] = force - high

    def build():
        for g in range(group):
            there = slice(g * lanes, (g + 1) * lanes)
            up, side = spread(ready[0, g : g + 1, :], kind), spread(ready[1, g : g + 1, :], kind)
            for i, ids in enumerate(height_ids):
                left[i * tile : (i + 1) * tile, there] = jnp.where(up == ids, one, none)
            masks = [side == ids for ids in across_ids]
            for n in range(2 * components):
                value = spread(ready[2 + n, g : g + 1, :], jnp.bfloat16)
                for i, mask in enumerate(masks):
                    place = slice(n * across + i * tile, n * across + (i + 1) * tile)
                    right[place, there] = jnp.where(mask, value, none)

    incoming[0].wait()
    fetch(0)
    convert()
    build()
    begin = 0
    for x in range(planes):

        def step(n, carry):
            fetch(n + 1)
            total[x] += lax.dot_general(
                right[...],
                left[...],
                (((1,), (1,)), ((), ())),
                preferred_element_type=jnp.float32,
            )
            convert()
            build()
            return carry

        end = work[1 + x]
        lax.fori_loop(begin, end, step, 0)
        begin = end
    wait_all(incoming[1:])

    wide = lane_iota((lanes, across))
    border = (wide == 0) | (wide == across - 1)

    outgoing = []
    for x in range(planes):
        for c in range(components):
            for p in range(parts):
                part = slice(p * lanes, (p + 1) * lanes)
                high = total[x, c * across : (c + 1) * across, part]
                low = total[x, (components + c) * across : (components + c + 1) * across, part]
                value = (high + low).T
                field[c, x, part, :] = value.astype(jnp.bfloat16)
                edge = pltpu.roll(edges[part, :], lanes - 1 - 2 * (c * planes + x), 1)
                rhs[c, x, part, :] = rhs[c, x, part, :] + value + jnp.where(border, edge, 0.0)
            copy = pltpu.make_async_copy(field.at[c, x], deposit_hbm.at[c, x], sems.at[c, x])
            copy.start()
            outgoing.append(copy)
    sums[2 * lines : 2 * lines + coefs.shape[0], :] = coefs[...]

    zero = jnp.zeros((components, planes, segments, across), jnp.float32)

    def of_step(t):
        return rhs[:, :, pl.ds(t, segments, stride=steps), :]

    def forward(t, carry):
        value, start, run, before = carry
        force = of_step(t)
        low, inverse = lower[:, pl.ds(t, segments, stride=steps), :], inv[t]
        value = force + (low * before)[None] * value
        swept[t] = inverse[None] * value
        run = run * (low * inverse)
        prefix[t] = run
        return value, start + first[t][None] * force, run, inverse

    one = jnp.ones((planes, segments, across), jnp.float32)
    value, start, _, inverse = lax.fori_loop(0, last, forward, (zero, zero, one, one), unroll=last)
    value = inverse[None] * value
    segment = lax.broadcasted_iota(jnp.int32, zero.shape, 2)
    after = jnp.where(segment == segments - 1, 0.0, jnp.roll(start, -1, axis=2))
    low_sep, up_sep = ends[2, :, :segments, :], ends[3, :, :segments, :]
    value = of_step(last) + low_sep[None] * value + up_sep[None] * after
    others = rhs[:, :, height - rest :, :]
    at_top = ends[0, :, :segments, :][None] * value + ends[0, :, segments:, :][None] * others
    at_bottom = ends[1, :, :segments, :][None] * value + ends[1, :, segments:, :][None] * others
    at_bottom = at_bottom + jnp.where(segment == 0, start, 0.0)
    for c in range(components):
        for x in range(planes):
            k = c * planes + x
            reduced[k * knots : k * knots + segments, :] = value[c, x]
            reduced[k * knots + segments : (k + 1) * knots, :] = others[c, x]
            sums[k : k + 1, :] = jnp.sum(at_top[c, x], 0, keepdims=True)
            sums[lines + k : lines + k + 1, :] = jnp.sum(at_bottom[c, x], 0, keepdims=True)

    wait_all(outgoing)


def finish_kernel(inner, reduced, swept, inv, prefix, upper, *refs):
    walls = len(refs) - 7
    received = refs[:walls]
    out_hbm, sums, tops, after, before, out, sems = refs[walls:]
    components, planes, height, across = out.shape
    steps = swept.shape[0] + 1
    last = steps - 1
    lines = components * planes
    knots = inner.shape[1] + 1
    rest = knots - segments
    me = lax.axis_index("wall")
    for n in range(walls):
        sums[lax.rem(me + walls - n, walls)] = received[n][...]

    def coef(k, n):
        start = 2 * lines + n * planes
        return sums[k, start : start + planes, :]

    def wide(value):
        return jnp.concatenate([value] * components, 0)

    d = jnp.ones((planes, across), jnp.float32)
    value = jnp.zeros((lines, across), jnp.float32)
    values, ratios = [], []
    for k in range(walls):
        low, own, up = coef(k, 0), coef(k, 1), coef(k, 2)
        right = sums[k, :lines, :]
        if k + 1 < walls:
            high = up * coef(k + 1, 4)
            killing = own + up * coef(k + 1, 3)
            right = right + wide(up) * sums[k + 1, lines : 2 * lines, :]
        else:
            high = jnp.zeros_like(up)
            killing = own + up
        e = killing + low * d
        inverse = reciprocal(high + e)
        d = e * inverse
        value = (right + wide(low) * value) * wide(inverse)
        values.append(value)
        ratios.append(wide(high * inverse))
    tops[0] = jnp.zeros((lines, across), jnp.float32)
    tops[walls] = values[-1]
    for k in reversed(range(walls - 1)):
        values[k] = values[k] + ratios[k] * values[k + 1]
        tops[k + 1] = values[k]

    def row(s):
        return pl.ds(s, lines, stride=knots)

    run = tops[me]
    before[row(0), :] = run
    found = []
    for s in range(knots - 1):
        run = reduced[row(s), :] * wide(inner[0, s]) + wide(inner[1, s]) * run
        found.append(run)
    run = tops[me + 1]
    after[row(knots - 1), :] = run
    for s in reversed(range(knots - 1)):
        run = found[s] + wide(inner[2, s]) * run
        after[row(s), :] = run
        if s + 1 < segments:
            before[row(s + 1), :] = run

    def put(c, x, t, value):
        out[c, x, pl.ds(t, segments, stride=steps), :] = value

    copies = []
    half = planes // 2 if planes % 2 == 0 else planes
    for start in range(0, planes, half):
        part = [(c, x) for c in range(components) for x in range(start, start + half)]
        bottoms, starts = [], []
        for c, x in part:
            base = (c * planes + x) * knots
            bottoms.append(before[base : base + segments, :])
            starts.append(after[base : base + segments, :])
            out[c, x, height - rest :, :] = after[base + segments : base + knots, :]
            put(c, x, last, starts[-1])

        def backward(n, values):
            t = last - 1 - n
            found = []
            ratios = {}
            for x in range(start, start + half):
                ratios[x] = upper[x, pl.ds(t, segments, stride=steps), :] * inv[t, x]
            for (c, x), value, bottom in zip(part, values, bottoms):
                value = (swept[t, c, x] + prefix[t, x] * bottom) + ratios[x] * value
                put(c, x, t, value)
                found.append(value)
            return tuple(found)

        lax.fori_loop(0, last, backward, tuple(starts), unroll=last)
        for here in part:
            copy = pltpu.make_async_copy(out.at[here], out_hbm.at[here], sems.at[here])
            copy.start()
            copies.append(copy)
    wait_all(copies)


def shifted(block, axis, distance):
    length = lax.axis_size(axis)
    route = [(i, (i + distance) % length) for i in range(length)]
    return lax.ppermute(block, axis, route)


def everyone(block, axis):
    return [block] + [shifted(block, axis, n) for n in range(1, lax.axis_size(axis))]


def local(velocity, lower_weight, upper_weight, forces, cells, counts):
    components, planes, height, across = velocity.shape
    receivers, capacity = forces.shape[3], forces.shape[5]
    senders = cells.shape[2]
    walls = lax.axis_size("wall")
    lines = components * planes
    chunks = capacity // lanes
    counts_shape, cells_shape = (planes, senders), (senders, planes, capacity)
    forces = forces.reshape(components, receivers, planes, capacity)
    cells = cells.reshape(senders, planes, capacity)
    counts = counts.reshape(senders, planes).T

    def hbm(*arrays):
        return [pltpu.with_memory_space_constraint(array, pltpu.HBM) for array in arrays]

    send, velocity_near, lower_near, upper_near, cells_near, counts_near = call(
        load_kernel,
        (
            pltpu.HBM((receivers, components, planes, capacity), jnp.float32),
            f32(*velocity.shape),
            f32(*lower_weight.shape),
            f32(*upper_weight.shape),
            jax.ShapeDtypeStruct(cells_shape, jnp.int32),
            jax.ShapeDtypeStruct(counts_shape, jnp.int32),
        ),
        (in_hbm, *[in_vmem] * 5),
        [in_hbm] * 6,
        [pltpu.SemaphoreType.DMA((2 * components + 4,))],
        2,
        1 << 16,
    )(*hbm(forces, velocity, lower_weight, upper_weight, cells, counts))
    got = lax.all_to_all(send, "span", 0, 0, tiled=True)
    edge_shape = (lines * height // lanes, lanes)
    first_column, last_column = call(
        edge_kernel,
        (f32(*edge_shape), f32(*edge_shape)),
        (in_vmem, in_vmem),
        [in_vmem],
        [scratch(height, across), scratch(height // lanes, lanes, lanes)],
        4,
        1 << 20,
    )(velocity_near)
    from_above = shifted(first_column, "span", -1)
    from_below = shifted(last_column, "span", 1)

    steps = height // segments - 1
    knots = height - segments * steps + segments
    step_shape = (steps - 1, planes, segments, across)
    work_shape = (planes * (senders * chunks + group) + 4 * group,)
    staged = [
        velocity.shape,
        step_shape,
        step_shape,
        (3, knots - 1, planes, across),
        (4, planes, knots, across),
        (5 * planes, across),
    ]
    prepared = call(
        prepare_kernel,
        (
            jax.ShapeDtypeStruct((senders * planes * chunks, lanes), jnp.int32),
            *[pltpu.HBM(shape, jnp.float32) for shape in staged],
            pltpu.HBM(work_shape, jnp.int32),
        ),
        [in_vmem] + [in_hbm] * 7,
        [in_vmem] * 5,
        [
            *[scratch(*shape) for shape in staged],
            pltpu.SMEM(work_shape, jnp.int32),
            pltpu.SMEM(counts_shape, jnp.int32),
            scratch(*step_shape),
            scratch(*step_shape),
            scratch(7, planes * knots, across),
            pltpu.SemaphoreType.DMA((8,)),
        ],
        12,
        1 << 24,
    )(counts_near, cells_near, velocity_near, lower_near, upper_near)
    (cell_rows, rhs_start, inv, first, inner, ends, coefs, work) = prepared

    sum_rows = -(-(2 * lines + 5 * planes) // 8) * 8
    wide = 2 * components * across
    deposit, swept, prefix, reduced, sums = call(
        deposit_kernel,
        (
            jax.ShapeDtypeStruct(velocity.shape, jnp.bfloat16),
            f32(steps - 1, components, planes, segments, across),
            f32(*step_shape),
            f32(lines * knots, across),
            f32(sum_rows, across),
        ),
        (in_hbm, *[in_vmem] * 4),
        [in_vmem] * 4 + [in_hbm] * 7,
        [
            pltpu.SMEM(work_shape, jnp.int32),
            *[scratch(*staged[n]) for n in (0, 1, 2, 4, 5)],
            scratch(*lower_weight.shape),
            scratch(senders * planes * chunks * components, lanes),
            scratch(components + 1, group, lanes),
            scratch(2 + 2 * components, group, lanes),
            pltpu.VMEM(velocity.shape, jnp.bfloat16),
            scratch(planes, wide, height),
            pltpu.VMEM((height, group * lanes), jnp.bfloat16),
            pltpu.VMEM((wide, group * lanes), jnp.bfloat16),
            scratch(height // lanes, lanes, lanes),
            scratch(height, lanes),
            pltpu.SemaphoreType.DMA((7,)),
            pltpu.SemaphoreType.DMA((components, planes)),
        ],
        24,
        1 << 32,
    )(
        got,
        from_above,
        from_below,
        cell_rows,
        *hbm(work, rhs_start, inv, first, ends, coefs, lower_weight),
    )
    all_sums = everyone(sums, "wall")

    velocity_next = call(
        finish_kernel,
        f32(*velocity.shape),
        in_hbm,
        [in_vmem] * (6 + walls),
        [
            scratch(walls, sum_rows, across),
            scratch(walls + 1, lines, across),
            scratch(lines * knots, across),
            scratch(lines * knots, across),
            scratch(*velocity.shape),
            pltpu.SemaphoreType.DMA((components, planes)),
        ],
        8,
        1 << 22,
    )(inner, reduced, swept, inv, prefix, upper_weight, *all_sums)
    return (velocity_next, deposit)


def solution(mesh):
    placed = (
        P(None, None, "wall", "span"),
        P(None, "wall", "span"),
        P(None, "wall", "span"),
        P(None, "wall", "span", None, None, None),
        P("wall", "span", None, None, None),
        P("wall", "span", None, None),
    )
    return jax.shard_map(
        local,
        mesh=mesh,
        in_specs=placed,
        out_specs=(P(None, None, "wall", "span"), P(None, None, "wall", "span")),
        check_vma=False,
    )
```

```python
import jax
import jax.numpy as jnp
from jax import lax
from jax.experimental import pallas as pl
from jax.experimental.pallas import tpu as pltpu
from jax.sharding import PartitionSpec as P

diffusion_number = 0.2
segments = 8
lanes = 128
group = 8
in_vmem = pl.BlockSpec(memory_space=pltpu.VMEM)
in_smem = pl.BlockSpec(memory_space=pltpu.SMEM)
in_hbm = pl.BlockSpec(memory_space=pltpu.HBM)


def call(body, out_shape, out_specs, in_specs, scratch, mebibytes, flops):
    return pl.pallas_call(
        body,
        out_shape=out_shape,
        in_specs=in_specs,
        out_specs=out_specs,
        scratch_shapes=scratch,
        compiler_params=pltpu.CompilerParams(vmem_limit_bytes=mebibytes << 20),
        cost_estimate=pl.CostEstimate(flops=flops, bytes_accessed=4 << 20, transcendentals=0),
    )


def f32(*shape):
    return jax.ShapeDtypeStruct(shape, jnp.float32)


def scratch(*shape):
    return pltpu.VMEM(shape, jnp.float32)


def lane_iota(shape):
    return lax.broadcasted_iota(jnp.int32, shape, len(shape) - 1)


def reciprocal(value):
    rough = pl.reciprocal(value, approx=True)
    return rough * (2.0 - value * rough)


def start_all(copies):
    for copy in copies:
        copy.start()


def wait_all(copies):
    for copy in copies:
        copy.wait()


def copies_of(sources, targets, sems, first=0):
    return [
        pltpu.make_async_copy(source, target, sems.at[first + n])
        for n, (source, target) in enumerate(zip(sources, targets))
    ]


def load_kernel(forces, velocity, lower, upper, cells, counts, send, *refs):
    near, slots, sems = refs[:5], refs[5], refs[6]
    components = forces.shape[0]
    sources = [forces.at[c] for c in range(components)]
    targets = [slots.at[c] for c in range(components)]
    sources += [velocity.at[c] for c in range(components)] + [lower, upper, cells, counts]
    targets += [near[0].at[c] for c in range(components)] + list(near[1:])
    copies = copies_of(sources, targets, sems)
    start_all(copies)
    outgoing = copies_of(
        targets[:components], [send.at[:, c] for c in range(components)], sems, len(copies)
    )
    for c in range(components):
        copies[c].wait()
        outgoing[c].start()
    wait_all(copies[components:])
    wait_all(outgoing)


def edge_kernel(velocity, first_out, last_out, columns, turned):
    components, planes, height, across = velocity.shape
    lines = components * planes
    lane = lane_iota((height, across))
    picked = jnp.zeros((height, across), jnp.float32)
    for k in range(lines):
        rolled = pltpu.roll(velocity[k // planes, k % planes], 2 * k + 1, 1)
        picked = jnp.where((lane >> 1) == k, rolled, picked)
    columns[...] = picked
    for p in range(height // lanes):
        turned[p] = columns[p * lanes : (p + 1) * lanes, :].T
        part = slice(p * lines, (p + 1) * lines)
        first_out[part, :] = turned[p, pl.ds(1, lines, stride=2), :]
        last_out[part, :] = turned[p, pl.ds(0, lines, stride=2), :]


def prepare_kernel(cells, velocity, lower, upper, cell_rows, *refs):
    (rhs, inv, first, inner, ends, coefs) = refs[6:12]
    (inv_b, gain_b, rows, sems) = refs[12:]
    outgoing = copies_of(refs[6:12], refs[:6], sems)
    components, planes, height, across = velocity.shape
    steps = inv.shape[0] + 1
    last = steps - 1
    rest = height - segments * steps
    knots = segments + rest
    senders, capacity = cells.shape[0], cells.shape[2]
    chunks = capacity // lanes

    def one_sender(s, carry):
        for k in range(chunks):
            start = s * planes * chunks + k
            value = cells[s, :, k * lanes : (k + 1) * lanes]
            cell_rows[pl.ds(start, planes, stride=chunks), :] = value
        return carry

    lax.fori_loop(0, senders, one_sender, 0, unroll=4)

    def of_step(ref, t):
        return ref[:, pl.ds(t, segments, stride=steps), :]

    one = jnp.ones((planes, segments, across), jnp.float32)
    zero = jnp.zeros_like(one)
    size = 8
    lane = lane_iota((size, across))

    def stencil_rows(n):
        return pl.ds(pl.multiple_of(n * size, size), size)

    def read_rows(n):
        part = stencil_rows(n)
        return [[velocity[c, x, part, :] for x in range(planes)] for c in range(components)]

    def stencil(values):
        found = []
        for x in range(planes):
            v = values[x]
            around = values[(x - 1) % planes] + values[(x + 1) % planes]
            around = around + jnp.where(lane == 0, 0.0, pltpu.roll(v, 1, 1))
            around = around + jnp.where(lane == across - 1, 0.0, pltpu.roll(v, across - 1, 1))
            found.append((1.0 - 4.0 * diffusion_number) * v + diffusion_number * around)
        return found

    def write_rows(n, values):
        part = stencil_rows(n)
        for c in range(components):
            for x in range(planes):
                rhs[c, x, part, :] = values[c][x]

    def factor(t, carry):
        d, d_b, low_gain, high_gain, sum_last, sum_first = carry
        back = last - 1 - t
        low, up = of_step(lower, t), of_step(upper, t)
        low_b, up_b = of_step(lower, back), of_step(upper, back)
        velocities = read_rows(t)
        e = 1.0 + low * d
        inverse = reciprocal(up + e)
        g = low * inverse
        e_b = 1.0 + up_b * d_b
        inverse_b = reciprocal(low_b + e_b)
        g_b = up_b * inverse_b
        found = [stencil(values) for values in velocities]
        inv[t] = inverse
        inv_b[back] = inverse_b
        gain_b[back] = g_b
        write_rows(t, found)
        return (
            e * inverse,
            e_b * inverse_b,
            low_gain * g,
            high_gain * g_b,
            inverse + g * sum_last,
            inverse_b + g_b * sum_first,
        )

    carry = lax.fori_loop(0, last, factor, (one, one, one, one, zero, zero))
    _, _, low_gain, high_gain, sum_last, sum_first = carry
    for n in range(last, height // size):
        write_rows(n, [stencil(values) for values in read_rows(n)])
    start_all(outgoing[:2])
    def weigh(t, q):
        first[t] = inv_b[t] * q
        return q * gain_b[t]

    lax.fori_loop(0, last, weigh, one, unroll=6)
    outgoing[2].start()

    low_sep, up_sep = of_step(lower, last), of_step(upper, last)
    segment = lax.broadcasted_iota(jnp.int32, one.shape, 1)
    is_end = segment == segments - 1
    above = jnp.where(is_end, 0.0, jnp.roll(sum_first, -1, axis=1))
    couple_high = up_sep * jnp.where(is_end, 1.0, jnp.roll(high_gain, -1, axis=1))
    killing = 1.0 + low_sep * sum_last + up_sep * above
    ends[2, :, :segments, :] = low_sep
    ends[3, :, :segments, :] = up_sep
    tail = slice(height - rest, height)
    low_rest, up_rest = lower[:, tail, :], upper[:, tail, :]
    for n, (value, other) in enumerate(
        (
            (low_sep * low_gain, low_rest),
            (couple_high, up_rest),
            (killing, jnp.ones_like(low_rest)),
        )
    ):
        for x in range(planes):
            rows[n, x * knots : x * knots + segments, :] = value[x]
            rows[n, x * knots + segments : (x + 1) * knots, :] = other[x]
    for x in range(planes):
        rows[3, x * knots : x * knots + segments, :] = high_gain[x]
        rows[4, x * knots : x * knots + segments, :] = sum_first[x]

    def row(n, s):
        return rows[n, pl.ds(s, planes, stride=knots), :]

    top = knots - 1
    one_row = jnp.ones((planes, across), jnp.float32)
    d, d_b = one_row, one_row
    inv_s, gain_s, ratio_s = [], [], []
    inv_sb, gain_sb = [None] * top, [None] * top
    for s in range(top):
        e = row(2, s) + row(0, s) * d
        inverse = reciprocal(row(1, s) + e)
        inv_s.append(inverse)
        gain_s.append(row(0, s) * inverse)
        ratio_s.append(row(1, s) * inverse)
        d = e * inverse
        back = top - 1 - s
        e_b = row(2, back) + row(1, back) * d_b
        inverse_b = reciprocal(row(0, back) + e_b)
        inv_sb[back] = inverse_b
        gain_sb[back] = row(1, back) * inverse_b
        d_b = e_b * inverse_b
        inner[0, s] = inv_s[s]
        inner[1, s] = gain_s[s]
        inner[2, s] = ratio_s[s]
    outgoing[3].start()
    run = row(0, top)
    low_total = one_row
    sum_top = one_row
    rows[5, pl.ds(top, planes, stride=knots), :] = one_row
    for s in reversed(range(top)):
        weight = run * inv_s[s]
        rows[5, pl.ds(s, planes, stride=knots), :] = weight
        sum_top = sum_top + weight * row(2, s)
        run = run * gain_s[s]
        low_total = low_total * gain_s[s]
    run = row(3, 0)
    high_total = one_row
    sum_bottom = row(4, 0)
    rows[6, pl.ds(top, planes, stride=knots), :] = jnp.zeros_like(one_row)
    for s in range(top):
        weight = run * inv_sb[s]
        rows[6, pl.ds(s, planes, stride=knots), :] = weight
        sum_bottom = sum_bottom + weight * row(2, s)
        run = run * gain_sb[s]
        high_total = high_total * ratio_s[s]
    coef = (
        row(0, top) * low_total,
        sum_top,
        row(1, top),
        sum_bottom,
        row(3, 0) * high_total,
    )
    for n, value in enumerate(coef):
        coefs[n * planes : (n + 1) * planes, :] = value
    for n in range(2):
        for x in range(planes):
            ends[n, x] = rows[5 + n, x * knots : (x + 1) * knots, :]
    start_all(outgoing[4:6])
    wait_all(outgoing)


def deposit_kernel(got, from_above, from_below, cell_rows, *refs):
    (deposit_hbm, swept, prefix, reduced, sums) = refs[7:12]
    (counts, rhs, inv, first, ends, coefs, lower) = refs[12:19]
    (slots, raw, ready, field, total, left, right, columns, edges, in_sems, sems) = refs[19:]
    incoming = copies_of(refs[:7], refs[12:19], in_sems)
    start_all(incoming)
    components, planes, height, across = rhs.shape
    steps = inv.shape[0] + 1
    last = steps - 1
    knots = ends.shape[2]
    rest = knots - segments
    senders, _, _, capacity = got.shape
    chunks = capacity // lanes
    parts = height // lanes
    shift = across.bit_length() - 1
    lines = components * planes
    kind = jnp.bfloat16 if max(height, across) <= 256 else jnp.float32

    def one_sender(s, carry):
        for c in range(components):
            for k in range(chunks):
                start = (s * planes * chunks + k) * components + c
                value = got[s, c, :, k * lanes : (k + 1) * lanes]
                slots[pl.ds(start, planes, stride=chunks * components), :] = value
        return carry

    lax.fori_loop(0, senders, one_sender, 0)
    total[...] = jnp.zeros_like(total)
    for p in range(parts):
        part = slice(p * lines, (p + 1) * lines)
        columns[p, pl.ds(0, lines, stride=2), :] = from_above[part, :]
        columns[p, pl.ds(1, lines, stride=2), :] = from_below[part, :]
        edges[p * lanes : (p + 1) * lanes, :] = diffusion_number * columns[p].T

    tile = 16
    base = lax.broadcasted_iota(jnp.int32, (tile, lanes), 0)
    height_ids = [(base + n * tile).astype(jnp.float32).astype(kind) for n in range(height // tile)]
    across_ids = height_ids[: across // tile]
    lane = lane_iota((1, lanes))
    one = jnp.ones((tile, lanes), jnp.bfloat16)
    none = jnp.zeros((tile, lanes), jnp.bfloat16)

    def spread(row, to):
        return jnp.broadcast_to(row, (tile, lanes)).astype(to)

    def fetch(place):
        x, s, k = place
        for g in range(group):
            sender = jnp.minimum(s, senders - 1)
            count = jnp.where(s < senders, counts[x, sender], 0)
            ident = (sender * planes + x) * chunks + k
            more = count > (k + 1) * lanes
            cell = jnp.where(lane < count - k * lanes, cell_rows[pl.ds(ident, 1), :], -1)
            k = jnp.where(more, k + 1, 0)
            s = jnp.where(more, s, s + 1)
            raw[components, g : g + 1, :] = cell.astype(jnp.float32)
            for c in range(components):
                raw[c, g : g + 1, :] = slots[pl.ds(ident * components + c, 1), :]
        done = s >= senders
        return jnp.where(done, jnp.minimum(x + 1, planes - 1), x), jnp.where(done, 0, s), k

    def convert():
        cell = raw[components].astype(jnp.int32)
        ready[0] = (cell >> shift).astype(jnp.float32)
        ready[1] = jnp.where(cell < 0, -1, cell & (across - 1)).astype(jnp.float32)
        for c in range(components):
            force = raw[c]
            high = force.astype(jnp.bfloat16).astype(jnp.float32)
            ready[2 + c] = high
            ready[2 + components + c] = force - high

    def build():
        for g in range(group):
            there = slice(g * lanes, (g + 1) * lanes)
            up, side = spread(ready[0, g : g + 1, :], kind), spread(ready[1, g : g + 1, :], kind)
            for i, ids in enumerate(height_ids):
                left[i * tile : (i + 1) * tile, there] = jnp.where(up == ids, one, none)
            masks = [side == ids for ids in across_ids]
            for n in range(2 * components):
                value = spread(ready[2 + n, g : g + 1, :], jnp.bfloat16)
                for i, mask in enumerate(masks):
                    place = slice(n * across + i * tile, n * across + (i + 1) * tile)
                    right[place, there] = jnp.where(mask, value, none)

    incoming[0].wait()

    def count_chunks(s, found):
        each = [jnp.maximum(lax.div(counts[x, s] + lanes - 1, lanes), 1) for x in range(planes)]
        return tuple(a + b for a, b in zip(found, each))

    lengths = lax.fori_loop(0, senders, count_chunks, (0,) * planes, unroll=8)
    place = fetch((0, 0, 0))
    convert()
    build()
    for x in range(planes):

        def step(n, place):
            place = fetch(place)
            total[x] += lax.dot_general(
                right[...],
                left[...],
                (((1,), (1,)), ((), ())),
                preferred_element_type=jnp.float32,
            )
            convert()
            build()
            return place

        place = lax.fori_loop(0, lax.div(lengths[x] + group - 1, group), step, place)
    wait_all(incoming[1:])

    wide = lane_iota((lanes, across))
    border = (wide == 0) | (wide == across - 1)

    def place_of(x):
        return [
            pltpu.make_async_copy(field.at[c, x], deposit_hbm.at[c, x], sems.at[c, x])
            for c in range(components)
        ]

    def combine(x, carry):
        for c in range(components):
            for p in range(parts):
                part = slice(p * lanes, (p + 1) * lanes)
                high = total[x, c * across : (c + 1) * across, part]
                low = total[x, (components + c) * across : (components + c + 1) * across, part]
                value = (high + low).T
                field[c, x, part, :] = value.astype(jnp.bfloat16)
                edge = pltpu.roll(edges[part, :], lanes - 1 - 2 * (c * planes + x), 1)
                rhs[c, x, part, :] = rhs[c, x, part, :] + value + jnp.where(border, edge, 0.0)
        start_all(place_of(x))
        return carry

    lax.fori_loop(0, planes, combine, 0)
    sums[2 * lines : 2 * lines + coefs.shape[0], :] = coefs[...]

    zero = jnp.zeros((components, planes, segments, across), jnp.float32)

    def of_step(t):
        return rhs[:, :, pl.ds(t, segments, stride=steps), :]

    def forward(t, carry):
        value, start, run, before = carry
        force = of_step(t)
        low, inverse = lower[:, pl.ds(t, segments, stride=steps), :], inv[t]
        value = force + (low * before)[None] * value
        swept[t] = inverse[None] * value
        run = run * (low * inverse)
        prefix[t] = run
        return value, start + first[t][None] * force, run, inverse

    one = jnp.ones((planes, segments, across), jnp.float32)
    value, start, _, inverse = lax.fori_loop(0, last, forward, (zero, zero, one, one), unroll=3)
    value = inverse[None] * value
    segment = lax.broadcasted_iota(jnp.int32, zero.shape, 2)
    after = jnp.where(segment == segments - 1, 0.0, jnp.roll(start, -1, axis=2))
    low_sep, up_sep = ends[2, :, :segments, :], ends[3, :, :segments, :]
    value = of_step(last) + low_sep[None] * value + up_sep[None] * after
    others = rhs[:, :, height - rest :, :]
    at_top = ends[0, :, :segments, :][None] * value + ends[0, :, segments:, :][None] * others
    at_bottom = ends[1, :, :segments, :][None] * value + ends[1, :, segments:, :][None] * others
    at_bottom = at_bottom + jnp.where(segment == 0, start, 0.0)
    for c in range(components):
        for x in range(planes):
            k = c * planes + x
            reduced[k * knots : k * knots + segments, :] = value[c, x]
            reduced[k * knots + segments : (k + 1) * knots, :] = others[c, x]
            sums[k : k + 1, :] = jnp.sum(at_top[c, x], 0, keepdims=True)
            sums[lines + k : lines + k + 1, :] = jnp.sum(at_bottom[c, x], 0, keepdims=True)

    for x in range(planes):
        wait_all(place_of(x))


def finish_kernel(inner, reduced, swept, inv, prefix, upper, *refs):
    walls = len(refs) - 7
    received = refs[:walls]
    out_hbm, sums, tops, after, before, out, sems = refs[walls:]
    components, planes, height, across = out.shape
    steps = swept.shape[0] + 1
    last = steps - 1
    lines = components * planes
    knots = inner.shape[1] + 1
    rest = knots - segments
    me = lax.axis_index("wall")
    for n in range(walls):
        sums[lax.rem(me + walls - n, walls)] = received[n][...]

    def coef(k, n):
        start = 2 * lines + n * planes
        return sums[k, start : start + planes, :]

    def wide(value):
        return jnp.concatenate([value] * components, 0)

    d = jnp.ones((planes, across), jnp.float32)
    value = jnp.zeros((lines, across), jnp.float32)
    values, ratios = [], []
    for k in range(walls):
        low, own, up = coef(k, 0), coef(k, 1), coef(k, 2)
        right = sums[k, :lines, :]
        if k + 1 < walls:
            high = up * coef(k + 1, 4)
            killing = own + up * coef(k + 1, 3)
            right = right + wide(up) * sums[k + 1, lines : 2 * lines, :]
        else:
            high = jnp.zeros_like(up)
            killing = own + up
        e = killing + low * d
        inverse = reciprocal(high + e)
        d = e * inverse
        value = (right + wide(low) * value) * wide(inverse)
        values.append(value)
        ratios.append(wide(high * inverse))
    tops[0] = jnp.zeros((lines, across), jnp.float32)
    tops[walls] = values[-1]
    for k in reversed(range(walls - 1)):
        values[k] = values[k] + ratios[k] * values[k + 1]
        tops[k + 1] = values[k]

    def row(s):
        return pl.ds(s, lines, stride=knots)

    run = tops[me]
    before[row(0), :] = run
    found = []
    for s in range(knots - 1):
        run = reduced[row(s), :] * wide(inner[0, s]) + wide(inner[1, s]) * run
        found.append(run)
    run = tops[me + 1]
    after[row(knots - 1), :] = run
    for s in reversed(range(knots - 1)):
        run = found[s] + wide(inner[2, s]) * run
        after[row(s), :] = run
        if s + 1 < segments:
            before[row(s + 1), :] = run

    def put(c, x, t, value):
        out[c, x, pl.ds(t, segments, stride=steps), :] = value

    copies = []
    half = planes // 2 if planes % 2 == 0 else planes
    for start in range(0, planes, half):
        part = [(c, x) for c in range(components) for x in range(start, start + half)]
        bottoms, starts = [], []
        for c, x in part:
            base = (c * planes + x) * knots
            bottoms.append(before[base : base + segments, :])
            starts.append(after[base : base + segments, :])
            out[c, x, height - rest :, :] = after[base + segments : base + knots, :]
            put(c, x, last, starts[-1])

        def backward(n, values):
            t = last - 1 - n
            found = []
            ratios = {}
            for x in range(start, start + half):
                ratios[x] = upper[x, pl.ds(t, segments, stride=steps), :] * inv[t, x]
            for (c, x), value, bottom in zip(part, values, bottoms):
                value = (swept[t, c, x] + prefix[t, x] * bottom) + ratios[x] * value
                put(c, x, t, value)
                found.append(value)
            return tuple(found)

        lax.fori_loop(0, last, backward, tuple(starts), unroll=5)
        for here in part:
            copy = pltpu.make_async_copy(out.at[here], out_hbm.at[here], sems.at[here])
            copy.start()
            copies.append(copy)
    wait_all(copies)


def shifted(block, axis, distance):
    length = lax.axis_size(axis)
    route = [(i, (i + distance) % length) for i in range(length)]
    return lax.ppermute(block, axis, route)


def everyone(block, axis):
    return [block] + [shifted(block, axis, n) for n in range(1, lax.axis_size(axis))]


def local(velocity, lower_weight, upper_weight, forces, cells, counts):
    components, planes, height, across = velocity.shape
    receivers, capacity = forces.shape[3], forces.shape[5]
    senders = cells.shape[2]
    walls = lax.axis_size("wall")
    lines = components * planes
    chunks = capacity // lanes
    counts_shape, cells_shape = (planes, senders), (senders, planes, capacity)
    forces = forces.reshape(components, receivers, planes, capacity)
    cells = cells.reshape(senders, planes, capacity)
    counts = counts.reshape(senders, planes).T

    def hbm(*arrays):
        return [pltpu.with_memory_space_constraint(array, pltpu.HBM) for array in arrays]

    send, velocity_near, lower_near, upper_near, cells_near, counts_near = call(
        load_kernel,
        (
            pltpu.HBM((receivers, components, planes, capacity), jnp.float32),
            f32(*velocity.shape),
            f32(*lower_weight.shape),
            f32(*upper_weight.shape),
            jax.ShapeDtypeStruct(cells_shape, jnp.int32),
            jax.ShapeDtypeStruct(counts_shape, jnp.int32),
        ),
        (in_hbm, *[in_vmem] * 5),
        [in_hbm] * 6,
        [scratch(*forces.shape), pltpu.SemaphoreType.DMA((3 * components + 4,))],
        4,
        1 << 16,
    )(*hbm(forces, velocity, lower_weight, upper_weight, cells, counts))
    got = lax.all_to_all(send, "span", 0, 0, tiled=True)
    edge_shape = (lines * height // lanes, lanes)
    first_column, last_column = call(
        edge_kernel,
        (f32(*edge_shape), f32(*edge_shape)),
        (in_vmem, in_vmem),
        [in_vmem],
        [scratch(height, across), scratch(height // lanes, lanes, lanes)],
        4,
        1 << 20,
    )(velocity_near)
    from_above = shifted(first_column, "span", -1)
    from_below = shifted(last_column, "span", 1)

    steps = height // segments - 1
    knots = height - segments * steps + segments
    step_shape = (steps - 1, planes, segments, across)
    staged = [
        velocity.shape,
        step_shape,
        step_shape,
        (3, knots - 1, planes, across),
        (4, planes, knots, across),
        (5 * planes, across),
    ]
    prepared = call(
        prepare_kernel,
        (
            jax.ShapeDtypeStruct((senders * planes * chunks, lanes), jnp.int32),
            *[pltpu.HBM(shape, jnp.float32) for shape in staged],
        ),
        [in_vmem] + [in_hbm] * 6,
        [in_vmem] * 4,
        [
            *[scratch(*shape) for shape in staged],
            scratch(*step_shape),
            scratch(*step_shape),
            scratch(7, planes * knots, across),
            pltpu.SemaphoreType.DMA((6,)),
        ],
        12,
        1 << 24,
    )(cells_near, velocity_near, lower_near, upper_near)
    (cell_rows, rhs_start, inv, first, inner, ends, coefs) = prepared

    sum_rows = -(-(2 * lines + 5 * planes) // 8) * 8
    wide = 2 * components * across
    deposit, swept, prefix, reduced, sums = call(
        deposit_kernel,
        (
            jax.ShapeDtypeStruct(velocity.shape, jnp.bfloat16),
            f32(steps - 1, components, planes, segments, across),
            f32(*step_shape),
            f32(lines * knots, across),
            f32(sum_rows, across),
        ),
        (in_hbm, *[in_vmem] * 4),
        [in_vmem] * 5 + [in_hbm] * 6,
        [
            pltpu.SMEM(counts_shape, jnp.int32),
            *[scratch(*staged[n]) for n in (0, 1, 2, 4, 5)],
            scratch(*lower_weight.shape),
            scratch(senders * planes * chunks * components, lanes),
            scratch(components + 1, group, lanes),
            scratch(2 + 2 * components, group, lanes),
            pltpu.VMEM(velocity.shape, jnp.bfloat16),
            scratch(planes, wide, height),
            pltpu.VMEM((height, group * lanes), jnp.bfloat16),
            pltpu.VMEM((wide, group * lanes), jnp.bfloat16),
            scratch(height // lanes, lanes, lanes),
            scratch(height, lanes),
            pltpu.SemaphoreType.DMA((7,)),
            pltpu.SemaphoreType.DMA((components, planes)),
        ],
        24,
        1 << 32,
    )(
        got,
        from_above,
        from_below,
        cell_rows,
        counts_near,
        *hbm(rhs_start, inv, first, ends, coefs, lower_weight),
    )
    all_sums = everyone(sums, "wall")

    velocity_next = call(
        finish_kernel,
        f32(*velocity.shape),
        in_hbm,
        [in_vmem] * (6 + walls),
        [
            scratch(walls, sum_rows, across),
            scratch(walls + 1, lines, across),
            scratch(lines * knots, across),
            scratch(lines * knots, across),
            scratch(*velocity.shape),
            pltpu.SemaphoreType.DMA((components, planes)),
        ],
        8,
        1 << 22,
    )(inner, reduced, swept, inv, prefix, upper_weight, *all_sums)
    return (velocity_next, deposit)


def solution(mesh):
    placed = (
        P(None, None, "wall", "span"),
        P(None, "wall", "span"),
        P(None, "wall", "span"),
        P(None, "wall", "span", None, None, None),
        P("wall", "span", None, None, None),
        P("wall", "span", None, None),
    )
    return jax.shard_map(
        local,
        mesh=mesh,
        in_specs=placed,
        out_specs=(P(None, None, "wall", "span"), P(None, None, "wall", "span")),
        check_vma=False,
    )
```

```python
import jax
import jax.numpy as jnp
from jax import lax
from jax.experimental import pallas as pl
from jax.experimental.pallas import tpu as pltpu
from jax.sharding import PartitionSpec as P

diffusion_number = 0.2
segments = 8
lanes = 128
group = 8
count_bits, plane_bit = 10, 24
in_vmem = pl.BlockSpec(memory_space=pltpu.VMEM)
in_smem = pl.BlockSpec(memory_space=pltpu.SMEM)
in_hbm = pl.BlockSpec(memory_space=pltpu.HBM)


def call(body, out_shape, out_specs, in_specs, scratch, mebibytes, flops):
    return pl.pallas_call(
        body,
        out_shape=out_shape,
        in_specs=in_specs,
        out_specs=out_specs,
        scratch_shapes=scratch,
        compiler_params=pltpu.CompilerParams(vmem_limit_bytes=mebibytes << 20),
        cost_estimate=pl.CostEstimate(flops=flops, bytes_accessed=4 << 20, transcendentals=0),
    )


def f32(*shape):
    return jax.ShapeDtypeStruct(shape, jnp.float32)


def scratch(*shape):
    return pltpu.VMEM(shape, jnp.float32)


def lane_iota(shape):
    return lax.broadcasted_iota(jnp.int32, shape, len(shape) - 1)


def reciprocal(value):
    rough = pl.reciprocal(value, approx=True)
    return rough * (2.0 - value * rough)


def start_all(copies):
    for copy in copies:
        copy.start()


def wait_all(copies):
    for copy in copies:
        copy.wait()


def copies_of(sources, targets, sems, first=0):
    return [
        pltpu.make_async_copy(source, target, sems.at[first + n])
        for n, (source, target) in enumerate(zip(sources, targets))
    ]


def load_kernel(forces, velocity, lower, upper, cells, counts_hbm, send, *refs):
    near, work_out, (slots, counts, work, sems) = refs[:4], refs[4], refs[5:]
    components, senders, planes, capacity = forces.shape
    chunks = capacity // lanes
    sources = [forces.at[c] for c in range(components)]
    targets = [slots.at[c] for c in range(components)]
    sources += [counts_hbm, cells, lower, upper] + [velocity.at[c] for c in range(components)]
    targets += [counts, near[0], near[1], near[2]] + [near[3].at[c] for c in range(components)]
    copies = copies_of(sources, targets, sems)
    start_all(copies)
    outgoing = copies_of(
        targets[:components] + [work],
        [send.at[:, c] for c in range(components)] + [work_out],
        sems,
        len(copies),
    )
    for c in range(components):
        copies[c].wait()
        outgoing[c].start()
    copies[components].wait()

    def one_plane(x, n):
        def one_sender(s, n):
            count = counts[x, s]
            base = (x << plane_bit) + (((s * planes + x) * chunks) << count_bits)
            for k in range(chunks):
                live = jnp.maximum(count - k * lanes, 0)
                work[group + n + k] = base + (k << count_bits) + live
            return n + lax.div(count + lanes - 1, lanes)

        n = lax.fori_loop(0, senders, one_sender, n, unroll=2)
        for extra in range(group):
            work[group + n + extra] = x << plane_bit
        return lax.div(n + group - 1, group) * group

    total = lax.fori_loop(0, planes, one_plane, 0)
    for extra in range(2 * group):
        work[group + total + extra] = 0
    work[0] = lax.div(total + 2 * group - 1, 2 * group)
    outgoing[components].start()
    wait_all(copies[components + 1 :])
    wait_all(outgoing)


def edge_kernel(velocity, first_out, last_out, columns, turned):
    components, planes, height, across = velocity.shape
    lines = components * planes
    lane = lane_iota((height, across))
    picked = jnp.zeros((height, across), jnp.float32)
    for k in range(lines):
        rolled = pltpu.roll(velocity[k // planes, k % planes], 2 * k + 1, 1)
        picked = jnp.where((lane >> 1) == k, rolled, picked)
    columns[...] = picked
    for p in range(height // lanes):
        turned[p] = columns[p * lanes : (p + 1) * lanes, :].T
        part = slice(p * lines, (p + 1) * lines)
        first_out[part, :] = turned[p, pl.ds(1, lines, stride=2), :]
        last_out[part, :] = turned[p, pl.ds(0, lines, stride=2), :]


def prepare_kernel(cells, velocity, lower, upper, cell_rows, inner, ends, coefs, *refs):
    (rhs, inv, first) = refs[3:6]
    (inv_b, gain_b, rows, sems) = refs[6:]
    outgoing = copies_of(refs[3:6], refs[:3], sems)
    components, planes, height, across = velocity.shape
    steps = inv.shape[0] + 1
    last = steps - 1
    rest = height - segments * steps
    knots = segments + rest
    senders, capacity = cells.shape[0], cells.shape[2]
    chunks = capacity // lanes

    def one_sender(s, carry):
        for k in range(chunks):
            start = s * planes * chunks + k
            value = cells[s, :, k * lanes : (k + 1) * lanes]
            cell_rows[pl.ds(start, planes, stride=chunks), :] = value
        return carry

    lax.fori_loop(0, senders, one_sender, 0, unroll=4)

    def of_step(ref, t):
        return ref[:, pl.ds(t, segments, stride=steps), :]

    one = jnp.ones((planes, segments, across), jnp.float32)
    zero = jnp.zeros_like(one)
    size = 8
    lane = lane_iota((size, across))

    def stencil_rows(n):
        return pl.ds(pl.multiple_of(n * size, size), size)

    def read_rows(n):
        part = stencil_rows(n)
        return [[velocity[c, x, part, :] for x in range(planes)] for c in range(components)]

    def stencil(values):
        found = []
        for x in range(planes):
            v = values[x]
            around = values[(x - 1) % planes] + values[(x + 1) % planes]
            around = around + jnp.where(lane == 0, 0.0, pltpu.roll(v, 1, 1))
            around = around + jnp.where(lane == across - 1, 0.0, pltpu.roll(v, across - 1, 1))
            found.append((1.0 - 4.0 * diffusion_number) * v + diffusion_number * around)
        return found

    def write_rows(n, values):
        part = stencil_rows(n)
        for c in range(components):
            for x in range(planes):
                rhs[c, x, part, :] = values[c][x]

    def factor(t, carry):
        d, d_b, low_gain, high_gain, sum_last, sum_first = carry
        back = last - 1 - t
        low, up = of_step(lower, t), of_step(upper, t)
        low_b, up_b = of_step(lower, back), of_step(upper, back)
        velocities = read_rows(t)
        e = 1.0 + low * d
        inverse = reciprocal(up + e)
        g = low * inverse
        e_b = 1.0 + up_b * d_b
        inverse_b = reciprocal(low_b + e_b)
        g_b = up_b * inverse_b
        found = [stencil(values) for values in velocities]
        inv[t] = inverse
        inv_b[back] = inverse_b
        gain_b[back] = g_b
        write_rows(t, found)
        return (
            e * inverse,
            e_b * inverse_b,
            low_gain * g,
            high_gain * g_b,
            inverse + g * sum_last,
            inverse_b + g_b * sum_first,
        )

    carry = lax.fori_loop(0, last, factor, (one, one, one, one, zero, zero), unroll=2)
    _, _, low_gain, high_gain, sum_last, sum_first = carry
    for n in range(last, height // size):
        write_rows(n, [stencil(values) for values in read_rows(n)])
    start_all(outgoing[:2])
    def weigh(t, q):
        first[t] = inv_b[t] * q
        return q * gain_b[t]

    lax.fori_loop(0, last, weigh, one, unroll=6)
    outgoing[2].start()

    low_sep, up_sep = of_step(lower, last), of_step(upper, last)
    segment = lax.broadcasted_iota(jnp.int32, one.shape, 1)
    is_end = segment == segments - 1
    above = jnp.where(is_end, 0.0, jnp.roll(sum_first, -1, axis=1))
    couple_high = up_sep * jnp.where(is_end, 1.0, jnp.roll(high_gain, -1, axis=1))
    killing = 1.0 + low_sep * sum_last + up_sep * above
    ends[2, :, :segments, :] = low_sep
    ends[3, :, :segments, :] = up_sep
    tail = slice(height - rest, height)
    low_rest, up_rest = lower[:, tail, :], upper[:, tail, :]
    for n, (value, other) in enumerate(
        (
            (low_sep * low_gain, low_rest),
            (couple_high, up_rest),
            (killing, jnp.ones_like(low_rest)),
        )
    ):
        for x in range(planes):
            rows[n, x * knots : x * knots + segments, :] = value[x]
            rows[n, x * knots + segments : (x + 1) * knots, :] = other[x]
    for x in range(planes):
        rows[3, x * knots : x * knots + segments, :] = high_gain[x]
        rows[4, x * knots : x * knots + segments, :] = sum_first[x]

    def row(n, s):
        return rows[n, pl.ds(s, planes, stride=knots), :]

    top = knots - 1
    one_row = jnp.ones((planes, across), jnp.float32)
    d, d_b = one_row, one_row
    inv_s, gain_s, ratio_s = [], [], []
    inv_sb, gain_sb = [None] * top, [None] * top
    for s in range(top):
        e = row(2, s) + row(0, s) * d
        inverse = reciprocal(row(1, s) + e)
        inv_s.append(inverse)
        gain_s.append(row(0, s) * inverse)
        ratio_s.append(row(1, s) * inverse)
        d = e * inverse
        back = top - 1 - s
        e_b = row(2, back) + row(1, back) * d_b
        inverse_b = reciprocal(row(0, back) + e_b)
        inv_sb[back] = inverse_b
        gain_sb[back] = row(1, back) * inverse_b
        d_b = e_b * inverse_b
        inner[0, s] = inv_s[s]
        inner[1, s] = gain_s[s]
        inner[2, s] = ratio_s[s]
    run = row(0, top)
    low_total = one_row
    sum_top = one_row
    rows[5, pl.ds(top, planes, stride=knots), :] = one_row
    for s in reversed(range(top)):
        weight = run * inv_s[s]
        rows[5, pl.ds(s, planes, stride=knots), :] = weight
        sum_top = sum_top + weight * row(2, s)
        run = run * gain_s[s]
        low_total = low_total * gain_s[s]
    run = row(3, 0)
    high_total = one_row
    sum_bottom = row(4, 0)
    rows[6, pl.ds(top, planes, stride=knots), :] = jnp.zeros_like(one_row)
    for s in range(top):
        weight = run * inv_sb[s]
        rows[6, pl.ds(s, planes, stride=knots), :] = weight
        sum_bottom = sum_bottom + weight * row(2, s)
        run = run * gain_sb[s]
        high_total = high_total * ratio_s[s]
    coef = (
        row(0, top) * low_total,
        sum_top,
        row(1, top),
        sum_bottom,
        row(3, 0) * high_total,
    )
    for n, value in enumerate(coef):
        coefs[n * planes : (n + 1) * planes, :] = value
    for n in range(2):
        for x in range(planes):
            ends[n, x] = rows[5 + n, x * knots : (x + 1) * knots, :]
    wait_all(outgoing)


def deposit_kernel(got, from_above, from_below, cell_rows, ends, coefs, *refs):
    (deposit_hbm, swept, prefix, reduced, sums) = refs[5:10]
    (work, rhs, inv, first, lower) = refs[10:15]
    (slots, field, total, lefts, rights, columns, edges, in_sems, sems) = refs[15:]
    incoming = copies_of(refs[:5], refs[10:15], in_sems)
    start_all(incoming)
    components, planes, height, across = rhs.shape
    steps = inv.shape[0] + 1
    last = steps - 1
    knots = ends.shape[2]
    rest = knots - segments
    senders, _, _, capacity = got.shape
    chunks = capacity // lanes
    parts = height // lanes
    shift = across.bit_length() - 1
    lines = components * planes
    kind = jnp.bfloat16 if max(height, across) <= 256 else jnp.float32

    def one_sender(s, carry):
        for c in range(components):
            for k in range(chunks):
                start = (s * planes * chunks + k) * components + c
                value = got[s, c, :, k * lanes : (k + 1) * lanes]
                slots[pl.ds(start, planes, stride=chunks * components), :] = value
        return carry

    lax.fori_loop(0, senders, one_sender, 0)
    total[...] = jnp.zeros_like(total)
    for p in range(parts):
        part = slice(p * lines, (p + 1) * lines)
        columns[p, pl.ds(0, lines, stride=2), :] = from_above[part, :]
        columns[p, pl.ds(1, lines, stride=2), :] = from_below[part, :]
        edges[p * lanes : (p + 1) * lanes, :] = diffusion_number * columns[p].T

    tile = 16
    base = lax.broadcasted_iota(jnp.int32, (tile, lanes), 0)
    height_ids = [(base + n * tile).astype(jnp.float32).astype(kind) for n in range(height // tile)]
    across_ids = height_ids[: across // tile]
    lane = lane_iota((1, lanes))
    one = jnp.ones((tile, lanes), jnp.bfloat16)
    none = jnp.zeros((tile, lanes), jnp.bfloat16)

    def spread(row, to):
        return jnp.broadcast_to(row, (tile, lanes)).astype(to)

    def build(n, half):
        for g in range(group):
            word = work[(n + 1) * group + g]
            ident = (word >> count_bits) & ((1 << (plane_bit - count_bits)) - 1)
            live = word & ((1 << count_bits) - 1)
            there = slice(g * lanes, (g + 1) * lanes)
            cell = cell_rows[pl.ds(ident, 1), :]
            up = jnp.where(lane < live, cell >> shift, -1).astype(jnp.float32)
            side = (cell & (across - 1)).astype(jnp.float32)
            up, side = spread(up, kind), spread(side, kind)
            for i, ids in enumerate(height_ids):
                lefts[half][i * tile : (i + 1) * tile, there] = jnp.where(up == ids, one, none)
            masks = [side == ids for ids in across_ids]
            for c in range(components):
                force = slots[pl.ds(ident * components + c, 1), :]
                rest_of = force - force.astype(jnp.bfloat16).astype(jnp.float32)
                for m, value in enumerate((force, rest_of)):
                    value = spread(value, jnp.bfloat16)
                    start = (m * components + c) * across
                    for i, mask in enumerate(masks):
                        place = slice(start + i * tile, start + (i + 1) * tile)
                        rights[half][place, there] = jnp.where(mask, value, none)

    def add(n, half):
        total[work[(n + 1) * group] >> plane_bit] += lax.dot_general(
            rights[half][...],
            lefts[half][...],
            (((1,), (1,)), ((), ())),
            preferred_element_type=jnp.float32,
        )

    def two_steps(n, carry):
        build(2 * n + 1, 1)
        add(2 * n, 0)
        build(2 * n + 2, 0)
        add(2 * n + 1, 1)
        return carry

    incoming[0].wait()
    build(0, 0)
    lax.fori_loop(0, work[0], two_steps, 0)
    wait_all(incoming[1:])

    wide = lane_iota((lanes, across))
    border = (wide == 0) | (wide == across - 1)

    def place(x):
        return [
            pltpu.make_async_copy(field.at[c, x], deposit_hbm.at[c, x], sems.at[c, x])
            for c in range(components)
        ]

    def combine(x, carry):
        for c in range(components):
            for p in range(parts):
                part = slice(p * lanes, (p + 1) * lanes)
                high = total[x, c * across : (c + 1) * across, part]
                low = total[x, (components + c) * across : (components + c + 1) * across, part]
                value = (high + low).T
                field[c, x, part, :] = value.astype(jnp.bfloat16)
                edge = pltpu.roll(edges[part, :], lanes - 1 - 2 * (c * planes + x), 1)
                rhs[c, x, part, :] = rhs[c, x, part, :] + value + jnp.where(border, edge, 0.0)
        start_all(place(x))
        return carry

    lax.fori_loop(0, planes, combine, 0)
    sums[2 * lines : 2 * lines + coefs.shape[0], :] = coefs[...]

    zero = jnp.zeros((components, planes, segments, across), jnp.float32)

    def of_step(t):
        return rhs[:, :, pl.ds(t, segments, stride=steps), :]

    def forward(t, carry):
        value, start, run, before = carry
        force = of_step(t)
        low, inverse = lower[:, pl.ds(t, segments, stride=steps), :], inv[t]
        value = force + (low * before)[None] * value
        swept[t] = inverse[None] * value
        run = run * (low * inverse)
        prefix[t] = run
        return value, start + first[t][None] * force, run, inverse

    one = jnp.ones((planes, segments, across), jnp.float32)
    value, start, _, inverse = lax.fori_loop(0, last, forward, (zero, zero, one, one), unroll=3)
    value = inverse[None] * value
    segment = lax.broadcasted_iota(jnp.int32, zero.shape, 2)
    after = jnp.where(segment == segments - 1, 0.0, jnp.roll(start, -1, axis=2))
    low_sep, up_sep = ends[2, :, :segments, :], ends[3, :, :segments, :]
    value = of_step(last) + low_sep[None] * value + up_sep[None] * after
    others = rhs[:, :, height - rest :, :]
    at_top = ends[0, :, :segments, :][None] * value + ends[0, :, segments:, :][None] * others
    at_bottom = ends[1, :, :segments, :][None] * value + ends[1, :, segments:, :][None] * others
    at_bottom = at_bottom + jnp.where(segment == 0, start, 0.0)
    for c in range(components):
        for x in range(planes):
            k = c * planes + x
            reduced[k * knots : k * knots + segments, :] = value[c, x]
            reduced[k * knots + segments : (k + 1) * knots, :] = others[c, x]
            sums[k : k + 1, :] = jnp.sum(at_top[c, x], 0, keepdims=True)
            sums[lines + k : lines + k + 1, :] = jnp.sum(at_bottom[c, x], 0, keepdims=True)

    for x in range(planes):
        wait_all(place(x))


def finish_kernel(inner, reduced, swept, inv, prefix, upper, *refs):
    walls = len(refs) - 7
    received = refs[:walls]
    out_hbm, sums, tops, after, before, out, sems = refs[walls:]
    components, planes, height, across = out.shape
    steps = swept.shape[0] + 1
    last = steps - 1
    lines = components * planes
    knots = inner.shape[1] + 1
    rest = knots - segments
    me = lax.axis_index("wall")
    for n in range(walls):
        sums[lax.rem(me + walls - n, walls)] = received[n][...]

    def coef(k, n):
        start = 2 * lines + n * planes
        return sums[k, start : start + planes, :]

    def wide(value):
        return jnp.concatenate([value] * components, 0)

    d = jnp.ones((planes, across), jnp.float32)
    value = jnp.zeros((lines, across), jnp.float32)
    values, ratios = [], []
    for k in range(walls):
        low, own, up = coef(k, 0), coef(k, 1), coef(k, 2)
        right = sums[k, :lines, :]
        if k + 1 < walls:
            high = up * coef(k + 1, 4)
            killing = own + up * coef(k + 1, 3)
            right = right + wide(up) * sums[k + 1, lines : 2 * lines, :]
        else:
            high = jnp.zeros_like(up)
            killing = own + up
        e = killing + low * d
        inverse = reciprocal(high + e)
        d = e * inverse
        value = (right + wide(low) * value) * wide(inverse)
        values.append(value)
        ratios.append(wide(high * inverse))
    tops[0] = jnp.zeros((lines, across), jnp.float32)
    tops[walls] = values[-1]
    for k in reversed(range(walls - 1)):
        values[k] = values[k] + ratios[k] * values[k + 1]
        tops[k + 1] = values[k]

    def row(s):
        return pl.ds(s, lines, stride=knots)

    run = tops[me]
    before[row(0), :] = run
    found = []
    for s in range(knots - 1):
        run = reduced[row(s), :] * wide(inner[0, s]) + wide(inner[1, s]) * run
        found.append(run)
    run = tops[me + 1]
    after[row(knots - 1), :] = run
    for s in reversed(range(knots - 1)):
        run = found[s] + wide(inner[2, s]) * run
        after[row(s), :] = run
        if s + 1 < segments:
            before[row(s + 1), :] = run

    def put(c, x, t, value):
        out[c, x, pl.ds(t, segments, stride=steps), :] = value

    copies = []
    half = planes // 2 if planes % 2 == 0 else planes
    for start in range(0, planes, half):
        part = [(c, x) for c in range(components) for x in range(start, start + half)]
        bottoms, starts = [], []
        for c, x in part:
            base = (c * planes + x) * knots
            bottoms.append(before[base : base + segments, :])
            starts.append(after[base : base + segments, :])
            out[c, x, height - rest :, :] = after[base + segments : base + knots, :]
            put(c, x, last, starts[-1])

        def backward(n, values):
            t = last - 1 - n
            found = []
            ratios = {}
            for x in range(start, start + half):
                ratios[x] = upper[x, pl.ds(t, segments, stride=steps), :] * inv[t, x]
            for (c, x), value, bottom in zip(part, values, bottoms):
                value = (swept[t, c, x] + prefix[t, x] * bottom) + ratios[x] * value
                put(c, x, t, value)
                found.append(value)
            return tuple(found)

        lax.fori_loop(0, last, backward, tuple(starts), unroll=5)
        for here in part:
            copy = pltpu.make_async_copy(out.at[here], out_hbm.at[here], sems.at[here])
            copy.start()
            copies.append(copy)
    wait_all(copies)


def shifted(block, axis, distance):
    length = lax.axis_size(axis)
    route = [(i, (i + distance) % length) for i in range(length)]
    return lax.ppermute(block, axis, route)


def everyone(block, axis):
    return [block] + [shifted(block, axis, n) for n in range(1, lax.axis_size(axis))]


def local(velocity, lower_weight, upper_weight, forces, cells, counts):
    components, planes, height, across = velocity.shape
    receivers, capacity = forces.shape[3], forces.shape[5]
    senders = cells.shape[2]
    walls = lax.axis_size("wall")
    lines = components * planes
    chunks = capacity // lanes
    counts_shape, cells_shape = (planes, senders), (senders, planes, capacity)
    forces = forces.reshape(components, receivers, planes, capacity)
    cells = cells.reshape(senders, planes, capacity)
    counts = counts.reshape(senders, planes).T

    def hbm(*arrays):
        return [pltpu.with_memory_space_constraint(array, pltpu.HBM) for array in arrays]

    work_shape = (planes * (senders * chunks + group) + 4 * group,)
    send, cells_near, lower_near, upper_near, velocity_near, work = call(
        load_kernel,
        (
            pltpu.HBM((receivers, components, planes, capacity), jnp.float32),
            jax.ShapeDtypeStruct(cells_shape, jnp.int32),
            f32(*lower_weight.shape),
            f32(*upper_weight.shape),
            f32(*velocity.shape),
            jax.ShapeDtypeStruct(work_shape, jnp.int32),
        ),
        (in_hbm, *[in_vmem] * 5),
        [in_hbm] * 6,
        [
            scratch(*forces.shape),
            pltpu.SMEM(counts_shape, jnp.int32),
            pltpu.SMEM(work_shape, jnp.int32),
            pltpu.SemaphoreType.DMA((3 * components + 5,)),
        ],
        4,
        1 << 16,
    )(*hbm(forces, velocity, lower_weight, upper_weight, cells, counts))
    got = lax.all_to_all(send, "span", 0, 0, tiled=True)
    edge_shape = (lines * height // lanes, lanes)
    first_column, last_column = call(
        edge_kernel,
        (f32(*edge_shape), f32(*edge_shape)),
        (in_vmem, in_vmem),
        [in_vmem],
        [scratch(height, across), scratch(height // lanes, lanes, lanes)],
        4,
        1 << 20,
    )(velocity_near)
    from_above = shifted(first_column, "span", -1)
    from_below = shifted(last_column, "span", 1)

    steps = height // segments - 1
    knots = height - segments * steps + segments
    step_shape = (steps - 1, planes, segments, across)
    staged = [velocity.shape, step_shape, step_shape]
    prepared = call(
        prepare_kernel,
        (
            jax.ShapeDtypeStruct((senders * planes * chunks, lanes), jnp.int32),
            f32(3, knots - 1, planes, across),
            f32(4, planes, knots, across),
            f32(5 * planes, across),
            *[pltpu.HBM(shape, jnp.float32) for shape in staged],
        ),
        [in_vmem] * 4 + [in_hbm] * 3,
        [in_vmem] * 4,
        [
            *[scratch(*shape) for shape in staged],
            scratch(*step_shape),
            scratch(*step_shape),
            scratch(7, planes * knots, across),
            pltpu.SemaphoreType.DMA((3,)),
        ],
        12,
        1 << 24,
    )(cells_near, velocity_near, lower_near, upper_near)
    (cell_rows, inner, ends, coefs, rhs_start, inv, first) = prepared

    sum_rows = -(-(2 * lines + 5 * planes) // 8) * 8
    wide = 2 * components * across
    deposit, swept, prefix, reduced, sums = call(
        deposit_kernel,
        (
            jax.ShapeDtypeStruct(velocity.shape, jnp.bfloat16),
            f32(steps - 1, components, planes, segments, across),
            f32(*step_shape),
            f32(lines * knots, across),
            f32(sum_rows, across),
        ),
        (in_hbm, *[in_vmem] * 4),
        [in_vmem] * 7 + [in_hbm] * 4,
        [
            pltpu.SMEM(work_shape, jnp.int32),
            *[scratch(*shape) for shape in staged],
            scratch(*lower_weight.shape),
            scratch(senders * planes * chunks * components, lanes),
            pltpu.VMEM(velocity.shape, jnp.bfloat16),
            scratch(planes, wide, height),
            [pltpu.VMEM((height, group * lanes), jnp.bfloat16)] * 2,
            [pltpu.VMEM((wide, group * lanes), jnp.bfloat16)] * 2,
            scratch(height // lanes, lanes, lanes),
            scratch(height, lanes),
            pltpu.SemaphoreType.DMA((5,)),
            pltpu.SemaphoreType.DMA((components, planes)),
        ],
        24,
        1 << 32,
    )(
        got,
        from_above,
        from_below,
        cell_rows,
        ends,
        coefs,
        work,
        *hbm(rhs_start, inv, first, lower_weight),
    )
    all_sums = everyone(sums, "wall")

    velocity_next = call(
        finish_kernel,
        f32(*velocity.shape),
        in_hbm,
        [in_vmem] * (6 + walls),
        [
            scratch(walls, sum_rows, across),
            scratch(walls + 1, lines, across),
            scratch(lines * knots, across),
            scratch(lines * knots, across),
            scratch(*velocity.shape),
            pltpu.SemaphoreType.DMA((components, planes)),
        ],
        8,
        1 << 22,
    )(inner, reduced, swept, inv, prefix, upper_weight, *all_sums)
    return (velocity_next, deposit)


def solution(mesh):
    placed = (
        P(None, None, "wall", "span"),
        P(None, "wall", "span"),
        P(None, "wall", "span"),
        P(None, "wall", "span", None, None, None),
        P("wall", "span", None, None, None),
        P("wall", "span", None, None),
    )
    return jax.shard_map(
        local,
        mesh=mesh,
        in_specs=placed,
        out_specs=(P(None, None, "wall", "span"), P(None, None, "wall", "span")),
        check_vma=False,
    )
```

```python
import jax
import jax.numpy as jnp
from jax import lax
from jax.experimental import pallas as pl
from jax.experimental.pallas import tpu as pltpu
from jax.sharding import PartitionSpec as P

diffusion_number = 0.2
segments = 8
lanes = 128
group = 8
count_bits, plane_bit = 10, 24
in_vmem = pl.BlockSpec(memory_space=pltpu.VMEM)
in_smem = pl.BlockSpec(memory_space=pltpu.SMEM)
in_hbm = pl.BlockSpec(memory_space=pltpu.HBM)


def call(body, out_shape, out_specs, in_specs, scratch, mebibytes, flops):
    return pl.pallas_call(
        body,
        out_shape=out_shape,
        in_specs=in_specs,
        out_specs=out_specs,
        scratch_shapes=scratch,
        compiler_params=pltpu.CompilerParams(vmem_limit_bytes=mebibytes << 20),
        cost_estimate=pl.CostEstimate(flops=flops, bytes_accessed=4 << 20, transcendentals=0),
    )


def f32(*shape):
    return jax.ShapeDtypeStruct(shape, jnp.float32)


def scratch(*shape):
    return pltpu.VMEM(shape, jnp.float32)


def lane_iota(shape):
    return lax.broadcasted_iota(jnp.int32, shape, len(shape) - 1)


def reciprocal(value):
    rough = pl.reciprocal(value, approx=True)
    return rough * (2.0 - value * rough)


def start_all(copies):
    for copy in copies:
        copy.start()


def wait_all(copies):
    for copy in copies:
        copy.wait()


def copies_of(sources, targets, sems, first=0):
    return [
        pltpu.make_async_copy(source, target, sems.at[first + n])
        for n, (source, target) in enumerate(zip(sources, targets))
    ]


def load_kernel(forces, velocity, lower, upper, cells, counts_hbm, send, *refs):
    near, work_out, (slots, counts, work, sems) = refs[:4], refs[4], refs[5:]
    components, senders, planes, capacity = forces.shape
    chunks = capacity // lanes
    sources = [forces.at[c] for c in range(components)]
    targets = [slots.at[c] for c in range(components)]
    sources += [counts_hbm, cells, lower, upper] + [velocity.at[c] for c in range(components)]
    targets += [counts, near[0], near[1], near[2]] + [near[3].at[c] for c in range(components)]
    copies = copies_of(sources, targets, sems)
    start_all(copies)
    outgoing = copies_of(
        targets[:components] + [work],
        [send.at[:, c] for c in range(components)] + [work_out],
        sems,
        len(copies),
    )
    for c in range(components):
        copies[c].wait()
        outgoing[c].start()
    copies[components].wait()

    def one_plane(x, n):
        def one_sender(s, n):
            count = counts[x, s]
            base = (x << plane_bit) + (((s * planes + x) * chunks) << count_bits)
            for k in range(chunks):
                live = jnp.maximum(count - k * lanes, 0)
                work[group + n + k] = base + (k << count_bits) + live
            return n + lax.div(count + lanes - 1, lanes)

        n = lax.fori_loop(0, senders, one_sender, n, unroll=2)
        for extra in range(group):
            work[group + n + extra] = x << plane_bit
        return lax.div(n + group - 1, group) * group

    total = lax.fori_loop(0, planes, one_plane, 0)
    for extra in range(2 * group):
        work[group + total + extra] = 0
    work[0] = lax.div(total + 2 * group - 1, 2 * group)
    outgoing[components].start()
    wait_all(copies[components + 1 :])
    wait_all(outgoing)


def edge_kernel(velocity, first_out, last_out, columns, turned):
    components, planes, height, across = velocity.shape
    lines = components * planes
    lane = lane_iota((height, across))
    picked = jnp.zeros((height, across), jnp.float32)
    for k in range(lines):
        rolled = pltpu.roll(velocity[k // planes, k % planes], 2 * k + 1, 1)
        picked = jnp.where((lane >> 1) == k, rolled, picked)
    columns[...] = picked
    for p in range(height // lanes):
        turned[p] = columns[p * lanes : (p + 1) * lanes, :].T
        part = slice(p * lines, (p + 1) * lines)
        first_out[part, :] = turned[p, pl.ds(1, lines, stride=2), :]
        last_out[part, :] = turned[p, pl.ds(0, lines, stride=2), :]


def prepare_kernel(cells, velocity, lower, upper, cell_rows, inner, ends, coefs, *refs):
    (rhs, inv, first) = refs[3:6]
    (inv_b, gain_b, rows, sems) = refs[6:]
    outgoing = copies_of(refs[3:6], refs[:3], sems)
    components, planes, height, across = velocity.shape
    steps = inv.shape[0] + 1
    last = steps - 1
    rest = height - segments * steps
    knots = segments + rest
    senders, capacity = cells.shape[0], cells.shape[2]
    chunks = capacity // lanes

    def one_sender(s, carry):
        for k in range(chunks):
            start = s * planes * chunks + k
            value = cells[s, :, k * lanes : (k + 1) * lanes]
            cell_rows[pl.ds(start, planes, stride=chunks), :] = value
        return carry

    lax.fori_loop(0, senders, one_sender, 0, unroll=4)

    def of_step(ref, t):
        return ref[:, pl.ds(t, segments, stride=steps), :]

    one = jnp.ones((planes, segments, across), jnp.float32)
    zero = jnp.zeros_like(one)
    size = 8
    lane = lane_iota((size, across))

    def stencil_rows(n):
        return pl.ds(pl.multiple_of(n * size, size), size)

    def read_rows(n):
        part = stencil_rows(n)
        return [[velocity[c, x, part, :] for x in range(planes)] for c in range(components)]

    def stencil(values):
        found = []
        for x in range(planes):
            v = values[x]
            around = values[(x - 1) % planes] + values[(x + 1) % planes]
            around = around + jnp.where(lane == 0, 0.0, pltpu.roll(v, 1, 1))
            around = around + jnp.where(lane == across - 1, 0.0, pltpu.roll(v, across - 1, 1))
            found.append((1.0 - 4.0 * diffusion_number) * v + diffusion_number * around)
        return found

    def write_rows(n, values):
        part = stencil_rows(n)
        for c in range(components):
            for x in range(planes):
                rhs[c, x, part, :] = values[c][x]

    def factor(t, carry):
        d, d_b, low_gain, high_gain, sum_last, sum_first = carry
        back = last - 1 - t
        low, up = of_step(lower, t), of_step(upper, t)
        low_b, up_b = of_step(lower, back), of_step(upper, back)
        velocities = read_rows(t)
        e = 1.0 + low * d
        inverse = reciprocal(up + e)
        g = low * inverse
        e_b = 1.0 + up_b * d_b
        inverse_b = reciprocal(low_b + e_b)
        g_b = up_b * inverse_b
        found = [stencil(values) for values in velocities]
        inv[t] = inverse
        inv_b[back] = inverse_b
        gain_b[back] = g_b
        write_rows(t, found)
        return (
            e * inverse,
            e_b * inverse_b,
            low_gain * g,
            high_gain * g_b,
            inverse + g * sum_last,
            inverse_b + g_b * sum_first,
        )

    carry = lax.fori_loop(0, last, factor, (one, one, one, one, zero, zero), unroll=2)
    _, _, low_gain, high_gain, sum_last, sum_first = carry
    for n in range(last, height // size):
        write_rows(n, [stencil(values) for values in read_rows(n)])
    start_all(outgoing[:2])
    def weigh(t, q):
        first[t] = inv_b[t] * q
        return q * gain_b[t]

    lax.fori_loop(0, last, weigh, one, unroll=6)
    outgoing[2].start()

    low_sep, up_sep = of_step(lower, last), of_step(upper, last)
    segment = lax.broadcasted_iota(jnp.int32, one.shape, 1)
    is_end = segment == segments - 1
    above = jnp.where(is_end, 0.0, jnp.roll(sum_first, -1, axis=1))
    couple_high = up_sep * jnp.where(is_end, 1.0, jnp.roll(high_gain, -1, axis=1))
    killing = 1.0 + low_sep * sum_last + up_sep * above
    ends[2, :, :segments, :] = low_sep
    ends[3, :, :segments, :] = up_sep
    tail = slice(height - rest, height)
    low_rest, up_rest = lower[:, tail, :], upper[:, tail, :]
    for n, (value, other) in enumerate(
        (
            (low_sep * low_gain, low_rest),
            (couple_high, up_rest),
            (killing, jnp.ones_like(low_rest)),
        )
    ):
        for x in range(planes):
            rows[n, x * knots : x * knots + segments, :] = value[x]
            rows[n, x * knots + segments : (x + 1) * knots, :] = other[x]
    for x in range(planes):
        rows[3, x * knots : x * knots + segments, :] = high_gain[x]
        rows[4, x * knots : x * knots + segments, :] = sum_first[x]

    def row(n, s):
        return rows[n, pl.ds(s, planes, stride=knots), :]

    top = knots - 1
    one_row = jnp.ones((planes, across), jnp.float32)
    d, d_b = one_row, one_row
    inv_s, gain_s, ratio_s = [], [], []
    inv_sb, gain_sb = [None] * top, [None] * top
    for s in range(top):
        e = row(2, s) + row(0, s) * d
        inverse = reciprocal(row(1, s) + e)
        inv_s.append(inverse)
        gain_s.append(row(0, s) * inverse)
        ratio_s.append(row(1, s) * inverse)
        d = e * inverse
        back = top - 1 - s
        e_b = row(2, back) + row(1, back) * d_b
        inverse_b = reciprocal(row(0, back) + e_b)
        inv_sb[back] = inverse_b
        gain_sb[back] = row(1, back) * inverse_b
        d_b = e_b * inverse_b
        inner[0, s] = inv_s[s]
        inner[1, s] = gain_s[s]
        inner[2, s] = ratio_s[s]
    run = row(0, top)
    low_total = one_row
    sum_top = one_row
    rows[5, pl.ds(top, planes, stride=knots), :] = one_row
    for s in reversed(range(top)):
        weight = run * inv_s[s]
        rows[5, pl.ds(s, planes, stride=knots), :] = weight
        sum_top = sum_top + weight * row(2, s)
        run = run * gain_s[s]
        low_total = low_total * gain_s[s]
    run = row(3, 0)
    high_total = one_row
    sum_bottom = row(4, 0)
    rows[6, pl.ds(top, planes, stride=knots), :] = jnp.zeros_like(one_row)
    for s in range(top):
        weight = run * inv_sb[s]
        rows[6, pl.ds(s, planes, stride=knots), :] = weight
        sum_bottom = sum_bottom + weight * row(2, s)
        run = run * gain_sb[s]
        high_total = high_total * ratio_s[s]
    coef = (
        row(0, top) * low_total,
        sum_top,
        row(1, top),
        sum_bottom,
        row(3, 0) * high_total,
    )
    for n, value in enumerate(coef):
        coefs[n * planes : (n + 1) * planes, :] = value
    for n in range(2):
        for x in range(planes):
            ends[n, x] = rows[5 + n, x * knots : (x + 1) * knots, :]
    wait_all(outgoing)


def deposit_kernel(got, from_above, from_below, cell_rows, ends, coefs, *refs):
    (deposit_hbm, swept, prefix, reduced, sums) = refs[5:10]
    (work, rhs, inv, first, lower) = refs[10:15]
    (slots, field, total, lefts, rights, columns, edges, in_sems, sems) = refs[15:]
    incoming = copies_of(refs[:5], refs[10:15], in_sems)
    start_all(incoming)
    components, planes, height, across = rhs.shape
    steps = inv.shape[0] + 1
    last = steps - 1
    knots = ends.shape[2]
    rest = knots - segments
    senders, _, _, capacity = got.shape
    chunks = capacity // lanes
    parts = height // lanes
    shift = across.bit_length() - 1
    lines = components * planes
    kind = jnp.bfloat16 if max(height, across) <= 256 else jnp.float32

    def one_sender(s, carry):
        for c in range(components):
            for k in range(chunks):
                start = (s * planes * chunks + k) * components + c
                value = got[s, c, :, k * lanes : (k + 1) * lanes]
                slots[pl.ds(start, planes, stride=chunks * components), :] = value
        return carry

    lax.fori_loop(0, senders, one_sender, 0)
    total[...] = jnp.zeros_like(total)
    for p in range(parts):
        part = slice(p * lines, (p + 1) * lines)
        columns[p, pl.ds(0, lines, stride=2), :] = from_above[part, :]
        columns[p, pl.ds(1, lines, stride=2), :] = from_below[part, :]
        edges[p * lanes : (p + 1) * lanes, :] = diffusion_number * columns[p].T

    tile = 16
    base = lax.broadcasted_iota(jnp.int32, (tile, lanes), 0)
    height_ids = [(base + n * tile).astype(jnp.float32).astype(kind) for n in range(height // tile)]
    across_ids = height_ids[: across // tile]
    lane = lane_iota((1, lanes))
    one = jnp.ones((tile, lanes), jnp.bfloat16)
    none = jnp.zeros((tile, lanes), jnp.bfloat16)

    def spread(row, to):
        return jnp.broadcast_to(row, (tile, lanes)).astype(to)

    def build(n, half):
        for g in range(group):
            word = work[(n + 1) * group + g]
            ident = (word >> count_bits) & ((1 << (plane_bit - count_bits)) - 1)
            live = word & ((1 << count_bits) - 1)
            there = slice(g * lanes, (g + 1) * lanes)
            cell = cell_rows[pl.ds(ident, 1), :]
            up = jnp.where(lane < live, cell >> shift, -1).astype(jnp.float32)
            side = (cell & (across - 1)).astype(jnp.float32)
            up, side = spread(up, kind), spread(side, kind)
            for i, ids in enumerate(height_ids):
                lefts[half][i * tile : (i + 1) * tile, there] = jnp.where(up == ids, one, none)
            masks = [side == ids for ids in across_ids]
            for c in range(components):
                force = slots[pl.ds(ident * components + c, 1), :]
                rest_of = force - force.astype(jnp.bfloat16).astype(jnp.float32)
                for m, value in enumerate((force, rest_of)):
                    value = spread(value, jnp.bfloat16)
                    start = (m * components + c) * across
                    for i, mask in enumerate(masks):
                        place = slice(start + i * tile, start + (i + 1) * tile)
                        rights[half][place, there] = jnp.where(mask, value, none)

    def add(n, half):
        total[work[(n + 1) * group] >> plane_bit] += lax.dot_general(
            lefts[half][...],
            rights[half][...],
            (((1,), (1,)), ((), ())),
            preferred_element_type=jnp.float32,
        )

    def two_steps(n, carry):
        build(2 * n + 1, 1)
        add(2 * n, 0)
        build(2 * n + 2, 0)
        add(2 * n + 1, 1)
        return carry

    incoming[0].wait()
    build(0, 0)
    lax.fori_loop(0, work[0], two_steps, 0)
    wait_all(incoming[1:])

    wide = lane_iota((lanes, across))
    border = (wide == 0) | (wide == across - 1)

    def place(x):
        return [
            pltpu.make_async_copy(field.at[c, x], deposit_hbm.at[c, x], sems.at[c, x])
            for c in range(components)
        ]

    def combine(x, carry):
        for c in range(components):
            for p in range(parts):
                part = slice(p * lanes, (p + 1) * lanes)
                high = total[x, part, c * across : (c + 1) * across]
                low = total[x, part, (components + c) * across : (components + c + 1) * across]
                value = high + low
                field[c, x, part, :] = value.astype(jnp.bfloat16)
                edge = pltpu.roll(edges[part, :], lanes - 1 - 2 * (c * planes + x), 1)
                rhs[c, x, part, :] = rhs[c, x, part, :] + value + jnp.where(border, edge, 0.0)
        start_all(place(x))
        return carry

    lax.fori_loop(0, planes, combine, 0)
    sums[2 * lines : 2 * lines + coefs.shape[0], :] = coefs[...]

    zero = jnp.zeros((components, planes, segments, across), jnp.float32)

    def of_step(t):
        return rhs[:, :, pl.ds(t, segments, stride=steps), :]

    def forward(t, carry):
        value, start, run, before = carry
        force = of_step(t)
        low, inverse = lower[:, pl.ds(t, segments, stride=steps), :], inv[t]
        value = force + (low * before)[None] * value
        swept[t] = inverse[None] * value
        run = run * (low * inverse)
        prefix[t] = run
        return value, start + first[t][None] * force, run, inverse

    one = jnp.ones((planes, segments, across), jnp.float32)
    value, start, _, inverse = lax.fori_loop(0, last, forward, (zero, zero, one, one), unroll=3)
    value = inverse[None] * value
    segment = lax.broadcasted_iota(jnp.int32, zero.shape, 2)
    after = jnp.where(segment == segments - 1, 0.0, jnp.roll(start, -1, axis=2))
    low_sep, up_sep = ends[2, :, :segments, :], ends[3, :, :segments, :]
    value = of_step(last) + low_sep[None] * value + up_sep[None] * after
    others = rhs[:, :, height - rest :, :]
    at_top = ends[0, :, :segments, :][None] * value + ends[0, :, segments:, :][None] * others
    at_bottom = ends[1, :, :segments, :][None] * value + ends[1, :, segments:, :][None] * others
    at_bottom = at_bottom + jnp.where(segment == 0, start, 0.0)
    for c in range(components):
        for x in range(planes):
            k = c * planes + x
            reduced[k * knots : k * knots + segments, :] = value[c, x]
            reduced[k * knots + segments : (k + 1) * knots, :] = others[c, x]
            sums[k : k + 1, :] = jnp.sum(at_top[c, x], 0, keepdims=True)
            sums[lines + k : lines + k + 1, :] = jnp.sum(at_bottom[c, x], 0, keepdims=True)

    for x in range(planes):
        wait_all(place(x))


def finish_kernel(inner, reduced, swept, inv, prefix, upper, *refs):
    walls = len(refs) - 7
    received = refs[:walls]
    out_hbm, sums, tops, after, before, out, sems = refs[walls:]
    components, planes, height, across = out.shape
    steps = swept.shape[0] + 1
    last = steps - 1
    lines = components * planes
    knots = inner.shape[1] + 1
    rest = knots - segments
    me = lax.axis_index("wall")
    for n in range(walls):
        sums[lax.rem(me + walls - n, walls)] = received[n][...]

    def coef(k, n):
        start = 2 * lines + n * planes
        return sums[k, start : start + planes, :]

    def wide(value):
        return jnp.concatenate([value] * components, 0)

    d = jnp.ones((planes, across), jnp.float32)
    value = jnp.zeros((lines, across), jnp.float32)
    values, ratios = [], []
    for k in range(walls):
        low, own, up = coef(k, 0), coef(k, 1), coef(k, 2)
        right = sums[k, :lines, :]
        if k + 1 < walls:
            high = up * coef(k + 1, 4)
            killing = own + up * coef(k + 1, 3)
            right = right + wide(up) * sums[k + 1, lines : 2 * lines, :]
        else:
            high = jnp.zeros_like(up)
            killing = own + up
        e = killing + low * d
        inverse = reciprocal(high + e)
        d = e * inverse
        value = (right + wide(low) * value) * wide(inverse)
        values.append(value)
        ratios.append(wide(high * inverse))
    tops[0] = jnp.zeros((lines, across), jnp.float32)
    tops[walls] = values[-1]
    for k in reversed(range(walls - 1)):
        values[k] = values[k] + ratios[k] * values[k + 1]
        tops[k + 1] = values[k]

    def row(s):
        return pl.ds(s, lines, stride=knots)

    run = tops[me]
    before[row(0), :] = run
    found = []
    for s in range(knots - 1):
        run = reduced[row(s), :] * wide(inner[0, s]) + wide(inner[1, s]) * run
        found.append(run)
    run = tops[me + 1]
    after[row(knots - 1), :] = run
    for s in reversed(range(knots - 1)):
        run = found[s] + wide(inner[2, s]) * run
        after[row(s), :] = run
        if s + 1 < segments:
            before[row(s + 1), :] = run

    def put(c, x, t, value):
        out[c, x, pl.ds(t, segments, stride=steps), :] = value

    copies = []
    half = planes // 2 if planes % 2 == 0 else planes
    for start in range(0, planes, half):
        part = [(c, x) for c in range(components) for x in range(start, start + half)]
        bottoms, starts = [], []
        for c, x in part:
            base = (c * planes + x) * knots
            bottoms.append(before[base : base + segments, :])
            starts.append(after[base : base + segments, :])
            out[c, x, height - rest :, :] = after[base + segments : base + knots, :]
            put(c, x, last, starts[-1])

        def backward(n, values):
            t = last - 1 - n
            found = []
            ratios = {}
            for x in range(start, start + half):
                ratios[x] = upper[x, pl.ds(t, segments, stride=steps), :] * inv[t, x]
            for (c, x), value, bottom in zip(part, values, bottoms):
                value = (swept[t, c, x] + prefix[t, x] * bottom) + ratios[x] * value
                put(c, x, t, value)
                found.append(value)
            return tuple(found)

        lax.fori_loop(0, last, backward, tuple(starts), unroll=5)
        for here in part:
            copy = pltpu.make_async_copy(out.at[here], out_hbm.at[here], sems.at[here])
            copy.start()
            copies.append(copy)
    wait_all(copies)


def shifted(block, axis, distance):
    length = lax.axis_size(axis)
    route = [(i, (i + distance) % length) for i in range(length)]
    return lax.ppermute(block, axis, route)


def everyone(block, axis):
    return [block] + [shifted(block, axis, n) for n in range(1, lax.axis_size(axis))]


def local(velocity, lower_weight, upper_weight, forces, cells, counts):
    components, planes, height, across = velocity.shape
    receivers, capacity = forces.shape[3], forces.shape[5]
    senders = cells.shape[2]
    walls = lax.axis_size("wall")
    lines = components * planes
    chunks = capacity // lanes
    counts_shape, cells_shape = (planes, senders), (senders, planes, capacity)
    forces = forces.reshape(components, receivers, planes, capacity)
    cells = cells.reshape(senders, planes, capacity)
    counts = counts.reshape(senders, planes).T

    def hbm(*arrays):
        return [pltpu.with_memory_space_constraint(array, pltpu.HBM) for array in arrays]

    work_shape = (planes * (senders * chunks + group) + 4 * group,)
    send, cells_near, lower_near, upper_near, velocity_near, work = call(
        load_kernel,
        (
            pltpu.HBM((receivers, components, planes, capacity), jnp.float32),
            jax.ShapeDtypeStruct(cells_shape, jnp.int32),
            f32(*lower_weight.shape),
            f32(*upper_weight.shape),
            f32(*velocity.shape),
            jax.ShapeDtypeStruct(work_shape, jnp.int32),
        ),
        (in_hbm, *[in_vmem] * 5),
        [in_hbm] * 6,
        [
            scratch(*forces.shape),
            pltpu.SMEM(counts_shape, jnp.int32),
            pltpu.SMEM(work_shape, jnp.int32),
            pltpu.SemaphoreType.DMA((3 * components + 5,)),
        ],
        4,
        1 << 16,
    )(*hbm(forces, velocity, lower_weight, upper_weight, cells, counts))
    got = lax.all_to_all(send, "span", 0, 0, tiled=True)
    edge_shape = (lines * height // lanes, lanes)
    first_column, last_column = call(
        edge_kernel,
        (f32(*edge_shape), f32(*edge_shape)),
        (in_vmem, in_vmem),
        [in_vmem],
        [scratch(height, across), scratch(height // lanes, lanes, lanes)],
        4,
        1 << 20,
    )(velocity_near)
    from_above = shifted(first_column, "span", -1)
    from_below = shifted(last_column, "span", 1)

    steps = height // segments - 1
    knots = height - segments * steps + segments
    step_shape = (steps - 1, planes, segments, across)
    staged = [velocity.shape, step_shape, step_shape]
    prepared = call(
        prepare_kernel,
        (
            jax.ShapeDtypeStruct((senders * planes * chunks, lanes), jnp.int32),
            f32(3, knots - 1, planes, across),
            f32(4, planes, knots, across),
            f32(5 * planes, across),
            *[pltpu.HBM(shape, jnp.float32) for shape in staged],
        ),
        [in_vmem] * 4 + [in_hbm] * 3,
        [in_vmem] * 4,
        [
            *[scratch(*shape) for shape in staged],
            scratch(*step_shape),
            scratch(*step_shape),
            scratch(7, planes * knots, across),
            pltpu.SemaphoreType.DMA((3,)),
        ],
        12,
        1 << 24,
    )(cells_near, velocity_near, lower_near, upper_near)
    (cell_rows, inner, ends, coefs, rhs_start, inv, first) = prepared

    sum_rows = -(-(2 * lines + 5 * planes) // 8) * 8
    wide = 2 * components * across
    deposit, swept, prefix, reduced, sums = call(
        deposit_kernel,
        (
            jax.ShapeDtypeStruct(velocity.shape, jnp.bfloat16),
            f32(steps - 1, components, planes, segments, across),
            f32(*step_shape),
            f32(lines * knots, across),
            f32(sum_rows, across),
        ),
        (in_hbm, *[in_vmem] * 4),
        [in_vmem] * 7 + [in_hbm] * 4,
        [
            pltpu.SMEM(work_shape, jnp.int32),
            *[scratch(*shape) for shape in staged],
            scratch(*lower_weight.shape),
            scratch(senders * planes * chunks * components, lanes),
            pltpu.VMEM(velocity.shape, jnp.bfloat16),
            scratch(planes, height, wide),
            [pltpu.VMEM((height, group * lanes), jnp.bfloat16)] * 2,
            [pltpu.VMEM((wide, group * lanes), jnp.bfloat16)] * 2,
            scratch(height // lanes, lanes, lanes),
            scratch(height, lanes),
            pltpu.SemaphoreType.DMA((5,)),
            pltpu.SemaphoreType.DMA((components, planes)),
        ],
        24,
        1 << 32,
    )(
        got,
        from_above,
        from_below,
        cell_rows,
        ends,
        coefs,
        work,
        *hbm(rhs_start, inv, first, lower_weight),
    )
    all_sums = everyone(sums, "wall")

    velocity_next = call(
        finish_kernel,
        f32(*velocity.shape),
        in_hbm,
        [in_vmem] * (6 + walls),
        [
            scratch(walls, sum_rows, across),
            scratch(walls + 1, lines, across),
            scratch(lines * knots, across),
            scratch(lines * knots, across),
            scratch(*velocity.shape),
            pltpu.SemaphoreType.DMA((components, planes)),
        ],
        8,
        1 << 22,
    )(inner, reduced, swept, inv, prefix, upper_weight, *all_sums)
    return (velocity_next, deposit)


def solution(mesh):
    placed = (
        P(None, None, "wall", "span"),
        P(None, "wall", "span"),
        P(None, "wall", "span"),
        P(None, "wall", "span", None, None, None),
        P("wall", "span", None, None, None),
        P("wall", "span", None, None),
    )
    return jax.shard_map(
        local,
        mesh=mesh,
        in_specs=placed,
        out_specs=(P(None, None, "wall", "span"), P(None, None, "wall", "span")),
        check_vma=False,
    )
```

```python
import jax
import jax.numpy as jnp
from jax import lax
from jax.experimental import pallas as pl
from jax.experimental.pallas import tpu as pltpu
from jax.sharding import PartitionSpec as P

diffusion_number = 0.2
segments = 8
lanes = 128
group = 8
count_bits, plane_bit = 10, 24
in_vmem = pl.BlockSpec(memory_space=pltpu.VMEM)
in_smem = pl.BlockSpec(memory_space=pltpu.SMEM)
in_hbm = pl.BlockSpec(memory_space=pltpu.HBM)


def call(body, out_shape, out_specs, in_specs, scratch, mebibytes, flops):
    return pl.pallas_call(
        body,
        out_shape=out_shape,
        in_specs=in_specs,
        out_specs=out_specs,
        scratch_shapes=scratch,
        compiler_params=pltpu.CompilerParams(vmem_limit_bytes=mebibytes << 20),
        cost_estimate=pl.CostEstimate(flops=flops, bytes_accessed=4 << 20, transcendentals=0),
    )


def f32(*shape):
    return jax.ShapeDtypeStruct(shape, jnp.float32)


def scratch(*shape):
    return pltpu.VMEM(shape, jnp.float32)


def lane_iota(shape):
    return lax.broadcasted_iota(jnp.int32, shape, len(shape) - 1)


def reciprocal(value):
    rough = pl.reciprocal(value, approx=True)
    return rough * (2.0 - value * rough)


def start_all(copies):
    for copy in copies:
        copy.start()


def wait_all(copies):
    for copy in copies:
        copy.wait()


def copies_of(sources, targets, sems, first=0):
    return [
        pltpu.make_async_copy(source, target, sems.at[first + n])
        for n, (source, target) in enumerate(zip(sources, targets))
    ]


def load_kernel(forces, velocity, lower, upper, cells, counts_hbm, send, *refs):
    near, work_out, (slots, counts, work, sems) = refs[:4], refs[4], refs[5:]
    components, senders, planes, capacity = forces.shape
    chunks = capacity // lanes
    sources = [forces.at[c] for c in range(components)]
    targets = [slots.at[c] for c in range(components)]
    sources += [counts_hbm, cells, lower, upper] + [velocity.at[c] for c in range(components)]
    targets += [counts, near[0], near[1], near[2]] + [near[3].at[c] for c in range(components)]
    copies = copies_of(sources, targets, sems)
    start_all(copies)
    outgoing = copies_of(
        targets[:components] + [work],
        [send.at[:, c] for c in range(components)] + [work_out],
        sems,
        len(copies),
    )
    for c in range(components):
        copies[c].wait()
        outgoing[c].start()
    copies[components].wait()

    def one_plane(x, n):
        def one_sender(s, n):
            count = counts[x, s]
            base = (x << plane_bit) + (((s * planes + x) * chunks) << count_bits)
            for k in range(chunks):
                live = jnp.maximum(count - k * lanes, 0)
                work[group + n + k] = base + (k << count_bits) + live
            return n + lax.div(count + lanes - 1, lanes)

        n = lax.fori_loop(0, senders, one_sender, n, unroll=2)
        for extra in range(group):
            work[group + n + extra] = x << plane_bit
        return lax.div(n + group - 1, group) * group

    total = lax.fori_loop(0, planes, one_plane, 0)
    for extra in range(2 * group):
        work[group + total + extra] = 0
    work[0] = lax.div(total + 2 * group - 1, 2 * group)
    outgoing[components].start()
    wait_all(copies[components + 1 :])
    wait_all(outgoing)


def edge_kernel(velocity, first_out, last_out, columns, turned):
    components, planes, height, across = velocity.shape
    lines = components * planes
    lane = lane_iota((height, across))
    picked = jnp.zeros((height, across), jnp.float32)
    for k in range(lines):
        rolled = pltpu.roll(velocity[k // planes, k % planes], 2 * k + 1, 1)
        picked = jnp.where((lane >> 1) == k, rolled, picked)
    columns[...] = picked
    for p in range(height // lanes):
        turned[p] = columns[p * lanes : (p + 1) * lanes, :].T
        part = slice(p * lines, (p + 1) * lines)
        first_out[part, :] = turned[p, pl.ds(1, lines, stride=2), :]
        last_out[part, :] = turned[p, pl.ds(0, lines, stride=2), :]


def prepare_kernel(cells, velocity, lower, upper, cell_rows, inner, ends, coefs, *refs):
    (rhs, inv, first) = refs[3:6]
    (inv_b, gain_b, rows, sems) = refs[6:]
    outgoing = copies_of(refs[3:6], refs[:3], sems)
    components, planes, height, across = velocity.shape
    steps = inv.shape[0] + 1
    last = steps - 1
    rest = height - segments * steps
    knots = segments + rest
    senders, capacity = cells.shape[0], cells.shape[2]
    chunks = capacity // lanes

    def one_sender(s, carry):
        for k in range(chunks):
            start = s * planes * chunks + k
            value = cells[s, :, k * lanes : (k + 1) * lanes]
            cell_rows[pl.ds(start, planes, stride=chunks), :] = value
        return carry

    lax.fori_loop(0, senders, one_sender, 0, unroll=4)

    def of_step(ref, t):
        return ref[:, pl.ds(t, segments, stride=steps), :]

    one = jnp.ones((planes, segments, across), jnp.float32)
    zero = jnp.zeros_like(one)
    size = 8
    lane = lane_iota((size, across))

    def stencil_rows(n):
        return pl.ds(pl.multiple_of(n * size, size), size)

    def read_rows(n):
        part = stencil_rows(n)
        return [[velocity[c, x, part, :] for x in range(planes)] for c in range(components)]

    def stencil(values):
        found = []
        for x in range(planes):
            v = values[x]
            around = values[(x - 1) % planes] + values[(x + 1) % planes]
            around = around + jnp.where(lane == 0, 0.0, pltpu.roll(v, 1, 1))
            around = around + jnp.where(lane == across - 1, 0.0, pltpu.roll(v, across - 1, 1))
            found.append((1.0 - 4.0 * diffusion_number) * v + diffusion_number * around)
        return found

    def write_rows(n, values):
        part = stencil_rows(n)
        for c in range(components):
            for x in range(planes):
                rhs[c, x, part, :] = values[c][x]

    def factor(t, carry):
        d, d_b, low_gain, high_gain, sum_last, sum_first = carry
        back = last - 1 - t
        low, up = of_step(lower, t), of_step(upper, t)
        low_b, up_b = of_step(lower, back), of_step(upper, back)
        velocities = read_rows(t)
        e = 1.0 + low * d
        inverse = reciprocal(up + e)
        g = low * inverse
        e_b = 1.0 + up_b * d_b
        inverse_b = reciprocal(low_b + e_b)
        g_b = up_b * inverse_b
        found = [stencil(values) for values in velocities]
        inv[t] = inverse
        inv_b[back] = inverse_b
        gain_b[back] = g_b
        write_rows(t, found)
        return (
            e * inverse,
            e_b * inverse_b,
            low_gain * g,
            high_gain * g_b,
            inverse + g * sum_last,
            inverse_b + g_b * sum_first,
        )

    carry = lax.fori_loop(0, last, factor, (one, one, one, one, zero, zero), unroll=2)
    _, _, low_gain, high_gain, sum_last, sum_first = carry
    for n in range(last, height // size):
        write_rows(n, [stencil(values) for values in read_rows(n)])
    start_all(outgoing[:2])
    def weigh(t, q):
        first[t] = inv_b[t] * q
        return q * gain_b[t]

    lax.fori_loop(0, last, weigh, one, unroll=6)
    outgoing[2].start()

    low_sep, up_sep = of_step(lower, last), of_step(upper, last)
    segment = lax.broadcasted_iota(jnp.int32, one.shape, 1)
    is_end = segment == segments - 1
    above = jnp.where(is_end, 0.0, jnp.roll(sum_first, -1, axis=1))
    couple_high = up_sep * jnp.where(is_end, 1.0, jnp.roll(high_gain, -1, axis=1))
    killing = 1.0 + low_sep * sum_last + up_sep * above
    ends[2, :, :segments, :] = low_sep
    ends[3, :, :segments, :] = up_sep
    tail = slice(height - rest, height)
    low_rest, up_rest = lower[:, tail, :], upper[:, tail, :]
    for n, (value, other) in enumerate(
        (
            (low_sep * low_gain, low_rest),
            (couple_high, up_rest),
            (killing, jnp.ones_like(low_rest)),
        )
    ):
        for x in range(planes):
            rows[n, x * knots : x * knots + segments, :] = value[x]
            rows[n, x * knots + segments : (x + 1) * knots, :] = other[x]
    for x in range(planes):
        rows[3, x * knots : x * knots + segments, :] = high_gain[x]
        rows[4, x * knots : x * knots + segments, :] = sum_first[x]

    def row(n, s):
        return rows[n, pl.ds(s, planes, stride=knots), :]

    top = knots - 1
    one_row = jnp.ones((planes, across), jnp.float32)
    d, d_b = one_row, one_row
    inv_s, gain_s, ratio_s = [], [], []
    inv_sb, gain_sb = [None] * top, [None] * top
    for s in range(top):
        e = row(2, s) + row(0, s) * d
        inverse = reciprocal(row(1, s) + e)
        inv_s.append(inverse)
        gain_s.append(row(0, s) * inverse)
        ratio_s.append(row(1, s) * inverse)
        d = e * inverse
        back = top - 1 - s
        e_b = row(2, back) + row(1, back) * d_b
        inverse_b = reciprocal(row(0, back) + e_b)
        inv_sb[back] = inverse_b
        gain_sb[back] = row(1, back) * inverse_b
        d_b = e_b * inverse_b
        inner[0, s] = inv_s[s]
        inner[1, s] = gain_s[s]
        inner[2, s] = ratio_s[s]
    run = row(0, top)
    low_total = one_row
    sum_top = one_row
    rows[5, pl.ds(top, planes, stride=knots), :] = one_row
    for s in reversed(range(top)):
        weight = run * inv_s[s]
        rows[5, pl.ds(s, planes, stride=knots), :] = weight
        sum_top = sum_top + weight * row(2, s)
        run = run * gain_s[s]
        low_total = low_total * gain_s[s]
    run = row(3, 0)
    high_total = one_row
    sum_bottom = row(4, 0)
    rows[6, pl.ds(top, planes, stride=knots), :] = jnp.zeros_like(one_row)
    for s in range(top):
        weight = run * inv_sb[s]
        rows[6, pl.ds(s, planes, stride=knots), :] = weight
        sum_bottom = sum_bottom + weight * row(2, s)
        run = run * gain_sb[s]
        high_total = high_total * ratio_s[s]
    coef = (
        row(0, top) * low_total,
        sum_top,
        row(1, top),
        sum_bottom,
        row(3, 0) * high_total,
    )
    for n, value in enumerate(coef):
        coefs[n * planes : (n + 1) * planes, :] = value
    for n in range(2):
        for x in range(planes):
            ends[n, x] = rows[5 + n, x * knots : (x + 1) * knots, :]
    wait_all(outgoing)


def deposit_kernel(got, from_above, from_below, cell_rows, ends, coefs, *refs):
    (deposit_hbm, swept, prefix, reduced, sums) = refs[5:10]
    (work, rhs, inv, first, lower) = refs[10:15]
    (slots, field, total, lefts, rights, columns, edges, in_sems, sems) = refs[15:]
    incoming = copies_of(refs[:5], refs[10:15], in_sems)
    start_all(incoming)
    components, planes, height, across = rhs.shape
    steps = inv.shape[0] + 1
    last = steps - 1
    knots = ends.shape[2]
    rest = knots - segments
    senders, _, _, capacity = got.shape
    chunks = capacity // lanes
    parts = height // lanes
    shift = across.bit_length() - 1
    lines = components * planes
    kind = jnp.bfloat16 if max(height, across) <= 256 else jnp.float32

    def one_sender(s, carry):
        for c in range(components):
            for k in range(chunks):
                start = (s * planes * chunks + k) * components + c
                value = got[s, c, :, k * lanes : (k + 1) * lanes]
                slots[pl.ds(start, planes, stride=chunks * components), :] = value
        return carry

    lax.fori_loop(0, senders, one_sender, 0)
    total[...] = jnp.zeros_like(total)
    for p in range(parts):
        part = slice(p * lines, (p + 1) * lines)
        columns[p, pl.ds(0, lines, stride=2), :] = from_above[part, :]
        columns[p, pl.ds(1, lines, stride=2), :] = from_below[part, :]
        edges[p * lanes : (p + 1) * lanes, :] = diffusion_number * columns[p].T

    tile = 16
    base = lax.broadcasted_iota(jnp.int32, (tile, lanes), 0)
    height_ids = [(base + n * tile).astype(jnp.float32).astype(kind) for n in range(height // tile)]
    across_ids = height_ids[: across // tile]
    lane = lane_iota((1, lanes))
    one = jnp.ones((tile, lanes), jnp.bfloat16)
    none = jnp.zeros((tile, lanes), jnp.bfloat16)

    def spread(row, to):
        return jnp.broadcast_to(row, (tile, lanes)).astype(to)

    def build(n, half, chosen=range(group)):
        for g in chosen:
            word = work[(n + 1) * group + g]
            ident = (word >> count_bits) & ((1 << (plane_bit - count_bits)) - 1)
            live = word & ((1 << count_bits) - 1)
            there = slice(g * lanes, (g + 1) * lanes)
            cell = cell_rows[pl.ds(ident, 1), :]
            up = jnp.where(lane < live, cell >> shift, -1).astype(jnp.float32)
            side = (cell & (across - 1)).astype(jnp.float32)
            up, side = spread(up, kind), spread(side, kind)
            for i, ids in enumerate(height_ids):
                lefts[half][i * tile : (i + 1) * tile, there] = jnp.where(up == ids, one, none)
            masks = [side == ids for ids in across_ids]
            for c in range(components):
                force = slots[pl.ds(ident * components + c, 1), :]
                rest_of = force - force.astype(jnp.bfloat16).astype(jnp.float32)
                for m, value in enumerate((force, rest_of)):
                    value = spread(value, jnp.bfloat16)
                    start = (m * components + c) * across
                    for i, mask in enumerate(masks):
                        place = slice(start + i * tile, start + (i + 1) * tile)
                        rights[half][place, there] = jnp.where(mask, value, none)

    parted = 3
    columns_each = 2 * components * across // parted

    def add(n, half, part):
        place = slice(part * columns_each, (part + 1) * columns_each)
        total[work[(n + 1) * group] >> plane_bit, :, place] += lax.dot_general(
            lefts[half][...],
            rights[half][place, :],
            (((1,), (1,)), ((), ())),
            preferred_element_type=jnp.float32,
        )

    def step(n, half):
        for part in range(parted):
            chosen = range(part * group // parted, (part + 1) * group // parted)
            build(n + 1, 1 - half, chosen)
            add(n, half, part)

    def two_steps(n, carry):
        step(2 * n, 0)
        step(2 * n + 1, 1)
        return carry

    incoming[0].wait()
    build(0, 0)
    lax.fori_loop(0, work[0], two_steps, 0)
    wait_all(incoming[1:])

    wide = lane_iota((lanes, across))
    border = (wide == 0) | (wide == across - 1)

    def place(x):
        return [
            pltpu.make_async_copy(field.at[c, x], deposit_hbm.at[c, x], sems.at[c, x])
            for c in range(components)
        ]

    def combine(x, carry):
        for c in range(components):
            for p in range(parts):
                part = slice(p * lanes, (p + 1) * lanes)
                high = total[x, part, c * across : (c + 1) * across]
                low = total[x, part, (components + c) * across : (components + c + 1) * across]
                value = high + low
                field[c, x, part, :] = value.astype(jnp.bfloat16)
                edge = pltpu.roll(edges[part, :], lanes - 1 - 2 * (c * planes + x), 1)
                rhs[c, x, part, :] = rhs[c, x, part, :] + value + jnp.where(border, edge, 0.0)
        start_all(place(x))
        return carry

    lax.fori_loop(0, planes, combine, 0)
    sums[2 * lines : 2 * lines + coefs.shape[0], :] = coefs[...]

    zero = jnp.zeros((components, planes, segments, across), jnp.float32)

    def of_step(t):
        return rhs[:, :, pl.ds(t, segments, stride=steps), :]

    def forward(t, carry):
        value, start, run, before = carry
        force = of_step(t)
        low, inverse = lower[:, pl.ds(t, segments, stride=steps), :], inv[t]
        value = force + (low * before)[None] * value
        swept[t] = inverse[None] * value
        run = run * (low * inverse)
        prefix[t] = run
        return value, start + first[t][None] * force, run, inverse

    one = jnp.ones((planes, segments, across), jnp.float32)
    value, start, _, inverse = lax.fori_loop(0, last, forward, (zero, zero, one, one), unroll=3)
    value = inverse[None] * value
    segment = lax.broadcasted_iota(jnp.int32, zero.shape, 2)
    after = jnp.where(segment == segments - 1, 0.0, jnp.roll(start, -1, axis=2))
    low_sep, up_sep = ends[2, :, :segments, :], ends[3, :, :segments, :]
    value = of_step(last) + low_sep[None] * value + up_sep[None] * after
    others = rhs[:, :, height - rest :, :]
    at_top = ends[0, :, :segments, :][None] * value + ends[0, :, segments:, :][None] * others
    at_bottom = ends[1, :, :segments, :][None] * value + ends[1, :, segments:, :][None] * others
    at_bottom = at_bottom + jnp.where(segment == 0, start, 0.0)
    for c in range(components):
        for x in range(planes):
            k = c * planes + x
            reduced[k * knots : k * knots + segments, :] = value[c, x]
            reduced[k * knots + segments : (k + 1) * knots, :] = others[c, x]
            sums[k : k + 1, :] = jnp.sum(at_top[c, x], 0, keepdims=True)
            sums[lines + k : lines + k + 1, :] = jnp.sum(at_bottom[c, x], 0, keepdims=True)

    for x in range(planes):
        wait_all(place(x))


def finish_kernel(inner, reduced, swept, inv, prefix, upper, *refs):
    walls = len(refs) - 7
    received = refs[:walls]
    out_hbm, sums, tops, after, before, out, sems = refs[walls:]
    components, planes, height, across = out.shape
    steps = swept.shape[0] + 1
    last = steps - 1
    lines = components * planes
    knots = inner.shape[1] + 1
    rest = knots - segments
    me = lax.axis_index("wall")
    for n in range(walls):
        sums[lax.rem(me + walls - n, walls)] = received[n][...]

    def coef(k, n):
        start = 2 * lines + n * planes
        return sums[k, start : start + planes, :]

    def wide(value):
        return jnp.concatenate([value] * components, 0)

    d = jnp.ones((planes, across), jnp.float32)
    value = jnp.zeros((lines, across), jnp.float32)
    values, ratios = [], []
    for k in range(walls):
        low, own, up = coef(k, 0), coef(k, 1), coef(k, 2)
        right = sums[k, :lines, :]
        if k + 1 < walls:
            high = up * coef(k + 1, 4)
            killing = own + up * coef(k + 1, 3)
            right = right + wide(up) * sums[k + 1, lines : 2 * lines, :]
        else:
            high = jnp.zeros_like(up)
            killing = own + up
        e = killing + low * d
        inverse = reciprocal(high + e)
        d = e * inverse
        value = (right + wide(low) * value) * wide(inverse)
        values.append(value)
        ratios.append(wide(high * inverse))
    tops[0] = jnp.zeros((lines, across), jnp.float32)
    tops[walls] = values[-1]
    for k in reversed(range(walls - 1)):
        values[k] = values[k] + ratios[k] * values[k + 1]
        tops[k + 1] = values[k]

    def row(s):
        return pl.ds(s, lines, stride=knots)

    run = tops[me]
    before[row(0), :] = run
    found = []
    for s in range(knots - 1):
        run = reduced[row(s), :] * wide(inner[0, s]) + wide(inner[1, s]) * run
        found.append(run)
    run = tops[me + 1]
    after[row(knots - 1), :] = run
    for s in reversed(range(knots - 1)):
        run = found[s] + wide(inner[2, s]) * run
        after[row(s), :] = run
        if s + 1 < segments:
            before[row(s + 1), :] = run

    def put(c, x, t, value):
        out[c, x, pl.ds(t, segments, stride=steps), :] = value

    copies = []
    half = planes // 2 if planes % 2 == 0 else planes
    for start in range(0, planes, half):
        part = [(c, x) for c in range(components) for x in range(start, start + half)]
        bottoms, starts = [], []
        for c, x in part:
            base = (c * planes + x) * knots
            bottoms.append(before[base : base + segments, :])
            starts.append(after[base : base + segments, :])
            out[c, x, height - rest :, :] = after[base + segments : base + knots, :]
            put(c, x, last, starts[-1])

        def backward(n, values):
            t = last - 1 - n
            found = []
            ratios = {}
            for x in range(start, start + half):
                ratios[x] = upper[x, pl.ds(t, segments, stride=steps), :] * inv[t, x]
            for (c, x), value, bottom in zip(part, values, bottoms):
                value = (swept[t, c, x] + prefix[t, x] * bottom) + ratios[x] * value
                put(c, x, t, value)
                found.append(value)
            return tuple(found)

        lax.fori_loop(0, last, backward, tuple(starts), unroll=5)
        for here in part:
            copy = pltpu.make_async_copy(out.at[here], out_hbm.at[here], sems.at[here])
            copy.start()
            copies.append(copy)
    wait_all(copies)


def shifted(block, axis, distance):
    length = lax.axis_size(axis)
    route = [(i, (i + distance) % length) for i in range(length)]
    return lax.ppermute(block, axis, route)


def everyone(block, axis):
    return [block] + [shifted(block, axis, n) for n in range(1, lax.axis_size(axis))]


def local(velocity, lower_weight, upper_weight, forces, cells, counts):
    components, planes, height, across = velocity.shape
    receivers, capacity = forces.shape[3], forces.shape[5]
    senders = cells.shape[2]
    walls = lax.axis_size("wall")
    lines = components * planes
    chunks = capacity // lanes
    counts_shape, cells_shape = (planes, senders), (senders, planes, capacity)
    forces = forces.reshape(components, receivers, planes, capacity)
    cells = cells.reshape(senders, planes, capacity)
    counts = counts.reshape(senders, planes).T

    def hbm(*arrays):
        return [pltpu.with_memory_space_constraint(array, pltpu.HBM) for array in arrays]

    work_shape = (planes * (senders * chunks + group) + 4 * group,)
    send, cells_near, lower_near, upper_near, velocity_near, work = call(
        load_kernel,
        (
            pltpu.HBM((receivers, components, planes, capacity), jnp.float32),
            jax.ShapeDtypeStruct(cells_shape, jnp.int32),
            f32(*lower_weight.shape),
            f32(*upper_weight.shape),
            f32(*velocity.shape),
            jax.ShapeDtypeStruct(work_shape, jnp.int32),
        ),
        (in_hbm, *[in_vmem] * 5),
        [in_hbm] * 6,
        [
            scratch(*forces.shape),
            pltpu.SMEM(counts_shape, jnp.int32),
            pltpu.SMEM(work_shape, jnp.int32),
            pltpu.SemaphoreType.DMA((3 * components + 5,)),
        ],
        4,
        1 << 16,
    )(*hbm(forces, velocity, lower_weight, upper_weight, cells, counts))
    got = lax.all_to_all(send, "span", 0, 0, tiled=True)
    edge_shape = (lines * height // lanes, lanes)
    first_column, last_column = call(
        edge_kernel,
        (f32(*edge_shape), f32(*edge_shape)),
        (in_vmem, in_vmem),
        [in_vmem],
        [scratch(height, across), scratch(height // lanes, lanes, lanes)],
        4,
        1 << 20,
    )(velocity_near)
    from_above = shifted(first_column, "span", -1)
    from_below = shifted(last_column, "span", 1)

    steps = height // segments - 1
    knots = height - segments * steps + segments
    step_shape = (steps - 1, planes, segments, across)
    staged = [velocity.shape, step_shape, step_shape]
    prepared = call(
        prepare_kernel,
        (
            jax.ShapeDtypeStruct((senders * planes * chunks, lanes), jnp.int32),
            f32(3, knots - 1, planes, across),
            f32(4, planes, knots, across),
            f32(5 * planes, across),
            *[pltpu.HBM(shape, jnp.float32) for shape in staged],
        ),
        [in_vmem] * 4 + [in_hbm] * 3,
        [in_vmem] * 4,
        [
            *[scratch(*shape) for shape in staged],
            scratch(*step_shape),
            scratch(*step_shape),
            scratch(7, planes * knots, across),
            pltpu.SemaphoreType.DMA((3,)),
        ],
        12,
        1 << 24,
    )(cells_near, velocity_near, lower_near, upper_near)
    (cell_rows, inner, ends, coefs, rhs_start, inv, first) = prepared

    sum_rows = -(-(2 * lines + 5 * planes) // 8) * 8
    wide = 2 * components * across
    deposit, swept, prefix, reduced, sums = call(
        deposit_kernel,
        (
            jax.ShapeDtypeStruct(velocity.shape, jnp.bfloat16),
            f32(steps - 1, components, planes, segments, across),
            f32(*step_shape),
            f32(lines * knots, across),
            f32(sum_rows, across),
        ),
        (in_hbm, *[in_vmem] * 4),
        [in_vmem] * 7 + [in_hbm] * 4,
        [
            pltpu.SMEM(work_shape, jnp.int32),
            *[scratch(*shape) for shape in staged],
            scratch(*lower_weight.shape),
            scratch(senders * planes * chunks * components, lanes),
            pltpu.VMEM(velocity.shape, jnp.bfloat16),
            scratch(planes, height, wide),
            [pltpu.VMEM((height, group * lanes), jnp.bfloat16)] * 2,
            [pltpu.VMEM((wide, group * lanes), jnp.bfloat16)] * 2,
            scratch(height // lanes, lanes, lanes),
            scratch(height, lanes),
            pltpu.SemaphoreType.DMA((5,)),
            pltpu.SemaphoreType.DMA((components, planes)),
        ],
        24,
        1 << 32,
    )(
        got,
        from_above,
        from_below,
        cell_rows,
        ends,
        coefs,
        work,
        *hbm(rhs_start, inv, first, lower_weight),
    )
    all_sums = everyone(sums, "wall")

    velocity_next = call(
        finish_kernel,
        f32(*velocity.shape),
        in_hbm,
        [in_vmem] * (6 + walls),
        [
            scratch(walls, sum_rows, across),
            scratch(walls + 1, lines, across),
            scratch(lines * knots, across),
            scratch(lines * knots, across),
            scratch(*velocity.shape),
            pltpu.SemaphoreType.DMA((components, planes)),
        ],
        8,
        1 << 22,
    )(inner, reduced, swept, inv, prefix, upper_weight, *all_sums)
    return (velocity_next, deposit)


def solution(mesh):
    placed = (
        P(None, None, "wall", "span"),
        P(None, "wall", "span"),
        P(None, "wall", "span"),
        P(None, "wall", "span", None, None, None),
        P("wall", "span", None, None, None),
        P("wall", "span", None, None),
    )
    return jax.shard_map(
        local,
        mesh=mesh,
        in_specs=placed,
        out_specs=(P(None, None, "wall", "span"), P(None, None, "wall", "span")),
        check_vma=False,
    )
```

```python
import jax
import jax.numpy as jnp
from jax import lax
from jax.experimental import pallas as pl
from jax.experimental.pallas import tpu as pltpu
from jax.sharding import PartitionSpec as P

diffusion_number = 0.2
segments = 8
lanes = 128
group = 16
count_bits, plane_bit = 10, 24
in_vmem = pl.BlockSpec(memory_space=pltpu.VMEM)
in_smem = pl.BlockSpec(memory_space=pltpu.SMEM)
in_hbm = pl.BlockSpec(memory_space=pltpu.HBM)


def call(body, out_shape, out_specs, in_specs, scratch, mebibytes, flops):
    return pl.pallas_call(
        body,
        out_shape=out_shape,
        in_specs=in_specs,
        out_specs=out_specs,
        scratch_shapes=scratch,
        compiler_params=pltpu.CompilerParams(vmem_limit_bytes=mebibytes << 20),
        cost_estimate=pl.CostEstimate(flops=flops, bytes_accessed=4 << 20, transcendentals=0),
    )


def f32(*shape):
    return jax.ShapeDtypeStruct(shape, jnp.float32)


def scratch(*shape):
    return pltpu.VMEM(shape, jnp.float32)


def lane_iota(shape):
    return lax.broadcasted_iota(jnp.int32, shape, len(shape) - 1)


def reciprocal(value):
    rough = pl.reciprocal(value, approx=True)
    return rough * (2.0 - value * rough)


def start_all(copies):
    for copy in copies:
        copy.start()


def wait_all(copies):
    for copy in copies:
        copy.wait()


def copies_of(sources, targets, sems, first=0):
    return [
        pltpu.make_async_copy(source, target, sems.at[first + n])
        for n, (source, target) in enumerate(zip(sources, targets))
    ]


def load_kernel(forces, velocity, lower, upper, cells, counts_hbm, send, *refs):
    near, work_out, (slots, counts, work, sems) = refs[:4], refs[4], refs[5:]
    components, senders, planes, capacity = forces.shape
    chunks = capacity // lanes
    sources = [forces.at[c] for c in range(components)]
    targets = [slots.at[c] for c in range(components)]
    sources += [counts_hbm, cells, lower, upper] + [velocity.at[c] for c in range(components)]
    targets += [counts, near[0], near[1], near[2]] + [near[3].at[c] for c in range(components)]
    copies = copies_of(sources, targets, sems)
    start_all(copies)
    outgoing = copies_of(
        targets[:components] + [work],
        [send.at[:, c] for c in range(components)] + [work_out],
        sems,
        len(copies),
    )
    for c in range(components):
        copies[c].wait()
        outgoing[c].start()
    copies[components].wait()

    def one_plane(x, n):
        def one_sender(s, n):
            count = counts[x, s]
            base = (x << plane_bit) + (((s * planes + x) * chunks) << count_bits)
            for k in range(chunks):
                live = jnp.maximum(count - k * lanes, 0)
                work[group + n + k] = base + (k << count_bits) + live
            return n + lax.div(count + lanes - 1, lanes)

        n = lax.fori_loop(0, senders, one_sender, n, unroll=2)
        for extra in range(group):
            work[group + n + extra] = x << plane_bit
        return lax.div(n + group - 1, group) * group

    total = lax.fori_loop(0, planes, one_plane, 0)
    work[0] = lax.div(total, group)
    outgoing[components].start()
    wait_all(copies[components + 1 :])
    wait_all(outgoing)


def edge_kernel(velocity, first_out, last_out, columns, turned):
    components, planes, height, across = velocity.shape
    lines = components * planes
    lane = lane_iota((height, across))
    picked = jnp.zeros((height, across), jnp.float32)
    for k in range(lines):
        rolled = pltpu.roll(velocity[k // planes, k % planes], 2 * k + 1, 1)
        picked = jnp.where((lane >> 1) == k, rolled, picked)
    columns[...] = picked
    for p in range(height // lanes):
        turned[p] = columns[p * lanes : (p + 1) * lanes, :].T
        part = slice(p * lines, (p + 1) * lines)
        first_out[part, :] = turned[p, pl.ds(1, lines, stride=2), :]
        last_out[part, :] = turned[p, pl.ds(0, lines, stride=2), :]


def prepare_kernel(cells, velocity, lower, upper, cell_rows, inner, ends, coefs, *refs):
    (rhs, inv, first) = refs[3:6]
    (inv_b, gain_b, rows, sems) = refs[6:]
    outgoing = copies_of(refs[3:6], refs[:3], sems)
    components, planes, height, across = velocity.shape
    steps = inv.shape[0] + 1
    last = steps - 1
    rest = height - segments * steps
    knots = segments + rest
    senders, capacity = cells.shape[0], cells.shape[2]
    chunks = capacity // lanes

    def one_sender(s, carry):
        for k in range(chunks):
            start = s * planes * chunks + k
            value = cells[s, :, k * lanes : (k + 1) * lanes]
            cell_rows[pl.ds(start, planes, stride=chunks), :] = value
        return carry

    lax.fori_loop(0, senders, one_sender, 0, unroll=4)

    def of_step(ref, t):
        return ref[:, pl.ds(t, segments, stride=steps), :]

    one = jnp.ones((planes, segments, across), jnp.float32)
    zero = jnp.zeros_like(one)
    size = 8
    lane = lane_iota((size, across))

    def stencil_rows(n):
        return pl.ds(pl.multiple_of(n * size, size), size)

    def read_rows(n):
        part = stencil_rows(n)
        return [[velocity[c, x, part, :] for x in range(planes)] for c in range(components)]

    def stencil(values):
        found = []
        for x in range(planes):
            v = values[x]
            around = values[(x - 1) % planes] + values[(x + 1) % planes]
            around = around + jnp.where(lane == 0, 0.0, pltpu.roll(v, 1, 1))
            around = around + jnp.where(lane == across - 1, 0.0, pltpu.roll(v, across - 1, 1))
            found.append((1.0 - 4.0 * diffusion_number) * v + diffusion_number * around)
        return found

    def write_rows(n, values):
        part = stencil_rows(n)
        for c in range(components):
            for x in range(planes):
                rhs[c, x, part, :] = values[c][x]

    def factor(t, carry):
        d, d_b, low_gain, high_gain, sum_last, sum_first = carry
        back = last - 1 - t
        low, up = of_step(lower, t), of_step(upper, t)
        low_b, up_b = of_step(lower, back), of_step(upper, back)
        velocities = read_rows(t)
        e = 1.0 + low * d
        inverse = reciprocal(up + e)
        g = low * inverse
        e_b = 1.0 + up_b * d_b
        inverse_b = reciprocal(low_b + e_b)
        g_b = up_b * inverse_b
        found = [stencil(values) for values in velocities]
        inv[t] = inverse
        inv_b[back] = inverse_b
        gain_b[back] = g_b
        write_rows(t, found)
        return (
            e * inverse,
            e_b * inverse_b,
            low_gain * g,
            high_gain * g_b,
            inverse + g * sum_last,
            inverse_b + g_b * sum_first,
        )

    carry = lax.fori_loop(0, last, factor, (one, one, one, one, zero, zero), unroll=2)
    _, _, low_gain, high_gain, sum_last, sum_first = carry
    for n in range(last, height // size):
        write_rows(n, [stencil(values) for values in read_rows(n)])
    start_all(outgoing[:2])
    def weigh(t, q):
        first[t] = inv_b[t] * q
        return q * gain_b[t]

    lax.fori_loop(0, last, weigh, one, unroll=6)
    outgoing[2].start()

    low_sep, up_sep = of_step(lower, last), of_step(upper, last)
    segment = lax.broadcasted_iota(jnp.int32, one.shape, 1)
    is_end = segment == segments - 1
    above = jnp.where(is_end, 0.0, jnp.roll(sum_first, -1, axis=1))
    couple_high = up_sep * jnp.where(is_end, 1.0, jnp.roll(high_gain, -1, axis=1))
    killing = 1.0 + low_sep * sum_last + up_sep * above
    ends[2, :, :segments, :] = low_sep
    ends[3, :, :segments, :] = up_sep
    tail = slice(height - rest, height)
    low_rest, up_rest = lower[:, tail, :], upper[:, tail, :]
    for n, (value, other) in enumerate(
        (
            (low_sep * low_gain, low_rest),
            (couple_high, up_rest),
            (killing, jnp.ones_like(low_rest)),
        )
    ):
        for x in range(planes):
            rows[n, x * knots : x * knots + segments, :] = value[x]
            rows[n, x * knots + segments : (x + 1) * knots, :] = other[x]
    for x in range(planes):
        rows[3, x * knots : x * knots + segments, :] = high_gain[x]
        rows[4, x * knots : x * knots + segments, :] = sum_first[x]

    def row(n, s):
        return rows[n, pl.ds(s, planes, stride=knots), :]

    top = knots - 1
    one_row = jnp.ones((planes, across), jnp.float32)
    d, d_b = one_row, one_row
    inv_s, gain_s, ratio_s = [], [], []
    inv_sb, gain_sb = [None] * top, [None] * top
    for s in range(top):
        e = row(2, s) + row(0, s) * d
        inverse = reciprocal(row(1, s) + e)
        inv_s.append(inverse)
        gain_s.append(row(0, s) * inverse)
        ratio_s.append(row(1, s) * inverse)
        d = e * inverse
        back = top - 1 - s
        e_b = row(2, back) + row(1, back) * d_b
        inverse_b = reciprocal(row(0, back) + e_b)
        inv_sb[back] = inverse_b
        gain_sb[back] = row(1, back) * inverse_b
        d_b = e_b * inverse_b
        inner[0, s] = inv_s[s]
        inner[1, s] = gain_s[s]
        inner[2, s] = ratio_s[s]
    run = row(0, top)
    low_total = one_row
    sum_top = one_row
    rows[5, pl.ds(top, planes, stride=knots), :] = one_row
    for s in reversed(range(top)):
        weight = run * inv_s[s]
        rows[5, pl.ds(s, planes, stride=knots), :] = weight
        sum_top = sum_top + weight * row(2, s)
        run = run * gain_s[s]
        low_total = low_total * gain_s[s]
    run = row(3, 0)
    high_total = one_row
    sum_bottom = row(4, 0)
    rows[6, pl.ds(top, planes, stride=knots), :] = jnp.zeros_like(one_row)
    for s in range(top):
        weight = run * inv_sb[s]
        rows[6, pl.ds(s, planes, stride=knots), :] = weight
        sum_bottom = sum_bottom + weight * row(2, s)
        run = run * gain_sb[s]
        high_total = high_total * ratio_s[s]
    coef = (
        row(0, top) * low_total,
        sum_top,
        row(1, top),
        sum_bottom,
        row(3, 0) * high_total,
    )
    for n, value in enumerate(coef):
        coefs[n * planes : (n + 1) * planes, :] = value
    for n in range(2):
        for x in range(planes):
            ends[n, x] = rows[5 + n, x * knots : (x + 1) * knots, :]
    wait_all(outgoing)


def deposit_kernel(got, from_above, from_below, cell_rows, ends, coefs, *refs):
    (deposit_hbm, swept, prefix, reduced, sums) = refs[5:10]
    (work, rhs, inv, first, lower) = refs[10:15]
    (slots, field, total, left, right, columns, edges, in_sems, sems) = refs[15:]
    incoming = copies_of(refs[:5], refs[10:15], in_sems)
    start_all(incoming)
    components, planes, height, across = rhs.shape
    steps = inv.shape[0] + 1
    last = steps - 1
    knots = ends.shape[2]
    rest = knots - segments
    senders, _, _, capacity = got.shape
    chunks = capacity // lanes
    parts = height // lanes
    shift = across.bit_length() - 1
    lines = components * planes
    kind = jnp.bfloat16 if max(height, across) <= 256 else jnp.float32

    def one_sender(s, carry):
        for c in range(components):
            for k in range(chunks):
                start = (s * planes * chunks + k) * components + c
                value = got[s, c, :, k * lanes : (k + 1) * lanes]
                slots[pl.ds(start, planes, stride=chunks * components), :] = value
        return carry

    lax.fori_loop(0, senders, one_sender, 0)
    total[...] = jnp.zeros_like(total)
    for p in range(parts):
        part = slice(p * lines, (p + 1) * lines)
        columns[p, pl.ds(0, lines, stride=2), :] = from_above[part, :]
        columns[p, pl.ds(1, lines, stride=2), :] = from_below[part, :]
        edges[p * lanes : (p + 1) * lanes, :] = diffusion_number * columns[p].T

    tile = 16
    base = lax.broadcasted_iota(jnp.int32, (tile, lanes), 0)
    height_ids = [(base + n * tile).astype(jnp.float32).astype(kind) for n in range(height // tile)]
    across_ids = height_ids[: across // tile]
    lane = lane_iota((1, lanes))
    one = jnp.ones((tile, lanes), jnp.bfloat16)
    none = jnp.zeros((tile, lanes), jnp.bfloat16)

    def spread(row, to):
        return jnp.broadcast_to(row, (tile, lanes)).astype(to)

    def build(n):
        for g in range(group):
            word = work[(n + 1) * group + g]
            ident = (word >> count_bits) & ((1 << (plane_bit - count_bits)) - 1)
            live = word & ((1 << count_bits) - 1)
            there = slice(g * lanes, (g + 1) * lanes)
            cell = cell_rows[pl.ds(ident, 1), :]
            up = jnp.where(lane < live, cell >> shift, -1).astype(jnp.float32)
            side = (cell & (across - 1)).astype(jnp.float32)
            up, side = spread(up, kind), spread(side, kind)
            for i, ids in enumerate(height_ids):
                left[i * tile : (i + 1) * tile, there] = jnp.where(up == ids, one, none)
            masks = [side == ids for ids in across_ids]
            for c in range(components):
                force = slots[pl.ds(ident * components + c, 1), :]
                rest_of = force - force.astype(jnp.bfloat16).astype(jnp.float32)
                for m, value in enumerate((force, rest_of)):
                    value = spread(value, jnp.bfloat16)
                    start = (m * components + c) * across
                    for i, mask in enumerate(masks):
                        place = slice(start + i * tile, start + (i + 1) * tile)
                        right[place, there] = jnp.where(mask, value, none)

    def step(n, carry):
        build(n)
        total[work[(n + 1) * group] >> plane_bit] += lax.dot_general(
            left[...],
            right[...],
            (((1,), (1,)), ((), ())),
            preferred_element_type=jnp.float32,
        )
        return carry

    incoming[0].wait()
    lax.fori_loop(0, work[0], step, 0)
    wait_all(incoming[1:])

    wide = lane_iota((lanes, across))
    border = (wide == 0) | (wide == across - 1)

    def place(x):
        return [
            pltpu.make_async_copy(field.at[c, x], deposit_hbm.at[c, x], sems.at[c, x])
            for c in range(components)
        ]

    def combine(x, carry):
        for c in range(components):
            for p in range(parts):
                part = slice(p * lanes, (p + 1) * lanes)
                high = total[x, part, c * across : (c + 1) * across]
                low = total[x, part, (components + c) * across : (components + c + 1) * across]
                value = high + low
                field[c, x, part, :] = value.astype(jnp.bfloat16)
                edge = pltpu.roll(edges[part, :], lanes - 1 - 2 * (c * planes + x), 1)
                rhs[c, x, part, :] = rhs[c, x, part, :] + value + jnp.where(border, edge, 0.0)
        start_all(place(x))
        return carry

    lax.fori_loop(0, planes, combine, 0)
    sums[2 * lines : 2 * lines + coefs.shape[0], :] = coefs[...]

    zero = jnp.zeros((components, planes, segments, across), jnp.float32)

    def of_step(t):
        return rhs[:, :, pl.ds(t, segments, stride=steps), :]

    def forward(t, carry):
        value, start, run, before = carry
        force = of_step(t)
        low, inverse = lower[:, pl.ds(t, segments, stride=steps), :], inv[t]
        value = force + (low * before)[None] * value
        swept[t] = inverse[None] * value
        run = run * (low * inverse)
        prefix[t] = run
        return value, start + first[t][None] * force, run, inverse

    one = jnp.ones((planes, segments, across), jnp.float32)
    value, start, _, inverse = lax.fori_loop(0, last, forward, (zero, zero, one, one), unroll=3)
    value = inverse[None] * value
    segment = lax.broadcasted_iota(jnp.int32, zero.shape, 2)
    after = jnp.where(segment == segments - 1, 0.0, jnp.roll(start, -1, axis=2))
    low_sep, up_sep = ends[2, :, :segments, :], ends[3, :, :segments, :]
    value = of_step(last) + low_sep[None] * value + up_sep[None] * after
    others = rhs[:, :, height - rest :, :]
    at_top = ends[0, :, :segments, :][None] * value + ends[0, :, segments:, :][None] * others
    at_bottom = ends[1, :, :segments, :][None] * value + ends[1, :, segments:, :][None] * others
    at_bottom = at_bottom + jnp.where(segment == 0, start, 0.0)
    for c in range(components):
        for x in range(planes):
            k = c * planes + x
            reduced[k * knots : k * knots + segments, :] = value[c, x]
            reduced[k * knots + segments : (k + 1) * knots, :] = others[c, x]
            sums[k : k + 1, :] = jnp.sum(at_top[c, x], 0, keepdims=True)
            sums[lines + k : lines + k + 1, :] = jnp.sum(at_bottom[c, x], 0, keepdims=True)

    for x in range(planes):
        wait_all(place(x))


def finish_kernel(inner, reduced, swept, inv, prefix, upper, *refs):
    walls = len(refs) - 7
    received = refs[:walls]
    out_hbm, sums, tops, after, before, out, sems = refs[walls:]
    components, planes, height, across = out.shape
    steps = swept.shape[0] + 1
    last = steps - 1
    lines = components * planes
    knots = inner.shape[1] + 1
    rest = knots - segments
    me = lax.axis_index("wall")
    for n in range(walls):
        sums[lax.rem(me + walls - n, walls)] = received[n][...]

    def coef(k, n):
        start = 2 * lines + n * planes
        return sums[k, start : start + planes, :]

    def wide(value):
        return jnp.concatenate([value] * components, 0)

    d = jnp.ones((planes, across), jnp.float32)
    value = jnp.zeros((lines, across), jnp.float32)
    values, ratios = [], []
    for k in range(walls):
        low, own, up = coef(k, 0), coef(k, 1), coef(k, 2)
        right = sums[k, :lines, :]
        if k + 1 < walls:
            high = up * coef(k + 1, 4)
            killing = own + up * coef(k + 1, 3)
            right = right + wide(up) * sums[k + 1, lines : 2 * lines, :]
        else:
            high = jnp.zeros_like(up)
            killing = own + up
        e = killing + low * d
        inverse = reciprocal(high + e)
        d = e * inverse
        value = (right + wide(low) * value) * wide(inverse)
        values.append(value)
        ratios.append(wide(high * inverse))
    tops[0] = jnp.zeros((lines, across), jnp.float32)
    tops[walls] = values[-1]
    for k in reversed(range(walls - 1)):
        values[k] = values[k] + ratios[k] * values[k + 1]
        tops[k + 1] = values[k]

    def row(s):
        return pl.ds(s, lines, stride=knots)

    run = tops[me]
    before[row(0), :] = run
    found = []
    for s in range(knots - 1):
        run = reduced[row(s), :] * wide(inner[0, s]) + wide(inner[1, s]) * run
        found.append(run)
    run = tops[me + 1]
    after[row(knots - 1), :] = run
    for s in reversed(range(knots - 1)):
        run = found[s] + wide(inner[2, s]) * run
        after[row(s), :] = run
        if s + 1 < segments:
            before[row(s + 1), :] = run

    def put(c, x, t, value):
        out[c, x, pl.ds(t, segments, stride=steps), :] = value

    copies = []
    half = planes // 2 if planes % 2 == 0 else planes
    for start in range(0, planes, half):
        part = [(c, x) for c in range(components) for x in range(start, start + half)]
        bottoms, starts = [], []
        for c, x in part:
            base = (c * planes + x) * knots
            bottoms.append(before[base : base + segments, :])
            starts.append(after[base : base + segments, :])
            out[c, x, height - rest :, :] = after[base + segments : base + knots, :]
            put(c, x, last, starts[-1])

        def backward(n, values):
            t = last - 1 - n
            found = []
            ratios = {}
            for x in range(start, start + half):
                ratios[x] = upper[x, pl.ds(t, segments, stride=steps), :] * inv[t, x]
            for (c, x), value, bottom in zip(part, values, bottoms):
                value = (swept[t, c, x] + prefix[t, x] * bottom) + ratios[x] * value
                put(c, x, t, value)
                found.append(value)
            return tuple(found)

        lax.fori_loop(0, last, backward, tuple(starts), unroll=5)
        for here in part:
            copy = pltpu.make_async_copy(out.at[here], out_hbm.at[here], sems.at[here])
            copy.start()
            copies.append(copy)
    wait_all(copies)


def shifted(block, axis, distance):
    length = lax.axis_size(axis)
    route = [(i, (i + distance) % length) for i in range(length)]
    return lax.ppermute(block, axis, route)


def everyone(block, axis):
    return [block] + [shifted(block, axis, n) for n in range(1, lax.axis_size(axis))]


def local(velocity, lower_weight, upper_weight, forces, cells, counts):
    components, planes, height, across = velocity.shape
    receivers, capacity = forces.shape[3], forces.shape[5]
    senders = cells.shape[2]
    walls = lax.axis_size("wall")
    lines = components * planes
    chunks = capacity // lanes
    counts_shape, cells_shape = (planes, senders), (senders, planes, capacity)
    forces = forces.reshape(components, receivers, planes, capacity)
    cells = cells.reshape(senders, planes, capacity)
    counts = counts.reshape(senders, planes).T

    def hbm(*arrays):
        return [pltpu.with_memory_space_constraint(array, pltpu.HBM) for array in arrays]

    work_shape = (planes * (senders * chunks + group) + 4 * group,)
    send, cells_near, lower_near, upper_near, velocity_near, work = call(
        load_kernel,
        (
            pltpu.HBM((receivers, components, planes, capacity), jnp.float32),
            jax.ShapeDtypeStruct(cells_shape, jnp.int32),
            f32(*lower_weight.shape),
            f32(*upper_weight.shape),
            f32(*velocity.shape),
            jax.ShapeDtypeStruct(work_shape, jnp.int32),
        ),
        (in_hbm, *[in_vmem] * 5),
        [in_hbm] * 6,
        [
            scratch(*forces.shape),
            pltpu.SMEM(counts_shape, jnp.int32),
            pltpu.SMEM(work_shape, jnp.int32),
            pltpu.SemaphoreType.DMA((3 * components + 5,)),
        ],
        4,
        1 << 16,
    )(*hbm(forces, velocity, lower_weight, upper_weight, cells, counts))
    got = lax.all_to_all(send, "span", 0, 0, tiled=True)
    edge_shape = (lines * height // lanes, lanes)
    first_column, last_column = call(
        edge_kernel,
        (f32(*edge_shape), f32(*edge_shape)),
        (in_vmem, in_vmem),
        [in_vmem],
        [scratch(height, across), scratch(height // lanes, lanes, lanes)],
        4,
        1 << 20,
    )(velocity_near)
    from_above = shifted(first_column, "span", -1)
    from_below = shifted(last_column, "span", 1)

    steps = height // segments - 1
    knots = height - segments * steps + segments
    step_shape = (steps - 1, planes, segments, across)
    staged = [velocity.shape, step_shape, step_shape]
    prepared = call(
        prepare_kernel,
        (
            jax.ShapeDtypeStruct((senders * planes * chunks, lanes), jnp.int32),
            f32(3, knots - 1, planes, across),
            f32(4, planes, knots, across),
            f32(5 * planes, across),
            *[pltpu.HBM(shape, jnp.float32) for shape in staged],
        ),
        [in_vmem] * 4 + [in_hbm] * 3,
        [in_vmem] * 4,
        [
            *[scratch(*shape) for shape in staged],
            scratch(*step_shape),
            scratch(*step_shape),
            scratch(7, planes * knots, across),
            pltpu.SemaphoreType.DMA((3,)),
        ],
        12,
        1 << 24,
    )(cells_near, velocity_near, lower_near, upper_near)
    (cell_rows, inner, ends, coefs, rhs_start, inv, first) = prepared

    sum_rows = -(-(2 * lines + 5 * planes) // 8) * 8
    wide = 2 * components * across
    deposit, swept, prefix, reduced, sums = call(
        deposit_kernel,
        (
            jax.ShapeDtypeStruct(velocity.shape, jnp.bfloat16),
            f32(steps - 1, components, planes, segments, across),
            f32(*step_shape),
            f32(lines * knots, across),
            f32(sum_rows, across),
        ),
        (in_hbm, *[in_vmem] * 4),
        [in_vmem] * 7 + [in_hbm] * 4,
        [
            pltpu.SMEM(work_shape, jnp.int32),
            *[scratch(*shape) for shape in staged],
            scratch(*lower_weight.shape),
            scratch(senders * planes * chunks * components, lanes),
            pltpu.VMEM(velocity.shape, jnp.bfloat16),
            scratch(planes, height, wide),
            pltpu.VMEM((height, group * lanes), jnp.bfloat16),
            pltpu.VMEM((wide, group * lanes), jnp.bfloat16),
            scratch(height // lanes, lanes, lanes),
            scratch(height, lanes),
            pltpu.SemaphoreType.DMA((5,)),
            pltpu.SemaphoreType.DMA((components, planes)),
        ],
        24,
        1 << 32,
    )(
        got,
        from_above,
        from_below,
        cell_rows,
        ends,
        coefs,
        work,
        *hbm(rhs_start, inv, first, lower_weight),
    )
    all_sums = everyone(sums, "wall")

    velocity_next = call(
        finish_kernel,
        f32(*velocity.shape),
        in_hbm,
        [in_vmem] * (6 + walls),
        [
            scratch(walls, sum_rows, across),
            scratch(walls + 1, lines, across),
            scratch(lines * knots, across),
            scratch(lines * knots, across),
            scratch(*velocity.shape),
            pltpu.SemaphoreType.DMA((components, planes)),
        ],
        8,
        1 << 22,
    )(inner, reduced, swept, inv, prefix, upper_weight, *all_sums)
    return (velocity_next, deposit)


def solution(mesh):
    placed = (
        P(None, None, "wall", "span"),
        P(None, "wall", "span"),
        P(None, "wall", "span"),
        P(None, "wall", "span", None, None, None),
        P("wall", "span", None, None, None),
        P("wall", "span", None, None),
    )
    return jax.shard_map(
        local,
        mesh=mesh,
        in_specs=placed,
        out_specs=(P(None, None, "wall", "span"), P(None, None, "wall", "span")),
        check_vma=False,
    )
```

```python
import jax
import jax.numpy as jnp
from jax import lax
from jax.experimental import pallas as pl
from jax.experimental.pallas import tpu as pltpu
from jax.sharding import PartitionSpec as P

diffusion_number = 0.2
segments = 8
lanes = 128
group = 8
count_bits, plane_bit = 10, 24
in_vmem = pl.BlockSpec(memory_space=pltpu.VMEM)
in_smem = pl.BlockSpec(memory_space=pltpu.SMEM)
in_hbm = pl.BlockSpec(memory_space=pltpu.HBM)


def call(body, out_shape, out_specs, in_specs, scratch, mebibytes, flops):
    return pl.pallas_call(
        body,
        out_shape=out_shape,
        in_specs=in_specs,
        out_specs=out_specs,
        scratch_shapes=scratch,
        compiler_params=pltpu.CompilerParams(vmem_limit_bytes=mebibytes << 20),
        cost_estimate=pl.CostEstimate(flops=flops, bytes_accessed=4 << 20, transcendentals=0),
    )


def f32(*shape):
    return jax.ShapeDtypeStruct(shape, jnp.float32)


def scratch(*shape):
    return pltpu.VMEM(shape, jnp.float32)


def lane_iota(shape):
    return lax.broadcasted_iota(jnp.int32, shape, len(shape) - 1)


def reciprocal(value):
    rough = pl.reciprocal(value, approx=True)
    return rough * (2.0 - value * rough)


def start_all(copies):
    for copy in copies:
        copy.start()


def wait_all(copies):
    for copy in copies:
        copy.wait()


def copies_of(sources, targets, sems, first=0):
    return [
        pltpu.make_async_copy(source, target, sems.at[first + n])
        for n, (source, target) in enumerate(zip(sources, targets))
    ]


def load_kernel(forces, counts_hbm, send, work_out, slots, counts, work, sems):
    components, senders, planes, capacity = forces.shape
    chunks = capacity // lanes
    sources = [forces.at[c] for c in range(components)]
    targets = [slots.at[c] for c in range(components)]
    copies = copies_of(sources + [counts_hbm], targets + [counts], sems)
    start_all(copies)
    outgoing = copies_of(
        targets[:components] + [work],
        [send.at[:, c] for c in range(components)] + [work_out],
        sems,
        len(copies),
    )
    for c in range(components):
        copies[c].wait()
        outgoing[c].start()
    copies[components].wait()

    def one_plane(x, n):
        def one_sender(s, n):
            count = counts[x, s]
            base = (x << plane_bit) + ((s * chunks) << count_bits)
            for k in range(chunks):
                live = jnp.maximum(count - k * lanes, 0)
                work[group + n + k] = base + (k << count_bits) + live
            return n + lax.div(count + lanes - 1, lanes)

        n = lax.fori_loop(0, senders, one_sender, n, unroll=2)
        for extra in range(group):
            work[group + n + extra] = x << plane_bit
        return lax.div(n + group - 1, group) * group

    total = lax.fori_loop(0, planes, one_plane, 0)
    for extra in range(2 * group):
        work[group + total + extra] = 0
    work[0] = lax.div(total + 2 * group - 1, 2 * group)
    outgoing[components].start()
    wait_all(outgoing)


def edge_kernel(velocity, work, first_out, last_out, columns, turned):
    del work
    components, planes, height, across = velocity.shape
    lines = components * planes
    lane = lane_iota((height, across))
    picked = jnp.zeros((height, across), jnp.float32)
    for k in range(lines):
        rolled = pltpu.roll(velocity[k // planes, k % planes], 2 * k + 1, 1)
        picked = jnp.where((lane >> 1) == k, rolled, picked)
    columns[...] = picked
    for p in range(height // lanes):
        turned[p] = columns[p * lanes : (p + 1) * lanes, :].T
        part = slice(p * lines, (p + 1) * lines)
        first_out[part, :] = turned[p, pl.ds(1, lines, stride=2), :]
        last_out[part, :] = turned[p, pl.ds(0, lines, stride=2), :]


def prepare_kernel(velocity, lower, upper, work, inner, ends, coefs, *refs):
    del work
    (rhs, inv, first) = refs[3:6]
    (inv_b, gain_b, rows, sems) = refs[6:]
    outgoing = copies_of(refs[3:6], refs[:3], sems)
    components, planes, height, across = velocity.shape
    steps = inv.shape[0] + 1
    last = steps - 1
    rest = height - segments * steps
    knots = segments + rest

    def of_step(ref, t):
        return ref[:, pl.ds(t, segments, stride=steps), :]

    one = jnp.ones((planes, segments, across), jnp.float32)
    zero = jnp.zeros_like(one)
    size = 8
    lane = lane_iota((size, across))

    def stencil_rows(n):
        return pl.ds(pl.multiple_of(n * size, size), size)

    def read_rows(n):
        part = stencil_rows(n)
        return [[velocity[c, x, part, :] for x in range(planes)] for c in range(components)]

    def stencil(values):
        found = []
        for x in range(planes):
            v = values[x]
            around = values[(x - 1) % planes] + values[(x + 1) % planes]
            around = around + jnp.where(lane == 0, 0.0, pltpu.roll(v, 1, 1))
            around = around + jnp.where(lane == across - 1, 0.0, pltpu.roll(v, across - 1, 1))
            found.append((1.0 - 4.0 * diffusion_number) * v + diffusion_number * around)
        return found

    def write_rows(n, values):
        part = stencil_rows(n)
        for c in range(components):
            for x in range(planes):
                rhs[c, x, part, :] = values[c][x]

    def factor(t, carry):
        d, d_b, low_gain, high_gain, sum_last, sum_first = carry
        back = last - 1 - t
        low, up = of_step(lower, t), of_step(upper, t)
        low_b, up_b = of_step(lower, back), of_step(upper, back)
        velocities = read_rows(t)
        e = 1.0 + low * d
        inverse = reciprocal(up + e)
        g = low * inverse
        e_b = 1.0 + up_b * d_b
        inverse_b = reciprocal(low_b + e_b)
        g_b = up_b * inverse_b
        found = [stencil(values) for values in velocities]
        inv[t] = inverse
        inv_b[back] = inverse_b
        gain_b[back] = g_b
        write_rows(t, found)
        return (
            e * inverse,
            e_b * inverse_b,
            low_gain * g,
            high_gain * g_b,
            inverse + g * sum_last,
            inverse_b + g_b * sum_first,
        )

    carry = lax.fori_loop(0, last, factor, (one, one, one, one, zero, zero), unroll=2)
    _, _, low_gain, high_gain, sum_last, sum_first = carry
    for n in range(last, height // size):
        write_rows(n, [stencil(values) for values in read_rows(n)])
    start_all(outgoing[:2])
    def weigh(t, q):
        first[t] = inv_b[t] * q
        return q * gain_b[t]

    lax.fori_loop(0, last, weigh, one, unroll=6)
    outgoing[2].start()

    low_sep, up_sep = of_step(lower, last), of_step(upper, last)
    segment = lax.broadcasted_iota(jnp.int32, one.shape, 1)
    is_end = segment == segments - 1
    above = jnp.where(is_end, 0.0, jnp.roll(sum_first, -1, axis=1))
    couple_high = up_sep * jnp.where(is_end, 1.0, jnp.roll(high_gain, -1, axis=1))
    killing = 1.0 + low_sep * sum_last + up_sep * above
    ends[2, :, :segments, :] = low_sep
    ends[3, :, :segments, :] = up_sep
    tail = slice(height - rest, height)
    low_rest, up_rest = lower[:, tail, :], upper[:, tail, :]
    for n, (value, other) in enumerate(
        (
            (low_sep * low_gain, low_rest),
            (couple_high, up_rest),
            (killing, jnp.ones_like(low_rest)),
        )
    ):
        for x in range(planes):
            rows[n, x * knots : x * knots + segments, :] = value[x]
            rows[n, x * knots + segments : (x + 1) * knots, :] = other[x]
    for x in range(planes):
        rows[3, x * knots : x * knots + segments, :] = high_gain[x]
        rows[4, x * knots : x * knots + segments, :] = sum_first[x]

    def row(n, s):
        return rows[n, pl.ds(s, planes, stride=knots), :]

    top = knots - 1
    one_row = jnp.ones((planes, across), jnp.float32)
    d, d_b = one_row, one_row
    inv_s, gain_s, ratio_s = [], [], []
    inv_sb, gain_sb = [None] * top, [None] * top
    for s in range(top):
        e = row(2, s) + row(0, s) * d
        inverse = reciprocal(row(1, s) + e)
        inv_s.append(inverse)
        gain_s.append(row(0, s) * inverse)
        ratio_s.append(row(1, s) * inverse)
        d = e * inverse
        back = top - 1 - s
        e_b = row(2, back) + row(1, back) * d_b
        inverse_b = reciprocal(row(0, back) + e_b)
        inv_sb[back] = inverse_b
        gain_sb[back] = row(1, back) * inverse_b
        d_b = e_b * inverse_b
        inner[0, s] = inv_s[s]
        inner[1, s] = gain_s[s]
        inner[2, s] = ratio_s[s]
    run = row(0, top)
    low_total = one_row
    sum_top = one_row
    rows[5, pl.ds(top, planes, stride=knots), :] = one_row
    for s in reversed(range(top)):
        weight = run * inv_s[s]
        rows[5, pl.ds(s, planes, stride=knots), :] = weight
        sum_top = sum_top + weight * row(2, s)
        run = run * gain_s[s]
        low_total = low_total * gain_s[s]
    run = row(3, 0)
    high_total = one_row
    sum_bottom = row(4, 0)
    rows[6, pl.ds(top, planes, stride=knots), :] = jnp.zeros_like(one_row)
    for s in range(top):
        weight = run * inv_sb[s]
        rows[6, pl.ds(s, planes, stride=knots), :] = weight
        sum_bottom = sum_bottom + weight * row(2, s)
        run = run * gain_sb[s]
        high_total = high_total * ratio_s[s]
    coef = (
        row(0, top) * low_total,
        sum_top,
        row(1, top),
        sum_bottom,
        row(3, 0) * high_total,
    )
    for n, value in enumerate(coef):
        coefs[n * planes : (n + 1) * planes, :] = value
    for n in range(2):
        for x in range(planes):
            ends[n, x] = rows[5 + n, x * knots : (x + 1) * knots, :]
    wait_all(outgoing)


def deposit_kernel(got, from_above, from_below, cells, ends, coefs, *refs):
    (deposit_hbm, swept, prefix, reduced, sums) = refs[5:10]
    (work, rhs, inv, first, lower) = refs[10:15]
    (field, total, lefts, rights, columns, edges, in_sems, sems) = refs[15:]
    incoming = copies_of(refs[:5], refs[10:15], in_sems)
    start_all(incoming)
    components, planes, height, across = rhs.shape
    steps = inv.shape[0] + 1
    last = steps - 1
    knots = ends.shape[2]
    rest = knots - segments
    chunks = got.shape[2]
    parts = height // lanes
    shift = across.bit_length() - 1
    lines = components * planes
    kind = jnp.bfloat16 if max(height, across) <= 256 else jnp.float32

    total[...] = jnp.zeros_like(total)
    for p in range(parts):
        part = slice(p * lines, (p + 1) * lines)
        columns[p, pl.ds(0, lines, stride=2), :] = from_above[part, :]
        columns[p, pl.ds(1, lines, stride=2), :] = from_below[part, :]
        edges[p * lanes : (p + 1) * lanes, :] = diffusion_number * columns[p].T

    tile = 16
    base = lax.broadcasted_iota(jnp.int32, (tile, lanes), 0)
    height_ids = [(base + n * tile).astype(jnp.float32).astype(kind) for n in range(height // tile)]
    across_ids = height_ids[: across // tile]
    lane = lane_iota((1, lanes))
    one = jnp.ones((tile, lanes), jnp.bfloat16)
    none = jnp.zeros((tile, lanes), jnp.bfloat16)

    def spread(row, to):
        return jnp.broadcast_to(row, (tile, lanes)).astype(to)

    def build(n, half):
        for g in range(group):
            word = work[(n + 1) * group + g]
            ident = (word >> count_bits) & ((1 << (plane_bit - count_bits)) - 1)
            live = word & ((1 << count_bits) - 1)
            there = slice(g * lanes, (g + 1) * lanes)
            sender, chunk = lax.div(ident, chunks), lax.rem(ident, chunks)
            x = word >> plane_bit
            cell = cells[sender, chunk, pl.ds(x, 1), :]
            up = jnp.where(lane < live, cell >> shift, -1).astype(jnp.float32)
            side = (cell & (across - 1)).astype(jnp.float32)
            up, side = spread(up, kind), spread(side, kind)
            for i, ids in enumerate(height_ids):
                lefts[half][i * tile : (i + 1) * tile, there] = jnp.where(up == ids, one, none)
            masks = [side == ids for ids in across_ids]
            for c in range(components):
                force = got[sender, c, chunk, pl.ds(x, 1), :]
                rest_of = force - force.astype(jnp.bfloat16).astype(jnp.float32)
                for m, value in enumerate((force, rest_of)):
                    value = spread(value, jnp.bfloat16)
                    start = (m * components + c) * across
                    for i, mask in enumerate(masks):
                        place = slice(start + i * tile, start + (i + 1) * tile)
                        rights[half][place, there] = jnp.where(mask, value, none)

    def add(n, half):
        total[work[(n + 1) * group] >> plane_bit] += lax.dot_general(
            lefts[half][...],
            rights[half][...],
            (((1,), (1,)), ((), ())),
            preferred_element_type=jnp.float32,
        )

    def two_steps(n, carry):
        add(2 * n, 0)
        build(2 * n + 1, 1)
        add(2 * n + 1, 1)
        build(2 * n + 2, 0)
        return carry

    incoming[0].wait()
    build(0, 0)
    lax.fori_loop(0, work[0], two_steps, 0)
    wait_all(incoming[1:])

    wide = lane_iota((lanes, across))
    border = (wide == 0) | (wide == across - 1)

    def place(x):
        return [
            pltpu.make_async_copy(field.at[c, x], deposit_hbm.at[c, x], sems.at[c, x])
            for c in range(components)
        ]

    def combine(x, carry):
        for c in range(components):
            for p in range(parts):
                part = slice(p * lanes, (p + 1) * lanes)
                high = total[x, part, c * across : (c + 1) * across]
                low = total[x, part, (components + c) * across : (components + c + 1) * across]
                value = high + low
                field[c, x, part, :] = value.astype(jnp.bfloat16)
                edge = pltpu.roll(edges[part, :], lanes - 1 - 2 * (c * planes + x), 1)
                rhs[c, x, part, :] = rhs[c, x, part, :] + value + jnp.where(border, edge, 0.0)
        start_all(place(x))
        return carry

    lax.fori_loop(0, planes, combine, 0)
    sums[2 * lines : 2 * lines + coefs.shape[0], :] = coefs[...]

    zero = jnp.zeros((components, planes, segments, across), jnp.float32)

    def of_step(t):
        return rhs[:, :, pl.ds(t, segments, stride=steps), :]

    def forward(t, carry):
        value, start, run, before = carry
        force = of_step(t)
        low, inverse = lower[:, pl.ds(t, segments, stride=steps), :], inv[t]
        value = force + (low * before)[None] * value
        swept[t] = inverse[None] * value
        run = run * (low * inverse)
        prefix[t] = run
        return value, start + first[t][None] * force, run, inverse

    one = jnp.ones((planes, segments, across), jnp.float32)
    value, start, _, inverse = lax.fori_loop(0, last, forward, (zero, zero, one, one), unroll=3)
    value = inverse[None] * value
    segment = lax.broadcasted_iota(jnp.int32, zero.shape, 2)
    after = jnp.where(segment == segments - 1, 0.0, jnp.roll(start, -1, axis=2))
    low_sep, up_sep = ends[2, :, :segments, :], ends[3, :, :segments, :]
    value = of_step(last) + low_sep[None] * value + up_sep[None] * after
    others = rhs[:, :, height - rest :, :]
    at_top = ends[0, :, :segments, :][None] * value + ends[0, :, segments:, :][None] * others
    at_bottom = ends[1, :, :segments, :][None] * value + ends[1, :, segments:, :][None] * others
    at_bottom = at_bottom + jnp.where(segment == 0, start, 0.0)
    for c in range(components):
        for x in range(planes):
            k = c * planes + x
            reduced[k * knots : k * knots + segments, :] = value[c, x]
            reduced[k * knots + segments : (k + 1) * knots, :] = others[c, x]
            sums[k : k + 1, :] = jnp.sum(at_top[c, x], 0, keepdims=True)
            sums[lines + k : lines + k + 1, :] = jnp.sum(at_bottom[c, x], 0, keepdims=True)

    for x in range(planes):
        wait_all(place(x))


def finish_kernel(inner, reduced, swept, inv, prefix, upper, *refs):
    walls = len(refs) - 7
    received = refs[:walls]
    out_hbm, sums, tops, after, before, out, sems = refs[walls:]
    components, planes, height, across = out.shape
    steps = swept.shape[0] + 1
    last = steps - 1
    lines = components * planes
    knots = inner.shape[1] + 1
    rest = knots - segments
    me = lax.axis_index("wall")
    for n in range(walls):
        sums[lax.rem(me + walls - n, walls)] = received[n][...]

    def coef(k, n):
        start = 2 * lines + n * planes
        return sums[k, start : start + planes, :]

    def wide(value):
        return jnp.concatenate([value] * components, 0)

    d = jnp.ones((planes, across), jnp.float32)
    value = jnp.zeros((lines, across), jnp.float32)
    values, ratios = [], []
    for k in range(walls):
        low, own, up = coef(k, 0), coef(k, 1), coef(k, 2)
        right = sums[k, :lines, :]
        if k + 1 < walls:
            high = up * coef(k + 1, 4)
            killing = own + up * coef(k + 1, 3)
            right = right + wide(up) * sums[k + 1, lines : 2 * lines, :]
        else:
            high = jnp.zeros_like(up)
            killing = own + up
        e = killing + low * d
        inverse = reciprocal(high + e)
        d = e * inverse
        value = (right + wide(low) * value) * wide(inverse)
        values.append(value)
        ratios.append(wide(high * inverse))
    tops[0] = jnp.zeros((lines, across), jnp.float32)
    tops[walls] = values[-1]
    for k in reversed(range(walls - 1)):
        values[k] = values[k] + ratios[k] * values[k + 1]
        tops[k + 1] = values[k]

    def row(s):
        return pl.ds(s, lines, stride=knots)

    run = tops[me]
    before[row(0), :] = run
    found = []
    for s in range(knots - 1):
        run = reduced[row(s), :] * wide(inner[0, s]) + wide(inner[1, s]) * run
        found.append(run)
    run = tops[me + 1]
    after[row(knots - 1), :] = run
    for s in reversed(range(knots - 1)):
        run = found[s] + wide(inner[2, s]) * run
        after[row(s), :] = run
        if s + 1 < segments:
            before[row(s + 1), :] = run

    def put(c, x, t, value):
        out[c, x, pl.ds(t, segments, stride=steps), :] = value

    copies = []
    half = planes // 2 if planes % 2 == 0 else planes
    for start in range(0, planes, half):
        part = [(c, x) for c in range(components) for x in range(start, start + half)]
        bottoms, starts = [], []
        for c, x in part:
            base = (c * planes + x) * knots
            bottoms.append(before[base : base + segments, :])
            starts.append(after[base : base + segments, :])
            out[c, x, height - rest :, :] = after[base + segments : base + knots, :]
            put(c, x, last, starts[-1])

        def backward(n, values):
            t = last - 1 - n
            found = []
            ratios = {}
            for x in range(start, start + half):
                ratios[x] = upper[x, pl.ds(t, segments, stride=steps), :] * inv[t, x]
            for (c, x), value, bottom in zip(part, values, bottoms):
                value = (swept[t, c, x] + prefix[t, x] * bottom) + ratios[x] * value
                put(c, x, t, value)
                found.append(value)
            return tuple(found)

        lax.fori_loop(0, last, backward, tuple(starts), unroll=5)
        for here in part:
            copy = pltpu.make_async_copy(out.at[here], out_hbm.at[here], sems.at[here])
            copy.start()
            copies.append(copy)
    wait_all(copies)


def shifted(block, axis, distance):
    length = lax.axis_size(axis)
    route = [(i, (i + distance) % length) for i in range(length)]
    return lax.ppermute(block, axis, route)


def everyone(block, axis):
    return [block] + [shifted(block, axis, n) for n in range(1, lax.axis_size(axis))]


def local(velocity, lower_weight, upper_weight, forces, cells, counts):
    components, planes, height, across = velocity.shape
    receivers, capacity = forces.shape[3], forces.shape[5]
    senders = cells.shape[2]
    walls = lax.axis_size("wall")
    lines = components * planes
    chunks = capacity // lanes
    counts_shape = (planes, senders)
    forces = forces.reshape(components, receivers, planes, capacity)
    cells = cells.reshape(senders, planes, capacity)
    counts = counts.reshape(senders, planes).T

    def hbm(*arrays):
        return [pltpu.with_memory_space_constraint(array, pltpu.HBM) for array in arrays]

    work_shape = (planes * (senders * chunks + group) + 4 * group,)
    send, work = call(
        load_kernel,
        (
            pltpu.HBM((receivers, components, planes, capacity), jnp.float32),
            jax.ShapeDtypeStruct(work_shape, jnp.int32),
        ),
        (in_hbm, in_vmem),
        [in_hbm] * 2,
        [
            scratch(*forces.shape),
            pltpu.SMEM(counts_shape, jnp.int32),
            pltpu.SMEM(work_shape, jnp.int32),
            pltpu.SemaphoreType.DMA((2 * components + 2,)),
        ],
        4,
        1 << 16,
    )(*hbm(forces, counts))
    got = lax.all_to_all(send, "span", 0, 0, tiled=True)
    got = got.reshape(senders, components, planes, chunks, lanes).transpose(0, 1, 3, 2, 4)
    cells = cells.reshape(senders, planes, chunks, lanes).transpose(0, 2, 1, 3)
    edge_shape = (lines * height // lanes, lanes)
    first_column, last_column = call(
        edge_kernel,
        (f32(*edge_shape), f32(*edge_shape)),
        (in_vmem, in_vmem),
        [in_vmem] * 2,
        [scratch(height, across), scratch(height // lanes, lanes, lanes)],
        4,
        1 << 20,
    )(velocity, work)
    from_above = shifted(first_column, "span", -1)
    from_below = shifted(last_column, "span", 1)

    steps = height // segments - 1
    knots = height - segments * steps + segments
    step_shape = (steps - 1, planes, segments, across)
    staged = [velocity.shape, step_shape, step_shape]
    prepared = call(
        prepare_kernel,
        (
            f32(3, knots - 1, planes, across),
            f32(4, planes, knots, across),
            f32(5 * planes, across),
            *[pltpu.HBM(shape, jnp.float32) for shape in staged],
        ),
        [in_vmem] * 3 + [in_hbm] * 3,
        [in_vmem] * 4,
        [
            *[scratch(*shape) for shape in staged],
            scratch(*step_shape),
            scratch(*step_shape),
            scratch(7, planes * knots, across),
            pltpu.SemaphoreType.DMA((3,)),
        ],
        12,
        1 << 24,
    )(velocity, lower_weight, upper_weight, work)
    (inner, ends, coefs, rhs_start, inv, first) = prepared

    sum_rows = -(-(2 * lines + 5 * planes) // 8) * 8
    wide = 2 * components * across
    deposit, swept, prefix, reduced, sums = call(
        deposit_kernel,
        (
            jax.ShapeDtypeStruct(velocity.shape, jnp.bfloat16),
            f32(steps - 1, components, planes, segments, across),
            f32(*step_shape),
            f32(lines * knots, across),
            f32(sum_rows, across),
        ),
        (in_hbm, *[in_vmem] * 4),
        [in_vmem] * 7 + [in_hbm] * 4,
        [
            pltpu.SMEM(work_shape, jnp.int32),
            *[scratch(*shape) for shape in staged],
            scratch(*lower_weight.shape),
            pltpu.VMEM(velocity.shape, jnp.bfloat16),
            scratch(planes, height, wide),
            [pltpu.VMEM((height, group * lanes), jnp.bfloat16)] * 2,
            [pltpu.VMEM((wide, group * lanes), jnp.bfloat16)] * 2,
            scratch(height // lanes, lanes, lanes),
            scratch(height, lanes),
            pltpu.SemaphoreType.DMA((5,)),
            pltpu.SemaphoreType.DMA((components, planes)),
        ],
        24,
        1 << 32,
    )(
        got,
        from_above,
        from_below,
        cells,
        ends,
        coefs,
        work,
        *hbm(rhs_start, inv, first, lower_weight),
    )
    all_sums = everyone(sums, "wall")

    velocity_next = call(
        finish_kernel,
        f32(*velocity.shape),
        in_hbm,
        [in_vmem] * (6 + walls),
        [
            scratch(walls, sum_rows, across),
            scratch(walls + 1, lines, across),
            scratch(lines * knots, across),
            scratch(lines * knots, across),
            scratch(*velocity.shape),
            pltpu.SemaphoreType.DMA((components, planes)),
        ],
        8,
        1 << 22,
    )(inner, reduced, swept, inv, prefix, upper_weight, *all_sums)
    return (velocity_next, deposit)


def solution(mesh):
    placed = (
        P(None, None, "wall", "span"),
        P(None, "wall", "span"),
        P(None, "wall", "span"),
        P(None, "wall", "span", None, None, None),
        P("wall", "span", None, None, None),
        P("wall", "span", None, None),
    )
    return jax.shard_map(
        local,
        mesh=mesh,
        in_specs=placed,
        out_specs=(P(None, None, "wall", "span"), P(None, None, "wall", "span")),
        check_vma=False,
    )
```

```python
import jax
import jax.numpy as jnp
from jax import lax
from jax.experimental import pallas as pl
from jax.experimental.pallas import tpu as pltpu
from jax.sharding import PartitionSpec as P

diffusion_number = 0.2
segments = 8
lanes = 128
group = 8
count_bits, plane_bit = 10, 24
in_vmem = pl.BlockSpec(memory_space=pltpu.VMEM)
in_smem = pl.BlockSpec(memory_space=pltpu.SMEM)
in_hbm = pl.BlockSpec(memory_space=pltpu.HBM)


def call(body, out_shape, out_specs, in_specs, scratch, mebibytes, flops):
    return pl.pallas_call(
        body,
        out_shape=out_shape,
        in_specs=in_specs,
        out_specs=out_specs,
        scratch_shapes=scratch,
        compiler_params=pltpu.CompilerParams(vmem_limit_bytes=mebibytes << 20),
        cost_estimate=pl.CostEstimate(flops=flops, bytes_accessed=4 << 20, transcendentals=0),
    )


def f32(*shape):
    return jax.ShapeDtypeStruct(shape, jnp.float32)


def scratch(*shape):
    return pltpu.VMEM(shape, jnp.float32)


def lane_iota(shape):
    return lax.broadcasted_iota(jnp.int32, shape, len(shape) - 1)


def reciprocal(value):
    rough = pl.reciprocal(value, approx=True)
    return rough * (2.0 - value * rough)


def start_all(copies):
    for copy in copies:
        copy.start()


def wait_all(copies):
    for copy in copies:
        copy.wait()


def copies_of(sources, targets, sems, first=0):
    return [
        pltpu.make_async_copy(source, target, sems.at[first + n])
        for n, (source, target) in enumerate(zip(sources, targets))
    ]


def load_kernel(forces, velocity, lower, upper, counts_hbm, send, *refs):
    near, work_out, (slots, counts, work, sems) = refs[:3], refs[3], refs[4:]
    components, senders, planes, capacity = forces.shape
    chunks = capacity // lanes
    sources = [counts_hbm] + [forces.at[c] for c in range(components)]
    targets = [counts] + [slots.at[c] for c in range(components)]
    sources += [lower, upper] + [velocity.at[c] for c in range(components)]
    targets += [near[0], near[1]] + [near[2].at[c] for c in range(components)]
    copies = copies_of(sources, targets, sems)
    start_all(copies)
    outgoing = copies_of(
        [slots.at[c] for c in range(components)] + [work],
        [send.at[:, c] for c in range(components)] + [work_out],
        sems,
        len(copies),
    )

    def one_plane(x, n):
        def one_sender(s, n):
            count = counts[x, s]
            base = (x << plane_bit) + ((s * chunks) << count_bits)
            for k in range(chunks):
                live = jnp.maximum(count - k * lanes, 0)
                work[group + n + k] = base + (k << count_bits) + live
            return n + lax.div(count + lanes - 1, lanes)

        n = lax.fori_loop(0, senders, one_sender, n, unroll=4)
        for extra in range(group):
            work[group + n + extra] = x << plane_bit
        return lax.div(n + group - 1, group) * group

    copies[0].wait()
    total = lax.fori_loop(0, planes // 2, one_plane, 0)
    for c in range(components):
        copies[1 + c].wait()
        outgoing[c].start()
    total = lax.fori_loop(planes // 2, planes, one_plane, total)
    for extra in range(2 * group):
        work[group + total + extra] = 0
    work[0] = lax.div(total + 2 * group - 1, 2 * group)
    outgoing[components].start()
    wait_all(copies[1 + components :])
    wait_all(outgoing)


def edge_kernel(velocity, first_out, last_out, columns, turned):
    components, planes, height, across = velocity.shape
    lines = components * planes
    lane = lane_iota((height, across))
    picked = jnp.zeros((height, across), jnp.float32)
    for k in range(lines):
        rolled = pltpu.roll(velocity[k // planes, k % planes], 2 * k + 1, 1)
        picked = jnp.where((lane >> 1) == k, rolled, picked)
    columns[...] = picked
    for p in range(height // lanes):
        turned[p] = columns[p * lanes : (p + 1) * lanes, :].T
        part = slice(p * lines, (p + 1) * lines)
        first_out[part, :] = turned[p, pl.ds(1, lines, stride=2), :]
        last_out[part, :] = turned[p, pl.ds(0, lines, stride=2), :]


def prepare_kernel(velocity, lower, upper, inner, ends, coefs, *refs):
    (rhs, inv, first) = refs[3:6]
    (inv_b, gain_b, rows, sems) = refs[6:]
    outgoing = copies_of(refs[3:6], refs[:3], sems)
    components, planes, height, across = velocity.shape
    steps = inv.shape[0] + 1
    last = steps - 1
    rest = height - segments * steps
    knots = segments + rest

    def of_step(ref, t):
        return ref[:, pl.ds(t, segments, stride=steps), :]

    one = jnp.ones((planes, segments, across), jnp.float32)
    zero = jnp.zeros_like(one)
    size = 8
    lane = lane_iota((size, across))

    def stencil_rows(n):
        return pl.ds(pl.multiple_of(n * size, size), size)

    def read_rows(n):
        part = stencil_rows(n)
        return [[velocity[c, x, part, :] for x in range(planes)] for c in range(components)]

    def stencil(values):
        found = []
        for x in range(planes):
            v = values[x]
            around = values[(x - 1) % planes] + values[(x + 1) % planes]
            around = around + jnp.where(lane == 0, 0.0, pltpu.roll(v, 1, 1))
            around = around + jnp.where(lane == across - 1, 0.0, pltpu.roll(v, across - 1, 1))
            found.append((1.0 - 4.0 * diffusion_number) * v + diffusion_number * around)
        return found

    def write_rows(n, values):
        part = stencil_rows(n)
        for c in range(components):
            for x in range(planes):
                rhs[c, x, part, :] = values[c][x]

    def factor(t, carry):
        d, d_b, low_gain, high_gain, sum_last, sum_first = carry
        back = last - 1 - t
        low, up = of_step(lower, t), of_step(upper, t)
        low_b, up_b = of_step(lower, back), of_step(upper, back)
        velocities = read_rows(t)
        e = 1.0 + low * d
        inverse = reciprocal(up + e)
        g = low * inverse
        e_b = 1.0 + up_b * d_b
        inverse_b = reciprocal(low_b + e_b)
        g_b = up_b * inverse_b
        found = [stencil(values) for values in velocities]
        inv[t] = inverse
        inv_b[back] = inverse_b
        gain_b[back] = g_b
        write_rows(t, found)
        return (
            e * inverse,
            e_b * inverse_b,
            low_gain * g,
            high_gain * g_b,
            inverse + g * sum_last,
            inverse_b + g_b * sum_first,
        )

    carry = lax.fori_loop(0, last, factor, (one, one, one, one, zero, zero), unroll=2)
    _, _, low_gain, high_gain, sum_last, sum_first = carry
    for n in range(last, height // size):
        write_rows(n, [stencil(values) for values in read_rows(n)])
    start_all(outgoing[:2])
    def weigh(t, q):
        first[t] = inv_b[t] * q
        return q * gain_b[t]

    lax.fori_loop(0, last, weigh, one, unroll=6)
    outgoing[2].start()

    low_sep, up_sep = of_step(lower, last), of_step(upper, last)
    segment = lax.broadcasted_iota(jnp.int32, one.shape, 1)
    is_end = segment == segments - 1
    above = jnp.where(is_end, 0.0, jnp.roll(sum_first, -1, axis=1))
    couple_high = up_sep * jnp.where(is_end, 1.0, jnp.roll(high_gain, -1, axis=1))
    killing = 1.0 + low_sep * sum_last + up_sep * above
    ends[2, :, :segments, :] = low_sep
    ends[3, :, :segments, :] = up_sep
    tail = slice(height - rest, height)
    low_rest, up_rest = lower[:, tail, :], upper[:, tail, :]
    for n, (value, other) in enumerate(
        (
            (low_sep * low_gain, low_rest),
            (couple_high, up_rest),
            (killing, jnp.ones_like(low_rest)),
        )
    ):
        for x in range(planes):
            rows[n, x * knots : x * knots + segments, :] = value[x]
            rows[n, x * knots + segments : (x + 1) * knots, :] = other[x]
    for x in range(planes):
        rows[3, x * knots : x * knots + segments, :] = high_gain[x]
        rows[4, x * knots : x * knots + segments, :] = sum_first[x]

    def row(n, s):
        return rows[n, pl.ds(s, planes, stride=knots), :]

    top = knots - 1
    one_row = jnp.ones((planes, across), jnp.float32)
    d, d_b = one_row, one_row
    inv_s, gain_s, ratio_s = [], [], []
    inv_sb, gain_sb = [None] * top, [None] * top
    for s in range(top):
        e = row(2, s) + row(0, s) * d
        inverse = reciprocal(row(1, s) + e)
        inv_s.append(inverse)
        gain_s.append(row(0, s) * inverse)
        ratio_s.append(row(1, s) * inverse)
        d = e * inverse
        back = top - 1 - s
        e_b = row(2, back) + row(1, back) * d_b
        inverse_b = reciprocal(row(0, back) + e_b)
        inv_sb[back] = inverse_b
        gain_sb[back] = row(1, back) * inverse_b
        d_b = e_b * inverse_b
        inner[0, s] = inv_s[s]
        inner[1, s] = gain_s[s]
        inner[2, s] = ratio_s[s]
    run = row(0, top)
    low_total = one_row
    sum_top = one_row
    rows[5, pl.ds(top, planes, stride=knots), :] = one_row
    for s in reversed(range(top)):
        weight = run * inv_s[s]
        rows[5, pl.ds(s, planes, stride=knots), :] = weight
        sum_top = sum_top + weight * row(2, s)
        run = run * gain_s[s]
        low_total = low_total * gain_s[s]
    run = row(3, 0)
    high_total = one_row
    sum_bottom = row(4, 0)
    rows[6, pl.ds(top, planes, stride=knots), :] = jnp.zeros_like(one_row)
    for s in range(top):
        weight = run * inv_sb[s]
        rows[6, pl.ds(s, planes, stride=knots), :] = weight
        sum_bottom = sum_bottom + weight * row(2, s)
        run = run * gain_sb[s]
        high_total = high_total * ratio_s[s]
    coef = (
        row(0, top) * low_total,
        sum_top,
        row(1, top),
        sum_bottom,
        row(3, 0) * high_total,
    )
    for n, value in enumerate(coef):
        coefs[n * planes : (n + 1) * planes, :] = value
    for n in range(2):
        for x in range(planes):
            ends[n, x] = rows[5 + n, x * knots : (x + 1) * knots, :]
    wait_all(outgoing)


def deposit_kernel(got, from_above, from_below, cells, ends, coefs, *refs):
    (deposit_hbm, swept, prefix, reduced, sums) = refs[5:10]
    (work, rhs, inv, first, lower) = refs[10:15]
    (field, total, lefts, rights, columns, edges, in_sems, sems) = refs[15:]
    incoming = copies_of(refs[:5], refs[10:15], in_sems)
    start_all(incoming)
    components, planes, height, across = rhs.shape
    steps = inv.shape[0] + 1
    last = steps - 1
    knots = ends.shape[2]
    rest = knots - segments
    chunks = got.shape[2]
    parts = height // lanes
    shift = across.bit_length() - 1
    lines = components * planes
    kind = jnp.bfloat16 if max(height, across) <= 256 else jnp.float32

    total[...] = jnp.zeros_like(total)
    for p in range(parts):
        part = slice(p * lines, (p + 1) * lines)
        columns[p, pl.ds(0, lines, stride=2), :] = from_above[part, :]
        columns[p, pl.ds(1, lines, stride=2), :] = from_below[part, :]
        edges[p * lanes : (p + 1) * lanes, :] = diffusion_number * columns[p].T

    tile = 16
    base = lax.broadcasted_iota(jnp.int32, (tile, lanes), 0)
    height_ids = [(base + n * tile).astype(jnp.float32).astype(kind) for n in range(height // tile)]
    across_ids = height_ids[: across // tile]
    lane = lane_iota((1, lanes))
    one = jnp.ones((tile, lanes), jnp.bfloat16)
    none = jnp.zeros((tile, lanes), jnp.bfloat16)

    def spread(row, to):
        return jnp.broadcast_to(row, (tile, lanes)).astype(to)

    def build(n, half):
        for g in range(group):
            word = work[(n + 1) * group + g]
            ident = (word >> count_bits) & ((1 << (plane_bit - count_bits)) - 1)
            live = word & ((1 << count_bits) - 1)
            there = slice(g * lanes, (g + 1) * lanes)
            sender, chunk = lax.div(ident, chunks), lax.rem(ident, chunks)
            x = word >> plane_bit
            cell = cells[sender, chunk, pl.ds(x, 1), :]
            up = jnp.where(lane < live, cell >> shift, -1).astype(jnp.float32)
            side = (cell & (across - 1)).astype(jnp.float32)
            up, side = spread(up, kind), spread(side, kind)
            for i, ids in enumerate(height_ids):
                lefts[half][i * tile : (i + 1) * tile, there] = jnp.where(up == ids, one, none)
            masks = [side == ids for ids in across_ids]
            for c in range(components):
                force = got[sender, c, chunk, pl.ds(x, 1), :]
                rest_of = force - force.astype(jnp.bfloat16).astype(jnp.float32)
                for m, value in enumerate((force, rest_of)):
                    value = spread(value, jnp.bfloat16)
                    start = (m * components + c) * across
                    for i, mask in enumerate(masks):
                        place = slice(start + i * tile, start + (i + 1) * tile)
                        rights[half][place, there] = jnp.where(mask, value, none)

    def add(n, half):
        total[work[(n + 1) * group] >> plane_bit] += lax.dot_general(
            lefts[half][...],
            rights[half][...],
            (((1,), (1,)), ((), ())),
            preferred_element_type=jnp.float32,
        )

    def two_steps(n, carry):
        add(2 * n, 0)
        build(2 * n + 1, 1)
        add(2 * n + 1, 1)
        build(2 * n + 2, 0)
        return carry

    incoming[0].wait()
    build(0, 0)
    lax.fori_loop(0, work[0], two_steps, 0)
    wait_all(incoming[1:])

    wide = lane_iota((lanes, across))
    border = (wide == 0) | (wide == across - 1)

    def place(x):
        return [
            pltpu.make_async_copy(field.at[c, x], deposit_hbm.at[c, x], sems.at[c, x])
            for c in range(components)
        ]

    def combine(x, carry):
        for c in range(components):
            for p in range(parts):
                part = slice(p * lanes, (p + 1) * lanes)
                high = total[x, part, c * across : (c + 1) * across]
                low = total[x, part, (components + c) * across : (components + c + 1) * across]
                value = high + low
                field[c, x, part, :] = value.astype(jnp.bfloat16)
                edge = pltpu.roll(edges[part, :], lanes - 1 - 2 * (c * planes + x), 1)
                rhs[c, x, part, :] = rhs[c, x, part, :] + value + jnp.where(border, edge, 0.0)
        start_all(place(x))
        return carry

    lax.fori_loop(0, planes, combine, 0)
    sums[2 * lines : 2 * lines + coefs.shape[0], :] = coefs[...]

    zero = jnp.zeros((components, planes, segments, across), jnp.float32)

    def of_step(t):
        return rhs[:, :, pl.ds(t, segments, stride=steps), :]

    def forward(t, carry):
        value, start, run, before = carry
        force = of_step(t)
        low, inverse = lower[:, pl.ds(t, segments, stride=steps), :], inv[t]
        value = force + (low * before)[None] * value
        swept[t] = inverse[None] * value
        run = run * (low * inverse)
        prefix[t] = run
        return value, start + first[t][None] * force, run, inverse

    one = jnp.ones((planes, segments, across), jnp.float32)
    value, start, _, inverse = lax.fori_loop(0, last, forward, (zero, zero, one, one), unroll=3)
    value = inverse[None] * value
    segment = lax.broadcasted_iota(jnp.int32, zero.shape, 2)
    after = jnp.where(segment == segments - 1, 0.0, jnp.roll(start, -1, axis=2))
    low_sep, up_sep = ends[2, :, :segments, :], ends[3, :, :segments, :]
    value = of_step(last) + low_sep[None] * value + up_sep[None] * after
    others = rhs[:, :, height - rest :, :]
    at_top = ends[0, :, :segments, :][None] * value + ends[0, :, segments:, :][None] * others
    at_bottom = ends[1, :, :segments, :][None] * value + ends[1, :, segments:, :][None] * others
    at_bottom = at_bottom + jnp.where(segment == 0, start, 0.0)
    for c in range(components):
        for x in range(planes):
            k = c * planes + x
            reduced[k * knots : k * knots + segments, :] = value[c, x]
            reduced[k * knots + segments : (k + 1) * knots, :] = others[c, x]
            sums[k : k + 1, :] = jnp.sum(at_top[c, x], 0, keepdims=True)
            sums[lines + k : lines + k + 1, :] = jnp.sum(at_bottom[c, x], 0, keepdims=True)

    for x in range(planes):
        wait_all(place(x))


def finish_kernel(inner, reduced, swept, inv, prefix, upper, *refs):
    walls = len(refs) - 7
    received = refs[:walls]
    out_hbm, sums, tops, after, before, out, sems = refs[walls:]
    components, planes, height, across = out.shape
    steps = swept.shape[0] + 1
    last = steps - 1
    lines = components * planes
    knots = inner.shape[1] + 1
    rest = knots - segments
    me = lax.axis_index("wall")
    for n in range(walls):
        sums[lax.rem(me + walls - n, walls)] = received[n][...]

    def coef(k, n):
        start = 2 * lines + n * planes
        return sums[k, start : start + planes, :]

    def wide(value):
        return jnp.concatenate([value] * components, 0)

    d = jnp.ones((planes, across), jnp.float32)
    value = jnp.zeros((lines, across), jnp.float32)
    values, ratios = [], []
    for k in range(walls):
        low, own, up = coef(k, 0), coef(k, 1), coef(k, 2)
        right = sums[k, :lines, :]
        if k + 1 < walls:
            high = up * coef(k + 1, 4)
            killing = own + up * coef(k + 1, 3)
            right = right + wide(up) * sums[k + 1, lines : 2 * lines, :]
        else:
            high = jnp.zeros_like(up)
            killing = own + up
        e = killing + low * d
        inverse = reciprocal(high + e)
        d = e * inverse
        value = (right + wide(low) * value) * wide(inverse)
        values.append(value)
        ratios.append(wide(high * inverse))
    tops[0] = jnp.zeros((lines, across), jnp.float32)
    tops[walls] = values[-1]
    for k in reversed(range(walls - 1)):
        values[k] = values[k] + ratios[k] * values[k + 1]
        tops[k + 1] = values[k]

    def row(s):
        return pl.ds(s, lines, stride=knots)

    run = tops[me]
    before[row(0), :] = run
    found = []
    for s in range(knots - 1):
        run = reduced[row(s), :] * wide(inner[0, s]) + wide(inner[1, s]) * run
        found.append(run)
    run = tops[me + 1]
    after[row(knots - 1), :] = run
    for s in reversed(range(knots - 1)):
        run = found[s] + wide(inner[2, s]) * run
        after[row(s), :] = run
        if s + 1 < segments:
            before[row(s + 1), :] = run

    def put(c, x, t, value):
        out[c, x, pl.ds(t, segments, stride=steps), :] = value

    copies = []
    half = planes // 2 if planes % 2 == 0 else planes
    for start in range(0, planes, half):
        part = [(c, x) for c in range(components) for x in range(start, start + half)]
        bottoms, starts = [], []
        for c, x in part:
            base = (c * planes + x) * knots
            bottoms.append(before[base : base + segments, :])
            starts.append(after[base : base + segments, :])
            out[c, x, height - rest :, :] = after[base + segments : base + knots, :]
            put(c, x, last, starts[-1])

        def backward(n, values):
            t = last - 1 - n
            found = []
            ratios = {}
            for x in range(start, start + half):
                ratios[x] = upper[x, pl.ds(t, segments, stride=steps), :] * inv[t, x]
            for (c, x), value, bottom in zip(part, values, bottoms):
                value = (swept[t, c, x] + prefix[t, x] * bottom) + ratios[x] * value
                put(c, x, t, value)
                found.append(value)
            return tuple(found)

        lax.fori_loop(0, last, backward, tuple(starts), unroll=5)
        for here in part:
            copy = pltpu.make_async_copy(out.at[here], out_hbm.at[here], sems.at[here])
            copy.start()
            copies.append(copy)
    wait_all(copies)


def shifted(block, axis, distance):
    length = lax.axis_size(axis)
    route = [(i, (i + distance) % length) for i in range(length)]
    return lax.ppermute(block, axis, route)


def everyone(block, axis):
    return [block] + [shifted(block, axis, n) for n in range(1, lax.axis_size(axis))]


def local(velocity, lower_weight, upper_weight, forces, cells, counts):
    components, planes, height, across = velocity.shape
    receivers, capacity = forces.shape[3], forces.shape[5]
    senders = cells.shape[2]
    walls = lax.axis_size("wall")
    lines = components * planes
    chunks = capacity // lanes
    counts_shape = (planes, senders)
    forces = forces.reshape(components, receivers, planes, capacity)
    cells = cells.reshape(senders, planes, capacity)
    counts = counts.reshape(senders, planes).T

    def hbm(*arrays):
        return [pltpu.with_memory_space_constraint(array, pltpu.HBM) for array in arrays]

    work_shape = (planes * (senders * chunks + group) + 4 * group,)
    send, lower_near, upper_near, velocity_near, work = call(
        load_kernel,
        (
            pltpu.HBM((receivers, components, planes, capacity), jnp.float32),
            f32(*lower_weight.shape),
            f32(*upper_weight.shape),
            f32(*velocity.shape),
            jax.ShapeDtypeStruct(work_shape, jnp.int32),
        ),
        (in_hbm, *[in_vmem] * 4),
        [in_hbm] * 5,
        [
            scratch(*forces.shape),
            pltpu.SMEM(counts_shape, jnp.int32),
            pltpu.SMEM(work_shape, jnp.int32),
            pltpu.SemaphoreType.DMA((3 * components + 4,)),
        ],
        4,
        1 << 16,
    )(*hbm(forces, velocity, lower_weight, upper_weight, counts))
    got = lax.all_to_all(send, "span", 0, 0, tiled=True)
    got = got.reshape(senders, components, planes, chunks, lanes).transpose(0, 1, 3, 2, 4)
    cells = cells.reshape(senders, planes, chunks, lanes).transpose(0, 2, 1, 3)
    edge_shape = (lines * height // lanes, lanes)
    first_column, last_column = call(
        edge_kernel,
        (f32(*edge_shape), f32(*edge_shape)),
        (in_vmem, in_vmem),
        [in_vmem],
        [scratch(height, across), scratch(height // lanes, lanes, lanes)],
        4,
        1 << 20,
    )(velocity_near)
    from_above = shifted(first_column, "span", -1)
    from_below = shifted(last_column, "span", 1)

    steps = height // segments - 1
    knots = height - segments * steps + segments
    step_shape = (steps - 1, planes, segments, across)
    staged = [velocity.shape, step_shape, step_shape]
    prepared = call(
        prepare_kernel,
        (
            f32(3, knots - 1, planes, across),
            f32(4, planes, knots, across),
            f32(5 * planes, across),
            *[pltpu.HBM(shape, jnp.float32) for shape in staged],
        ),
        [in_vmem] * 3 + [in_hbm] * 3,
        [in_vmem] * 3,
        [
            *[scratch(*shape) for shape in staged],
            scratch(*step_shape),
            scratch(*step_shape),
            scratch(7, planes * knots, across),
            pltpu.SemaphoreType.DMA((3,)),
        ],
        12,
        1 << 24,
    )(velocity_near, lower_near, upper_near)
    (inner, ends, coefs, rhs_start, inv, first) = prepared

    sum_rows = -(-(2 * lines + 5 * planes) // 8) * 8
    wide = 2 * components * across
    deposit, swept, prefix, reduced, sums = call(
        deposit_kernel,
        (
            jax.ShapeDtypeStruct(velocity.shape, jnp.bfloat16),
            f32(steps - 1, components, planes, segments, across),
            f32(*step_shape),
            f32(lines * knots, across),
            f32(sum_rows, across),
        ),
        (in_hbm, *[in_vmem] * 4),
        [in_vmem] * 7 + [in_hbm] * 4,
        [
            pltpu.SMEM(work_shape, jnp.int32),
            *[scratch(*shape) for shape in staged],
            scratch(*lower_weight.shape),
            pltpu.VMEM(velocity.shape, jnp.bfloat16),
            scratch(planes, height, wide),
            [pltpu.VMEM((height, group * lanes), jnp.bfloat16)] * 2,
            [pltpu.VMEM((wide, group * lanes), jnp.bfloat16)] * 2,
            scratch(height // lanes, lanes, lanes),
            scratch(height, lanes),
            pltpu.SemaphoreType.DMA((5,)),
            pltpu.SemaphoreType.DMA((components, planes)),
        ],
        24,
        1 << 32,
    )(
        got,
        from_above,
        from_below,
        cells,
        ends,
        coefs,
        work,
        *hbm(rhs_start, inv, first, lower_weight),
    )
    all_sums = everyone(sums, "wall")

    velocity_next = call(
        finish_kernel,
        f32(*velocity.shape),
        in_hbm,
        [in_vmem] * (6 + walls),
        [
            scratch(walls, sum_rows, across),
            scratch(walls + 1, lines, across),
            scratch(lines * knots, across),
            scratch(lines * knots, across),
            scratch(*velocity.shape),
            pltpu.SemaphoreType.DMA((components, planes)),
        ],
        8,
        1 << 22,
    )(inner, reduced, swept, inv, prefix, upper_weight, *all_sums)
    return (velocity_next, deposit)


def solution(mesh):
    placed = (
        P(None, None, "wall", "span"),
        P(None, "wall", "span"),
        P(None, "wall", "span"),
        P(None, "wall", "span", None, None, None),
        P("wall", "span", None, None, None),
        P("wall", "span", None, None),
    )
    return jax.shard_map(
        local,
        mesh=mesh,
        in_specs=placed,
        out_specs=(P(None, None, "wall", "span"), P(None, None, "wall", "span")),
        check_vma=False,
    )
```

```python
import jax
import jax.numpy as jnp
from jax import lax
from jax.experimental import pallas as pl
from jax.experimental.pallas import tpu as pltpu
from jax.sharding import PartitionSpec as P

diffusion_number = 0.2
segments = 8
lanes = 128
group = 8
count_bits, plane_bit = 10, 24
in_vmem = pl.BlockSpec(memory_space=pltpu.VMEM)
in_smem = pl.BlockSpec(memory_space=pltpu.SMEM)
in_hbm = pl.BlockSpec(memory_space=pltpu.HBM)


def call(body, out_shape, out_specs, in_specs, scratch, mebibytes, flops):
    return pl.pallas_call(
        body,
        out_shape=out_shape,
        in_specs=in_specs,
        out_specs=out_specs,
        scratch_shapes=scratch,
        compiler_params=pltpu.CompilerParams(vmem_limit_bytes=mebibytes << 20),
        cost_estimate=pl.CostEstimate(flops=flops, bytes_accessed=4 << 20, transcendentals=0),
    )


def f32(*shape):
    return jax.ShapeDtypeStruct(shape, jnp.float32)


def scratch(*shape):
    return pltpu.VMEM(shape, jnp.float32)


def lane_iota(shape):
    return lax.broadcasted_iota(jnp.int32, shape, len(shape) - 1)


def reciprocal(value):
    rough = pl.reciprocal(value, approx=True)
    return rough * (2.0 - value * rough)


def start_all(copies):
    for copy in copies:
        copy.start()


def wait_all(copies):
    for copy in copies:
        copy.wait()


def copies_of(sources, targets, sems, first=0):
    return [
        pltpu.make_async_copy(source, target, sems.at[first + n])
        for n, (source, target) in enumerate(zip(sources, targets))
    ]


def load_kernel(forces, velocity, lower, upper, counts_hbm, send, *refs):
    near, work_out, (slots, counts, work, sems) = refs[:3], refs[3], refs[4:]
    components, senders, planes, capacity = forces.shape
    chunks = capacity // lanes
    sources = [counts_hbm] + [forces.at[c] for c in range(components)]
    targets = [counts] + [slots.at[c] for c in range(components)]
    sources += [lower, upper] + [velocity.at[c] for c in range(components)]
    targets += [near[0], near[1]] + [near[2].at[c] for c in range(components)]
    copies = copies_of(sources, targets, sems)
    start_all(copies)
    outgoing = copies_of(
        [slots.at[c] for c in range(components)] + [work],
        [send.at[:, c] for c in range(components)] + [work_out],
        sems,
        len(copies),
    )

    def one_plane(x, n):
        def one_sender(s, n):
            count = counts[x, s]
            base = (x << plane_bit) + ((s * chunks) << count_bits)
            for k in range(chunks):
                live = jnp.maximum(count - k * lanes, 0)
                work[group + n + k] = base + (k << count_bits) + live
            return n + lax.div(count + lanes - 1, lanes)

        n = lax.fori_loop(0, senders, one_sender, n, unroll=4)
        for extra in range(group):
            work[group + n + extra] = x << plane_bit
        return lax.div(n + group - 1, group) * group

    copies[0].wait()
    total = lax.fori_loop(0, planes // 2, one_plane, 0)
    for c in range(components):
        copies[1 + c].wait()
        outgoing[c].start()
    total = lax.fori_loop(planes // 2, planes, one_plane, total)
    for extra in range(2 * group):
        work[group + total + extra] = 0
    work[0] = lax.div(total, group)
    outgoing[components].start()
    wait_all(copies[1 + components :])
    wait_all(outgoing)


def edge_kernel(velocity, first_out, last_out, columns, turned):
    components, planes, height, across = velocity.shape
    lines = components * planes
    lane = lane_iota((height, across))
    picked = jnp.zeros((height, across), jnp.float32)
    for k in range(lines):
        rolled = pltpu.roll(velocity[k // planes, k % planes], 2 * k + 1, 1)
        picked = jnp.where((lane >> 1) == k, rolled, picked)
    columns[...] = picked
    for p in range(height // lanes):
        turned[p] = columns[p * lanes : (p + 1) * lanes, :].T
        part = slice(p * lines, (p + 1) * lines)
        first_out[part, :] = turned[p, pl.ds(1, lines, stride=2), :]
        last_out[part, :] = turned[p, pl.ds(0, lines, stride=2), :]


def prepare_kernel(velocity, lower, upper, inner, ends, coefs, *refs):
    (rhs, inv, first) = refs[3:6]
    (inv_b, gain_b, rows, sems) = refs[6:]
    outgoing = copies_of(refs[3:6], refs[:3], sems)
    components, planes, height, across = velocity.shape
    steps = inv.shape[0] + 1
    last = steps - 1
    rest = height - segments * steps
    knots = segments + rest

    def of_step(ref, t):
        return ref[:, pl.ds(t, segments, stride=steps), :]

    one = jnp.ones((planes, segments, across), jnp.float32)
    zero = jnp.zeros_like(one)
    size = 8
    lane = lane_iota((size, across))

    def stencil_rows(n):
        return pl.ds(pl.multiple_of(n * size, size), size)

    def read_rows(n):
        part = stencil_rows(n)
        return [[velocity[c, x, part, :] for x in range(planes)] for c in range(components)]

    def stencil(values):
        found = []
        for x in range(planes):
            v = values[x]
            around = values[(x - 1) % planes] + values[(x + 1) % planes]
            around = around + jnp.where(lane == 0, 0.0, pltpu.roll(v, 1, 1))
            around = around + jnp.where(lane == across - 1, 0.0, pltpu.roll(v, across - 1, 1))
            found.append((1.0 - 4.0 * diffusion_number) * v + diffusion_number * around)
        return found

    def write_rows(n, values):
        part = stencil_rows(n)
        for c in range(components):
            for x in range(planes):
                rhs[c, x, part, :] = values[c][x]

    def factor(t, carry):
        d, d_b, low_gain, high_gain, sum_last, sum_first = carry
        back = last - 1 - t
        low, up = of_step(lower, t), of_step(upper, t)
        low_b, up_b = of_step(lower, back), of_step(upper, back)
        velocities = read_rows(t)
        e = 1.0 + low * d
        inverse = reciprocal(up + e)
        g = low * inverse
        e_b = 1.0 + up_b * d_b
        inverse_b = reciprocal(low_b + e_b)
        g_b = up_b * inverse_b
        found = [stencil(values) for values in velocities]
        inv[t] = inverse
        inv_b[back] = inverse_b
        gain_b[back] = g_b
        write_rows(t, found)
        return (
            e * inverse,
            e_b * inverse_b,
            low_gain * g,
            high_gain * g_b,
            inverse + g * sum_last,
            inverse_b + g_b * sum_first,
        )

    carry = lax.fori_loop(0, last, factor, (one, one, one, one, zero, zero), unroll=2)
    _, _, low_gain, high_gain, sum_last, sum_first = carry
    for n in range(last, height // size):
        write_rows(n, [stencil(values) for values in read_rows(n)])
    start_all(outgoing[:2])
    def weigh(t, q):
        first[t] = inv_b[t] * q
        return q * gain_b[t]

    lax.fori_loop(0, last, weigh, one, unroll=6)
    outgoing[2].start()

    low_sep, up_sep = of_step(lower, last), of_step(upper, last)
    segment = lax.broadcasted_iota(jnp.int32, one.shape, 1)
    is_end = segment == segments - 1
    above = jnp.where(is_end, 0.0, jnp.roll(sum_first, -1, axis=1))
    couple_high = up_sep * jnp.where(is_end, 1.0, jnp.roll(high_gain, -1, axis=1))
    killing = 1.0 + low_sep * sum_last + up_sep * above
    ends[2, :, :segments, :] = low_sep
    ends[3, :, :segments, :] = up_sep
    tail = slice(height - rest, height)
    low_rest, up_rest = lower[:, tail, :], upper[:, tail, :]
    for n, (value, other) in enumerate(
        (
            (low_sep * low_gain, low_rest),
            (couple_high, up_rest),
            (killing, jnp.ones_like(low_rest)),
        )
    ):
        for x in range(planes):
            rows[n, x * knots : x * knots + segments, :] = value[x]
            rows[n, x * knots + segments : (x + 1) * knots, :] = other[x]
    for x in range(planes):
        rows[3, x * knots : x * knots + segments, :] = high_gain[x]
        rows[4, x * knots : x * knots + segments, :] = sum_first[x]

    def row(n, s):
        return rows[n, pl.ds(s, planes, stride=knots), :]

    top = knots - 1
    one_row = jnp.ones((planes, across), jnp.float32)
    d, d_b = one_row, one_row
    inv_s, gain_s, ratio_s = [], [], []
    inv_sb, gain_sb = [None] * top, [None] * top
    for s in range(top):
        e = row(2, s) + row(0, s) * d
        inverse = reciprocal(row(1, s) + e)
        inv_s.append(inverse)
        gain_s.append(row(0, s) * inverse)
        ratio_s.append(row(1, s) * inverse)
        d = e * inverse
        back = top - 1 - s
        e_b = row(2, back) + row(1, back) * d_b
        inverse_b = reciprocal(row(0, back) + e_b)
        inv_sb[back] = inverse_b
        gain_sb[back] = row(1, back) * inverse_b
        d_b = e_b * inverse_b
        inner[0, s] = inv_s[s]
        inner[1, s] = gain_s[s]
        inner[2, s] = ratio_s[s]
    run = row(0, top)
    low_total = one_row
    sum_top = one_row
    rows[5, pl.ds(top, planes, stride=knots), :] = one_row
    for s in reversed(range(top)):
        weight = run * inv_s[s]
        rows[5, pl.ds(s, planes, stride=knots), :] = weight
        sum_top = sum_top + weight * row(2, s)
        run = run * gain_s[s]
        low_total = low_total * gain_s[s]
    run = row(3, 0)
    high_total = one_row
    sum_bottom = row(4, 0)
    rows[6, pl.ds(top, planes, stride=knots), :] = jnp.zeros_like(one_row)
    for s in range(top):
        weight = run * inv_sb[s]
        rows[6, pl.ds(s, planes, stride=knots), :] = weight
        sum_bottom = sum_bottom + weight * row(2, s)
        run = run * gain_sb[s]
        high_total = high_total * ratio_s[s]
    coef = (
        row(0, top) * low_total,
        sum_top,
        row(1, top),
        sum_bottom,
        row(3, 0) * high_total,
    )
    for n, value in enumerate(coef):
        coefs[n * planes : (n + 1) * planes, :] = value
    for n in range(2):
        for x in range(planes):
            ends[n, x] = rows[5 + n, x * knots : (x + 1) * knots, :]
    wait_all(outgoing)


def deposit_kernel(got, from_above, from_below, cells, ends, coefs, *refs):
    (deposit_hbm, swept, prefix, ratio, reduced, sums) = refs[6:12]
    (work, rhs, inv, first, lower, upper) = refs[12:18]
    (field, total, lefts, rights, columns, edges, in_sems, sems) = refs[18:]
    incoming = copies_of(refs[:6], refs[12:18], in_sems)
    start_all(incoming)
    components, planes, height, across = rhs.shape
    steps = inv.shape[0] + 1
    last = steps - 1
    knots = ends.shape[2]
    rest = knots - segments
    chunks = got.shape[2]
    parts = height // lanes
    shift = across.bit_length() - 1
    lines = components * planes
    kind = jnp.bfloat16 if max(height, across) <= 256 else jnp.float32

    total[...] = jnp.zeros_like(total)
    for p in range(parts):
        part = slice(p * lines, (p + 1) * lines)
        columns[p, pl.ds(0, lines, stride=2), :] = from_above[part, :]
        columns[p, pl.ds(1, lines, stride=2), :] = from_below[part, :]
        edges[p * lanes : (p + 1) * lanes, :] = diffusion_number * columns[p].T

    tile = 16
    base = lax.broadcasted_iota(jnp.int32, (tile, lanes), 0)
    height_ids = [(base + n * tile).astype(jnp.float32).astype(kind) for n in range(height // tile)]
    across_ids = height_ids[: across // tile]
    lane = lane_iota((1, lanes))
    one = jnp.ones((tile, lanes), jnp.bfloat16)
    none = jnp.zeros((tile, lanes), jnp.bfloat16)

    def spread(row, to):
        return jnp.broadcast_to(row, (tile, lanes)).astype(to)

    def build(n, half):
        for g in range(group):
            word = work[(n + 1) * group + g]
            ident = (word >> count_bits) & ((1 << (plane_bit - count_bits)) - 1)
            live = word & ((1 << count_bits) - 1)
            there = slice(g * lanes, (g + 1) * lanes)
            sender, chunk = lax.div(ident, chunks), lax.rem(ident, chunks)
            x = word >> plane_bit
            cell = cells[sender, chunk, pl.ds(x, 1), :]
            up = jnp.where(lane < live, cell >> shift, -1).astype(jnp.float32)
            side = (cell & (across - 1)).astype(jnp.float32)
            up, side = spread(up, kind), spread(side, kind)
            for i, ids in enumerate(height_ids):
                lefts[half][i * tile : (i + 1) * tile, there] = jnp.where(up == ids, one, none)
            masks = [side == ids for ids in across_ids]
            for c in range(components):
                force = got[sender, c, chunk, pl.ds(x, 1), :]
                rest_of = force - force.astype(jnp.bfloat16).astype(jnp.float32)
                for m, value in enumerate((force, rest_of)):
                    value = spread(value, jnp.bfloat16)
                    start = (m * components + c) * across
                    for i, mask in enumerate(masks):
                        place = slice(start + i * tile, start + (i + 1) * tile)
                        rights[half][place, there] = jnp.where(mask, value, none)

    def add(n, half):
        total[work[(n + 1) * group] >> plane_bit] += lax.dot_general(
            lefts[half][...],
            rights[half][...],
            (((1,), (1,)), ((), ())),
            preferred_element_type=jnp.float32,
        )

    def two_steps(n, carry):
        add(2 * n, 0)
        build(2 * n + 1, 1)
        add(2 * n + 1, 1)
        build(2 * n + 2, 0)
        return carry

    incoming[0].wait()
    build(0, 0)
    count = work[0]
    lax.fori_loop(0, lax.div(count, 2), two_steps, 0)

    @pl.when(lax.rem(count, 2) == 1)
    def _():
        add(count - 1, 0)

    wait_all(incoming[1:])

    wide = lane_iota((lanes, across))
    border = (wide == 0) | (wide == across - 1)

    def place(x):
        return [
            pltpu.make_async_copy(field.at[c, x], deposit_hbm.at[c, x], sems.at[c, x])
            for c in range(components)
        ]

    def combine(x, carry):
        for c in range(components):
            for p in range(parts):
                part = slice(p * lanes, (p + 1) * lanes)
                high = total[x, part, c * across : (c + 1) * across]
                low = total[x, part, (components + c) * across : (components + c + 1) * across]
                value = high + low
                field[c, x, part, :] = value.astype(jnp.bfloat16)
                edge = pltpu.roll(edges[part, :], lanes - 1 - 2 * (c * planes + x), 1)
                rhs[c, x, part, :] = rhs[c, x, part, :] + value + jnp.where(border, edge, 0.0)
        start_all(place(x))
        return carry

    lax.fori_loop(0, planes, combine, 0)
    copies = sums.shape[0]
    for n in range(copies):
        sums[n, 2 * lines : 2 * lines + coefs.shape[0], :] = coefs[...]

    zero = jnp.zeros((components, planes, segments, across), jnp.float32)

    def of_step(t):
        return rhs[:, :, pl.ds(t, segments, stride=steps), :]

    def forward(t, carry):
        value, start, run, before = carry
        force = of_step(t)
        low, inverse = lower[:, pl.ds(t, segments, stride=steps), :], inv[t]
        value = force + (low * before)[None] * value
        swept[t] = inverse[None] * value
        run = run * (low * inverse)
        prefix[t] = run
        ratio[t] = upper[:, pl.ds(t, segments, stride=steps), :] * inverse
        return value, start + first[t][None] * force, run, inverse

    one = jnp.ones((planes, segments, across), jnp.float32)
    value, start, _, inverse = lax.fori_loop(0, last, forward, (zero, zero, one, one), unroll=3)
    value = inverse[None] * value
    segment = lax.broadcasted_iota(jnp.int32, zero.shape, 2)
    after = jnp.where(segment == segments - 1, 0.0, jnp.roll(start, -1, axis=2))
    low_sep, up_sep = ends[2, :, :segments, :], ends[3, :, :segments, :]
    value = of_step(last) + low_sep[None] * value + up_sep[None] * after
    others = rhs[:, :, height - rest :, :]
    at_top = ends[0, :, :segments, :][None] * value + ends[0, :, segments:, :][None] * others
    at_bottom = ends[1, :, :segments, :][None] * value + ends[1, :, segments:, :][None] * others
    at_bottom = at_bottom + jnp.where(segment == 0, start, 0.0)
    for c in range(components):
        for x in range(planes):
            k = c * planes + x
            reduced[k * knots : k * knots + segments, :] = value[c, x]
            reduced[k * knots + segments : (k + 1) * knots, :] = others[c, x]
            top = jnp.sum(at_top[c, x], 0, keepdims=True)
            bottom = jnp.sum(at_bottom[c, x], 0, keepdims=True)
            for n in range(copies):
                sums[n, k : k + 1, :] = top
                sums[n, lines + k : lines + k + 1, :] = bottom

    for x in range(planes):
        wait_all(place(x))


def finish_kernel(sums, inner, reduced, swept, ratio, prefix, *refs):
    walls = sums.shape[0]
    out_hbm, tops, after, before, out, sems = refs
    components, planes, height, across = out.shape
    steps = swept.shape[0] + 1
    last = steps - 1
    lines = components * planes
    knots = inner.shape[1] + 1
    rest = knots - segments
    me = lax.axis_index("wall")

    def coef(k, n):
        start = 2 * lines + n * planes
        return sums[k, start : start + planes, :]

    def wide(value):
        return jnp.concatenate([value] * components, 0)

    d = jnp.ones((planes, across), jnp.float32)
    value = jnp.zeros((lines, across), jnp.float32)
    values, ratios = [], []
    for k in range(walls):
        low, own, up = coef(k, 0), coef(k, 1), coef(k, 2)
        right = sums[k, :lines, :]
        if k + 1 < walls:
            high = up * coef(k + 1, 4)
            killing = own + up * coef(k + 1, 3)
            right = right + wide(up) * sums[k + 1, lines : 2 * lines, :]
        else:
            high = jnp.zeros_like(up)
            killing = own + up
        e = killing + low * d
        inverse = reciprocal(high + e)
        d = e * inverse
        value = (right + wide(low) * value) * wide(inverse)
        values.append(value)
        ratios.append(wide(high * inverse))
    tops[0] = jnp.zeros((lines, across), jnp.float32)
    tops[walls] = values[-1]
    for k in reversed(range(walls - 1)):
        values[k] = values[k] + ratios[k] * values[k + 1]
        tops[k + 1] = values[k]

    def row(s):
        return pl.ds(s, lines, stride=knots)

    run = tops[me]
    before[row(0), :] = run
    found = []
    for s in range(knots - 1):
        run = reduced[row(s), :] * wide(inner[0, s]) + wide(inner[1, s]) * run
        found.append(run)
    run = tops[me + 1]
    after[row(knots - 1), :] = run
    for s in reversed(range(knots - 1)):
        run = found[s] + wide(inner[2, s]) * run
        after[row(s), :] = run
        if s + 1 < segments:
            before[row(s + 1), :] = run

    def put(c, x, t, value):
        out[c, x, pl.ds(t, segments, stride=steps), :] = value

    copies = []
    half = planes // 2 if planes % 2 == 0 else planes
    for start in range(0, planes, half):
        part = [(c, x) for c in range(components) for x in range(start, start + half)]
        bottoms, starts = [], []
        for c, x in part:
            base = (c * planes + x) * knots
            bottoms.append(before[base : base + segments, :])
            starts.append(after[base : base + segments, :])
            out[c, x, height - rest :, :] = after[base + segments : base + knots, :]
            put(c, x, last, starts[-1])

        def backward(n, values):
            t = last - 1 - n
            found = []
            for (c, x), value, bottom in zip(part, values, bottoms):
                value = (swept[t, c, x] + prefix[t, x] * bottom) + ratio[t, x] * value
                put(c, x, t, value)
                found.append(value)
            return tuple(found)

        lax.fori_loop(0, last, backward, tuple(starts), unroll=5)
        for here in part:
            copy = pltpu.make_async_copy(out.at[here], out_hbm.at[here], sems.at[here])
            copy.start()
            copies.append(copy)
    wait_all(copies)


def shifted(block, axis, distance):
    length = lax.axis_size(axis)
    route = [(i, (i + distance) % length) for i in range(length)]
    return lax.ppermute(block, axis, route)


def local(velocity, lower_weight, upper_weight, forces, cells, counts):
    components, planes, height, across = velocity.shape
    receivers, capacity = forces.shape[3], forces.shape[5]
    senders = cells.shape[2]
    walls = lax.axis_size("wall")
    lines = components * planes
    chunks = capacity // lanes
    counts_shape = (planes, senders)
    forces = forces.reshape(components, receivers, planes, capacity)
    cells = cells.reshape(senders, planes, capacity)
    counts = counts.reshape(senders, planes).T

    def hbm(*arrays):
        return [pltpu.with_memory_space_constraint(array, pltpu.HBM) for array in arrays]

    work_shape = (planes * (senders * chunks + group) + 4 * group,)
    send, lower_near, upper_near, velocity_near, work = call(
        load_kernel,
        (
            pltpu.HBM((receivers, components, planes, capacity), jnp.float32),
            f32(*lower_weight.shape),
            f32(*upper_weight.shape),
            f32(*velocity.shape),
            jax.ShapeDtypeStruct(work_shape, jnp.int32),
        ),
        (in_hbm, *[in_vmem] * 4),
        [in_hbm] * 5,
        [
            scratch(*forces.shape),
            pltpu.SMEM(counts_shape, jnp.int32),
            pltpu.SMEM(work_shape, jnp.int32),
            pltpu.SemaphoreType.DMA((3 * components + 4,)),
        ],
        4,
        1 << 16,
    )(*hbm(forces, velocity, lower_weight, upper_weight, counts))
    got = lax.all_to_all(send, "span", 0, 0, tiled=True)
    got = got.reshape(senders, components, planes, chunks, lanes).transpose(0, 1, 3, 2, 4)
    cells = cells.reshape(senders, planes, chunks, lanes).transpose(0, 2, 1, 3)
    edge_shape = (lines * height // lanes, lanes)
    first_column, last_column = call(
        edge_kernel,
        (f32(*edge_shape), f32(*edge_shape)),
        (in_vmem, in_vmem),
        [in_vmem],
        [scratch(height, across), scratch(height // lanes, lanes, lanes)],
        4,
        1 << 20,
    )(velocity_near)
    from_above = shifted(first_column, "span", -1)
    from_below = shifted(last_column, "span", 1)

    steps = height // segments - 1
    knots = height - segments * steps + segments
    step_shape = (steps - 1, planes, segments, across)
    staged = [velocity.shape, step_shape, step_shape]
    prepared = call(
        prepare_kernel,
        (
            f32(3, knots - 1, planes, across),
            f32(4, planes, knots, across),
            f32(5 * planes, across),
            *[pltpu.HBM(shape, jnp.float32) for shape in staged],
        ),
        [in_vmem] * 3 + [in_hbm] * 3,
        [in_vmem] * 3,
        [
            *[scratch(*shape) for shape in staged],
            scratch(*step_shape),
            scratch(*step_shape),
            scratch(7, planes * knots, across),
            pltpu.SemaphoreType.DMA((3,)),
        ],
        12,
        1 << 24,
    )(velocity_near, lower_near, upper_near)
    (inner, ends, coefs, rhs_start, inv, first) = prepared

    sum_rows = -(-(2 * lines + 5 * planes) // 8) * 8
    wide = 2 * components * across
    deposit, swept, prefix, ratio, reduced, sums = call(
        deposit_kernel,
        (
            jax.ShapeDtypeStruct(velocity.shape, jnp.bfloat16),
            f32(steps - 1, components, planes, segments, across),
            f32(*step_shape),
            f32(*step_shape),
            f32(lines * knots, across),
            f32(walls, sum_rows, across),
        ),
        (in_hbm, *[in_vmem] * 5),
        [in_vmem] * 7 + [in_hbm] * 5,
        [
            pltpu.SMEM(work_shape, jnp.int32),
            *[scratch(*shape) for shape in staged],
            scratch(*lower_weight.shape),
            scratch(*upper_weight.shape),
            pltpu.VMEM(velocity.shape, jnp.bfloat16),
            scratch(planes, height, wide),
            [pltpu.VMEM((height, group * lanes), jnp.bfloat16)] * 2,
            [pltpu.VMEM((wide, group * lanes), jnp.bfloat16)] * 2,
            scratch(height // lanes, lanes, lanes),
            scratch(height, lanes),
            pltpu.SemaphoreType.DMA((6,)),
            pltpu.SemaphoreType.DMA((components, planes)),
        ],
        24,
        1 << 32,
    )(
        got,
        from_above,
        from_below,
        cells,
        ends,
        coefs,
        work,
        *hbm(rhs_start, inv, first, lower_weight, upper_weight),
    )
    all_sums = lax.all_to_all(sums, "wall", 0, 0, tiled=True)

    velocity_next = call(
        finish_kernel,
        f32(*velocity.shape),
        in_hbm,
        [in_vmem] * 6,
        [
            scratch(walls + 1, lines, across),
            scratch(lines * knots, across),
            scratch(lines * knots, across),
            scratch(*velocity.shape),
            pltpu.SemaphoreType.DMA((components, planes)),
        ],
        8,
        1 << 22,
    )(all_sums, inner, reduced, swept, ratio, prefix)
    return (velocity_next, deposit)


def solution(mesh):
    placed = (
        P(None, None, "wall", "span"),
        P(None, "wall", "span"),
        P(None, "wall", "span"),
        P(None, "wall", "span", None, None, None),
        P("wall", "span", None, None, None),
        P("wall", "span", None, None),
    )
    return jax.shard_map(
        local,
        mesh=mesh,
        in_specs=placed,
        out_specs=(P(None, None, "wall", "span"), P(None, None, "wall", "span")),
        check_vma=False,
    )
```

```python
import jax
import jax.numpy as jnp
from jax import lax
from jax.experimental import pallas as pl
from jax.experimental.pallas import tpu as pltpu
from jax.sharding import PartitionSpec as P

diffusion_number = 0.2
segments = 8
lanes = 128
group = 8
count_bits, plane_bit = 10, 24
in_vmem = pl.BlockSpec(memory_space=pltpu.VMEM)
in_smem = pl.BlockSpec(memory_space=pltpu.SMEM)
in_hbm = pl.BlockSpec(memory_space=pltpu.HBM)


def call(body, out_shape, out_specs, in_specs, scratch, mebibytes, flops):
    return pl.pallas_call(
        body,
        out_shape=out_shape,
        in_specs=in_specs,
        out_specs=out_specs,
        scratch_shapes=scratch,
        compiler_params=pltpu.CompilerParams(vmem_limit_bytes=mebibytes << 20),
        cost_estimate=pl.CostEstimate(flops=flops, bytes_accessed=4 << 20, transcendentals=0),
    )


def f32(*shape):
    return jax.ShapeDtypeStruct(shape, jnp.float32)


def scratch(*shape):
    return pltpu.VMEM(shape, jnp.float32)


def lane_iota(shape):
    return lax.broadcasted_iota(jnp.int32, shape, len(shape) - 1)


def reciprocal(value):
    rough = pl.reciprocal(value, approx=True)
    return rough * (2.0 - value * rough)


def start_all(copies):
    for copy in copies:
        copy.start()


def wait_all(copies):
    for copy in copies:
        copy.wait()


def copies_of(sources, targets, sems, first=0):
    return [
        pltpu.make_async_copy(source, target, sems.at[first + n])
        for n, (source, target) in enumerate(zip(sources, targets))
    ]


def load_kernel(forces, velocity, lower, upper, counts_hbm, send, *refs):
    near, work_out, (slots, counts, work, sems) = refs[:3], refs[3], refs[4:]
    components, senders, planes, capacity = forces.shape
    chunks = capacity // lanes
    sources = [counts_hbm] + [forces.at[c] for c in range(components)]
    targets = [counts] + [slots.at[c] for c in range(components)]
    sources += [lower, upper] + [velocity.at[c] for c in range(components)]
    targets += [near[0], near[1]] + [near[2].at[c] for c in range(components)]
    copies = copies_of(sources, targets, sems)
    start_all(copies)
    outgoing = copies_of(
        [slots.at[c] for c in range(components)] + [work],
        [send.at[:, c] for c in range(components)] + [work_out],
        sems,
        len(copies),
    )

    def one_plane(x, n):
        def one_sender(s, n):
            count = counts[x, s]
            base = (x << plane_bit) + ((s * chunks) << count_bits)
            for k in range(chunks):
                live = jnp.maximum(count - k * lanes, 0)
                work[group + n + k] = base + (k << count_bits) + live
            return n + lax.div(count + lanes - 1, lanes)

        n = lax.fori_loop(0, senders, one_sender, n, unroll=4)
        for extra in range(group):
            work[group + n + extra] = x << plane_bit
        return lax.div(n + group - 1, group) * group

    copies[0].wait()
    total = lax.fori_loop(0, planes // 2, one_plane, 0)
    for c in range(components):
        copies[1 + c].wait()
        outgoing[c].start()
    total = lax.fori_loop(planes // 2, planes, one_plane, total)
    for extra in range(2 * group):
        work[group + total + extra] = 0
    work[0] = lax.div(total, group)
    outgoing[components].start()
    wait_all(copies[1 + components :])
    wait_all(outgoing)


def edge_kernel(velocity, first_out, last_out, columns, turned):
    components, planes, height, across = velocity.shape
    lines = components * planes
    lane = lane_iota((height, across))
    picked = jnp.zeros((height, across), jnp.float32)
    for k in range(lines):
        rolled = pltpu.roll(velocity[k // planes, k % planes], 2 * k + 1, 1)
        picked = jnp.where((lane >> 1) == k, rolled, picked)
    columns[...] = picked
    for p in range(height // lanes):
        turned[p] = columns[p * lanes : (p + 1) * lanes, :].T
        part = slice(p * lines, (p + 1) * lines)
        first_out[part, :] = turned[p, pl.ds(1, lines, stride=2), :]
        last_out[part, :] = turned[p, pl.ds(0, lines, stride=2), :]


def prepare_kernel(velocity, lower, upper, inner, ends, coefs, *refs):
    (rhs, inv, first) = refs[3:6]
    (inv_b, gain_b, rows, sems) = refs[6:]
    outgoing = copies_of(refs[3:6], refs[:3], sems)
    components, planes, height, across = velocity.shape
    steps = inv.shape[0] + 1
    last = steps - 1
    rest = height - segments * steps
    knots = segments + rest

    def of_step(ref, t):
        return ref[:, pl.ds(t, segments, stride=steps), :]

    one = jnp.ones((planes, segments, across), jnp.float32)
    zero = jnp.zeros_like(one)
    size = 8
    lane = lane_iota((size, across))

    def stencil_rows(n):
        return pl.ds(pl.multiple_of(n * size, size), size)

    def read_rows(n):
        part = stencil_rows(n)
        return [[velocity[c, x, part, :] for x in range(planes)] for c in range(components)]

    def stencil(values):
        found = []
        for x in range(planes):
            v = values[x]
            around = values[(x - 1) % planes] + values[(x + 1) % planes]
            around = around + jnp.where(lane == 0, 0.0, pltpu.roll(v, 1, 1))
            around = around + jnp.where(lane == across - 1, 0.0, pltpu.roll(v, across - 1, 1))
            found.append((1.0 - 4.0 * diffusion_number) * v + diffusion_number * around)
        return found

    def write_rows(n, values):
        part = stencil_rows(n)
        for c in range(components):
            for x in range(planes):
                rhs[c, x, part, :] = values[c][x]

    def factor(t, carry):
        d, d_b, low_gain, high_gain, sum_last, sum_first = carry
        back = last - 1 - t
        low, up = of_step(lower, t), of_step(upper, t)
        low_b, up_b = of_step(lower, back), of_step(upper, back)
        velocities = read_rows(t)
        e = 1.0 + low * d
        inverse = reciprocal(up + e)
        g = low * inverse
        e_b = 1.0 + up_b * d_b
        inverse_b = reciprocal(low_b + e_b)
        g_b = up_b * inverse_b
        found = [stencil(values) for values in velocities]
        inv[t] = inverse
        inv_b[back] = inverse_b
        gain_b[back] = g_b
        write_rows(t, found)
        return (
            e * inverse,
            e_b * inverse_b,
            low_gain * g,
            high_gain * g_b,
            inverse + g * sum_last,
            inverse_b + g_b * sum_first,
        )

    carry = lax.fori_loop(0, last, factor, (one, one, one, one, zero, zero), unroll=2)
    _, _, low_gain, high_gain, sum_last, sum_first = carry
    for n in range(last, height // size):
        write_rows(n, [stencil(values) for values in read_rows(n)])
    start_all(outgoing[:2])
    def weigh(t, q):
        first[t] = inv_b[t] * q
        return q * gain_b[t]

    lax.fori_loop(0, last, weigh, one, unroll=6)
    outgoing[2].start()

    low_sep, up_sep = of_step(lower, last), of_step(upper, last)
    segment = lax.broadcasted_iota(jnp.int32, one.shape, 1)
    is_end = segment == segments - 1
    above = jnp.where(is_end, 0.0, jnp.roll(sum_first, -1, axis=1))
    couple_high = up_sep * jnp.where(is_end, 1.0, jnp.roll(high_gain, -1, axis=1))
    killing = 1.0 + low_sep * sum_last + up_sep * above
    ends[2, :, :segments, :] = low_sep
    ends[3, :, :segments, :] = up_sep
    tail = slice(height - rest, height)
    low_rest, up_rest = lower[:, tail, :], upper[:, tail, :]
    for n, (value, other) in enumerate(
        (
            (low_sep * low_gain, low_rest),
            (couple_high, up_rest),
            (killing, jnp.ones_like(low_rest)),
        )
    ):
        for x in range(planes):
            rows[n, x * knots : x * knots + segments, :] = value[x]
            rows[n, x * knots + segments : (x + 1) * knots, :] = other[x]
    for x in range(planes):
        rows[3, x * knots : x * knots + segments, :] = high_gain[x]
        rows[4, x * knots : x * knots + segments, :] = sum_first[x]

    def row(n, s):
        return rows[n, pl.ds(s, planes, stride=knots), :]

    top = knots - 1
    one_row = jnp.ones((planes, across), jnp.float32)
    d, d_b = one_row, one_row
    inv_s, gain_s, ratio_s = [], [], []
    inv_sb, gain_sb = [None] * top, [None] * top
    for s in range(top):
        e = row(2, s) + row(0, s) * d
        inverse = reciprocal(row(1, s) + e)
        inv_s.append(inverse)
        gain_s.append(row(0, s) * inverse)
        ratio_s.append(row(1, s) * inverse)
        d = e * inverse
        back = top - 1 - s
        e_b = row(2, back) + row(1, back) * d_b
        inverse_b = reciprocal(row(0, back) + e_b)
        inv_sb[back] = inverse_b
        gain_sb[back] = row(1, back) * inverse_b
        d_b = e_b * inverse_b
        inner[0, s] = inv_s[s]
        inner[1, s] = gain_s[s]
        inner[2, s] = ratio_s[s]
    run = row(0, top)
    low_total = one_row
    sum_top = one_row
    rows[5, pl.ds(top, planes, stride=knots), :] = one_row
    for s in reversed(range(top)):
        weight = run * inv_s[s]
        rows[5, pl.ds(s, planes, stride=knots), :] = weight
        sum_top = sum_top + weight * row(2, s)
        run = run * gain_s[s]
        low_total = low_total * gain_s[s]
    run = row(3, 0)
    high_total = one_row
    sum_bottom = row(4, 0)
    rows[6, pl.ds(top, planes, stride=knots), :] = jnp.zeros_like(one_row)
    for s in range(top):
        weight = run * inv_sb[s]
        rows[6, pl.ds(s, planes, stride=knots), :] = weight
        sum_bottom = sum_bottom + weight * row(2, s)
        run = run * gain_sb[s]
        high_total = high_total * ratio_s[s]
    coef = (
        row(0, top) * low_total,
        sum_top,
        row(1, top),
        sum_bottom,
        row(3, 0) * high_total,
    )
    for n, value in enumerate(coef):
        coefs[n * planes : (n + 1) * planes, :] = value
    for n in range(2):
        for x in range(planes):
            ends[n, x] = rows[5 + n, x * knots : (x + 1) * knots, :]
    wait_all(outgoing)


def deposit_kernel(got, from_above, from_below, cells, ends, coefs, *refs):
    (deposit_hbm, swept, prefix, ratio, reduced, sums) = refs[6:12]
    (work, rhs, inv, first, lower, upper) = refs[12:18]
    (field, total, lefts, rights, columns, edges, in_sems, sems) = refs[18:]
    incoming = copies_of(refs[:6], refs[12:18], in_sems)
    start_all(incoming)
    components, planes, height, across = rhs.shape
    steps = inv.shape[0] + 1
    last = steps - 1
    knots = ends.shape[2]
    rest = knots - segments
    chunks = got.shape[2]
    parts = height // lanes
    shift = across.bit_length() - 1
    lines = components * planes
    kind = jnp.bfloat16 if max(height, across) <= 256 else jnp.float32

    total[...] = jnp.zeros_like(total)
    for p in range(parts):
        part = slice(p * lines, (p + 1) * lines)
        columns[p, pl.ds(0, lines, stride=2), :] = from_above[part, :]
        columns[p, pl.ds(1, lines, stride=2), :] = from_below[part, :]
        edges[p * lanes : (p + 1) * lanes, :] = diffusion_number * columns[p].T

    tile = 16
    base = lax.broadcasted_iota(jnp.int32, (tile, lanes), 0)
    height_ids = [(base + n * tile).astype(jnp.float32).astype(kind) for n in range(height // tile)]
    across_ids = height_ids[: across // tile]
    lane = lane_iota((1, lanes))
    one = jnp.ones((tile, lanes), jnp.bfloat16)
    none = jnp.zeros((tile, lanes), jnp.bfloat16)

    def spread(row, to):
        return jnp.broadcast_to(row, (tile, lanes)).astype(to)

    def build(n, half):
        for g in range(group):
            word = work[(n + 1) * group + g]
            ident = (word >> count_bits) & ((1 << (plane_bit - count_bits)) - 1)
            live = word & ((1 << count_bits) - 1)
            there = slice(g * lanes, (g + 1) * lanes)
            sender, chunk = lax.div(ident, chunks), lax.rem(ident, chunks)
            x = word >> plane_bit
            cell = cells[sender, chunk, pl.ds(x, 1), :]
            up = jnp.where(lane < live, cell >> shift, -1).astype(jnp.float32)
            side = (cell & (across - 1)).astype(jnp.float32)
            up, side = spread(up, kind), spread(side, kind)
            for i, ids in enumerate(height_ids):
                lefts[half][i * tile : (i + 1) * tile, there] = jnp.where(up == ids, one, none)
            masks = [side == ids for ids in across_ids]
            for c in range(components):
                force = got[sender, c, chunk, pl.ds(x, 1), :]
                rest_of = force - force.astype(jnp.bfloat16).astype(jnp.float32)
                for m, value in enumerate((force, rest_of)):
                    value = spread(value, jnp.bfloat16)
                    start = (m * components + c) * across
                    for i, mask in enumerate(masks):
                        place = slice(start + i * tile, start + (i + 1) * tile)
                        rights[half][place, there] = jnp.where(mask, value, none)

    def add(n, half):
        total[work[(n + 1) * group] >> plane_bit] += lax.dot_general(
            lefts[half][...],
            rights[half][...],
            (((1,), (1,)), ((), ())),
            preferred_element_type=jnp.float32,
        )

    def two_steps(n, carry):
        add(2 * n, 0)
        build(2 * n + 1, 1)
        add(2 * n + 1, 1)
        build(2 * n + 2, 0)
        return carry

    incoming[0].wait()
    build(0, 0)
    count = work[0]
    lax.fori_loop(0, lax.div(count, 2), two_steps, 0)

    @pl.when(lax.rem(count, 2) == 1)
    def _():
        add(count - 1, 0)

    wait_all(incoming[1:])

    wide = lane_iota((lanes, across))
    border = (wide == 0) | (wide == across - 1)

    def place(x):
        return [
            pltpu.make_async_copy(field.at[c, x], deposit_hbm.at[c, x], sems.at[c, x])
            for c in range(components)
        ]

    def combine(x, carry):
        for c in range(components):
            for p in range(parts):
                part = slice(p * lanes, (p + 1) * lanes)
                high = total[x, part, c * across : (c + 1) * across]
                low = total[x, part, (components + c) * across : (components + c + 1) * across]
                value = high + low
                field[c, x, part, :] = value.astype(jnp.bfloat16)
                edge = pltpu.roll(edges[part, :], lanes - 1 - 2 * (c * planes + x), 1)
                rhs[c, x, part, :] = rhs[c, x, part, :] + value + jnp.where(border, edge, 0.0)
        start_all(place(x))
        return carry

    lax.fori_loop(0, planes, combine, 0)
    sums[2 * lines : 2 * lines + coefs.shape[0], :] = coefs[...]

    zero = jnp.zeros((components, planes, segments, across), jnp.float32)

    def of_step(t):
        return rhs[:, :, pl.ds(t, segments, stride=steps), :]

    def forward(t, carry):
        value, start, run, before = carry
        force = of_step(t)
        low, inverse = lower[:, pl.ds(t, segments, stride=steps), :], inv[t]
        value = force + (low * before)[None] * value
        swept[t] = inverse[None] * value
        run = run * (low * inverse)
        prefix[t] = run
        ratio[t] = upper[:, pl.ds(t, segments, stride=steps), :] * inverse
        return value, start + first[t][None] * force, run, inverse

    one = jnp.ones((planes, segments, across), jnp.float32)
    value, start, _, inverse = lax.fori_loop(0, last, forward, (zero, zero, one, one), unroll=6)
    value = inverse[None] * value
    segment = lax.broadcasted_iota(jnp.int32, zero.shape, 2)
    after = jnp.where(segment == segments - 1, 0.0, jnp.roll(start, -1, axis=2))
    low_sep, up_sep = ends[2, :, :segments, :], ends[3, :, :segments, :]
    value = of_step(last) + low_sep[None] * value + up_sep[None] * after
    others = rhs[:, :, height - rest :, :]
    at_top = ends[0, :, :segments, :][None] * value + ends[0, :, segments:, :][None] * others
    at_bottom = ends[1, :, :segments, :][None] * value + ends[1, :, segments:, :][None] * others
    at_bottom = at_bottom + jnp.where(segment == 0, start, 0.0)
    for c in range(components):
        for x in range(planes):
            k = c * planes + x
            reduced[k * knots : k * knots + segments, :] = value[c, x]
            reduced[k * knots + segments : (k + 1) * knots, :] = others[c, x]
            top = jnp.sum(at_top[c, x], 0, keepdims=True)
            bottom = jnp.sum(at_bottom[c, x], 0, keepdims=True)
            sums[k : k + 1, :] = top
            sums[lines + k : lines + k + 1, :] = bottom

    for x in range(planes):
        wait_all(place(x))


def finish_kernel(inner, reduced, swept, ratio, prefix, *refs):
    walls = len(refs) - 7
    received = refs[:walls]
    out_hbm, sums, tops, after, before, out, sems = refs[walls:]
    components, planes, height, across = out.shape
    steps = swept.shape[0] + 1
    last = steps - 1
    lines = components * planes
    knots = inner.shape[1] + 1
    rest = knots - segments
    me = lax.axis_index("wall")
    for n in range(walls):
        sums[lax.rem(me + walls - n, walls)] = received[n][...]

    def coef(k, n):
        start = 2 * lines + n * planes
        return sums[k, start : start + planes, :]

    def wide(value):
        return jnp.concatenate([value] * components, 0)

    d = jnp.ones((planes, across), jnp.float32)
    value = jnp.zeros((lines, across), jnp.float32)
    values, ratios = [], []
    for k in range(walls):
        low, own, up = coef(k, 0), coef(k, 1), coef(k, 2)
        right = sums[k, :lines, :]
        if k + 1 < walls:
            high = up * coef(k + 1, 4)
            killing = own + up * coef(k + 1, 3)
            right = right + wide(up) * sums[k + 1, lines : 2 * lines, :]
        else:
            high = jnp.zeros_like(up)
            killing = own + up
        e = killing + low * d
        inverse = reciprocal(high + e)
        d = e * inverse
        value = (right + wide(low) * value) * wide(inverse)
        values.append(value)
        ratios.append(wide(high * inverse))
    tops[0] = jnp.zeros((lines, across), jnp.float32)
    tops[walls] = values[-1]
    for k in reversed(range(walls - 1)):
        values[k] = values[k] + ratios[k] * values[k + 1]
        tops[k + 1] = values[k]

    def row(s):
        return pl.ds(s, lines, stride=knots)

    run = tops[me]
    before[row(0), :] = run
    found = []
    for s in range(knots - 1):
        run = reduced[row(s), :] * wide(inner[0, s]) + wide(inner[1, s]) * run
        found.append(run)
    run = tops[me + 1]
    after[row(knots - 1), :] = run
    for s in reversed(range(knots - 1)):
        run = found[s] + wide(inner[2, s]) * run
        after[row(s), :] = run
        if s + 1 < segments:
            before[row(s + 1), :] = run

    def put(c, x, t, value):
        out[c, x, pl.ds(t, segments, stride=steps), :] = value

    copies = []
    half = planes // 2 if planes % 2 == 0 else planes
    for start in range(0, planes, half):
        part = [(c, x) for c in range(components) for x in range(start, start + half)]
        bottoms, starts = [], []
        for c, x in part:
            base = (c * planes + x) * knots
            bottoms.append(before[base : base + segments, :])
            starts.append(after[base : base + segments, :])
            out[c, x, height - rest :, :] = after[base + segments : base + knots, :]
            put(c, x, last, starts[-1])

        def backward(n, values):
            t = last - 1 - n
            found = []
            for (c, x), value, bottom in zip(part, values, bottoms):
                value = (swept[t, c, x] + prefix[t, x] * bottom) + ratio[t, x] * value
                put(c, x, t, value)
                found.append(value)
            return tuple(found)

        lax.fori_loop(0, last, backward, tuple(starts), unroll=10)
        for here in part:
            copy = pltpu.make_async_copy(out.at[here], out_hbm.at[here], sems.at[here])
            copy.start()
            copies.append(copy)
    wait_all(copies)


def shifted(block, axis, distance):
    length = lax.axis_size(axis)
    route = [(i, (i + distance) % length) for i in range(length)]
    return lax.ppermute(block, axis, route)


def everyone(block, axis):
    return [block] + [shifted(block, axis, n) for n in range(1, lax.axis_size(axis))]


def local(velocity, lower_weight, upper_weight, forces, cells, counts):
    components, planes, height, across = velocity.shape
    receivers, capacity = forces.shape[3], forces.shape[5]
    senders = cells.shape[2]
    walls = lax.axis_size("wall")
    lines = components * planes
    chunks = capacity // lanes
    counts_shape = (planes, senders)
    forces = forces.reshape(components, receivers, planes, capacity)
    cells = cells.reshape(senders, planes, capacity)
    counts = counts.reshape(senders, planes).T

    def hbm(*arrays):
        return [pltpu.with_memory_space_constraint(array, pltpu.HBM) for array in arrays]

    work_shape = (planes * (senders * chunks + group) + 4 * group,)
    send, lower_near, upper_near, velocity_near, work = call(
        load_kernel,
        (
            pltpu.HBM((receivers, components, planes, capacity), jnp.float32),
            f32(*lower_weight.shape),
            f32(*upper_weight.shape),
            f32(*velocity.shape),
            jax.ShapeDtypeStruct(work_shape, jnp.int32),
        ),
        (in_hbm, *[in_vmem] * 4),
        [in_hbm] * 5,
        [
            scratch(*forces.shape),
            pltpu.SMEM(counts_shape, jnp.int32),
            pltpu.SMEM(work_shape, jnp.int32),
            pltpu.SemaphoreType.DMA((3 * components + 4,)),
        ],
        4,
        1 << 16,
    )(*hbm(forces, velocity, lower_weight, upper_weight, counts))
    got = lax.all_to_all(send, "span", 0, 0, tiled=True)
    got = got.reshape(senders, components, planes, chunks, lanes).transpose(0, 1, 3, 2, 4)
    cells = cells.reshape(senders, planes, chunks, lanes).transpose(0, 2, 1, 3)
    edge_shape = (lines * height // lanes, lanes)
    first_column, last_column = call(
        edge_kernel,
        (f32(*edge_shape), f32(*edge_shape)),
        (in_vmem, in_vmem),
        [in_vmem],
        [scratch(height, across), scratch(height // lanes, lanes, lanes)],
        4,
        1 << 20,
    )(velocity_near)
    from_above = shifted(first_column, "span", -1)
    from_below = shifted(last_column, "span", 1)

    steps = height // segments - 1
    knots = height - segments * steps + segments
    step_shape = (steps - 1, planes, segments, across)
    staged = [velocity.shape, step_shape, step_shape]
    prepared = call(
        prepare_kernel,
        (
            f32(3, knots - 1, planes, across),
            f32(4, planes, knots, across),
            f32(5 * planes, across),
            *[pltpu.HBM(shape, jnp.float32) for shape in staged],
        ),
        [in_vmem] * 3 + [in_hbm] * 3,
        [in_vmem] * 3,
        [
            *[scratch(*shape) for shape in staged],
            scratch(*step_shape),
            scratch(*step_shape),
            scratch(7, planes * knots, across),
            pltpu.SemaphoreType.DMA((3,)),
        ],
        12,
        1 << 24,
    )(velocity_near, lower_near, upper_near)
    (inner, ends, coefs, rhs_start, inv, first) = prepared

    sum_rows = -(-(2 * lines + 5 * planes) // 8) * 8
    wide = 2 * components * across
    deposit, swept, prefix, ratio, reduced, sums = call(
        deposit_kernel,
        (
            jax.ShapeDtypeStruct(velocity.shape, jnp.bfloat16),
            f32(steps - 1, components, planes, segments, across),
            f32(*step_shape),
            f32(*step_shape),
            f32(lines * knots, across),
            f32(sum_rows, across),
        ),
        (in_hbm, *[in_vmem] * 5),
        [in_vmem] * 7 + [in_hbm] * 5,
        [
            pltpu.SMEM(work_shape, jnp.int32),
            *[scratch(*shape) for shape in staged],
            scratch(*lower_weight.shape),
            scratch(*upper_weight.shape),
            pltpu.VMEM(velocity.shape, jnp.bfloat16),
            scratch(planes, height, wide),
            [pltpu.VMEM((height, group * lanes), jnp.bfloat16)] * 2,
            [pltpu.VMEM((wide, group * lanes), jnp.bfloat16)] * 2,
            scratch(height // lanes, lanes, lanes),
            scratch(height, lanes),
            pltpu.SemaphoreType.DMA((6,)),
            pltpu.SemaphoreType.DMA((components, planes)),
        ],
        24,
        1 << 32,
    )(
        got,
        from_above,
        from_below,
        cells,
        ends,
        coefs,
        work,
        *hbm(rhs_start, inv, first, lower_weight, upper_weight),
    )
    all_sums = everyone(sums, "wall")

    velocity_next = call(
        finish_kernel,
        f32(*velocity.shape),
        in_hbm,
        [in_vmem] * (5 + walls),
        [
            scratch(walls, sum_rows, across),
            scratch(walls + 1, lines, across),
            scratch(lines * knots, across),
            scratch(lines * knots, across),
            scratch(*velocity.shape),
            pltpu.SemaphoreType.DMA((components, planes)),
        ],
        8,
        1 << 22,
    )(inner, reduced, swept, ratio, prefix, *all_sums)
    return (velocity_next, deposit)


def solution(mesh):
    placed = (
        P(None, None, "wall", "span"),
        P(None, "wall", "span"),
        P(None, "wall", "span"),
        P(None, "wall", "span", None, None, None),
        P("wall", "span", None, None, None),
        P("wall", "span", None, None),
    )
    return jax.shard_map(
        local,
        mesh=mesh,
        in_specs=placed,
        out_specs=(P(None, None, "wall", "span"), P(None, None, "wall", "span")),
        check_vma=False,
    )
```

```python
import jax
import jax.numpy as jnp
from jax import lax
from jax.experimental import pallas as pl
from jax.experimental.pallas import tpu as pltpu
from jax.sharding import PartitionSpec as P

diffusion_number = 0.2
segments = 8
lanes = 128
group = 8
count_bits, plane_bit = 10, 24
in_vmem = pl.BlockSpec(memory_space=pltpu.VMEM)
in_smem = pl.BlockSpec(memory_space=pltpu.SMEM)
in_hbm = pl.BlockSpec(memory_space=pltpu.HBM)


def call(body, out_shape, out_specs, in_specs, scratch, mebibytes, flops):
    return pl.pallas_call(
        body,
        out_shape=out_shape,
        in_specs=in_specs,
        out_specs=out_specs,
        scratch_shapes=scratch,
        compiler_params=pltpu.CompilerParams(vmem_limit_bytes=mebibytes << 20),
        cost_estimate=pl.CostEstimate(flops=flops, bytes_accessed=4 << 20, transcendentals=0),
    )


def f32(*shape):
    return jax.ShapeDtypeStruct(shape, jnp.float32)


def scratch(*shape):
    return pltpu.VMEM(shape, jnp.float32)


def lane_iota(shape):
    return lax.broadcasted_iota(jnp.int32, shape, len(shape) - 1)


def reciprocal(value):
    rough = pl.reciprocal(value, approx=True)
    return rough * (2.0 - value * rough)


def start_all(copies):
    for copy in copies:
        copy.start()


def wait_all(copies):
    for copy in copies:
        copy.wait()


def copies_of(sources, targets, sems, first=0):
    return [
        pltpu.make_async_copy(source, target, sems.at[first + n])
        for n, (source, target) in enumerate(zip(sources, targets))
    ]


def load_kernel(forces, velocity, lower, upper, counts_hbm, send, *refs):
    near, work_out, (slots, counts, work, sems) = refs[:3], refs[3], refs[4:]
    components, senders, planes, capacity = forces.shape
    chunks = capacity // lanes
    sources = [counts_hbm] + [forces.at[c] for c in range(components)]
    targets = [counts] + [slots.at[c] for c in range(components)]
    sources += [lower, upper] + [velocity.at[c] for c in range(components)]
    targets += [near[0], near[1]] + [near[2].at[c] for c in range(components)]
    copies = copies_of(sources, targets, sems)
    start_all(copies)
    outgoing = copies_of(
        [slots.at[c] for c in range(components)] + [work],
        [send.at[:, c] for c in range(components)] + [work_out],
        sems,
        len(copies),
    )

    def one_plane(x, n):
        def one_sender(s, n):
            count = counts[x, s]
            base = (x << plane_bit) + ((s * chunks) << count_bits)
            for k in range(chunks):
                live = jnp.maximum(count - k * lanes, 0)
                work[group + n + k] = base + (k << count_bits) + live
            return n + lax.div(count + lanes - 1, lanes)

        n = lax.fori_loop(0, senders, one_sender, n, unroll=4)
        for extra in range(group):
            work[group + n + extra] = x << plane_bit
        return lax.div(n + group - 1, group) * group

    copies[0].wait()
    total = lax.fori_loop(0, planes // 2, one_plane, 0)
    for c in range(components):
        copies[1 + c].wait()
        outgoing[c].start()
    total = lax.fori_loop(planes // 2, planes, one_plane, total)
    for extra in range(2 * group):
        work[group + total + extra] = 0
    work[0] = lax.div(total, group)
    outgoing[components].start()
    wait_all(copies[1 + components :])
    wait_all(outgoing)


def edge_kernel(velocity, first_out, last_out, columns, turned):
    components, planes, height, across = velocity.shape
    lines = components * planes
    lane = lane_iota((height, across))
    picked = jnp.zeros((height, across), jnp.float32)
    for k in range(lines):
        rolled = pltpu.roll(velocity[k // planes, k % planes], 2 * k + 1, 1)
        picked = jnp.where((lane >> 1) == k, rolled, picked)
    columns[...] = picked
    for p in range(height // lanes):
        turned[p] = columns[p * lanes : (p + 1) * lanes, :].T
        part = slice(p * lines, (p + 1) * lines)
        first_out[part, :] = turned[p, pl.ds(1, lines, stride=2), :]
        last_out[part, :] = turned[p, pl.ds(0, lines, stride=2), :]


def prepare_kernel(velocity, lower, upper, inner, ends, coefs, *refs):
    (rhs, inv, first) = refs[3:6]
    (inv_b, gain_b, rows, sems) = refs[6:]
    outgoing = copies_of(refs[3:6], refs[:3], sems)
    components, planes, height, across = velocity.shape
    steps = inv.shape[0] + 1
    last = steps - 1
    rest = height - segments * steps
    knots = segments + rest

    def of_step(ref, t):
        return ref[:, pl.ds(t, segments, stride=steps), :]

    one = jnp.ones((planes, segments, across), jnp.float32)
    zero = jnp.zeros_like(one)
    size = 8
    lane = lane_iota((size, across))

    def stencil_rows(n):
        return pl.ds(pl.multiple_of(n * size, size), size)

    def read_rows(n):
        part = stencil_rows(n)
        return [[velocity[c, x, part, :] for x in range(planes)] for c in range(components)]

    def stencil(values):
        found = []
        for x in range(planes):
            v = values[x]
            around = values[(x - 1) % planes] + values[(x + 1) % planes]
            around = around + jnp.where(lane == 0, 0.0, pltpu.roll(v, 1, 1))
            around = around + jnp.where(lane == across - 1, 0.0, pltpu.roll(v, across - 1, 1))
            found.append((1.0 - 4.0 * diffusion_number) * v + diffusion_number * around)
        return found

    def write_rows(n, values):
        part = stencil_rows(n)
        for c in range(components):
            for x in range(planes):
                rhs[c, x, part, :] = values[c][x]

    def factor(t, carry):
        d, d_b, low_gain, high_gain, sum_last, sum_first = carry
        back = last - 1 - t
        low, up = of_step(lower, t), of_step(upper, t)
        low_b, up_b = of_step(lower, back), of_step(upper, back)
        velocities = read_rows(t)
        e = 1.0 + low * d
        inverse = reciprocal(up + e)
        g = low * inverse
        e_b = 1.0 + up_b * d_b
        inverse_b = reciprocal(low_b + e_b)
        g_b = up_b * inverse_b
        found = [stencil(values) for values in velocities]
        inv[t] = inverse
        inv_b[back] = inverse_b
        gain_b[back] = g_b
        write_rows(t, found)
        return (
            e * inverse,
            e_b * inverse_b,
            low_gain * g,
            high_gain * g_b,
            inverse + g * sum_last,
            inverse_b + g_b * sum_first,
        )

    carry = lax.fori_loop(0, last, factor, (one, one, one, one, zero, zero), unroll=2)
    _, _, low_gain, high_gain, sum_last, sum_first = carry
    for n in range(last, height // size):
        write_rows(n, [stencil(values) for values in read_rows(n)])
    start_all(outgoing[:2])
    def weigh(t, q):
        first[t] = inv_b[t] * q
        return q * gain_b[t]

    lax.fori_loop(0, last, weigh, one, unroll=6)
    outgoing[2].start()

    low_sep, up_sep = of_step(lower, last), of_step(upper, last)
    segment = lax.broadcasted_iota(jnp.int32, one.shape, 1)
    is_end = segment == segments - 1
    above = jnp.where(is_end, 0.0, jnp.roll(sum_first, -1, axis=1))
    couple_high = up_sep * jnp.where(is_end, 1.0, jnp.roll(high_gain, -1, axis=1))
    killing = 1.0 + low_sep * sum_last + up_sep * above
    ends[2, :, :segments, :] = low_sep
    ends[3, :, :segments, :] = up_sep
    tail = slice(height - rest, height)
    low_rest, up_rest = lower[:, tail, :], upper[:, tail, :]
    for n, (value, other) in enumerate(
        (
            (low_sep * low_gain, low_rest),
            (couple_high, up_rest),
            (killing, jnp.ones_like(low_rest)),
        )
    ):
        for x in range(planes):
            rows[n, x * knots : x * knots + segments, :] = value[x]
            rows[n, x * knots + segments : (x + 1) * knots, :] = other[x]
    for x in range(planes):
        rows[3, x * knots : x * knots + segments, :] = high_gain[x]
        rows[4, x * knots : x * knots + segments, :] = sum_first[x]

    def row(n, s):
        return rows[n, pl.ds(s, planes, stride=knots), :]

    top = knots - 1
    one_row = jnp.ones((planes, across), jnp.float32)
    d, d_b = one_row, one_row
    inv_s, gain_s, ratio_s = [], [], []
    inv_sb, gain_sb = [None] * top, [None] * top
    for s in range(top):
        e = row(2, s) + row(0, s) * d
        inverse = reciprocal(row(1, s) + e)
        inv_s.append(inverse)
        gain_s.append(row(0, s) * inverse)
        ratio_s.append(row(1, s) * inverse)
        d = e * inverse
        back = top - 1 - s
        e_b = row(2, back) + row(1, back) * d_b
        inverse_b = reciprocal(row(0, back) + e_b)
        inv_sb[back] = inverse_b
        gain_sb[back] = row(1, back) * inverse_b
        d_b = e_b * inverse_b
        inner[0, s] = inv_s[s]
        inner[1, s] = gain_s[s]
        inner[2, s] = ratio_s[s]
    run = row(0, top)
    low_total = one_row
    sum_top = one_row
    rows[5, pl.ds(top, planes, stride=knots), :] = one_row
    for s in reversed(range(top)):
        weight = run * inv_s[s]
        rows[5, pl.ds(s, planes, stride=knots), :] = weight
        sum_top = sum_top + weight * row(2, s)
        run = run * gain_s[s]
        low_total = low_total * gain_s[s]
    run = row(3, 0)
    high_total = one_row
    sum_bottom = row(4, 0)
    rows[6, pl.ds(top, planes, stride=knots), :] = jnp.zeros_like(one_row)
    for s in range(top):
        weight = run * inv_sb[s]
        rows[6, pl.ds(s, planes, stride=knots), :] = weight
        sum_bottom = sum_bottom + weight * row(2, s)
        run = run * gain_sb[s]
        high_total = high_total * ratio_s[s]
    coef = (
        row(0, top) * low_total,
        sum_top,
        row(1, top),
        sum_bottom,
        row(3, 0) * high_total,
    )
    for n, value in enumerate(coef):
        coefs[n * planes : (n + 1) * planes, :] = value
    for n in range(2):
        for x in range(planes):
            ends[n, x] = rows[5 + n, x * knots : (x + 1) * knots, :]
    wait_all(outgoing)


def scatter_kernel(got, cells, work_in, coefs, total, work, lefts, rights, sem):
    del coefs
    listed = pltpu.make_async_copy(work_in, work, sem)
    listed.start()
    components, chunks = got.shape[1], got.shape[2]
    _, height, wide = total.shape
    across = wide // (2 * components)
    shift = across.bit_length() - 1
    kind = jnp.bfloat16 if max(height, across) <= 256 else jnp.float32
    total[...] = jnp.zeros_like(total)

    tile = 16
    base = lax.broadcasted_iota(jnp.int32, (tile, lanes), 0)
    height_ids = [(base + n * tile).astype(jnp.float32).astype(kind) for n in range(height // tile)]
    across_ids = height_ids[: across // tile]
    lane = lane_iota((1, lanes))
    one = jnp.ones((tile, lanes), jnp.bfloat16)
    none = jnp.zeros((tile, lanes), jnp.bfloat16)

    def spread(row, to):
        return jnp.broadcast_to(row, (tile, lanes)).astype(to)

    def build(n, half):
        for g in range(group):
            word = work[(n + 1) * group + g]
            ident = (word >> count_bits) & ((1 << (plane_bit - count_bits)) - 1)
            live = word & ((1 << count_bits) - 1)
            there = slice(g * lanes, (g + 1) * lanes)
            sender, chunk = lax.div(ident, chunks), lax.rem(ident, chunks)
            x = word >> plane_bit
            cell = cells[sender, chunk, pl.ds(x, 1), :]
            up = jnp.where(lane < live, cell >> shift, -1).astype(jnp.float32)
            side = (cell & (across - 1)).astype(jnp.float32)
            up, side = spread(up, kind), spread(side, kind)
            for i, ids in enumerate(height_ids):
                lefts[half][i * tile : (i + 1) * tile, there] = jnp.where(up == ids, one, none)
            masks = [side == ids for ids in across_ids]
            for c in range(components):
                force = got[sender, c, chunk, pl.ds(x, 1), :]
                rest_of = force - force.astype(jnp.bfloat16).astype(jnp.float32)
                for m, value in enumerate((force, rest_of)):
                    value = spread(value, jnp.bfloat16)
                    start = (m * components + c) * across
                    for i, mask in enumerate(masks):
                        place = slice(start + i * tile, start + (i + 1) * tile)
                        rights[half][place, there] = jnp.where(mask, value, none)

    def add(n, half):
        total[work[(n + 1) * group] >> plane_bit] += lax.dot_general(
            lefts[half][...],
            rights[half][...],
            (((1,), (1,)), ((), ())),
            preferred_element_type=jnp.float32,
        )

    def two_steps(n, carry):
        add(2 * n, 0)
        build(2 * n + 1, 1)
        add(2 * n + 1, 1)
        build(2 * n + 2, 0)
        return carry

    listed.wait()
    build(0, 0)
    count = work[0]
    lax.fori_loop(0, lax.div(count, 2), two_steps, 0)

    @pl.when(lax.rem(count, 2) == 1)
    def _():
        add(count - 1, 0)


def sweep_kernel(total, from_above, from_below, rhs_start, inv, first, lower, upper, *refs):
    (ends, coefs, deposit_hbm, swept, prefix, ratio, reduced, sums) = refs[:8]
    (rhs, field, columns, edges, sems) = refs[8:]
    components, planes, height, across = rhs.shape
    steps = inv.shape[0] + 1
    last = steps - 1
    knots = ends.shape[2]
    rest = knots - segments
    parts = height // lanes
    lines = components * planes
    for p in range(parts):
        part = slice(p * lines, (p + 1) * lines)
        columns[p, pl.ds(0, lines, stride=2), :] = from_above[part, :]
        columns[p, pl.ds(1, lines, stride=2), :] = from_below[part, :]
        edges[p * lanes : (p + 1) * lanes, :] = diffusion_number * columns[p].T

    wide = lane_iota((lanes, across))
    border = (wide == 0) | (wide == across - 1)

    def place(x):
        return [
            pltpu.make_async_copy(field.at[c, x], deposit_hbm.at[c, x], sems.at[c, x])
            for c in range(components)
        ]

    def combine(x, carry):
        for c in range(components):
            for p in range(parts):
                part = slice(p * lanes, (p + 1) * lanes)
                high = total[x, part, c * across : (c + 1) * across]
                low = total[x, part, (components + c) * across : (components + c + 1) * across]
                value = high + low
                field[c, x, part, :] = value.astype(jnp.bfloat16)
                edge = pltpu.roll(edges[part, :], lanes - 1 - 2 * (c * planes + x), 1)
                rhs[c, x, part, :] = rhs_start[c, x, part, :] + value + jnp.where(border, edge, 0.0)
        start_all(place(x))
        return carry

    lax.fori_loop(0, planes, combine, 0)
    sums[2 * lines : 2 * lines + coefs.shape[0], :] = coefs[...]

    zero = jnp.zeros((components, planes, segments, across), jnp.float32)

    def of_step(t):
        return rhs[:, :, pl.ds(t, segments, stride=steps), :]

    def forward(t, carry):
        value, start, run, before = carry
        force = of_step(t)
        low, inverse = lower[:, pl.ds(t, segments, stride=steps), :], inv[t]
        value = force + (low * before)[None] * value
        swept[t] = inverse[None] * value
        run = run * (low * inverse)
        prefix[t] = run
        ratio[t] = upper[:, pl.ds(t, segments, stride=steps), :] * inverse
        return value, start + first[t][None] * force, run, inverse

    one = jnp.ones((planes, segments, across), jnp.float32)
    value, start, _, inverse = lax.fori_loop(0, last, forward, (zero, zero, one, one), unroll=6)
    value = inverse[None] * value
    segment = lax.broadcasted_iota(jnp.int32, zero.shape, 2)
    after = jnp.where(segment == segments - 1, 0.0, jnp.roll(start, -1, axis=2))
    low_sep, up_sep = ends[2, :, :segments, :], ends[3, :, :segments, :]
    value = of_step(last) + low_sep[None] * value + up_sep[None] * after
    others = rhs[:, :, height - rest :, :]
    at_top = ends[0, :, :segments, :][None] * value + ends[0, :, segments:, :][None] * others
    at_bottom = ends[1, :, :segments, :][None] * value + ends[1, :, segments:, :][None] * others
    at_bottom = at_bottom + jnp.where(segment == 0, start, 0.0)
    for c in range(components):
        for x in range(planes):
            k = c * planes + x
            reduced[k * knots : k * knots + segments, :] = value[c, x]
            reduced[k * knots + segments : (k + 1) * knots, :] = others[c, x]
            top = jnp.sum(at_top[c, x], 0, keepdims=True)
            bottom = jnp.sum(at_bottom[c, x], 0, keepdims=True)
            sums[k : k + 1, :] = top
            sums[lines + k : lines + k + 1, :] = bottom

    for x in range(planes):
        wait_all(place(x))


def finish_kernel(inner, reduced, swept, ratio, prefix, *refs):
    walls = len(refs) - 7
    received = refs[:walls]
    out_hbm, sums, tops, after, before, out, sems = refs[walls:]
    components, planes, height, across = out.shape
    steps = swept.shape[0] + 1
    last = steps - 1
    lines = components * planes
    knots = inner.shape[1] + 1
    rest = knots - segments
    me = lax.axis_index("wall")
    for n in range(walls):
        sums[lax.rem(me + walls - n, walls)] = received[n][...]

    def coef(k, n):
        start = 2 * lines + n * planes
        return sums[k, start : start + planes, :]

    def wide(value):
        return jnp.concatenate([value] * components, 0)

    d = jnp.ones((planes, across), jnp.float32)
    value = jnp.zeros((lines, across), jnp.float32)
    values, ratios = [], []
    for k in range(walls):
        low, own, up = coef(k, 0), coef(k, 1), coef(k, 2)
        right = sums[k, :lines, :]
        if k + 1 < walls:
            high = up * coef(k + 1, 4)
            killing = own + up * coef(k + 1, 3)
            right = right + wide(up) * sums[k + 1, lines : 2 * lines, :]
        else:
            high = jnp.zeros_like(up)
            killing = own + up
        e = killing + low * d
        inverse = reciprocal(high + e)
        d = e * inverse
        value = (right + wide(low) * value) * wide(inverse)
        values.append(value)
        ratios.append(wide(high * inverse))
    tops[0] = jnp.zeros((lines, across), jnp.float32)
    tops[walls] = values[-1]
    for k in reversed(range(walls - 1)):
        values[k] = values[k] + ratios[k] * values[k + 1]
        tops[k + 1] = values[k]

    def row(s):
        return pl.ds(s, lines, stride=knots)

    run = tops[me]
    before[row(0), :] = run
    found = []
    for s in range(knots - 1):
        run = reduced[row(s), :] * wide(inner[0, s]) + wide(inner[1, s]) * run
        found.append(run)
    run = tops[me + 1]
    after[row(knots - 1), :] = run
    for s in reversed(range(knots - 1)):
        run = found[s] + wide(inner[2, s]) * run
        after[row(s), :] = run
        if s + 1 < segments:
            before[row(s + 1), :] = run

    def put(c, x, t, value):
        out[c, x, pl.ds(t, segments, stride=steps), :] = value

    copies = []
    half = planes // 2 if planes % 2 == 0 else planes
    for start in range(0, planes, half):
        part = [(c, x) for c in range(components) for x in range(start, start + half)]
        bottoms, starts = [], []
        for c, x in part:
            base = (c * planes + x) * knots
            bottoms.append(before[base : base + segments, :])
            starts.append(after[base : base + segments, :])
            out[c, x, height - rest :, :] = after[base + segments : base + knots, :]
            put(c, x, last, starts[-1])

        def backward(n, values):
            t = last - 1 - n
            found = []
            for (c, x), value, bottom in zip(part, values, bottoms):
                value = (swept[t, c, x] + prefix[t, x] * bottom) + ratio[t, x] * value
                put(c, x, t, value)
                found.append(value)
            return tuple(found)

        lax.fori_loop(0, last, backward, tuple(starts), unroll=10)
        for here in part:
            copy = pltpu.make_async_copy(out.at[here], out_hbm.at[here], sems.at[here])
            copy.start()
            copies.append(copy)
    wait_all(copies)


def shifted(block, axis, distance):
    length = lax.axis_size(axis)
    route = [(i, (i + distance) % length) for i in range(length)]
    return lax.ppermute(block, axis, route)


def everyone(block, axis):
    return [block] + [shifted(block, axis, n) for n in range(1, lax.axis_size(axis))]


def local(velocity, lower_weight, upper_weight, forces, cells, counts):
    components, planes, height, across = velocity.shape
    receivers, capacity = forces.shape[3], forces.shape[5]
    senders = cells.shape[2]
    walls = lax.axis_size("wall")
    lines = components * planes
    chunks = capacity // lanes
    counts_shape = (planes, senders)
    forces = forces.reshape(components, receivers, planes, capacity)
    cells = cells.reshape(senders, planes, capacity)
    counts = counts.reshape(senders, planes).T

    def hbm(*arrays):
        return [pltpu.with_memory_space_constraint(array, pltpu.HBM) for array in arrays]

    work_shape = (planes * (senders * chunks + group) + 4 * group,)
    send, lower_near, upper_near, velocity_near, work = call(
        load_kernel,
        (
            pltpu.HBM((receivers, components, planes, capacity), jnp.float32),
            f32(*lower_weight.shape),
            f32(*upper_weight.shape),
            f32(*velocity.shape),
            jax.ShapeDtypeStruct(work_shape, jnp.int32),
        ),
        (in_hbm, *[in_vmem] * 4),
        [in_hbm] * 5,
        [
            scratch(*forces.shape),
            pltpu.SMEM(counts_shape, jnp.int32),
            pltpu.SMEM(work_shape, jnp.int32),
            pltpu.SemaphoreType.DMA((3 * components + 4,)),
        ],
        4,
        1 << 16,
    )(*hbm(forces, velocity, lower_weight, upper_weight, counts))
    got = lax.all_to_all(send, "span", 0, 0, tiled=True)
    got = got.reshape(senders, components, planes, chunks, lanes).transpose(0, 1, 3, 2, 4)
    cells = cells.reshape(senders, planes, chunks, lanes).transpose(0, 2, 1, 3)
    edge_shape = (lines * height // lanes, lanes)
    first_column, last_column = call(
        edge_kernel,
        (f32(*edge_shape), f32(*edge_shape)),
        (in_vmem, in_vmem),
        [in_vmem],
        [scratch(height, across), scratch(height // lanes, lanes, lanes)],
        4,
        1 << 20,
    )(velocity_near)
    from_above = shifted(first_column, "span", -1)
    from_below = shifted(last_column, "span", 1)

    steps = height // segments - 1
    knots = height - segments * steps + segments
    step_shape = (steps - 1, planes, segments, across)
    staged = [velocity.shape, step_shape, step_shape]
    prepared = call(
        prepare_kernel,
        (
            f32(3, knots - 1, planes, across),
            f32(4, planes, knots, across),
            f32(5 * planes, across),
            *[pltpu.HBM(shape, jnp.float32) for shape in staged],
        ),
        [in_vmem] * 3 + [in_hbm] * 3,
        [in_vmem] * 3,
        [
            *[scratch(*shape) for shape in staged],
            scratch(*step_shape),
            scratch(*step_shape),
            scratch(7, planes * knots, across),
            pltpu.SemaphoreType.DMA((3,)),
        ],
        12,
        1 << 24,
    )(velocity_near, lower_near, upper_near)
    (inner, ends, coefs, rhs_start, inv, first) = prepared

    sum_rows = -(-(2 * lines + 5 * planes) // 8) * 8
    wide = 2 * components * across
    total = call(
        scatter_kernel,
        f32(planes, height, wide),
        in_vmem,
        [in_vmem] * 4,
        [
            pltpu.SMEM(work_shape, jnp.int32),
            [pltpu.VMEM((height, group * lanes), jnp.bfloat16)] * 2,
            [pltpu.VMEM((wide, group * lanes), jnp.bfloat16)] * 2,
            pltpu.SemaphoreType.DMA,
        ],
        16,
        1 << 32,
    )(got, cells, work, coefs)

    deposit, swept, prefix, ratio, reduced, sums = call(
        sweep_kernel,
        (
            jax.ShapeDtypeStruct(velocity.shape, jnp.bfloat16),
            f32(steps - 1, components, planes, segments, across),
            f32(*step_shape),
            f32(*step_shape),
            f32(lines * knots, across),
            f32(sum_rows, across),
        ),
        (in_hbm, *[in_vmem] * 5),
        [in_vmem] * 10,
        [
            scratch(*velocity.shape),
            pltpu.VMEM(velocity.shape, jnp.bfloat16),
            scratch(height // lanes, lanes, lanes),
            scratch(height, lanes),
            pltpu.SemaphoreType.DMA((components, planes)),
        ],
        8,
        1 << 24,
    )(
        total,
        from_above,
        from_below,
        rhs_start,
        inv,
        first,
        lower_weight,
        upper_weight,
        ends,
        coefs,
    )
    all_sums = everyone(sums, "wall")

    velocity_next = call(
        finish_kernel,
        f32(*velocity.shape),
        in_hbm,
        [in_vmem] * (5 + walls),
        [
            scratch(walls, sum_rows, across),
            scratch(walls + 1, lines, across),
            scratch(lines * knots, across),
            scratch(lines * knots, across),
            scratch(*velocity.shape),
            pltpu.SemaphoreType.DMA((components, planes)),
        ],
        8,
        1 << 22,
    )(inner, reduced, swept, ratio, prefix, *all_sums)
    return (velocity_next, deposit)


def solution(mesh):
    placed = (
        P(None, None, "wall", "span"),
        P(None, "wall", "span"),
        P(None, "wall", "span"),
        P(None, "wall", "span", None, None, None),
        P("wall", "span", None, None, None),
        P("wall", "span", None, None),
    )
    return jax.shard_map(
        local,
        mesh=mesh,
        in_specs=placed,
        out_specs=(P(None, None, "wall", "span"), P(None, None, "wall", "span")),
        check_vma=False,
    )
```

```python
import jax
import jax.numpy as jnp
from jax import lax
from jax.experimental import pallas as pl
from jax.experimental.pallas import tpu as pltpu
from jax.sharding import PartitionSpec as P

diffusion_number = 0.2
segments = 8
lanes = 128
group = 8
count_bits, plane_bit = 10, 24
in_vmem = pl.BlockSpec(memory_space=pltpu.VMEM)
in_smem = pl.BlockSpec(memory_space=pltpu.SMEM)
in_hbm = pl.BlockSpec(memory_space=pltpu.HBM)


def call(body, out_shape, out_specs, in_specs, scratch, mebibytes, flops):
    return pl.pallas_call(
        body,
        out_shape=out_shape,
        in_specs=in_specs,
        out_specs=out_specs,
        scratch_shapes=scratch,
        compiler_params=pltpu.CompilerParams(vmem_limit_bytes=mebibytes << 20),
        cost_estimate=pl.CostEstimate(flops=flops, bytes_accessed=4 << 20, transcendentals=0),
    )


def f32(*shape):
    return jax.ShapeDtypeStruct(shape, jnp.float32)


def scratch(*shape):
    return pltpu.VMEM(shape, jnp.float32)


def lane_iota(shape):
    return lax.broadcasted_iota(jnp.int32, shape, len(shape) - 1)


def reciprocal(value):
    rough = pl.reciprocal(value, approx=True)
    return rough * (2.0 - value * rough)


def start_all(copies):
    for copy in copies:
        copy.start()


def wait_all(copies):
    for copy in copies:
        copy.wait()


def copies_of(sources, targets, sems, first=0):
    return [
        pltpu.make_async_copy(source, target, sems.at[first + n])
        for n, (source, target) in enumerate(zip(sources, targets))
    ]


def load_kernel(forces, velocity, lower, upper, counts_hbm, send, *refs):
    near, work_out, (slots, counts, work, sems) = refs[:3], refs[3], refs[4:]
    components, senders, planes, capacity = forces.shape
    chunks = capacity // lanes
    sources = [counts_hbm] + [forces.at[c] for c in range(components)]
    targets = [counts] + [slots.at[c] for c in range(components)]
    sources += [lower, upper] + [velocity.at[c] for c in range(components)]
    targets += [near[0], near[1]] + [near[2].at[c] for c in range(components)]
    copies = copies_of(sources, targets, sems)
    start_all(copies)
    outgoing = copies_of(
        [slots.at[c] for c in range(components)] + [work],
        [send.at[:, c] for c in range(components)] + [work_out],
        sems,
        len(copies),
    )

    def one_plane(x, n):
        def one_sender(s, n):
            count = counts[x, s]
            base = (x << plane_bit) + ((s * chunks) << count_bits)
            for k in range(chunks):
                live = jnp.maximum(count - k * lanes, 0)
                work[group + n + k] = base + (k << count_bits) + live
            return n + lax.div(count + lanes - 1, lanes)

        n = lax.fori_loop(0, senders, one_sender, n, unroll=4)
        for extra in range(group):
            work[group + n + extra] = x << plane_bit
        return lax.div(n + group - 1, group) * group

    copies[0].wait()
    total = lax.fori_loop(0, planes // 2, one_plane, 0)
    for c in range(components):
        copies[1 + c].wait()
        outgoing[c].start()
    total = lax.fori_loop(planes // 2, planes, one_plane, total)
    for extra in range(2 * group):
        work[group + total + extra] = 0
    work[0] = lax.div(total, group)
    outgoing[components].start()
    wait_all(copies[1 + components :])
    wait_all(outgoing)


def edge_kernel(velocity, first_out, last_out, columns, turned):
    components, planes, height, across = velocity.shape
    lines = components * planes
    lane = lane_iota((height, across))
    picked = jnp.zeros((height, across), jnp.float32)
    for k in range(lines):
        rolled = pltpu.roll(velocity[k // planes, k % planes], 2 * k + 1, 1)
        picked = jnp.where((lane >> 1) == k, rolled, picked)
    columns[...] = picked
    for p in range(height // lanes):
        turned[p] = columns[p * lanes : (p + 1) * lanes, :].T
        part = slice(p * lines, (p + 1) * lines)
        first_out[part, :] = turned[p, pl.ds(1, lines, stride=2), :]
        last_out[part, :] = turned[p, pl.ds(0, lines, stride=2), :]


def prepare_kernel(velocity, lower, upper, inner, ends, coefs, *refs):
    (rhs, inv, first) = refs[3:6]
    (inv_b, gain_b, rows, sems) = refs[6:]
    outgoing = copies_of(refs[3:6], refs[:3], sems)
    components, planes, height, across = velocity.shape
    steps = inv.shape[0] + 1
    last = steps - 1
    rest = height - segments * steps
    knots = segments + rest

    def of_step(ref, t):
        return ref[:, pl.ds(t, segments, stride=steps), :]

    one = jnp.ones((planes, segments, across), jnp.float32)
    zero = jnp.zeros_like(one)
    size = 8
    lane = lane_iota((size, across))

    def stencil_rows(n):
        return pl.ds(pl.multiple_of(n * size, size), size)

    def read_rows(n):
        part = stencil_rows(n)
        return [[velocity[c, x, part, :] for x in range(planes)] for c in range(components)]

    def stencil(values):
        found = []
        for x in range(planes):
            v = values[x]
            around = values[(x - 1) % planes] + values[(x + 1) % planes]
            around = around + jnp.where(lane == 0, 0.0, pltpu.roll(v, 1, 1))
            around = around + jnp.where(lane == across - 1, 0.0, pltpu.roll(v, across - 1, 1))
            found.append((1.0 - 4.0 * diffusion_number) * v + diffusion_number * around)
        return found

    def write_rows(n, values):
        part = stencil_rows(n)
        for c in range(components):
            for x in range(planes):
                rhs[c, x, part, :] = values[c][x]

    def factor(t, carry):
        d, d_b, low_gain, high_gain, sum_last, sum_first = carry
        back = last - 1 - t
        low, up = of_step(lower, t), of_step(upper, t)
        low_b, up_b = of_step(lower, back), of_step(upper, back)
        velocities = read_rows(t)
        e = 1.0 + low * d
        inverse = reciprocal(up + e)
        g = low * inverse
        e_b = 1.0 + up_b * d_b
        inverse_b = reciprocal(low_b + e_b)
        g_b = up_b * inverse_b
        found = [stencil(values) for values in velocities]
        inv[t] = inverse
        inv_b[back] = inverse_b
        gain_b[back] = g_b
        write_rows(t, found)
        return (
            e * inverse,
            e_b * inverse_b,
            low_gain * g,
            high_gain * g_b,
            inverse + g * sum_last,
            inverse_b + g_b * sum_first,
        )

    carry = lax.fori_loop(0, last, factor, (one, one, one, one, zero, zero), unroll=2)
    _, _, low_gain, high_gain, sum_last, sum_first = carry
    for n in range(last, height // size):
        write_rows(n, [stencil(values) for values in read_rows(n)])
    start_all(outgoing[:2])
    def weigh(t, q):
        first[t] = inv_b[t] * q
        return q * gain_b[t]

    lax.fori_loop(0, last, weigh, one, unroll=6)
    outgoing[2].start()

    low_sep, up_sep = of_step(lower, last), of_step(upper, last)
    segment = lax.broadcasted_iota(jnp.int32, one.shape, 1)
    is_end = segment == segments - 1
    above = jnp.where(is_end, 0.0, jnp.roll(sum_first, -1, axis=1))
    couple_high = up_sep * jnp.where(is_end, 1.0, jnp.roll(high_gain, -1, axis=1))
    killing = 1.0 + low_sep * sum_last + up_sep * above
    ends[2, :, :segments, :] = low_sep
    ends[3, :, :segments, :] = up_sep
    tail = slice(height - rest, height)
    low_rest, up_rest = lower[:, tail, :], upper[:, tail, :]
    for n, (value, other) in enumerate(
        (
            (low_sep * low_gain, low_rest),
            (couple_high, up_rest),
            (killing, jnp.ones_like(low_rest)),
        )
    ):
        for x in range(planes):
            rows[n, x * knots : x * knots + segments, :] = value[x]
            rows[n, x * knots + segments : (x + 1) * knots, :] = other[x]
    for x in range(planes):
        rows[3, x * knots : x * knots + segments, :] = high_gain[x]
        rows[4, x * knots : x * knots + segments, :] = sum_first[x]

    def row(n, s):
        return rows[n, pl.ds(s, planes, stride=knots), :]

    top = knots - 1
    one_row = jnp.ones((planes, across), jnp.float32)
    d, d_b = one_row, one_row
    inv_s, gain_s, ratio_s = [], [], []
    inv_sb, gain_sb = [None] * top, [None] * top
    for s in range(top):
        e = row(2, s) + row(0, s) * d
        inverse = reciprocal(row(1, s) + e)
        inv_s.append(inverse)
        gain_s.append(row(0, s) * inverse)
        ratio_s.append(row(1, s) * inverse)
        d = e * inverse
        back = top - 1 - s
        e_b = row(2, back) + row(1, back) * d_b
        inverse_b = reciprocal(row(0, back) + e_b)
        inv_sb[back] = inverse_b
        gain_sb[back] = row(1, back) * inverse_b
        d_b = e_b * inverse_b
        inner[0, s] = inv_s[s]
        inner[1, s] = gain_s[s]
        inner[2, s] = ratio_s[s]
    run = row(0, top)
    low_total = one_row
    sum_top = one_row
    rows[5, pl.ds(top, planes, stride=knots), :] = one_row
    for s in reversed(range(top)):
        weight = run * inv_s[s]
        rows[5, pl.ds(s, planes, stride=knots), :] = weight
        sum_top = sum_top + weight * row(2, s)
        run = run * gain_s[s]
        low_total = low_total * gain_s[s]
    run = row(3, 0)
    high_total = one_row
    sum_bottom = row(4, 0)
    rows[6, pl.ds(top, planes, stride=knots), :] = jnp.zeros_like(one_row)
    for s in range(top):
        weight = run * inv_sb[s]
        rows[6, pl.ds(s, planes, stride=knots), :] = weight
        sum_bottom = sum_bottom + weight * row(2, s)
        run = run * gain_sb[s]
        high_total = high_total * ratio_s[s]
    coef = (
        row(0, top) * low_total,
        sum_top,
        row(1, top),
        sum_bottom,
        row(3, 0) * high_total,
    )
    for n, value in enumerate(coef):
        coefs[n * planes : (n + 1) * planes, :] = value
    for n in range(2):
        for x in range(planes):
            ends[n, x] = rows[5 + n, x * knots : (x + 1) * knots, :]
    wait_all(outgoing)


def scatter_kernel(got, cells, work_in, coefs, total, work, lefts, rights, sem):
    del coefs
    listed = pltpu.make_async_copy(work_in, work, sem)
    listed.start()
    components, chunks = got.shape[1], got.shape[2]
    _, height, wide = total.shape
    across = wide // (2 * components)
    shift = across.bit_length() - 1
    kind = jnp.bfloat16 if max(height, across) <= 256 else jnp.float32
    total[...] = jnp.zeros_like(total)

    tile = 16
    base = lax.broadcasted_iota(jnp.int32, (tile, lanes), 0)
    height_ids = [(base + n * tile).astype(jnp.float32).astype(kind) for n in range(height // tile)]
    across_ids = height_ids[: across // tile]
    lane = lane_iota((1, lanes))
    one = jnp.ones((tile, lanes), jnp.bfloat16)
    none = jnp.zeros((tile, lanes), jnp.bfloat16)

    def spread(row, to):
        return jnp.broadcast_to(row, (tile, lanes)).astype(to)

    def build(n, half):
        for g in range(group):
            word = work[(n + 1) * group + g]
            ident = (word >> count_bits) & ((1 << (plane_bit - count_bits)) - 1)
            live = word & ((1 << count_bits) - 1)
            there = slice(g * lanes, (g + 1) * lanes)
            sender, chunk = lax.div(ident, chunks), lax.rem(ident, chunks)
            x = word >> plane_bit
            cell = cells[sender, chunk, pl.ds(x, 1), :]
            up = jnp.where(lane < live, cell >> shift, -1).astype(jnp.float32)
            side = (cell & (across - 1)).astype(jnp.float32)
            up, side = spread(up, kind), spread(side, kind)
            for i, ids in enumerate(height_ids):
                lefts[half][i * tile : (i + 1) * tile, there] = jnp.where(up == ids, one, none)
            masks = [side == ids for ids in across_ids]
            for c in range(components):
                force = got[sender, c, chunk, pl.ds(x, 1), :]
                rest_of = force - force.astype(jnp.bfloat16).astype(jnp.float32)
                for m, value in enumerate((force, rest_of)):
                    value = spread(value, jnp.bfloat16)
                    start = (m * components + c) * across
                    for i, mask in enumerate(masks):
                        place = slice(start + i * tile, start + (i + 1) * tile)
                        rights[half][place, there] = jnp.where(mask, value, none)

    def add(n, half):
        total[work[(n + 1) * group] >> plane_bit] += lax.dot_general(
            lefts[half][...],
            rights[half][...],
            (((1,), (1,)), ((), ())),
            preferred_element_type=jnp.float32,
        )

    def two_steps(n, carry):
        add(2 * n, 0)
        build(2 * n + 1, 1)
        add(2 * n + 1, 1)
        build(2 * n + 2, 0)
        return carry

    listed.wait()
    build(0, 0)
    count = work[0]
    lax.fori_loop(0, lax.div(count, 2), two_steps, 0)

    @pl.when(lax.rem(count, 2) == 1)
    def _():
        add(count - 1, 0)


def sweep_kernel(total, from_above, from_below, rhs_start, inv, first, lower, upper, *refs):
    (ends, coefs, deposit_hbm, swept, prefix, ratio, reduced, sums) = refs[:8]
    (rhs, field, columns, edges, sems) = refs[8:]
    components, planes, height, across = rhs.shape
    steps = inv.shape[0] + 1
    last = steps - 1
    knots = ends.shape[2]
    rest = knots - segments
    parts = height // lanes
    lines = components * planes
    for p in range(parts):
        part = slice(p * lines, (p + 1) * lines)
        columns[p, pl.ds(0, lines, stride=2), :] = from_above[part, :]
        columns[p, pl.ds(1, lines, stride=2), :] = from_below[part, :]
        edges[p * lanes : (p + 1) * lanes, :] = diffusion_number * columns[p].T

    wide = lane_iota((lanes, across))
    border = (wide == 0) | (wide == across - 1)

    def place(x):
        return [
            pltpu.make_async_copy(field.at[c, x], deposit_hbm.at[c, x], sems.at[c, x])
            for c in range(components)
        ]

    def combine(x, carry):
        for c in range(components):
            for p in range(parts):
                part = slice(p * lanes, (p + 1) * lanes)
                high = total[x, part, c * across : (c + 1) * across]
                low = total[x, part, (components + c) * across : (components + c + 1) * across]
                value = high + low
                field[c, x, part, :] = value.astype(jnp.bfloat16)
                edge = pltpu.roll(edges[part, :], lanes - 1 - 2 * (c * planes + x), 1)
                rhs[c, x, part, :] = rhs_start[c, x, part, :] + value + jnp.where(border, edge, 0.0)
        start_all(place(x))
        return carry

    lax.fori_loop(0, planes, combine, 0)
    sums[2 * lines : 2 * lines + coefs.shape[0], :] = coefs[...]

    zero = jnp.zeros((components, planes, segments, across), jnp.float32)

    def of_step(t):
        return rhs[:, :, pl.ds(t, segments, stride=steps), :]

    def forward(t, carry):
        value, start, run, before = carry
        force = of_step(t)
        low, inverse = lower[:, pl.ds(t, segments, stride=steps), :], inv[t]
        value = force + (low * before)[None] * value
        swept[t] = inverse[None] * value
        run = run * (low * inverse)
        prefix[t] = run
        ratio[t] = upper[:, pl.ds(t, segments, stride=steps), :] * inverse
        return value, start + first[t][None] * force, run, inverse

    one = jnp.ones((planes, segments, across), jnp.float32)
    value, start, _, inverse = lax.fori_loop(0, last, forward, (zero, zero, one, one), unroll=6)
    value = inverse[None] * value
    segment = lax.broadcasted_iota(jnp.int32, zero.shape, 2)
    after = jnp.where(segment == segments - 1, 0.0, jnp.roll(start, -1, axis=2))
    low_sep, up_sep = ends[2, :, :segments, :], ends[3, :, :segments, :]
    value = of_step(last) + low_sep[None] * value + up_sep[None] * after
    others = rhs[:, :, height - rest :, :]
    at_top = ends[0, :, :segments, :][None] * value + ends[0, :, segments:, :][None] * others
    at_bottom = ends[1, :, :segments, :][None] * value + ends[1, :, segments:, :][None] * others
    at_bottom = at_bottom + jnp.where(segment == 0, start, 0.0)
    for c in range(components):
        for x in range(planes):
            k = c * planes + x
            reduced[k * knots : k * knots + segments, :] = value[c, x]
            reduced[k * knots + segments : (k + 1) * knots, :] = others[c, x]
            top = jnp.sum(at_top[c, x], 0, keepdims=True)
            bottom = jnp.sum(at_bottom[c, x], 0, keepdims=True)
            sums[k : k + 1, :] = top
            sums[lines + k : lines + k + 1, :] = bottom

    for x in range(planes):
        wait_all(place(x))


def finish_kernel(inner, reduced, swept, ratio, prefix, *refs):
    received = refs[: len(refs) - 7]
    out_hbm, sums, tops, after, before, out, sems = refs[len(refs) - 7 :]
    walls = sums.shape[0]
    components, planes, height, across = out.shape
    steps = swept.shape[0] + 1
    last = steps - 1
    lines = components * planes
    knots = inner.shape[1] + 1
    rest = knots - segments
    me = lax.axis_index("wall")
    sums[...] = jnp.zeros_like(sums)
    sums[me] = received[0][...]
    for (kind, value, _), block in zip(wall_routes(walls), received[1:]):
        source = jnp.clip(me - value, 0, walls - 1) if kind == "shift" else value
        sums[source] += block[...]

    def coef(k, n):
        start = 2 * lines + n * planes
        return sums[k, start : start + planes, :]

    def wide(value):
        return jnp.concatenate([value] * components, 0)

    d = jnp.ones((planes, across), jnp.float32)
    value = jnp.zeros((lines, across), jnp.float32)
    values, ratios = [], []
    for k in range(walls):
        low, own, up = coef(k, 0), coef(k, 1), coef(k, 2)
        right = sums[k, :lines, :]
        if k + 1 < walls:
            high = up * coef(k + 1, 4)
            killing = own + up * coef(k + 1, 3)
            right = right + wide(up) * sums[k + 1, lines : 2 * lines, :]
        else:
            high = jnp.zeros_like(up)
            killing = own + up
        e = killing + low * d
        inverse = reciprocal(high + e)
        d = e * inverse
        value = (right + wide(low) * value) * wide(inverse)
        values.append(value)
        ratios.append(wide(high * inverse))
    tops[0] = jnp.zeros((lines, across), jnp.float32)
    tops[walls] = values[-1]
    for k in reversed(range(walls - 1)):
        values[k] = values[k] + ratios[k] * values[k + 1]
        tops[k + 1] = values[k]

    def row(s):
        return pl.ds(s, lines, stride=knots)

    run = tops[me]
    before[row(0), :] = run
    found = []
    for s in range(knots - 1):
        run = reduced[row(s), :] * wide(inner[0, s]) + wide(inner[1, s]) * run
        found.append(run)
    run = tops[me + 1]
    after[row(knots - 1), :] = run
    for s in reversed(range(knots - 1)):
        run = found[s] + wide(inner[2, s]) * run
        after[row(s), :] = run
        if s + 1 < segments:
            before[row(s + 1), :] = run

    def put(c, x, t, value):
        out[c, x, pl.ds(t, segments, stride=steps), :] = value

    copies = []
    half = planes // 2 if planes % 2 == 0 else planes
    for start in range(0, planes, half):
        part = [(c, x) for c in range(components) for x in range(start, start + half)]
        bottoms, starts = [], []
        for c, x in part:
            base = (c * planes + x) * knots
            bottoms.append(before[base : base + segments, :])
            starts.append(after[base : base + segments, :])
            out[c, x, height - rest :, :] = after[base + segments : base + knots, :]
            put(c, x, last, starts[-1])

        def backward(n, values):
            t = last - 1 - n
            found = []
            for (c, x), value, bottom in zip(part, values, bottoms):
                value = (swept[t, c, x] + prefix[t, x] * bottom) + ratio[t, x] * value
                put(c, x, t, value)
                found.append(value)
            return tuple(found)

        lax.fori_loop(0, last, backward, tuple(starts), unroll=10)
        for here in part:
            copy = pltpu.make_async_copy(out.at[here], out_hbm.at[here], sems.at[here])
            copy.start()
            copies.append(copy)
    wait_all(copies)


def shifted(block, axis, distance):
    length = lax.axis_size(axis)
    route = [(i, (i + distance) % length) for i in range(length)]
    return lax.ppermute(block, axis, route)


def wall_routes(walls):
    routes = [("to_first", k, [(k, 0)]) for k in reversed(range(1, walls))]
    routes += [("from_first", 0, [(0, k)]) for k in range(1, walls)]
    for shift in reversed(range(1, walls - 1)):
        routes.append(("shift", -shift, [(i, i - shift) for i in range(1 + shift, walls)]))
    for shift in range(1, walls - 1):
        routes.append(("shift", shift, [(i, i + shift) for i in range(1, walls - shift)]))
    return routes


def everyone(block, axis):
    routes = wall_routes(lax.axis_size(axis))
    return [block] + [lax.ppermute(block, axis, route) for _, _, route in routes]


def local(velocity, lower_weight, upper_weight, forces, cells, counts):
    components, planes, height, across = velocity.shape
    receivers, capacity = forces.shape[3], forces.shape[5]
    senders = cells.shape[2]
    walls = lax.axis_size("wall")
    lines = components * planes
    chunks = capacity // lanes
    counts_shape = (planes, senders)
    forces = forces.reshape(components, receivers, planes, capacity)
    cells = cells.reshape(senders, planes, capacity)
    counts = counts.reshape(senders, planes).T

    def hbm(*arrays):
        return [pltpu.with_memory_space_constraint(array, pltpu.HBM) for array in arrays]

    work_shape = (planes * (senders * chunks + group) + 4 * group,)
    send, lower_near, upper_near, velocity_near, work = call(
        load_kernel,
        (
            pltpu.HBM((receivers, components, planes, capacity), jnp.float32),
            f32(*lower_weight.shape),
            f32(*upper_weight.shape),
            f32(*velocity.shape),
            jax.ShapeDtypeStruct(work_shape, jnp.int32),
        ),
        (in_hbm, *[in_vmem] * 4),
        [in_hbm] * 5,
        [
            scratch(*forces.shape),
            pltpu.SMEM(counts_shape, jnp.int32),
            pltpu.SMEM(work_shape, jnp.int32),
            pltpu.SemaphoreType.DMA((3 * components + 4,)),
        ],
        4,
        1 << 16,
    )(*hbm(forces, velocity, lower_weight, upper_weight, counts))
    got = lax.all_to_all(send, "span", 0, 0, tiled=True)
    got = got.reshape(senders, components, planes, chunks, lanes).transpose(0, 1, 3, 2, 4)
    cells = cells.reshape(senders, planes, chunks, lanes).transpose(0, 2, 1, 3)
    edge_shape = (lines * height // lanes, lanes)
    first_column, last_column = call(
        edge_kernel,
        (f32(*edge_shape), f32(*edge_shape)),
        (in_vmem, in_vmem),
        [in_vmem],
        [scratch(height, across), scratch(height // lanes, lanes, lanes)],
        4,
        1 << 20,
    )(velocity_near)
    from_above = shifted(first_column, "span", -1)
    from_below = shifted(last_column, "span", 1)

    steps = height // segments - 1
    knots = height - segments * steps + segments
    step_shape = (steps - 1, planes, segments, across)
    staged = [velocity.shape, step_shape, step_shape]
    prepared = call(
        prepare_kernel,
        (
            f32(3, knots - 1, planes, across),
            f32(4, planes, knots, across),
            f32(5 * planes, across),
            *[pltpu.HBM(shape, jnp.float32) for shape in staged],
        ),
        [in_vmem] * 3 + [in_hbm] * 3,
        [in_vmem] * 3,
        [
            *[scratch(*shape) for shape in staged],
            scratch(*step_shape),
            scratch(*step_shape),
            scratch(7, planes * knots, across),
            pltpu.SemaphoreType.DMA((3,)),
        ],
        12,
        1 << 24,
    )(velocity_near, lower_near, upper_near)
    (inner, ends, coefs, rhs_start, inv, first) = prepared

    sum_rows = -(-(2 * lines + 5 * planes) // 8) * 8
    wide = 2 * components * across
    total = call(
        scatter_kernel,
        f32(planes, height, wide),
        in_vmem,
        [in_vmem] * 4,
        [
            pltpu.SMEM(work_shape, jnp.int32),
            [pltpu.VMEM((height, group * lanes), jnp.bfloat16)] * 2,
            [pltpu.VMEM((wide, group * lanes), jnp.bfloat16)] * 2,
            pltpu.SemaphoreType.DMA,
        ],
        16,
        1 << 32,
    )(got, cells, work, coefs)

    deposit, swept, prefix, ratio, reduced, sums = call(
        sweep_kernel,
        (
            jax.ShapeDtypeStruct(velocity.shape, jnp.bfloat16),
            f32(steps - 1, components, planes, segments, across),
            f32(*step_shape),
            f32(*step_shape),
            f32(lines * knots, across),
            f32(sum_rows, across),
        ),
        (in_hbm, *[in_vmem] * 5),
        [in_vmem] * 10,
        [
            scratch(*velocity.shape),
            pltpu.VMEM(velocity.shape, jnp.bfloat16),
            scratch(height // lanes, lanes, lanes),
            scratch(height, lanes),
            pltpu.SemaphoreType.DMA((components, planes)),
        ],
        8,
        1 << 24,
    )(
        total,
        from_above,
        from_below,
        rhs_start,
        inv,
        first,
        lower_weight,
        upper_weight,
        ends,
        coefs,
    )
    all_sums = everyone(sums, "wall")

    velocity_next = call(
        finish_kernel,
        f32(*velocity.shape),
        in_hbm,
        [in_vmem] * (5 + len(all_sums)),
        [
            scratch(walls, sum_rows, across),
            scratch(walls + 1, lines, across),
            scratch(lines * knots, across),
            scratch(lines * knots, across),
            scratch(*velocity.shape),
            pltpu.SemaphoreType.DMA((components, planes)),
        ],
        8,
        1 << 22,
    )(inner, reduced, swept, ratio, prefix, *all_sums)
    return (velocity_next, deposit)


def solution(mesh):
    placed = (
        P(None, None, "wall", "span"),
        P(None, "wall", "span"),
        P(None, "wall", "span"),
        P(None, "wall", "span", None, None, None),
        P("wall", "span", None, None, None),
        P("wall", "span", None, None),
    )
    return jax.shard_map(
        local,
        mesh=mesh,
        in_specs=placed,
        out_specs=(P(None, None, "wall", "span"), P(None, None, "wall", "span")),
        check_vma=False,
    )
```

```python
import jax
import jax.numpy as jnp
from jax import lax
from jax.experimental import pallas as pl
from jax.experimental.pallas import tpu as pltpu
from jax.sharding import PartitionSpec as P

diffusion_number = 0.2
segments = 8
lanes = 128
group = 8
count_bits, plane_bit = 10, 24
in_vmem = pl.BlockSpec(memory_space=pltpu.VMEM)
in_smem = pl.BlockSpec(memory_space=pltpu.SMEM)
in_hbm = pl.BlockSpec(memory_space=pltpu.HBM)


def call(body, out_shape, out_specs, in_specs, scratch, mebibytes, flops):
    return pl.pallas_call(
        body,
        out_shape=out_shape,
        in_specs=in_specs,
        out_specs=out_specs,
        scratch_shapes=scratch,
        compiler_params=pltpu.CompilerParams(vmem_limit_bytes=mebibytes << 20),
        cost_estimate=pl.CostEstimate(flops=flops, bytes_accessed=4 << 20, transcendentals=0),
    )


def f32(*shape):
    return jax.ShapeDtypeStruct(shape, jnp.float32)


def scratch(*shape):
    return pltpu.VMEM(shape, jnp.float32)


def lane_iota(shape):
    return lax.broadcasted_iota(jnp.int32, shape, len(shape) - 1)


def reciprocal(value):
    rough = pl.reciprocal(value, approx=True)
    return rough * (2.0 - value * rough)


def start_all(copies):
    for copy in copies:
        copy.start()


def wait_all(copies):
    for copy in copies:
        copy.wait()


def copies_of(sources, targets, sems, first=0):
    return [
        pltpu.make_async_copy(source, target, sems.at[first + n])
        for n, (source, target) in enumerate(zip(sources, targets))
    ]


def load_kernel(forces, velocity, lower, upper, counts_hbm, send, *refs):
    near, work_out, (slots, counts, work, sems) = refs[:3], refs[3], refs[4:]
    components, senders, planes, capacity = forces.shape
    chunks = capacity // lanes
    halves = [pl.ds(0, senders // 2), pl.ds(senders // 2, senders - senders // 2)]
    pieces = [(c, part) for part in halves for c in range(components)]
    sources = [counts_hbm] + [forces.at[piece] for piece in pieces]
    targets = [counts] + [slots.at[piece] for piece in pieces]
    arrivals = len(sources)
    sources += [lower, upper] + [velocity.at[c] for c in range(components)]
    targets += [near[0], near[1]] + [near[2].at[c] for c in range(components)]
    copies = copies_of(sources, targets, sems)
    start_all(copies)
    outgoing = copies_of(
        [slots.at[:, d] for d in range(senders)] + [work],
        [send.at[d] for d in range(senders)] + [work_out],
        sems,
        len(copies),
    )

    def one_plane(x, n):
        def one_sender(s, n):
            count = counts[x, s]
            base = (x << plane_bit) + ((s * chunks) << count_bits)
            for k in range(chunks):
                live = jnp.maximum(count - k * lanes, 0)
                work[group + n + k] = base + (k << count_bits) + live
            return n + lax.div(count + lanes - 1, lanes)

        n = lax.fori_loop(0, senders, one_sender, n, unroll=4)
        for extra in range(group):
            work[group + n + extra] = x << plane_bit
        return lax.div(n + group - 1, group) * group

    copies[0].wait()
    total = lax.fori_loop(0, planes // 2, one_plane, 0)
    wait_all(copies[1:arrivals])
    start_all(outgoing[:senders])
    total = lax.fori_loop(planes // 2, planes, one_plane, total)
    for extra in range(2 * group):
        work[group + total + extra] = 0
    work[0] = lax.div(total, group)
    outgoing[senders].start()
    wait_all(copies[arrivals:])
    wait_all(outgoing)


def edge_kernel(velocity, first_out, last_out, columns, turned):
    components, planes, height, across = velocity.shape
    lines = components * planes
    lane = lane_iota((height, across))
    picked = jnp.zeros((height, across), jnp.float32)
    for k in range(lines):
        rolled = pltpu.roll(velocity[k // planes, k % planes], 2 * k + 1, 1)
        picked = jnp.where((lane >> 1) == k, rolled, picked)
    columns[...] = picked
    for p in range(height // lanes):
        turned[p] = columns[p * lanes : (p + 1) * lanes, :].T
        part = slice(p * lines, (p + 1) * lines)
        first_out[part, :] = turned[p, pl.ds(1, lines, stride=2), :]
        last_out[part, :] = turned[p, pl.ds(0, lines, stride=2), :]


def prepare_kernel(velocity, lower, upper, inner, ends, coefs, *refs):
    (rhs, inv, first) = refs[3:6]
    (inv_b, gain_b, rows, sems) = refs[6:]
    outgoing = copies_of(refs[3:6], refs[:3], sems)
    components, planes, height, across = velocity.shape
    steps = inv.shape[0] + 1
    last = steps - 1
    rest = height - segments * steps
    knots = segments + rest

    def of_step(ref, t):
        return ref[:, pl.ds(t, segments, stride=steps), :]

    one = jnp.ones((planes, segments, across), jnp.float32)
    zero = jnp.zeros_like(one)
    size = 8
    lane = lane_iota((size, across))

    def stencil_rows(n):
        return pl.ds(pl.multiple_of(n * size, size), size)

    def read_rows(n):
        part = stencil_rows(n)
        return [[velocity[c, x, part, :] for x in range(planes)] for c in range(components)]

    def stencil(values):
        found = []
        for x in range(planes):
            v = values[x]
            around = values[(x - 1) % planes] + values[(x + 1) % planes]
            around = around + jnp.where(lane == 0, 0.0, pltpu.roll(v, 1, 1))
            around = around + jnp.where(lane == across - 1, 0.0, pltpu.roll(v, across - 1, 1))
            found.append((1.0 - 4.0 * diffusion_number) * v + diffusion_number * around)
        return found

    def write_rows(n, values):
        part = stencil_rows(n)
        for c in range(components):
            for x in range(planes):
                rhs[c, x, part, :] = values[c][x]

    def factor(t, carry):
        d, d_b, low_gain, high_gain, sum_last, sum_first = carry
        back = last - 1 - t
        low, up = of_step(lower, t), of_step(upper, t)
        low_b, up_b = of_step(lower, back), of_step(upper, back)
        velocities = read_rows(t)
        e = 1.0 + low * d
        inverse = reciprocal(up + e)
        g = low * inverse
        e_b = 1.0 + up_b * d_b
        inverse_b = reciprocal(low_b + e_b)
        g_b = up_b * inverse_b
        found = [stencil(values) for values in velocities]
        inv[t] = inverse
        inv_b[back] = inverse_b
        gain_b[back] = g_b
        write_rows(t, found)
        return (
            e * inverse,
            e_b * inverse_b,
            low_gain * g,
            high_gain * g_b,
            inverse + g * sum_last,
            inverse_b + g_b * sum_first,
        )

    carry = lax.fori_loop(0, last, factor, (one, one, one, one, zero, zero), unroll=2)
    _, _, low_gain, high_gain, sum_last, sum_first = carry
    for n in range(last, height // size):
        write_rows(n, [stencil(values) for values in read_rows(n)])
    start_all(outgoing[:2])
    def weigh(t, q):
        first[t] = inv_b[t] * q
        return q * gain_b[t]

    lax.fori_loop(0, last, weigh, one, unroll=6)
    outgoing[2].start()

    low_sep, up_sep = of_step(lower, last), of_step(upper, last)
    segment = lax.broadcasted_iota(jnp.int32, one.shape, 1)
    is_end = segment == segments - 1
    above = jnp.where(is_end, 0.0, jnp.roll(sum_first, -1, axis=1))
    couple_high = up_sep * jnp.where(is_end, 1.0, jnp.roll(high_gain, -1, axis=1))
    killing = 1.0 + low_sep * sum_last + up_sep * above
    ends[2, :, :segments, :] = low_sep
    ends[3, :, :segments, :] = up_sep
    tail = slice(height - rest, height)
    low_rest, up_rest = lower[:, tail, :], upper[:, tail, :]
    for n, (value, other) in enumerate(
        (
            (low_sep * low_gain, low_rest),
            (couple_high, up_rest),
            (killing, jnp.ones_like(low_rest)),
        )
    ):
        for x in range(planes):
            rows[n, x * knots : x * knots + segments, :] = value[x]
            rows[n, x * knots + segments : (x + 1) * knots, :] = other[x]
    for x in range(planes):
        rows[3, x * knots : x * knots + segments, :] = high_gain[x]
        rows[4, x * knots : x * knots + segments, :] = sum_first[x]

    def row(n, s):
        return rows[n, pl.ds(s, planes, stride=knots), :]

    top = knots - 1
    one_row = jnp.ones((planes, across), jnp.float32)
    d, d_b = one_row, one_row
    inv_s, gain_s, ratio_s = [], [], []
    inv_sb, gain_sb = [None] * top, [None] * top
    for s in range(top):
        e = row(2, s) + row(0, s) * d
        inverse = reciprocal(row(1, s) + e)
        inv_s.append(inverse)
        gain_s.append(row(0, s) * inverse)
        ratio_s.append(row(1, s) * inverse)
        d = e * inverse
        back = top - 1 - s
        e_b = row(2, back) + row(1, back) * d_b
        inverse_b = reciprocal(row(0, back) + e_b)
        inv_sb[back] = inverse_b
        gain_sb[back] = row(1, back) * inverse_b
        d_b = e_b * inverse_b
        inner[0, s] = inv_s[s]
        inner[1, s] = gain_s[s]
        inner[2, s] = ratio_s[s]
    run = row(0, top)
    low_total = one_row
    sum_top = one_row
    rows[5, pl.ds(top, planes, stride=knots), :] = one_row
    for s in reversed(range(top)):
        weight = run * inv_s[s]
        rows[5, pl.ds(s, planes, stride=knots), :] = weight
        sum_top = sum_top + weight * row(2, s)
        run = run * gain_s[s]
        low_total = low_total * gain_s[s]
    run = row(3, 0)
    high_total = one_row
    sum_bottom = row(4, 0)
    rows[6, pl.ds(top, planes, stride=knots), :] = jnp.zeros_like(one_row)
    for s in range(top):
        weight = run * inv_sb[s]
        rows[6, pl.ds(s, planes, stride=knots), :] = weight
        sum_bottom = sum_bottom + weight * row(2, s)
        run = run * gain_sb[s]
        high_total = high_total * ratio_s[s]
    coef = (
        row(0, top) * low_total,
        sum_top,
        row(1, top),
        sum_bottom,
        row(3, 0) * high_total,
    )
    for n, value in enumerate(coef):
        coefs[n * planes : (n + 1) * planes, :] = value
    for n in range(2):
        for x in range(planes):
            ends[n, x] = rows[5 + n, x * knots : (x + 1) * knots, :]
    wait_all(outgoing)


def scatter_kernel(got, cells, work_in, coefs, total, work, lefts, rights, sem):
    del coefs
    listed = pltpu.make_async_copy(work_in, work, sem)
    listed.start()
    components, chunks = got.shape[1], got.shape[2]
    _, height, wide = total.shape
    across = wide // (2 * components)
    shift = across.bit_length() - 1
    kind = jnp.bfloat16 if max(height, across) <= 256 else jnp.float32
    total[...] = jnp.zeros_like(total)

    tile = 16
    base = lax.broadcasted_iota(jnp.int32, (tile, lanes), 0)
    height_ids = [(base + n * tile).astype(jnp.float32).astype(kind) for n in range(height // tile)]
    across_ids = height_ids[: across // tile]
    lane = lane_iota((1, lanes))
    one = jnp.ones((tile, lanes), jnp.bfloat16)
    none = jnp.zeros((tile, lanes), jnp.bfloat16)

    def spread(row, to):
        return jnp.broadcast_to(row, (tile, lanes)).astype(to)

    def build(n, half):
        for g in range(group):
            word = work[(n + 1) * group + g]
            ident = (word >> count_bits) & ((1 << (plane_bit - count_bits)) - 1)
            live = word & ((1 << count_bits) - 1)
            there = slice(g * lanes, (g + 1) * lanes)
            sender, chunk = lax.div(ident, chunks), lax.rem(ident, chunks)
            x = word >> plane_bit
            cell = cells[sender, chunk, pl.ds(x, 1), :]
            up = jnp.where(lane < live, cell >> shift, -1).astype(jnp.float32)
            side = (cell & (across - 1)).astype(jnp.float32)
            up, side = spread(up, kind), spread(side, kind)
            for i, ids in enumerate(height_ids):
                lefts[half][i * tile : (i + 1) * tile, there] = jnp.where(up == ids, one, none)
            masks = [side == ids for ids in across_ids]
            for c in range(components):
                force = got[sender, c, chunk, pl.ds(x, 1), :]
                rest_of = force - force.astype(jnp.bfloat16).astype(jnp.float32)
                for m, value in enumerate((force, rest_of)):
                    value = spread(value, jnp.bfloat16)
                    start = (m * components + c) * across
                    for i, mask in enumerate(masks):
                        place = slice(start + i * tile, start + (i + 1) * tile)
                        rights[half][place, there] = jnp.where(mask, value, none)

    def add(n, half):
        total[work[(n + 1) * group] >> plane_bit] += lax.dot_general(
            lefts[half][...],
            rights[half][...],
            (((1,), (1,)), ((), ())),
            preferred_element_type=jnp.float32,
        )

    def two_steps(n, carry):
        add(2 * n, 0)
        build(2 * n + 1, 1)
        add(2 * n + 1, 1)
        build(2 * n + 2, 0)
        return carry

    listed.wait()
    build(0, 0)
    count = work[0]
    lax.fori_loop(0, lax.div(count, 2), two_steps, 0)

    @pl.when(lax.rem(count, 2) == 1)
    def _():
        add(count - 1, 0)


def sweep_kernel(total, from_above, from_below, rhs_start, inv, first, lower, upper, *refs):
    (ends, coefs, deposit_hbm, swept, prefix, ratio, reduced, sums) = refs[:8]
    (rhs, field, columns, edges, sems) = refs[8:]
    components, planes, height, across = rhs.shape
    steps = inv.shape[0] + 1
    last = steps - 1
    knots = ends.shape[2]
    rest = knots - segments
    parts = height // lanes
    lines = components * planes
    for p in range(parts):
        part = slice(p * lines, (p + 1) * lines)
        columns[p, pl.ds(0, lines, stride=2), :] = from_above[part, :]
        columns[p, pl.ds(1, lines, stride=2), :] = from_below[part, :]
        edges[p * lanes : (p + 1) * lanes, :] = diffusion_number * columns[p].T

    wide = lane_iota((lanes, across))
    border = (wide == 0) | (wide == across - 1)

    def place(x):
        return [
            pltpu.make_async_copy(field.at[c, x], deposit_hbm.at[c, x], sems.at[c, x])
            for c in range(components)
        ]

    def combine(x, carry):
        for c in range(components):
            for p in range(parts):
                part = slice(p * lanes, (p + 1) * lanes)
                high = total[x, part, c * across : (c + 1) * across]
                low = total[x, part, (components + c) * across : (components + c + 1) * across]
                value = high + low
                field[c, x, part, :] = value.astype(jnp.bfloat16)
                edge = pltpu.roll(edges[part, :], lanes - 1 - 2 * (c * planes + x), 1)
                rhs[c, x, part, :] = rhs_start[c, x, part, :] + value + jnp.where(border, edge, 0.0)
        start_all(place(x))
        return carry

    lax.fori_loop(0, planes, combine, 0, unroll=2)
    sums[2 * lines : 2 * lines + coefs.shape[0], :] = coefs[...]

    zero = jnp.zeros((components, planes, segments, across), jnp.float32)

    def of_step(t):
        return rhs[:, :, pl.ds(t, segments, stride=steps), :]

    def forward(t, carry):
        value, start, run, before = carry
        force = of_step(t)
        low, inverse = lower[:, pl.ds(t, segments, stride=steps), :], inv[t]
        value = force + (low * before)[None] * value
        swept[t] = inverse[None] * value
        run = run * (low * inverse)
        prefix[t] = run
        ratio[t] = upper[:, pl.ds(t, segments, stride=steps), :] * inverse
        return value, start + first[t][None] * force, run, inverse

    one = jnp.ones((planes, segments, across), jnp.float32)
    value, start, _, inverse = lax.fori_loop(0, last, forward, (zero, zero, one, one), unroll=6)
    value = inverse[None] * value
    segment = lax.broadcasted_iota(jnp.int32, zero.shape, 2)
    after = jnp.where(segment == segments - 1, 0.0, jnp.roll(start, -1, axis=2))
    low_sep, up_sep = ends[2, :, :segments, :], ends[3, :, :segments, :]
    value = of_step(last) + low_sep[None] * value + up_sep[None] * after
    others = rhs[:, :, height - rest :, :]
    at_top = ends[0, :, :segments, :][None] * value + ends[0, :, segments:, :][None] * others
    at_bottom = ends[1, :, :segments, :][None] * value + ends[1, :, segments:, :][None] * others
    at_bottom = at_bottom + jnp.where(segment == 0, start, 0.0)
    for c in range(components):
        for x in range(planes):
            k = c * planes + x
            reduced[k * knots : k * knots + segments, :] = value[c, x]
            reduced[k * knots + segments : (k + 1) * knots, :] = others[c, x]
            top = jnp.sum(at_top[c, x], 0, keepdims=True)
            bottom = jnp.sum(at_bottom[c, x], 0, keepdims=True)
            sums[k : k + 1, :] = top
            sums[lines + k : lines + k + 1, :] = bottom

    for x in range(planes):
        wait_all(place(x))


def finish_kernel(inner, reduced, swept, ratio, prefix, *refs):
    walls = len(refs) - 7
    received = refs[:walls]
    out_hbm, sums, tops, after, before, out, sems = refs[walls:]
    components, planes, height, across = out.shape
    steps = swept.shape[0] + 1
    last = steps - 1
    lines = components * planes
    knots = inner.shape[1] + 1
    rest = knots - segments
    me = lax.axis_index("wall")
    for n in range(walls):
        sums[lax.rem(me + walls - n, walls)] = received[n][...]

    def coef(k, n):
        start = 2 * lines + n * planes
        return sums[k, start : start + planes, :]

    def wide(value):
        return jnp.concatenate([value] * components, 0)

    d = jnp.ones((planes, across), jnp.float32)
    value = jnp.zeros((lines, across), jnp.float32)
    values, ratios = [], []
    for k in range(walls):
        low, own, up = coef(k, 0), coef(k, 1), coef(k, 2)
        right = sums[k, :lines, :]
        if k + 1 < walls:
            high = up * coef(k + 1, 4)
            killing = own + up * coef(k + 1, 3)
            right = right + wide(up) * sums[k + 1, lines : 2 * lines, :]
        else:
            high = jnp.zeros_like(up)
            killing = own + up
        e = killing + low * d
        inverse = reciprocal(high + e)
        d = e * inverse
        value = (right + wide(low) * value) * wide(inverse)
        values.append(value)
        ratios.append(wide(high * inverse))
    tops[0] = jnp.zeros((lines, across), jnp.float32)
    tops[walls] = values[-1]
    for k in reversed(range(walls - 1)):
        values[k] = values[k] + ratios[k] * values[k + 1]
        tops[k + 1] = values[k]

    def row(s):
        return pl.ds(s, lines, stride=knots)

    run = tops[me]
    before[row(0), :] = run
    found = []
    for s in range(knots - 1):
        run = reduced[row(s), :] * wide(inner[0, s]) + wide(inner[1, s]) * run
        found.append(run)
    run = tops[me + 1]
    after[row(knots - 1), :] = run
    for s in reversed(range(knots - 1)):
        run = found[s] + wide(inner[2, s]) * run
        after[row(s), :] = run
        if s + 1 < segments:
            before[row(s + 1), :] = run

    def put(c, x, t, value):
        out[c, x, pl.ds(t, segments, stride=steps), :] = value

    copies = []
    half = planes // 2 if planes % 2 == 0 else planes
    for start in range(0, planes, half):
        part = [(c, x) for c in range(components) for x in range(start, start + half)]
        bottoms, starts = [], []
        for c, x in part:
            base = (c * planes + x) * knots
            bottoms.append(before[base : base + segments, :])
            starts.append(after[base : base + segments, :])
            out[c, x, height - rest :, :] = after[base + segments : base + knots, :]
            put(c, x, last, starts[-1])

        def backward(n, values):
            t = last - 1 - n
            found = []
            for (c, x), value, bottom in zip(part, values, bottoms):
                value = (swept[t, c, x] + prefix[t, x] * bottom) + ratio[t, x] * value
                put(c, x, t, value)
                found.append(value)
            return tuple(found)

        lax.fori_loop(0, last, backward, tuple(starts), unroll=10)
        for here in part:
            copy = pltpu.make_async_copy(out.at[here], out_hbm.at[here], sems.at[here])
            copy.start()
            copies.append(copy)
    wait_all(copies)


def shifted(block, axis, distance):
    length = lax.axis_size(axis)
    route = [(i, (i + distance) % length) for i in range(length)]
    return lax.ppermute(block, axis, route)


def everyone(block, axis):
    return [block] + [shifted(block, axis, n) for n in range(1, lax.axis_size(axis))]


def local(velocity, lower_weight, upper_weight, forces, cells, counts):
    components, planes, height, across = velocity.shape
    receivers, capacity = forces.shape[3], forces.shape[5]
    senders = cells.shape[2]
    walls = lax.axis_size("wall")
    lines = components * planes
    chunks = capacity // lanes
    counts_shape = (planes, senders)
    forces = forces.reshape(components, receivers, planes, capacity)
    cells = cells.reshape(senders, planes, capacity)
    counts = counts.reshape(senders, planes).T

    def hbm(*arrays):
        return [pltpu.with_memory_space_constraint(array, pltpu.HBM) for array in arrays]

    work_shape = (planes * (senders * chunks + group) + 4 * group,)
    send, lower_near, upper_near, velocity_near, work = call(
        load_kernel,
        (
            pltpu.HBM((receivers, components, planes, capacity), jnp.float32),
            f32(*lower_weight.shape),
            f32(*upper_weight.shape),
            f32(*velocity.shape),
            jax.ShapeDtypeStruct(work_shape, jnp.int32),
        ),
        (in_hbm, *[in_vmem] * 4),
        [in_hbm] * 5,
        [
            scratch(*forces.shape),
            pltpu.SMEM(counts_shape, jnp.int32),
            pltpu.SMEM(work_shape, jnp.int32),
            pltpu.SemaphoreType.DMA((3 * components + receivers + 4,)),
        ],
        4,
        1 << 16,
    )(*hbm(forces, velocity, lower_weight, upper_weight, counts))
    got = lax.all_to_all(send, "span", 0, 0, tiled=True)
    got = got.reshape(senders, components, planes, chunks, lanes).transpose(0, 1, 3, 2, 4)
    cells = cells.reshape(senders, planes, chunks, lanes).transpose(0, 2, 1, 3)
    edge_shape = (lines * height // lanes, lanes)
    first_column, last_column = call(
        edge_kernel,
        (f32(*edge_shape), f32(*edge_shape)),
        (in_vmem, in_vmem),
        [in_vmem],
        [scratch(height, across), scratch(height // lanes, lanes, lanes)],
        4,
        1 << 20,
    )(velocity_near)
    from_above = shifted(first_column, "span", -1)
    from_below = shifted(last_column, "span", 1)

    steps = height // segments - 1
    knots = height - segments * steps + segments
    step_shape = (steps - 1, planes, segments, across)
    staged = [velocity.shape, step_shape, step_shape]
    prepared = call(
        prepare_kernel,
        (
            f32(3, knots - 1, planes, across),
            f32(4, planes, knots, across),
            f32(5 * planes, across),
            *[pltpu.HBM(shape, jnp.float32) for shape in staged],
        ),
        [in_vmem] * 3 + [in_hbm] * 3,
        [in_vmem] * 3,
        [
            *[scratch(*shape) for shape in staged],
            scratch(*step_shape),
            scratch(*step_shape),
            scratch(7, planes * knots, across),
            pltpu.SemaphoreType.DMA((3,)),
        ],
        12,
        1 << 24,
    )(velocity_near, lower_near, upper_near)
    (inner, ends, coefs, rhs_start, inv, first) = prepared

    sum_rows = -(-(2 * lines + 5 * planes) // 8) * 8
    wide = 2 * components * across
    total = call(
        scatter_kernel,
        f32(planes, height, wide),
        in_vmem,
        [in_vmem] * 4,
        [
            pltpu.SMEM(work_shape, jnp.int32),
            [pltpu.VMEM((height, group * lanes), jnp.bfloat16)] * 2,
            [pltpu.VMEM((wide, group * lanes), jnp.bfloat16)] * 2,
            pltpu.SemaphoreType.DMA,
        ],
        16,
        1 << 32,
    )(got, cells, work, coefs)

    deposit, swept, prefix, ratio, reduced, sums = call(
        sweep_kernel,
        (
            jax.ShapeDtypeStruct(velocity.shape, jnp.bfloat16),
            f32(steps - 1, components, planes, segments, across),
            f32(*step_shape),
            f32(*step_shape),
            f32(lines * knots, across),
            f32(sum_rows, across),
        ),
        (in_hbm, *[in_vmem] * 5),
        [in_vmem] * 10,
        [
            scratch(*velocity.shape),
            pltpu.VMEM(velocity.shape, jnp.bfloat16),
            scratch(height // lanes, lanes, lanes),
            scratch(height, lanes),
            pltpu.SemaphoreType.DMA((components, planes)),
        ],
        8,
        1 << 24,
    )(
        total,
        from_above,
        from_below,
        rhs_start,
        inv,
        first,
        lower_weight,
        upper_weight,
        ends,
        coefs,
    )
    all_sums = everyone(sums, "wall")

    velocity_next = call(
        finish_kernel,
        f32(*velocity.shape),
        in_hbm,
        [in_vmem] * (5 + walls),
        [
            scratch(walls, sum_rows, across),
            scratch(walls + 1, lines, across),
            scratch(lines * knots, across),
            scratch(lines * knots, across),
            scratch(*velocity.shape),
            pltpu.SemaphoreType.DMA((components, planes)),
        ],
        8,
        1 << 22,
    )(inner, reduced, swept, ratio, prefix, *all_sums)
    return (velocity_next, deposit)


def solution(mesh):
    placed = (
        P(None, None, "wall", "span"),
        P(None, "wall", "span"),
        P(None, "wall", "span"),
        P(None, "wall", "span", None, None, None),
        P("wall", "span", None, None, None),
        P("wall", "span", None, None),
    )
    return jax.shard_map(
        local,
        mesh=mesh,
        in_specs=placed,
        out_specs=(P(None, None, "wall", "span"), P(None, None, "wall", "span")),
        check_vma=False,
    )
```

```python
import jax
import jax.numpy as jnp
from jax import lax
from jax.experimental import pallas as pl
from jax.experimental.pallas import tpu as pltpu
from jax.sharding import PartitionSpec as P

diffusion_number = 0.2
segments = 8
lanes = 128
group = 8
count_bits, plane_bit = 10, 24
in_vmem = pl.BlockSpec(memory_space=pltpu.VMEM)
in_smem = pl.BlockSpec(memory_space=pltpu.SMEM)
in_hbm = pl.BlockSpec(memory_space=pltpu.HBM)


def call(body, out_shape, out_specs, in_specs, scratch, mebibytes, flops):
    return pl.pallas_call(
        body,
        out_shape=out_shape,
        in_specs=in_specs,
        out_specs=out_specs,
        scratch_shapes=scratch,
        compiler_params=pltpu.CompilerParams(vmem_limit_bytes=mebibytes << 20),
        cost_estimate=pl.CostEstimate(flops=flops, bytes_accessed=4 << 20, transcendentals=0),
    )


def f32(*shape):
    return jax.ShapeDtypeStruct(shape, jnp.float32)


def scratch(*shape):
    return pltpu.VMEM(shape, jnp.float32)


def lane_iota(shape):
    return lax.broadcasted_iota(jnp.int32, shape, len(shape) - 1)


def reciprocal(value):
    rough = pl.reciprocal(value, approx=True)
    return rough * (2.0 - value * rough)


def start_all(copies):
    for copy in copies:
        copy.start()


def wait_all(copies):
    for copy in copies:
        copy.wait()


def copies_of(sources, targets, sems, first=0):
    return [
        pltpu.make_async_copy(source, target, sems.at[first + n])
        for n, (source, target) in enumerate(zip(sources, targets))
    ]


def load_kernel(forces, velocity, lower, upper, counts_hbm, send, *refs):
    near, work_out, (slots, counts, work, sems) = refs[:3], refs[3], refs[4:]
    components, senders, planes, capacity = forces.shape
    chunks = capacity // lanes
    sources = [counts_hbm] + [forces.at[c] for c in range(components)]
    targets = [counts] + [slots.at[c] for c in range(components)]
    sources += [lower, upper] + [velocity.at[c] for c in range(components)]
    targets += [near[0], near[1]] + [near[2].at[c] for c in range(components)]
    copies = copies_of(sources, targets, sems)
    start_all(copies)
    outgoing = copies_of(
        [slots.at[c] for c in range(components)] + [work],
        [send.at[:, c] for c in range(components)] + [work_out],
        sems,
        len(copies),
    )

    def one_plane(x, n):
        def one_sender(s, n):
            count = counts[x, s]
            base = (x << plane_bit) + ((s * chunks) << count_bits)
            for k in range(chunks):
                live = jnp.maximum(count - k * lanes, 0)
                work[group + n + k] = base + (k << count_bits) + live
            return n + lax.div(count + lanes - 1, lanes)

        n = lax.fori_loop(0, senders, one_sender, n, unroll=4)
        for extra in range(group):
            work[group + n + extra] = x << plane_bit
        return lax.div(n + group - 1, group) * group

    copies[0].wait()
    total = lax.fori_loop(0, planes // 2, one_plane, 0)
    for c in range(components):
        copies[1 + c].wait()
        outgoing[c].start()
    total = lax.fori_loop(planes // 2, planes, one_plane, total)
    for extra in range(2 * group):
        work[group + total + extra] = 0
    work[0] = lax.div(total, group)
    outgoing[components].start()
    wait_all(copies[1 + components :])
    wait_all(outgoing)


def edge_kernel(velocity, first_out, last_out, columns, turned):
    components, planes, height, across = velocity.shape
    lines = components * planes
    lane = lane_iota((height, across))
    picked = jnp.zeros((height, across), jnp.float32)
    for k in range(lines):
        rolled = pltpu.roll(velocity[k // planes, k % planes], 2 * k + 1, 1)
        picked = jnp.where((lane >> 1) == k, rolled, picked)
    columns[...] = picked
    for p in range(height // lanes):
        turned[p] = columns[p * lanes : (p + 1) * lanes, :].T
        part = slice(p * lines, (p + 1) * lines)
        first_out[part, :] = turned[p, pl.ds(1, lines, stride=2), :]
        last_out[part, :] = turned[p, pl.ds(0, lines, stride=2), :]


def prepare_kernel(velocity, lower, upper, inner, ends, coefs, *refs):
    (rhs, inv, first) = refs[3:6]
    (inv_b, gain_b, rows, sems) = refs[6:]
    outgoing = copies_of(refs[3:6], refs[:3], sems)
    components, planes, height, across = velocity.shape
    steps = inv.shape[0] + 1
    last = steps - 1
    rest = height - segments * steps
    knots = segments + rest

    def of_step(ref, t):
        return ref[:, pl.ds(t, segments, stride=steps), :]

    one = jnp.ones((planes, segments, across), jnp.float32)
    zero = jnp.zeros_like(one)
    size = 8
    lane = lane_iota((size, across))

    def stencil_rows(n):
        return pl.ds(pl.multiple_of(n * size, size), size)

    def read_rows(n):
        part = stencil_rows(n)
        return [[velocity[c, x, part, :] for x in range(planes)] for c in range(components)]

    def stencil(values):
        found = []
        for x in range(planes):
            v = values[x]
            around = values[(x - 1) % planes] + values[(x + 1) % planes]
            around = around + jnp.where(lane == 0, 0.0, pltpu.roll(v, 1, 1))
            around = around + jnp.where(lane == across - 1, 0.0, pltpu.roll(v, across - 1, 1))
            found.append((1.0 - 4.0 * diffusion_number) * v + diffusion_number * around)
        return found

    def write_rows(n, values):
        part = stencil_rows(n)
        for c in range(components):
            for x in range(planes):
                rhs[c, x, part, :] = values[c][x]

    def factor(t, carry):
        d, d_b, low_gain, high_gain, sum_last, sum_first = carry
        back = last - 1 - t
        low, up = of_step(lower, t), of_step(upper, t)
        low_b, up_b = of_step(lower, back), of_step(upper, back)
        velocities = read_rows(t)
        e = 1.0 + low * d
        inverse = reciprocal(up + e)
        g = low * inverse
        e_b = 1.0 + up_b * d_b
        inverse_b = reciprocal(low_b + e_b)
        g_b = up_b * inverse_b
        found = [stencil(values) for values in velocities]
        inv[t] = inverse
        inv_b[back] = inverse_b
        gain_b[back] = g_b
        write_rows(t, found)
        return (
            e * inverse,
            e_b * inverse_b,
            low_gain * g,
            high_gain * g_b,
            inverse + g * sum_last,
            inverse_b + g_b * sum_first,
        )

    carry = lax.fori_loop(0, last, factor, (one, one, one, one, zero, zero), unroll=2)
    _, _, low_gain, high_gain, sum_last, sum_first = carry
    for n in range(last, height // size):
        write_rows(n, [stencil(values) for values in read_rows(n)])
    start_all(outgoing[:2])
    def weigh(t, q):
        first[t] = inv_b[t] * q
        return q * gain_b[t]

    lax.fori_loop(0, last, weigh, one, unroll=6)
    outgoing[2].start()

    low_sep, up_sep = of_step(lower, last), of_step(upper, last)
    segment = lax.broadcasted_iota(jnp.int32, one.shape, 1)
    is_end = segment == segments - 1
    above = jnp.where(is_end, 0.0, jnp.roll(sum_first, -1, axis=1))
    couple_high = up_sep * jnp.where(is_end, 1.0, jnp.roll(high_gain, -1, axis=1))
    killing = 1.0 + low_sep * sum_last + up_sep * above
    ends[2, :, :segments, :] = low_sep
    ends[3, :, :segments, :] = up_sep
    tail = slice(height - rest, height)
    low_rest, up_rest = lower[:, tail, :], upper[:, tail, :]
    for n, (value, other) in enumerate(
        (
            (low_sep * low_gain, low_rest),
            (couple_high, up_rest),
            (killing, jnp.ones_like(low_rest)),
        )
    ):
        for x in range(planes):
            rows[n, x * knots : x * knots + segments, :] = value[x]
            rows[n, x * knots + segments : (x + 1) * knots, :] = other[x]
    for x in range(planes):
        rows[3, x * knots : x * knots + segments, :] = high_gain[x]
        rows[4, x * knots : x * knots + segments, :] = sum_first[x]

    def row(n, s):
        return rows[n, pl.ds(s, planes, stride=knots), :]

    top = knots - 1
    one_row = jnp.ones((planes, across), jnp.float32)
    d, d_b = one_row, one_row
    inv_s, gain_s, ratio_s = [], [], []
    inv_sb, gain_sb = [None] * top, [None] * top
    for s in range(top):
        e = row(2, s) + row(0, s) * d
        inverse = reciprocal(row(1, s) + e)
        inv_s.append(inverse)
        gain_s.append(row(0, s) * inverse)
        ratio_s.append(row(1, s) * inverse)
        d = e * inverse
        back = top - 1 - s
        e_b = row(2, back) + row(1, back) * d_b
        inverse_b = reciprocal(row(0, back) + e_b)
        inv_sb[back] = inverse_b
        gain_sb[back] = row(1, back) * inverse_b
        d_b = e_b * inverse_b
        inner[0, s] = inv_s[s]
        inner[1, s] = gain_s[s]
        inner[2, s] = ratio_s[s]
    run = row(0, top)
    low_total = one_row
    sum_top = one_row
    rows[5, pl.ds(top, planes, stride=knots), :] = one_row
    for s in reversed(range(top)):
        weight = run * inv_s[s]
        rows[5, pl.ds(s, planes, stride=knots), :] = weight
        sum_top = sum_top + weight * row(2, s)
        run = run * gain_s[s]
        low_total = low_total * gain_s[s]
    run = row(3, 0)
    high_total = one_row
    sum_bottom = row(4, 0)
    rows[6, pl.ds(top, planes, stride=knots), :] = jnp.zeros_like(one_row)
    for s in range(top):
        weight = run * inv_sb[s]
        rows[6, pl.ds(s, planes, stride=knots), :] = weight
        sum_bottom = sum_bottom + weight * row(2, s)
        run = run * gain_sb[s]
        high_total = high_total * ratio_s[s]
    coef = (
        row(0, top) * low_total,
        sum_top,
        row(1, top),
        sum_bottom,
        row(3, 0) * high_total,
    )
    for n, value in enumerate(coef):
        coefs[n * planes : (n + 1) * planes, :] = value
    for n in range(2):
        for x in range(planes):
            ends[n, x] = rows[5 + n, x * knots : (x + 1) * knots, :]
    wait_all(outgoing)


def scatter_kernel(got, cells, work_in, coefs, total, work, lefts, rights, sem):
    del coefs
    listed = pltpu.make_async_copy(work_in, work, sem)
    listed.start()
    components, chunks = got.shape[1], got.shape[2]
    _, height, wide = total.shape
    across = wide // (2 * components)
    shift = across.bit_length() - 1
    kind = jnp.bfloat16 if max(height, across) <= 256 else jnp.float32
    total[...] = jnp.zeros_like(total)

    tile = 16
    base = lax.broadcasted_iota(jnp.int32, (tile, lanes), 0)
    height_ids = [(base + n * tile).astype(jnp.float32).astype(kind) for n in range(height // tile)]
    across_ids = height_ids[: across // tile]
    lane = lane_iota((1, lanes))
    one = jnp.ones((tile, lanes), jnp.bfloat16)
    none = jnp.zeros((tile, lanes), jnp.bfloat16)

    def spread(row, to):
        return jnp.broadcast_to(row, (tile, lanes)).astype(to)

    def build(n, half):
        for g in range(group):
            word = work[(n + 1) * group + g]
            ident = (word >> count_bits) & ((1 << (plane_bit - count_bits)) - 1)
            live = word & ((1 << count_bits) - 1)
            there = slice(g * lanes, (g + 1) * lanes)
            sender, chunk = lax.div(ident, chunks), lax.rem(ident, chunks)
            x = word >> plane_bit
            cell = cells[sender, chunk, pl.ds(x, 1), :]
            up = jnp.where(lane < live, cell >> shift, -1).astype(jnp.float32)
            side = (cell & (across - 1)).astype(jnp.float32)
            up, side = spread(up, kind), spread(side, kind)
            for i, ids in enumerate(height_ids):
                lefts[half][i * tile : (i + 1) * tile, there] = jnp.where(up == ids, one, none)
            masks = [side == ids for ids in across_ids]
            for c in range(components):
                force = got[sender, c, chunk, pl.ds(x, 1), :]
                rest_of = force - force.astype(jnp.bfloat16).astype(jnp.float32)
                for m, value in enumerate((force, rest_of)):
                    value = spread(value, jnp.bfloat16)
                    start = (m * components + c) * across
                    for i, mask in enumerate(masks):
                        place = slice(start + i * tile, start + (i + 1) * tile)
                        rights[half][place, there] = jnp.where(mask, value, none)

    def add(n, half):
        total[work[(n + 1) * group] >> plane_bit] += lax.dot_general(
            lefts[half][...],
            rights[half][...],
            (((1,), (1,)), ((), ())),
            preferred_element_type=jnp.float32,
        )

    def two_steps(n, carry):
        add(2 * n, 0)
        build(2 * n + 1, 1)
        add(2 * n + 1, 1)
        build(2 * n + 2, 0)
        return carry

    listed.wait()
    build(0, 0)
    count = work[0]
    lax.fori_loop(0, lax.div(count, 2), two_steps, 0)

    @pl.when(lax.rem(count, 2) == 1)
    def _():
        add(count - 1, 0)


def sweep_kernel(total, from_above, from_below, rhs_start, inv, first, lower, upper, *refs):
    (ends, coefs, deposit_hbm, swept, prefix, ratio, reduced, sums) = refs[:8]
    (rhs, field, columns, edges, sems) = refs[8:]
    components, planes, height, across = rhs.shape
    steps = inv.shape[0] + 1
    last = steps - 1
    knots = ends.shape[2]
    rest = knots - segments
    parts = height // lanes
    lines = components * planes
    for p in range(parts):
        part = slice(p * lines, (p + 1) * lines)
        columns[p, pl.ds(0, lines, stride=2), :] = from_above[part, :]
        columns[p, pl.ds(1, lines, stride=2), :] = from_below[part, :]
        edges[p * lanes : (p + 1) * lanes, :] = diffusion_number * columns[p].T

    wide = lane_iota((lanes, across))
    border = (wide == 0) | (wide == across - 1)

    def place(x):
        return [
            pltpu.make_async_copy(field.at[c, x], deposit_hbm.at[c, x], sems.at[c, x])
            for c in range(components)
        ]

    def combine(x, carry):
        for c in range(components):
            for p in range(parts):
                part = slice(p * lanes, (p + 1) * lanes)
                high = total[x, part, c * across : (c + 1) * across]
                low = total[x, part, (components + c) * across : (components + c + 1) * across]
                value = high + low
                field[c, x, part, :] = value.astype(jnp.bfloat16)
                edge = pltpu.roll(edges[part, :], lanes - 1 - 2 * (c * planes + x), 1)
                rhs[c, x, part, :] = rhs_start[c, x, part, :] + value + jnp.where(border, edge, 0.0)
        start_all(place(x))
        return carry

    lax.fori_loop(0, planes, combine, 0, unroll=planes)
    sums[2 * lines : 2 * lines + coefs.shape[0], :] = coefs[...]

    zero = jnp.zeros((components, planes, segments, across), jnp.float32)

    def of_step(t):
        return rhs[:, :, pl.ds(t, segments, stride=steps), :]

    def forward(t, carry):
        value, start, run, before = carry
        force = of_step(t)
        low, inverse = lower[:, pl.ds(t, segments, stride=steps), :], inv[t]
        value = force + (low * before)[None] * value
        swept[t] = inverse[None] * value
        run = run * (low * inverse)
        prefix[t] = run
        ratio[t] = upper[:, pl.ds(t, segments, stride=steps), :] * inverse
        return value, start + first[t][None] * force, run, inverse

    one = jnp.ones((planes, segments, across), jnp.float32)
    value, start, _, inverse = lax.fori_loop(0, last, forward, (zero, zero, one, one), unroll=6)
    value = inverse[None] * value
    segment = lax.broadcasted_iota(jnp.int32, zero.shape, 2)
    after = jnp.where(segment == segments - 1, 0.0, jnp.roll(start, -1, axis=2))
    low_sep, up_sep = ends[2, :, :segments, :], ends[3, :, :segments, :]
    value = of_step(last) + low_sep[None] * value + up_sep[None] * after
    others = rhs[:, :, height - rest :, :]
    at_top = ends[0, :, :segments, :][None] * value + ends[0, :, segments:, :][None] * others
    at_bottom = ends[1, :, :segments, :][None] * value + ends[1, :, segments:, :][None] * others
    at_bottom = at_bottom + jnp.where(segment == 0, start, 0.0)
    for c in range(components):
        for x in range(planes):
            k = c * planes + x
            reduced[k * knots : k * knots + segments, :] = value[c, x]
            reduced[k * knots + segments : (k + 1) * knots, :] = others[c, x]
            top = jnp.sum(at_top[c, x], 0, keepdims=True)
            bottom = jnp.sum(at_bottom[c, x], 0, keepdims=True)
            sums[k : k + 1, :] = top
            sums[lines + k : lines + k + 1, :] = bottom

    for x in range(planes):
        wait_all(place(x))


def finish_kernel(inner, reduced, swept, ratio, prefix, *refs):
    walls = len(refs) - 7
    received = refs[:walls]
    out_hbm, sums, tops, after, before, out, sems = refs[walls:]
    components, planes, height, across = out.shape
    steps = swept.shape[0] + 1
    last = steps - 1
    lines = components * planes
    knots = inner.shape[1] + 1
    rest = knots - segments
    me = lax.axis_index("wall")
    for n in range(walls):
        sums[lax.rem(me + walls - n, walls)] = received[n][...]

    def coef(k, n):
        start = 2 * lines + n * planes
        return sums[k, start : start + planes, :]

    def wide(value):
        return jnp.concatenate([value] * components, 0)

    d = jnp.ones((planes, across), jnp.float32)
    value = jnp.zeros((lines, across), jnp.float32)
    values, ratios = [], []
    for k in range(walls):
        low, own, up = coef(k, 0), coef(k, 1), coef(k, 2)
        right = sums[k, :lines, :]
        if k + 1 < walls:
            high = up * coef(k + 1, 4)
            killing = own + up * coef(k + 1, 3)
            right = right + wide(up) * sums[k + 1, lines : 2 * lines, :]
        else:
            high = jnp.zeros_like(up)
            killing = own + up
        e = killing + low * d
        inverse = reciprocal(high + e)
        d = e * inverse
        value = (right + wide(low) * value) * wide(inverse)
        values.append(value)
        ratios.append(wide(high * inverse))
    tops[0] = jnp.zeros((lines, across), jnp.float32)
    tops[walls] = values[-1]
    for k in reversed(range(walls - 1)):
        values[k] = values[k] + ratios[k] * values[k + 1]
        tops[k + 1] = values[k]

    def row(s):
        return pl.ds(s, lines, stride=knots)

    run = tops[me]
    before[row(0), :] = run
    found = []
    for s in range(knots - 1):
        run = reduced[row(s), :] * wide(inner[0, s]) + wide(inner[1, s]) * run
        found.append(run)
    run = tops[me + 1]
    after[row(knots - 1), :] = run
    for s in reversed(range(knots - 1)):
        run = found[s] + wide(inner[2, s]) * run
        after[row(s), :] = run
        if s + 1 < segments:
            before[row(s + 1), :] = run

    def put(c, x, t, value):
        out[c, x, pl.ds(t, segments, stride=steps), :] = value

    copies = []
    half = planes // 2 if planes % 2 == 0 else planes
    for start in range(0, planes, half):
        part = [(c, x) for c in range(components) for x in range(start, start + half)]
        bottoms, starts = [], []
        for c, x in part:
            base = (c * planes + x) * knots
            bottoms.append(before[base : base + segments, :])
            starts.append(after[base : base + segments, :])
            out[c, x, height - rest :, :] = after[base + segments : base + knots, :]
            put(c, x, last, starts[-1])

        def backward(n, values):
            t = last - 1 - n
            found = []
            for (c, x), value, bottom in zip(part, values, bottoms):
                value = (swept[t, c, x] + prefix[t, x] * bottom) + ratio[t, x] * value
                put(c, x, t, value)
                found.append(value)
            return tuple(found)

        lax.fori_loop(0, last, backward, tuple(starts), unroll=10)
        for here in part:
            copy = pltpu.make_async_copy(out.at[here], out_hbm.at[here], sems.at[here])
            copy.start()
            copies.append(copy)
    wait_all(copies)


def shifted(block, axis, distance):
    length = lax.axis_size(axis)
    route = [(i, (i + distance) % length) for i in range(length)]
    return lax.ppermute(block, axis, route)


def everyone(block, axis):
    return [block] + [shifted(block, axis, n) for n in range(1, lax.axis_size(axis))]


def local(velocity, lower_weight, upper_weight, forces, cells, counts):
    components, planes, height, across = velocity.shape
    receivers, capacity = forces.shape[3], forces.shape[5]
    senders = cells.shape[2]
    walls = lax.axis_size("wall")
    lines = components * planes
    chunks = capacity // lanes
    counts_shape = (planes, senders)
    forces = forces.reshape(components, receivers, planes, capacity)
    cells = cells.reshape(senders, planes, capacity)
    counts = counts.reshape(senders, planes).T

    def hbm(*arrays):
        return [pltpu.with_memory_space_constraint(array, pltpu.HBM) for array in arrays]

    work_shape = (planes * (senders * chunks + group) + 4 * group,)
    send, lower_near, upper_near, velocity_near, work = call(
        load_kernel,
        (
            pltpu.HBM((receivers, components, planes, capacity), jnp.float32),
            f32(*lower_weight.shape),
            f32(*upper_weight.shape),
            f32(*velocity.shape),
            jax.ShapeDtypeStruct(work_shape, jnp.int32),
        ),
        (in_hbm, *[in_vmem] * 4),
        [in_hbm] * 5,
        [
            scratch(*forces.shape),
            pltpu.SMEM(counts_shape, jnp.int32),
            pltpu.SMEM(work_shape, jnp.int32),
            pltpu.SemaphoreType.DMA((3 * components + 4,)),
        ],
        4,
        1 << 16,
    )(*hbm(forces, velocity, lower_weight, upper_weight, counts))
    got = lax.all_to_all(send, "span", 0, 0, tiled=True)
    got = got.reshape(senders, components, planes, chunks, lanes).transpose(0, 1, 3, 2, 4)
    cells = cells.reshape(senders, planes, chunks, lanes).transpose(0, 2, 1, 3)
    edge_shape = (lines * height // lanes, lanes)
    first_column, last_column = call(
        edge_kernel,
        (f32(*edge_shape), f32(*edge_shape)),
        (in_vmem, in_vmem),
        [in_vmem],
        [scratch(height, across), scratch(height // lanes, lanes, lanes)],
        4,
        1 << 20,
    )(velocity_near)
    from_above = shifted(first_column, "span", -1)
    from_below = shifted(last_column, "span", 1)

    steps = height // segments - 1
    knots = height - segments * steps + segments
    step_shape = (steps - 1, planes, segments, across)
    staged = [velocity.shape, step_shape, step_shape]
    prepared = call(
        prepare_kernel,
        (
            f32(3, knots - 1, planes, across),
            f32(4, planes, knots, across),
            f32(5 * planes, across),
            *[pltpu.HBM(shape, jnp.float32) for shape in staged],
        ),
        [in_vmem] * 3 + [in_hbm] * 3,
        [in_vmem] * 3,
        [
            *[scratch(*shape) for shape in staged],
            scratch(*step_shape),
            scratch(*step_shape),
            scratch(7, planes * knots, across),
            pltpu.SemaphoreType.DMA((3,)),
        ],
        12,
        1 << 24,
    )(velocity_near, lower_near, upper_near)
    (inner, ends, coefs, rhs_start, inv, first) = prepared

    sum_rows = -(-(2 * lines + 5 * planes) // 8) * 8
    wide = 2 * components * across
    total = call(
        scatter_kernel,
        f32(planes, height, wide),
        in_vmem,
        [in_vmem] * 4,
        [
            pltpu.SMEM(work_shape, jnp.int32),
            [pltpu.VMEM((height, group * lanes), jnp.bfloat16)] * 2,
            [pltpu.VMEM((wide, group * lanes), jnp.bfloat16)] * 2,
            pltpu.SemaphoreType.DMA,
        ],
        16,
        1 << 32,
    )(got, cells, work, coefs)

    deposit, swept, prefix, ratio, reduced, sums = call(
        sweep_kernel,
        (
            jax.ShapeDtypeStruct(velocity.shape, jnp.bfloat16),
            f32(steps - 1, components, planes, segments, across),
            f32(*step_shape),
            f32(*step_shape),
            f32(lines * knots, across),
            f32(sum_rows, across),
        ),
        (in_hbm, *[in_vmem] * 5),
        [in_vmem] * 10,
        [
            scratch(*velocity.shape),
            pltpu.VMEM(velocity.shape, jnp.bfloat16),
            scratch(height // lanes, lanes, lanes),
            scratch(height, lanes),
            pltpu.SemaphoreType.DMA((components, planes)),
        ],
        8,
        1 << 24,
    )(
        total,
        from_above,
        from_below,
        rhs_start,
        inv,
        first,
        lower_weight,
        upper_weight,
        ends,
        coefs,
    )
    all_sums = everyone(sums, "wall")

    velocity_next = call(
        finish_kernel,
        f32(*velocity.shape),
        in_hbm,
        [in_vmem] * (5 + walls),
        [
            scratch(walls, sum_rows, across),
            scratch(walls + 1, lines, across),
            scratch(lines * knots, across),
            scratch(lines * knots, across),
            scratch(*velocity.shape),
            pltpu.SemaphoreType.DMA((components, planes)),
        ],
        8,
        1 << 22,
    )(inner, reduced, swept, ratio, prefix, *all_sums)
    return (velocity_next, deposit)


def solution(mesh):
    placed = (
        P(None, None, "wall", "span"),
        P(None, "wall", "span"),
        P(None, "wall", "span"),
        P(None, "wall", "span", None, None, None),
        P("wall", "span", None, None, None),
        P("wall", "span", None, None),
    )
    return jax.shard_map(
        local,
        mesh=mesh,
        in_specs=placed,
        out_specs=(P(None, None, "wall", "span"), P(None, None, "wall", "span")),
        check_vma=False,
    )
```

```python
import jax
import jax.numpy as jnp
from jax import lax
from jax.experimental import pallas as pl
from jax.experimental.pallas import tpu as pltpu
from jax.sharding import PartitionSpec as P

diffusion_number = 0.2
segments = 8
lanes = 128
group = 8
count_bits, plane_bit = 10, 24
in_vmem = pl.BlockSpec(memory_space=pltpu.VMEM)
in_smem = pl.BlockSpec(memory_space=pltpu.SMEM)
in_hbm = pl.BlockSpec(memory_space=pltpu.HBM)


def call(body, out_shape, out_specs, in_specs, scratch, mebibytes, flops):
    return pl.pallas_call(
        body,
        out_shape=out_shape,
        in_specs=in_specs,
        out_specs=out_specs,
        scratch_shapes=scratch,
        compiler_params=pltpu.CompilerParams(vmem_limit_bytes=mebibytes << 20),
        cost_estimate=pl.CostEstimate(flops=flops, bytes_accessed=4 << 20, transcendentals=0),
    )


def f32(*shape):
    return jax.ShapeDtypeStruct(shape, jnp.float32)


def scratch(*shape):
    return pltpu.VMEM(shape, jnp.float32)


def lane_iota(shape):
    return lax.broadcasted_iota(jnp.int32, shape, len(shape) - 1)


def reciprocal(value):
    rough = pl.reciprocal(value, approx=True)
    return rough * (2.0 - value * rough)


def start_all(copies):
    for copy in copies:
        copy.start()


def wait_all(copies):
    for copy in copies:
        copy.wait()


def copies_of(sources, targets, sems, first=0):
    return [
        pltpu.make_async_copy(source, target, sems.at[first + n])
        for n, (source, target) in enumerate(zip(sources, targets))
    ]


def load_kernel(forces, velocity, lower, upper, counts_hbm, send, *refs):
    near, work_out, (slots, counts, work, sems) = refs[:3], refs[3], refs[4:]
    components, senders, planes, capacity = forces.shape
    chunks = capacity // lanes
    sources = [counts_hbm] + [forces.at[c] for c in range(components)]
    targets = [counts] + [slots.at[c] for c in range(components)]
    sources += [lower, upper] + [velocity.at[c] for c in range(components)]
    targets += [near[0], near[1]] + [near[2].at[c] for c in range(components)]
    copies = copies_of(sources, targets, sems)
    start_all(copies)
    outgoing = copies_of(
        [slots.at[c] for c in range(components)] + [work],
        [send.at[:, c] for c in range(components)] + [work_out],
        sems,
        len(copies),
    )

    def one_plane(x, n):
        def one_sender(s, n):
            count = counts[x, s]
            base = (x << plane_bit) + ((s * chunks) << count_bits)
            for k in range(chunks):
                live = jnp.maximum(count - k * lanes, 0)
                work[group + n + k] = base + (k << count_bits) + live
            return n + lax.div(count + lanes - 1, lanes)

        n = lax.fori_loop(0, senders, one_sender, n, unroll=4)
        for extra in range(group):
            work[group + n + extra] = x << plane_bit
        return lax.div(n + group - 1, group) * group

    copies[0].wait()
    total = lax.fori_loop(0, planes // 2, one_plane, 0)
    for c in range(components):
        copies[1 + c].wait()
        outgoing[c].start()
    total = lax.fori_loop(planes // 2, planes, one_plane, total)
    for extra in range(2 * group):
        work[group + total + extra] = 0
    work[0] = lax.div(total, group)
    outgoing[components].start()
    wait_all(copies[1 + components :])
    wait_all(outgoing)


def edge_kernel(velocity, first_out, last_out, columns, turned):
    components, planes, height, across = velocity.shape
    lines = components * planes
    lane = lane_iota((height, across))
    picked = jnp.zeros((height, across), jnp.float32)
    for k in range(lines):
        rolled = pltpu.roll(velocity[k // planes, k % planes], 2 * k + 1, 1)
        picked = jnp.where((lane >> 1) == k, rolled, picked)
    columns[...] = picked
    for p in range(height // lanes):
        turned[p] = columns[p * lanes : (p + 1) * lanes, :].T
        part = slice(p * lines, (p + 1) * lines)
        first_out[part, :] = turned[p, pl.ds(1, lines, stride=2), :]
        last_out[part, :] = turned[p, pl.ds(0, lines, stride=2), :]


def prepare_kernel(velocity, lower, upper, inner, ends, coefs, *refs):
    (rhs, inv, first) = refs[3:6]
    (inv_b, gain_b, rows, sems) = refs[6:]
    outgoing = copies_of(refs[3:6], refs[:3], sems)
    components, planes, height, across = velocity.shape
    steps = inv.shape[0] + 1
    last = steps - 1
    rest = height - segments * steps
    knots = segments + rest

    def of_step(ref, t):
        return ref[:, pl.ds(t, segments, stride=steps), :]

    one = jnp.ones((planes, segments, across), jnp.float32)
    zero = jnp.zeros_like(one)
    size = 8
    lane = lane_iota((size, across))

    def stencil_rows(n):
        return pl.ds(pl.multiple_of(n * size, size), size)

    def read_rows(n):
        part = stencil_rows(n)
        return [[velocity[c, x, part, :] for x in range(planes)] for c in range(components)]

    def stencil(values):
        found = []
        for x in range(planes):
            v = values[x]
            around = values[(x - 1) % planes] + values[(x + 1) % planes]
            around = around + jnp.where(lane == 0, 0.0, pltpu.roll(v, 1, 1))
            around = around + jnp.where(lane == across - 1, 0.0, pltpu.roll(v, across - 1, 1))
            found.append((1.0 - 4.0 * diffusion_number) * v + diffusion_number * around)
        return found

    def write_rows(n, values):
        part = stencil_rows(n)
        for c in range(components):
            for x in range(planes):
                rhs[c, x, part, :] = values[c][x]

    def factor(t, carry):
        d, d_b, low_gain, high_gain, sum_last, sum_first = carry
        back = last - 1 - t
        low, up = of_step(lower, t), of_step(upper, t)
        low_b, up_b = of_step(lower, back), of_step(upper, back)
        velocities = read_rows(t)
        e = 1.0 + low * d
        inverse = reciprocal(up + e)
        g = low * inverse
        e_b = 1.0 + up_b * d_b
        inverse_b = reciprocal(low_b + e_b)
        g_b = up_b * inverse_b
        found = [stencil(values) for values in velocities]
        inv[t] = inverse
        inv_b[back] = inverse_b
        gain_b[back] = g_b
        write_rows(t, found)
        return (
            e * inverse,
            e_b * inverse_b,
            low_gain * g,
            high_gain * g_b,
            inverse + g * sum_last,
            inverse_b + g_b * sum_first,
        )

    carry = lax.fori_loop(0, last, factor, (one, one, one, one, zero, zero), unroll=2)
    _, _, low_gain, high_gain, sum_last, sum_first = carry
    for n in range(last, height // size):
        write_rows(n, [stencil(values) for values in read_rows(n)])
    start_all(outgoing[:2])
    def weigh(t, q):
        first[t] = inv_b[t] * q
        return q * gain_b[t]

    lax.fori_loop(0, last, weigh, one, unroll=6)
    outgoing[2].start()

    low_sep, up_sep = of_step(lower, last), of_step(upper, last)
    segment = lax.broadcasted_iota(jnp.int32, one.shape, 1)
    is_end = segment == segments - 1
    above = jnp.where(is_end, 0.0, jnp.roll(sum_first, -1, axis=1))
    couple_high = up_sep * jnp.where(is_end, 1.0, jnp.roll(high_gain, -1, axis=1))
    killing = 1.0 + low_sep * sum_last + up_sep * above
    ends[2, :, :segments, :] = low_sep
    ends[3, :, :segments, :] = up_sep
    tail = slice(height - rest, height)
    low_rest, up_rest = lower[:, tail, :], upper[:, tail, :]
    for n, (value, other) in enumerate(
        (
            (low_sep * low_gain, low_rest),
            (couple_high, up_rest),
            (killing, jnp.ones_like(low_rest)),
        )
    ):
        for x in range(planes):
            rows[n, x * knots : x * knots + segments, :] = value[x]
            rows[n, x * knots + segments : (x + 1) * knots, :] = other[x]
    for x in range(planes):
        rows[3, x * knots : x * knots + segments, :] = high_gain[x]
        rows[4, x * knots : x * knots + segments, :] = sum_first[x]

    def row(n, s):
        return rows[n, pl.ds(s, planes, stride=knots), :]

    top = knots - 1
    one_row = jnp.ones((planes, across), jnp.float32)
    d, d_b = one_row, one_row
    inv_s, gain_s, ratio_s = [], [], []
    inv_sb, gain_sb = [None] * top, [None] * top
    for s in range(top):
        e = row(2, s) + row(0, s) * d
        inverse = reciprocal(row(1, s) + e)
        inv_s.append(inverse)
        gain_s.append(row(0, s) * inverse)
        ratio_s.append(row(1, s) * inverse)
        d = e * inverse
        back = top - 1 - s
        e_b = row(2, back) + row(1, back) * d_b
        inverse_b = reciprocal(row(0, back) + e_b)
        inv_sb[back] = inverse_b
        gain_sb[back] = row(1, back) * inverse_b
        d_b = e_b * inverse_b
        inner[0, s] = inv_s[s]
        inner[1, s] = gain_s[s]
        inner[2, s] = ratio_s[s]
    run = row(0, top)
    low_total = one_row
    sum_top = one_row
    rows[5, pl.ds(top, planes, stride=knots), :] = one_row
    for s in reversed(range(top)):
        weight = run * inv_s[s]
        rows[5, pl.ds(s, planes, stride=knots), :] = weight
        sum_top = sum_top + weight * row(2, s)
        run = run * gain_s[s]
        low_total = low_total * gain_s[s]
    run = row(3, 0)
    high_total = one_row
    sum_bottom = row(4, 0)
    rows[6, pl.ds(top, planes, stride=knots), :] = jnp.zeros_like(one_row)
    for s in range(top):
        weight = run * inv_sb[s]
        rows[6, pl.ds(s, planes, stride=knots), :] = weight
        sum_bottom = sum_bottom + weight * row(2, s)
        run = run * gain_sb[s]
        high_total = high_total * ratio_s[s]
    coef = (
        row(0, top) * low_total,
        sum_top,
        row(1, top),
        sum_bottom,
        row(3, 0) * high_total,
    )
    for n, value in enumerate(coef):
        coefs[n * planes : (n + 1) * planes, :] = value
    for n in range(2):
        for x in range(planes):
            ends[n, x] = rows[5 + n, x * knots : (x + 1) * knots, :]
    wait_all(outgoing)


def scatter_kernel(got, cells, work_in, coefs, total, work, lefts, rights, sem):
    del coefs
    listed = pltpu.make_async_copy(work_in, work, sem)
    listed.start()
    components, chunks = got.shape[1], got.shape[2]
    _, wide, height = total.shape
    across = wide // (2 * components)
    shift = across.bit_length() - 1
    kind = jnp.bfloat16 if max(height, across) <= 256 else jnp.float32
    total[...] = jnp.zeros_like(total)

    tile = 16
    base = lax.broadcasted_iota(jnp.int32, (tile, lanes), 0)
    height_ids = [(base + n * tile).astype(jnp.float32).astype(kind) for n in range(height // tile)]
    across_ids = height_ids[: across // tile]
    lane = lane_iota((1, lanes))
    one = jnp.ones((tile, lanes), jnp.bfloat16)
    none = jnp.zeros((tile, lanes), jnp.bfloat16)

    def spread(row, to):
        return jnp.broadcast_to(row, (tile, lanes)).astype(to)

    def build(n, half):
        for g in range(group):
            word = work[(n + 1) * group + g]
            ident = (word >> count_bits) & ((1 << (plane_bit - count_bits)) - 1)
            live = word & ((1 << count_bits) - 1)
            there = slice(g * lanes, (g + 1) * lanes)
            sender, chunk = lax.div(ident, chunks), lax.rem(ident, chunks)
            x = word >> plane_bit
            cell = cells[sender, chunk, pl.ds(x, 1), :]
            up = jnp.where(lane < live, cell >> shift, -1).astype(jnp.float32)
            side = (cell & (across - 1)).astype(jnp.float32)
            up, side = spread(up, kind), spread(side, kind)
            for i, ids in enumerate(height_ids):
                lefts[half][i * tile : (i + 1) * tile, there] = jnp.where(up == ids, one, none)
            masks = [side == ids for ids in across_ids]
            for c in range(components):
                force = got[sender, c, chunk, pl.ds(x, 1), :]
                rest_of = force - force.astype(jnp.bfloat16).astype(jnp.float32)
                for m, value in enumerate((force, rest_of)):
                    value = spread(value, jnp.bfloat16)
                    start = (m * components + c) * across
                    for i, mask in enumerate(masks):
                        place = slice(start + i * tile, start + (i + 1) * tile)
                        rights[half][place, there] = jnp.where(mask, value, none)

    def add(n, half):
        total[work[(n + 1) * group] >> plane_bit] += lax.dot_general(
            rights[half][...],
            lefts[half][...],
            (((1,), (1,)), ((), ())),
            preferred_element_type=jnp.float32,
        )

    def two_steps(n, carry):
        add(2 * n, 0)
        build(2 * n + 1, 1)
        add(2 * n + 1, 1)
        build(2 * n + 2, 0)
        return carry

    listed.wait()
    build(0, 0)
    count = work[0]
    lax.fori_loop(0, lax.div(count, 2), two_steps, 0)

    @pl.when(lax.rem(count, 2) == 1)
    def _():
        add(count - 1, 0)


def sweep_kernel(total, from_above, from_below, rhs_start, inv, first, lower, upper, *refs):
    (ends, coefs, deposit_hbm, swept, prefix, ratio, reduced, sums) = refs[:8]
    (rhs, field, columns, edges, sems) = refs[8:]
    components, planes, height, across = rhs.shape
    steps = inv.shape[0] + 1
    last = steps - 1
    knots = ends.shape[2]
    rest = knots - segments
    parts = height // lanes
    lines = components * planes
    for p in range(parts):
        part = slice(p * lines, (p + 1) * lines)
        columns[p, pl.ds(0, lines, stride=2), :] = from_above[part, :]
        columns[p, pl.ds(1, lines, stride=2), :] = from_below[part, :]
        edges[p * lanes : (p + 1) * lanes, :] = diffusion_number * columns[p].T

    wide = lane_iota((lanes, across))
    border = (wide == 0) | (wide == across - 1)

    def place(x):
        return [
            pltpu.make_async_copy(field.at[c, x], deposit_hbm.at[c, x], sems.at[c, x])
            for c in range(components)
        ]

    def combine(x, carry):
        for c in range(components):
            for p in range(parts):
                part = slice(p * lanes, (p + 1) * lanes)
                high = total[x, c * across : (c + 1) * across, part]
                low = total[x, (components + c) * across : (components + c + 1) * across, part]
                value = (high + low).T
                field[c, x, part, :] = value.astype(jnp.bfloat16)
                edge = pltpu.roll(edges[part, :], lanes - 1 - 2 * (c * planes + x), 1)
                rhs[c, x, part, :] = rhs_start[c, x, part, :] + value + jnp.where(border, edge, 0.0)
        start_all(place(x))
        return carry

    lax.fori_loop(0, planes, combine, 0, unroll=planes)
    sums[2 * lines : 2 * lines + coefs.shape[0], :] = coefs[...]

    zero = jnp.zeros((components, planes, segments, across), jnp.float32)

    def of_step(t):
        return rhs[:, :, pl.ds(t, segments, stride=steps), :]

    def forward(t, carry):
        value, start, run, before = carry
        force = of_step(t)
        low, inverse = lower[:, pl.ds(t, segments, stride=steps), :], inv[t]
        value = force + (low * before)[None] * value
        swept[t] = inverse[None] * value
        run = run * (low * inverse)
        prefix[t] = run
        ratio[t] = upper[:, pl.ds(t, segments, stride=steps), :] * inverse
        return value, start + first[t][None] * force, run, inverse

    one = jnp.ones((planes, segments, across), jnp.float32)
    value, start, _, inverse = lax.fori_loop(0, last, forward, (zero, zero, one, one), unroll=6)
    value = inverse[None] * value
    segment = lax.broadcasted_iota(jnp.int32, zero.shape, 2)
    after = jnp.where(segment == segments - 1, 0.0, jnp.roll(start, -1, axis=2))
    low_sep, up_sep = ends[2, :, :segments, :], ends[3, :, :segments, :]
    value = of_step(last) + low_sep[None] * value + up_sep[None] * after
    others = rhs[:, :, height - rest :, :]
    at_top = ends[0, :, :segments, :][None] * value + ends[0, :, segments:, :][None] * others
    at_bottom = ends[1, :, :segments, :][None] * value + ends[1, :, segments:, :][None] * others
    at_bottom = at_bottom + jnp.where(segment == 0, start, 0.0)
    for c in range(components):
        for x in range(planes):
            k = c * planes + x
            reduced[k * knots : k * knots + segments, :] = value[c, x]
            reduced[k * knots + segments : (k + 1) * knots, :] = others[c, x]
            top = jnp.sum(at_top[c, x], 0, keepdims=True)
            bottom = jnp.sum(at_bottom[c, x], 0, keepdims=True)
            sums[k : k + 1, :] = top
            sums[lines + k : lines + k + 1, :] = bottom

    for x in range(planes):
        wait_all(place(x))


def finish_kernel(inner, reduced, swept, ratio, prefix, *refs):
    walls = len(refs) - 7
    received = refs[:walls]
    out_hbm, sums, tops, after, before, out, sems = refs[walls:]
    components, planes, height, across = out.shape
    steps = swept.shape[0] + 1
    last = steps - 1
    lines = components * planes
    knots = inner.shape[1] + 1
    rest = knots - segments
    me = lax.axis_index("wall")
    for n in range(walls):
        sums[lax.rem(me + walls - n, walls)] = received[n][...]

    def coef(k, n):
        start = 2 * lines + n * planes
        return sums[k, start : start + planes, :]

    def wide(value):
        return jnp.concatenate([value] * components, 0)

    d = jnp.ones((planes, across), jnp.float32)
    value = jnp.zeros((lines, across), jnp.float32)
    values, ratios = [], []
    for k in range(walls):
        low, own, up = coef(k, 0), coef(k, 1), coef(k, 2)
        right = sums[k, :lines, :]
        if k + 1 < walls:
            high = up * coef(k + 1, 4)
            killing = own + up * coef(k + 1, 3)
            right = right + wide(up) * sums[k + 1, lines : 2 * lines, :]
        else:
            high = jnp.zeros_like(up)
            killing = own + up
        e = killing + low * d
        inverse = reciprocal(high + e)
        d = e * inverse
        value = (right + wide(low) * value) * wide(inverse)
        values.append(value)
        ratios.append(wide(high * inverse))
    tops[0] = jnp.zeros((lines, across), jnp.float32)
    tops[walls] = values[-1]
    for k in reversed(range(walls - 1)):
        values[k] = values[k] + ratios[k] * values[k + 1]
        tops[k + 1] = values[k]

    def row(s):
        return pl.ds(s, lines, stride=knots)

    run = tops[me]
    before[row(0), :] = run
    found = []
    for s in range(knots - 1):
        run = reduced[row(s), :] * wide(inner[0, s]) + wide(inner[1, s]) * run
        found.append(run)
    run = tops[me + 1]
    after[row(knots - 1), :] = run
    for s in reversed(range(knots - 1)):
        run = found[s] + wide(inner[2, s]) * run
        after[row(s), :] = run
        if s + 1 < segments:
            before[row(s + 1), :] = run

    def put(c, x, t, value):
        out[c, x, pl.ds(t, segments, stride=steps), :] = value

    copies = []
    half = planes // 2 if planes % 2 == 0 else planes
    for start in range(0, planes, half):
        part = [(c, x) for c in range(components) for x in range(start, start + half)]
        bottoms, starts = [], []
        for c, x in part:
            base = (c * planes + x) * knots
            bottoms.append(before[base : base + segments, :])
            starts.append(after[base : base + segments, :])
            out[c, x, height - rest :, :] = after[base + segments : base + knots, :]
            put(c, x, last, starts[-1])

        def backward(n, values):
            t = last - 1 - n
            found = []
            for (c, x), value, bottom in zip(part, values, bottoms):
                value = (swept[t, c, x] + prefix[t, x] * bottom) + ratio[t, x] * value
                put(c, x, t, value)
                found.append(value)
            return tuple(found)

        lax.fori_loop(0, last, backward, tuple(starts), unroll=10)
        for here in part:
            copy = pltpu.make_async_copy(out.at[here], out_hbm.at[here], sems.at[here])
            copy.start()
            copies.append(copy)
    wait_all(copies)


def shifted(block, axis, distance):
    length = lax.axis_size(axis)
    route = [(i, (i + distance) % length) for i in range(length)]
    return lax.ppermute(block, axis, route)


def everyone(block, axis):
    return [block] + [shifted(block, axis, n) for n in range(1, lax.axis_size(axis))]


def local(velocity, lower_weight, upper_weight, forces, cells, counts):
    components, planes, height, across = velocity.shape
    receivers, capacity = forces.shape[3], forces.shape[5]
    senders = cells.shape[2]
    walls = lax.axis_size("wall")
    lines = components * planes
    chunks = capacity // lanes
    counts_shape = (planes, senders)
    forces = forces.reshape(components, receivers, planes, capacity)
    cells = cells.reshape(senders, planes, capacity)
    counts = counts.reshape(senders, planes).T

    def hbm(*arrays):
        return [pltpu.with_memory_space_constraint(array, pltpu.HBM) for array in arrays]

    work_shape = (planes * (senders * chunks + group) + 4 * group,)
    send, lower_near, upper_near, velocity_near, work = call(
        load_kernel,
        (
            pltpu.HBM((receivers, components, planes, capacity), jnp.float32),
            f32(*lower_weight.shape),
            f32(*upper_weight.shape),
            f32(*velocity.shape),
            jax.ShapeDtypeStruct(work_shape, jnp.int32),
        ),
        (in_hbm, *[in_vmem] * 4),
        [in_hbm] * 5,
        [
            scratch(*forces.shape),
            pltpu.SMEM(counts_shape, jnp.int32),
            pltpu.SMEM(work_shape, jnp.int32),
            pltpu.SemaphoreType.DMA((3 * components + 4,)),
        ],
        4,
        1 << 16,
    )(*hbm(forces, velocity, lower_weight, upper_weight, counts))
    got = lax.all_to_all(send, "span", 0, 0, tiled=True)
    got = got.reshape(senders, components, planes, chunks, lanes).transpose(0, 1, 3, 2, 4)
    cells = cells.reshape(senders, planes, chunks, lanes).transpose(0, 2, 1, 3)
    edge_shape = (lines * height // lanes, lanes)
    first_column, last_column = call(
        edge_kernel,
        (f32(*edge_shape), f32(*edge_shape)),
        (in_vmem, in_vmem),
        [in_vmem],
        [scratch(height, across), scratch(height // lanes, lanes, lanes)],
        4,
        1 << 20,
    )(velocity_near)
    from_above = shifted(first_column, "span", -1)
    from_below = shifted(last_column, "span", 1)

    steps = height // segments - 1
    knots = height - segments * steps + segments
    step_shape = (steps - 1, planes, segments, across)
    staged = [velocity.shape, step_shape, step_shape]
    prepared = call(
        prepare_kernel,
        (
            f32(3, knots - 1, planes, across),
            f32(4, planes, knots, across),
            f32(5 * planes, across),
            *[pltpu.HBM(shape, jnp.float32) for shape in staged],
        ),
        [in_vmem] * 3 + [in_hbm] * 3,
        [in_vmem] * 3,
        [
            *[scratch(*shape) for shape in staged],
            scratch(*step_shape),
            scratch(*step_shape),
            scratch(7, planes * knots, across),
            pltpu.SemaphoreType.DMA((3,)),
        ],
        12,
        1 << 24,
    )(velocity_near, lower_near, upper_near)
    (inner, ends, coefs, rhs_start, inv, first) = prepared

    sum_rows = -(-(2 * lines + 5 * planes) // 8) * 8
    wide = 2 * components * across
    total = call(
        scatter_kernel,
        f32(planes, wide, height),
        in_vmem,
        [in_vmem] * 4,
        [
            pltpu.SMEM(work_shape, jnp.int32),
            [pltpu.VMEM((height, group * lanes), jnp.bfloat16)] * 2,
            [pltpu.VMEM((wide, group * lanes), jnp.bfloat16)] * 2,
            pltpu.SemaphoreType.DMA,
        ],
        16,
        1 << 32,
    )(got, cells, work, coefs)

    deposit, swept, prefix, ratio, reduced, sums = call(
        sweep_kernel,
        (
            jax.ShapeDtypeStruct(velocity.shape, jnp.bfloat16),
            f32(steps - 1, components, planes, segments, across),
            f32(*step_shape),
            f32(*step_shape),
            f32(lines * knots, across),
            f32(sum_rows, across),
        ),
        (in_hbm, *[in_vmem] * 5),
        [in_vmem] * 10,
        [
            scratch(*velocity.shape),
            pltpu.VMEM(velocity.shape, jnp.bfloat16),
            scratch(height // lanes, lanes, lanes),
            scratch(height, lanes),
            pltpu.SemaphoreType.DMA((components, planes)),
        ],
        8,
        1 << 24,
    )(
        total,
        from_above,
        from_below,
        rhs_start,
        inv,
        first,
        lower_weight,
        upper_weight,
        ends,
        coefs,
    )
    all_sums = everyone(sums, "wall")

    velocity_next = call(
        finish_kernel,
        f32(*velocity.shape),
        in_hbm,
        [in_vmem] * (5 + walls),
        [
            scratch(walls, sum_rows, across),
            scratch(walls + 1, lines, across),
            scratch(lines * knots, across),
            scratch(lines * knots, across),
            scratch(*velocity.shape),
            pltpu.SemaphoreType.DMA((components, planes)),
        ],
        8,
        1 << 22,
    )(inner, reduced, swept, ratio, prefix, *all_sums)
    return (velocity_next, deposit)


def solution(mesh):
    placed = (
        P(None, None, "wall", "span"),
        P(None, "wall", "span"),
        P(None, "wall", "span"),
        P(None, "wall", "span", None, None, None),
        P("wall", "span", None, None, None),
        P("wall", "span", None, None),
    )
    return jax.shard_map(
        local,
        mesh=mesh,
        in_specs=placed,
        out_specs=(P(None, None, "wall", "span"), P(None, None, "wall", "span")),
        check_vma=False,
    )
```

```python
import jax
import jax.numpy as jnp
from jax import lax
from jax.experimental import pallas as pl
from jax.experimental.pallas import tpu as pltpu
from jax.sharding import PartitionSpec as P

diffusion_number = 0.2
segments = 8
lanes = 128
group = 8
count_bits, plane_bit = 10, 24
in_vmem = pl.BlockSpec(memory_space=pltpu.VMEM)
in_smem = pl.BlockSpec(memory_space=pltpu.SMEM)
in_hbm = pl.BlockSpec(memory_space=pltpu.HBM)


def call(body, out_shape, out_specs, in_specs, scratch, mebibytes, flops):
    return pl.pallas_call(
        body,
        out_shape=out_shape,
        in_specs=in_specs,
        out_specs=out_specs,
        scratch_shapes=scratch,
        compiler_params=pltpu.CompilerParams(vmem_limit_bytes=mebibytes << 20),
        cost_estimate=pl.CostEstimate(flops=flops, bytes_accessed=4 << 20, transcendentals=0),
    )


def f32(*shape):
    return jax.ShapeDtypeStruct(shape, jnp.float32)


def scratch(*shape):
    return pltpu.VMEM(shape, jnp.float32)


def lane_iota(shape):
    return lax.broadcasted_iota(jnp.int32, shape, len(shape) - 1)


def reciprocal(value):
    rough = pl.reciprocal(value, approx=True)
    return rough * (2.0 - value * rough)


def start_all(copies):
    for copy in copies:
        copy.start()


def wait_all(copies):
    for copy in copies:
        copy.wait()


def copies_of(sources, targets, sems, first=0):
    return [
        pltpu.make_async_copy(source, target, sems.at[first + n])
        for n, (source, target) in enumerate(zip(sources, targets))
    ]


def load_kernel(forces, velocity, lower, upper, counts_hbm, send, *refs):
    near, work_out, (slots, counts, work, sems) = refs[:3], refs[3], refs[4:]
    components, senders, planes, capacity = forces.shape
    chunks = capacity // lanes
    sources = [counts_hbm] + [forces.at[c] for c in range(components)]
    targets = [counts] + [slots.at[c] for c in range(components)]
    sources += [lower, upper] + [velocity.at[c] for c in range(components)]
    targets += [near[0], near[1]] + [near[2].at[c] for c in range(components)]
    copies = copies_of(sources, targets, sems)
    start_all(copies)
    outgoing = copies_of(
        [slots.at[c] for c in range(components)] + [work],
        [send.at[:, c] for c in range(components)] + [work_out],
        sems,
        len(copies),
    )

    def one_plane(x, n):
        def one_sender(s, n):
            count = counts[x, s]
            base = (x << plane_bit) + ((s * chunks) << count_bits)
            for k in range(chunks):
                live = jnp.maximum(count - k * lanes, 0)
                work[group + n + k] = base + (k << count_bits) + live
            return n + lax.div(count + lanes - 1, lanes)

        n = lax.fori_loop(0, senders, one_sender, n, unroll=4)
        for extra in range(group):
            work[group + n + extra] = x << plane_bit
        return lax.div(n + group - 1, group) * group

    copies[0].wait()
    total = lax.fori_loop(0, planes // 2, one_plane, 0)
    for c in range(components):
        copies[1 + c].wait()
        outgoing[c].start()
    total = lax.fori_loop(planes // 2, planes, one_plane, total)
    for extra in range(2 * group):
        work[group + total + extra] = 0
    work[0] = lax.div(total, group)
    outgoing[components].start()
    wait_all(copies[1 + components :])
    wait_all(outgoing)


def edge_kernel(velocity, first_out, last_out, columns, turned):
    components, planes, height, across = velocity.shape
    lines = components * planes
    lane = lane_iota((height, across))
    picked = jnp.zeros((height, across), jnp.float32)
    for k in range(lines):
        rolled = pltpu.roll(velocity[k // planes, k % planes], 2 * k + 1, 1)
        picked = jnp.where((lane >> 1) == k, rolled, picked)
    columns[...] = picked
    for p in range(height // lanes):
        turned[p] = columns[p * lanes : (p + 1) * lanes, :].T
        part = slice(p * lines, (p + 1) * lines)
        first_out[part, :] = turned[p, pl.ds(1, lines, stride=2), :]
        last_out[part, :] = turned[p, pl.ds(0, lines, stride=2), :]


def prepare_kernel(velocity, lower, upper, inner, ends, coefs, *refs):
    (rhs, inv, first) = refs[3:6]
    (inv_b, gain_b, rows, sems) = refs[6:]
    outgoing = copies_of(refs[3:6], refs[:3], sems)
    components, planes, height, across = velocity.shape
    steps = inv.shape[0] + 1
    last = steps - 1
    rest = height - segments * steps
    knots = segments + rest

    def of_step(ref, t):
        return ref[:, pl.ds(t, segments, stride=steps), :]

    one = jnp.ones((planes, segments, across), jnp.float32)
    zero = jnp.zeros_like(one)
    size = 8
    lane = lane_iota((size, across))

    def stencil_rows(n):
        return pl.ds(pl.multiple_of(n * size, size), size)

    def read_rows(n):
        part = stencil_rows(n)
        return [[velocity[c, x, part, :] for x in range(planes)] for c in range(components)]

    def stencil(values):
        found = []
        for x in range(planes):
            v = values[x]
            around = values[(x - 1) % planes] + values[(x + 1) % planes]
            around = around + jnp.where(lane == 0, 0.0, pltpu.roll(v, 1, 1))
            around = around + jnp.where(lane == across - 1, 0.0, pltpu.roll(v, across - 1, 1))
            found.append((1.0 - 4.0 * diffusion_number) * v + diffusion_number * around)
        return found

    def write_rows(n, values):
        part = stencil_rows(n)
        for c in range(components):
            for x in range(planes):
                rhs[c, x, part, :] = values[c][x]

    def factor(t, carry):
        d, d_b, low_gain, high_gain, sum_last, sum_first = carry
        back = last - 1 - t
        low, up = of_step(lower, t), of_step(upper, t)
        low_b, up_b = of_step(lower, back), of_step(upper, back)
        velocities = read_rows(t)
        e = 1.0 + low * d
        inverse = reciprocal(up + e)
        g = low * inverse
        e_b = 1.0 + up_b * d_b
        inverse_b = reciprocal(low_b + e_b)
        g_b = up_b * inverse_b
        found = [stencil(values) for values in velocities]
        inv[t] = inverse
        inv_b[back] = inverse_b
        gain_b[back] = g_b
        write_rows(t, found)
        return (
            e * inverse,
            e_b * inverse_b,
            low_gain * g,
            high_gain * g_b,
            inverse + g * sum_last,
            inverse_b + g_b * sum_first,
        )

    carry = lax.fori_loop(0, last, factor, (one, one, one, one, zero, zero), unroll=2)
    _, _, low_gain, high_gain, sum_last, sum_first = carry
    for n in range(last, height // size):
        write_rows(n, [stencil(values) for values in read_rows(n)])
    start_all(outgoing[:2])
    def weigh(t, q):
        first[t] = inv_b[t] * q
        return q * gain_b[t]

    lax.fori_loop(0, last, weigh, one, unroll=6)
    outgoing[2].start()

    low_sep, up_sep = of_step(lower, last), of_step(upper, last)
    segment = lax.broadcasted_iota(jnp.int32, one.shape, 1)
    is_end = segment == segments - 1
    above = jnp.where(is_end, 0.0, jnp.roll(sum_first, -1, axis=1))
    couple_high = up_sep * jnp.where(is_end, 1.0, jnp.roll(high_gain, -1, axis=1))
    killing = 1.0 + low_sep * sum_last + up_sep * above
    ends[2, :, :segments, :] = low_sep
    ends[3, :, :segments, :] = up_sep
    tail = slice(height - rest, height)
    low_rest, up_rest = lower[:, tail, :], upper[:, tail, :]
    for n, (value, other) in enumerate(
        (
            (low_sep * low_gain, low_rest),
            (couple_high, up_rest),
            (killing, jnp.ones_like(low_rest)),
        )
    ):
        for x in range(planes):
            rows[n, x * knots : x * knots + segments, :] = value[x]
            rows[n, x * knots + segments : (x + 1) * knots, :] = other[x]
    for x in range(planes):
        rows[3, x * knots : x * knots + segments, :] = high_gain[x]
        rows[4, x * knots : x * knots + segments, :] = sum_first[x]

    def row(n, s):
        return rows[n, pl.ds(s, planes, stride=knots), :]

    top = knots - 1
    one_row = jnp.ones((planes, across), jnp.float32)
    d, d_b = one_row, one_row
    inv_s, gain_s, ratio_s = [], [], []
    inv_sb, gain_sb = [None] * top, [None] * top
    for s in range(top):
        e = row(2, s) + row(0, s) * d
        inverse = reciprocal(row(1, s) + e)
        inv_s.append(inverse)
        gain_s.append(row(0, s) * inverse)
        ratio_s.append(row(1, s) * inverse)
        d = e * inverse
        back = top - 1 - s
        e_b = row(2, back) + row(1, back) * d_b
        inverse_b = reciprocal(row(0, back) + e_b)
        inv_sb[back] = inverse_b
        gain_sb[back] = row(1, back) * inverse_b
        d_b = e_b * inverse_b
        inner[0, s] = inv_s[s]
        inner[1, s] = gain_s[s]
        inner[2, s] = ratio_s[s]
    run = row(0, top)
    low_total = one_row
    sum_top = one_row
    rows[5, pl.ds(top, planes, stride=knots), :] = one_row
    for s in reversed(range(top)):
        weight = run * inv_s[s]
        rows[5, pl.ds(s, planes, stride=knots), :] = weight
        sum_top = sum_top + weight * row(2, s)
        run = run * gain_s[s]
        low_total = low_total * gain_s[s]
    run = row(3, 0)
    high_total = one_row
    sum_bottom = row(4, 0)
    rows[6, pl.ds(top, planes, stride=knots), :] = jnp.zeros_like(one_row)
    for s in range(top):
        weight = run * inv_sb[s]
        rows[6, pl.ds(s, planes, stride=knots), :] = weight
        sum_bottom = sum_bottom + weight * row(2, s)
        run = run * gain_sb[s]
        high_total = high_total * ratio_s[s]
    coef = (
        row(0, top) * low_total,
        sum_top,
        row(1, top),
        sum_bottom,
        row(3, 0) * high_total,
    )
    for n, value in enumerate(coef):
        coefs[n * planes : (n + 1) * planes, :] = value
    for n in range(2):
        for x in range(planes):
            ends[n, x] = rows[5 + n, x * knots : (x + 1) * knots, :]
    wait_all(outgoing)


def scatter_kernel(got, cells, work_in, coefs, total, work, lefts, rights, sem):
    del coefs
    listed = pltpu.make_async_copy(work_in, work, sem)
    listed.start()
    components, chunks = got.shape[1], got.shape[2]
    _, height, wide = total.shape
    across = wide // (2 * components)
    shift = across.bit_length() - 1
    kind = jnp.bfloat16 if max(height, across) <= 256 else jnp.float32
    total[...] = jnp.zeros_like(total)

    tile = 16
    base = lax.broadcasted_iota(jnp.int32, (tile, lanes), 0)
    height_ids = [(base + n * tile).astype(jnp.float32).astype(kind) for n in range(height // tile)]
    across_ids = height_ids[: across // tile]
    lane = lane_iota((1, lanes))
    one = jnp.ones((tile, lanes), jnp.bfloat16)
    none = jnp.zeros((tile, lanes), jnp.bfloat16)

    def spread(row, to):
        return jnp.broadcast_to(row, (tile, lanes)).astype(to)

    def build(n, half):
        for g in range(group):
            word = work[(n + 1) * group + g]
            ident = (word >> count_bits) & ((1 << (plane_bit - count_bits)) - 1)
            live = word & ((1 << count_bits) - 1)
            there = slice(g * lanes, (g + 1) * lanes)
            sender, chunk = lax.div(ident, chunks), lax.rem(ident, chunks)
            x = word >> plane_bit
            cell = cells[sender, chunk, pl.ds(x, 1), :]
            up = jnp.where(lane < live, cell >> shift, -1).astype(jnp.float32)
            side = (cell & (across - 1)).astype(jnp.float32)
            up, side = spread(up, kind), spread(side, kind)
            for i, ids in enumerate(height_ids):
                lefts[half][i * tile : (i + 1) * tile, there] = jnp.where(up == ids, one, none)
            masks = [side == ids for ids in across_ids]
            for c in range(components):
                force = got[sender, c, chunk, pl.ds(x, 1), :]
                rest_of = force - force.astype(jnp.bfloat16).astype(jnp.float32)
                for m, value in enumerate((force, rest_of)):
                    value = spread(value, jnp.bfloat16)
                    start = (m * components + c) * across
                    for i, mask in enumerate(masks):
                        place = slice(start + i * tile, start + (i + 1) * tile)
                        rights[half][place, there] = jnp.where(mask, value, none)

    def add(n, half):
        total[work[(n + 1) * group] >> plane_bit] += lax.dot_general(
            lefts[half][...],
            rights[half][...],
            (((1,), (1,)), ((), ())),
            preferred_element_type=jnp.float32,
        )

    def two_steps(n, carry):
        add(2 * n, 0)
        build(2 * n + 1, 1)
        add(2 * n + 1, 1)
        build(2 * n + 2, 0)
        return carry

    listed.wait()
    build(0, 0)
    count = work[0]
    lax.fori_loop(0, lax.div(count, 2), two_steps, 0)

    @pl.when(lax.rem(count, 2) == 1)
    def _():
        add(count - 1, 0)


def sweep_kernel(total, from_above, from_below, rhs_start, inv, first, lower, upper, *refs):
    (ends, coefs, deposit_hbm, swept, prefix, ratio, reduced, sums) = refs[:8]
    (rhs, field, columns, edges, sems) = refs[8:]
    components, planes, height, across = rhs.shape
    steps = inv.shape[0] + 1
    last = steps - 1
    knots = ends.shape[2]
    rest = knots - segments
    parts = height // lanes
    lines = components * planes
    for p in range(parts):
        part = slice(p * lines, (p + 1) * lines)
        columns[p, pl.ds(0, lines, stride=2), :] = from_above[part, :]
        columns[p, pl.ds(1, lines, stride=2), :] = from_below[part, :]
        edges[p * lanes : (p + 1) * lanes, :] = diffusion_number * columns[p].T

    wide = lane_iota((lanes, across))
    border = (wide == 0) | (wide == across - 1)

    def place(x):
        return [
            pltpu.make_async_copy(field.at[c, x], deposit_hbm.at[c, x], sems.at[c, x])
            for c in range(components)
        ]

    def combine(x, carry):
        for c in range(components):
            for p in range(parts):
                part = slice(p * lanes, (p + 1) * lanes)
                high = total[x, part, c * across : (c + 1) * across]
                low = total[x, part, (components + c) * across : (components + c + 1) * across]
                value = high + low
                field[c, x, part, :] = value.astype(jnp.bfloat16)
                edge = pltpu.roll(edges[part, :], lanes - 1 - 2 * (c * planes + x), 1)
                rhs[c, x, part, :] = rhs_start[c, x, part, :] + value + jnp.where(border, edge, 0.0)
        start_all(place(x))
        return carry

    lax.fori_loop(0, planes, combine, 0, unroll=planes)
    sums[2 * lines : 2 * lines + coefs.shape[0], :] = coefs[...]

    zero = jnp.zeros((components, planes, segments, across), jnp.float32)

    def of_step(t):
        return rhs[:, :, pl.ds(t, segments, stride=steps), :]

    def forward(t, carry):
        value, start, run, before = carry
        force = of_step(t)
        low, inverse = lower[:, pl.ds(t, segments, stride=steps), :], inv[t]
        value = force + (low * before)[None] * value
        swept[t] = inverse[None] * value
        run = run * (low * inverse)
        prefix[t] = run
        ratio[t] = upper[:, pl.ds(t, segments, stride=steps), :] * inverse
        return value, start + first[t][None] * force, run, inverse

    one = jnp.ones((planes, segments, across), jnp.float32)
    value, start, _, inverse = lax.fori_loop(0, last, forward, (zero, zero, one, one), unroll=6)
    value = inverse[None] * value
    segment = lax.broadcasted_iota(jnp.int32, zero.shape, 2)
    after = jnp.where(segment == segments - 1, 0.0, jnp.roll(start, -1, axis=2))
    low_sep, up_sep = ends[2, :, :segments, :], ends[3, :, :segments, :]
    value = of_step(last) + low_sep[None] * value + up_sep[None] * after
    others = rhs[:, :, height - rest :, :]
    at_top = ends[0, :, :segments, :][None] * value + ends[0, :, segments:, :][None] * others
    at_bottom = ends[1, :, :segments, :][None] * value + ends[1, :, segments:, :][None] * others
    at_bottom = at_bottom + jnp.where(segment == 0, start, 0.0)
    for c in range(components):
        for x in range(planes):
            k = c * planes + x
            reduced[k * knots : k * knots + segments, :] = value[c, x]
            reduced[k * knots + segments : (k + 1) * knots, :] = others[c, x]
            top = jnp.sum(at_top[c, x], 0, keepdims=True)
            bottom = jnp.sum(at_bottom[c, x], 0, keepdims=True)
            sums[k : k + 1, :] = top
            sums[lines + k : lines + k + 1, :] = bottom

    for x in range(planes):
        wait_all(place(x))


def finish_kernel(inner, reduced, swept, ratio, prefix, *refs):
    walls = len(refs) - 7
    received = refs[:walls]
    out_hbm, sums, tops, after, before, out, sems = refs[walls:]
    components, planes, height, across = out.shape
    steps = swept.shape[0] + 1
    last = steps - 1
    lines = components * planes
    knots = inner.shape[1] + 1
    rest = knots - segments
    me = lax.axis_index("wall")
    for n in range(walls):
        sums[lax.rem(me + walls - n, walls)] = received[n][...]

    def coef(k, n):
        start = 2 * lines + n * planes
        return sums[k, start : start + planes, :]

    def wide(value):
        return jnp.concatenate([value] * components, 0)

    d = jnp.ones((planes, across), jnp.float32)
    value = jnp.zeros((lines, across), jnp.float32)
    values, ratios = [], []
    for k in range(walls):
        low, own, up = coef(k, 0), coef(k, 1), coef(k, 2)
        right = sums[k, :lines, :]
        if k + 1 < walls:
            high = up * coef(k + 1, 4)
            killing = own + up * coef(k + 1, 3)
            right = right + wide(up) * sums[k + 1, lines : 2 * lines, :]
        else:
            high = jnp.zeros_like(up)
            killing = own + up
        e = killing + low * d
        inverse = reciprocal(high + e)
        d = e * inverse
        value = (right + wide(low) * value) * wide(inverse)
        values.append(value)
        ratios.append(wide(high * inverse))
    tops[0] = jnp.zeros((lines, across), jnp.float32)
    tops[walls] = values[-1]
    for k in reversed(range(walls - 1)):
        values[k] = values[k] + ratios[k] * values[k + 1]
        tops[k + 1] = values[k]

    def row(s):
        return pl.ds(s, lines, stride=knots)

    run = tops[me]
    before[row(0), :] = run
    found = []
    for s in range(knots - 1):
        run = reduced[row(s), :] * wide(inner[0, s]) + wide(inner[1, s]) * run
        found.append(run)
    run = tops[me + 1]
    after[row(knots - 1), :] = run
    for s in reversed(range(knots - 1)):
        run = found[s] + wide(inner[2, s]) * run
        after[row(s), :] = run
        if s + 1 < segments:
            before[row(s + 1), :] = run

    def put(c, x, t, value):
        out[c, x, pl.ds(t, segments, stride=steps), :] = value

    copies = []
    half = planes
    for start in range(0, planes, half):
        part = [(c, x) for c in range(components) for x in range(start, start + half)]
        bottoms, starts = [], []
        for c, x in part:
            base = (c * planes + x) * knots
            bottoms.append(before[base : base + segments, :])
            starts.append(after[base : base + segments, :])
            out[c, x, height - rest :, :] = after[base + segments : base + knots, :]
            put(c, x, last, starts[-1])

        def backward(n, values):
            t = last - 1 - n
            found = []
            for (c, x), value, bottom in zip(part, values, bottoms):
                value = (swept[t, c, x] + prefix[t, x] * bottom) + ratio[t, x] * value
                put(c, x, t, value)
                found.append(value)
            return tuple(found)

        lax.fori_loop(0, last, backward, tuple(starts), unroll=10)
        for here in part:
            copy = pltpu.make_async_copy(out.at[here], out_hbm.at[here], sems.at[here])
            copy.start()
            copies.append(copy)
    wait_all(copies)


def shifted(block, axis, distance):
    length = lax.axis_size(axis)
    route = [(i, (i + distance) % length) for i in range(length)]
    return lax.ppermute(block, axis, route)


def everyone(block, axis):
    return [block] + [shifted(block, axis, n) for n in range(1, lax.axis_size(axis))]


def local(velocity, lower_weight, upper_weight, forces, cells, counts):
    components, planes, height, across = velocity.shape
    receivers, capacity = forces.shape[3], forces.shape[5]
    senders = cells.shape[2]
    walls = lax.axis_size("wall")
    lines = components * planes
    chunks = capacity // lanes
    counts_shape = (planes, senders)
    forces = forces.reshape(components, receivers, planes, capacity)
    cells = cells.reshape(senders, planes, capacity)
    counts = counts.reshape(senders, planes).T

    def hbm(*arrays):
        return [pltpu.with_memory_space_constraint(array, pltpu.HBM) for array in arrays]

    work_shape = (planes * (senders * chunks + group) + 4 * group,)
    send, lower_near, upper_near, velocity_near, work = call(
        load_kernel,
        (
            pltpu.HBM((receivers, components, planes, capacity), jnp.float32),
            f32(*lower_weight.shape),
            f32(*upper_weight.shape),
            f32(*velocity.shape),
            jax.ShapeDtypeStruct(work_shape, jnp.int32),
        ),
        (in_hbm, *[in_vmem] * 4),
        [in_hbm] * 5,
        [
            scratch(*forces.shape),
            pltpu.SMEM(counts_shape, jnp.int32),
            pltpu.SMEM(work_shape, jnp.int32),
            pltpu.SemaphoreType.DMA((3 * components + 4,)),
        ],
        4,
        1 << 16,
    )(*hbm(forces, velocity, lower_weight, upper_weight, counts))
    got = lax.all_to_all(send, "span", 0, 0, tiled=True)
    got = got.reshape(senders, components, planes, chunks, lanes).transpose(0, 1, 3, 2, 4)
    cells = cells.reshape(senders, planes, chunks, lanes).transpose(0, 2, 1, 3)
    edge_shape = (lines * height // lanes, lanes)
    first_column, last_column = call(
        edge_kernel,
        (f32(*edge_shape), f32(*edge_shape)),
        (in_vmem, in_vmem),
        [in_vmem],
        [scratch(height, across), scratch(height // lanes, lanes, lanes)],
        4,
        1 << 20,
    )(velocity_near)
    from_above = shifted(first_column, "span", -1)
    from_below = shifted(last_column, "span", 1)

    steps = height // segments - 1
    knots = height - segments * steps + segments
    step_shape = (steps - 1, planes, segments, across)
    staged = [velocity.shape, step_shape, step_shape]
    prepared = call(
        prepare_kernel,
        (
            f32(3, knots - 1, planes, across),
            f32(4, planes, knots, across),
            f32(5 * planes, across),
            *[pltpu.HBM(shape, jnp.float32) for shape in staged],
        ),
        [in_vmem] * 3 + [in_hbm] * 3,
        [in_vmem] * 3,
        [
            *[scratch(*shape) for shape in staged],
            scratch(*step_shape),
            scratch(*step_shape),
            scratch(7, planes * knots, across),
            pltpu.SemaphoreType.DMA((3,)),
        ],
        12,
        1 << 24,
    )(velocity_near, lower_near, upper_near)
    (inner, ends, coefs, rhs_start, inv, first) = prepared

    sum_rows = -(-(2 * lines + 5 * planes) // 8) * 8
    wide = 2 * components * across
    total = call(
        scatter_kernel,
        f32(planes, height, wide),
        in_vmem,
        [in_vmem] * 4,
        [
            pltpu.SMEM(work_shape, jnp.int32),
            [pltpu.VMEM((height, group * lanes), jnp.bfloat16)] * 2,
            [pltpu.VMEM((wide, group * lanes), jnp.bfloat16)] * 2,
            pltpu.SemaphoreType.DMA,
        ],
        16,
        1 << 32,
    )(got, cells, work, coefs)

    deposit, swept, prefix, ratio, reduced, sums = call(
        sweep_kernel,
        (
            jax.ShapeDtypeStruct(velocity.shape, jnp.bfloat16),
            f32(steps - 1, components, planes, segments, across),
            f32(*step_shape),
            f32(*step_shape),
            f32(lines * knots, across),
            f32(sum_rows, across),
        ),
        (in_hbm, *[in_vmem] * 5),
        [in_vmem] * 10,
        [
            scratch(*velocity.shape),
            pltpu.VMEM(velocity.shape, jnp.bfloat16),
            scratch(height // lanes, lanes, lanes),
            scratch(height, lanes),
            pltpu.SemaphoreType.DMA((components, planes)),
        ],
        8,
        1 << 24,
    )(
        total,
        from_above,
        from_below,
        rhs_start,
        inv,
        first,
        lower_weight,
        upper_weight,
        ends,
        coefs,
    )
    all_sums = everyone(sums, "wall")

    velocity_next = call(
        finish_kernel,
        f32(*velocity.shape),
        in_hbm,
        [in_vmem] * (5 + walls),
        [
            scratch(walls, sum_rows, across),
            scratch(walls + 1, lines, across),
            scratch(lines * knots, across),
            scratch(lines * knots, across),
            scratch(*velocity.shape),
            pltpu.SemaphoreType.DMA((components, planes)),
        ],
        8,
        1 << 22,
    )(inner, reduced, swept, ratio, prefix, *all_sums)
    return (velocity_next, deposit)


def solution(mesh):
    placed = (
        P(None, None, "wall", "span"),
        P(None, "wall", "span"),
        P(None, "wall", "span"),
        P(None, "wall", "span", None, None, None),
        P("wall", "span", None, None, None),
        P("wall", "span", None, None),
    )
    return jax.shard_map(
        local,
        mesh=mesh,
        in_specs=placed,
        out_specs=(P(None, None, "wall", "span"), P(None, None, "wall", "span")),
        check_vma=False,
    )
```
